32 devices in a mesh: section: 2 (over core), dp: 4 (over y, x), mp: 4 (over z).
Axes of the slice: x: 2, y: 2, z: 4, core: 2. Of those that a mesh axis runs over, the one named last changes fastest.
Arguments:
- tokens: bfloat16 [2, 4, 1024, 1024], P(None, 'dp', 'mp'), may hold values from -6 to 6
- cotangent: bfloat16 [2, 4, 1024, 1024], P(None, 'dp', 'mp'), may hold values from -6 to 6
- lengths: int32 [2, 4], P(None, 'dp'), may hold values from 128 to 1024, as said below
- gain_attn: float32 [2, 1024], P('section'), may hold values from 0.5 to 1.5
- w_qkv: bfloat16 [2, 3, 1024, 1024], P('section', None, 'mp'), may hold values from -0.1875 to 0.1875
- w_out: bfloat16 [2, 1024, 1024], P('section', 'mp'), may hold values from -3 to 3
- gain_ffn: float32 [2, 1024], P('section'), may hold values from 0.5 to 1.5
- w_gate_up: bfloat16 [2, 2, 2816, 1024], P('section', None, 'mp'), may hold values from -0.1875 to 0.1875
- w_down: bfloat16 [2, 2816, 1024], P('section', 'mp'), may hold values from -0.109375 to 0.109375
Outputs:
- layer_out: bfloat16 [2, 2, 4, 1024, 1024], P('section', None, 'dp', 'mp')
- input_grads: float32 [2, 2, 4, 1024, 1024], P('section', None, 'dp', 'mp')
- grad_gain_attn: float32 [2, 1024], P('section')
- grad_w_qkv: float32 [2, 3, 1024, 1024], P('section', None, 'mp')
- grad_w_out: float32 [2, 1024, 1024], P('section', 'mp')
- grad_gain_ffn: float32 [2, 1024], P('section')
- grad_w_gate_up: float32 [2, 2, 2816, 1024], P('section', None, 'mp')
- grad_w_down: float32 [2, 2816, 1024], P('section', 'mp')
- value_norms: float32 [2], P('section')
The draws below stay inside these ranges and needn't reach their ends.
Inputs may be any that keep to these rules, and one draw needn't show every extreme that they name: `lengths`: each length lies in 128 to 1024; for every index of dp, one of the 2 x 1 slots it holds has length 1024, which one drawn from the seed.
All inputs are finite; a program needn't handle non-finite values.
Results may differ from the reference program's by a relative error of at most 0.025.
Values may be sent and summed in bfloat16 or wider, within the bound.
A program may use at most 256 MiB of HBM per device.

```python
import jax
import jax.numpy as jnp
from jax import lax

D = 1024
H = 16
HD = 64
FF = 2816
SLOT = 1024
LEAST = 128
MB = 2
SEQ_DP = 1
SEQS = 4


def draw_lengths(key, part):
    key = jax.random.fold_in(key, 11)
    base = jax.random.randint(jax.random.fold_in(key, 1), (MB, SEQS), LEAST, SLOT + 1)
    groups = SEQS // SEQ_DP
    pick = jax.random.randint(jax.random.fold_in(key, 2), (groups,), 0, MB * SEQ_DP)
    slot_batch = jnp.arange(MB, dtype=jnp.int32)[:, None]
    slot_seq = jnp.arange(SEQS, dtype=jnp.int32)[None, :]
    within = slot_batch * SEQ_DP + slot_seq % SEQ_DP
    chosen = within == pick[slot_seq // SEQ_DP]
    return jnp.where(chosen, SLOT, base).astype(jnp.int32)


def block_scale(rng, shape, cuts, least, largest):
    level = 1.0
    for dim, parts in cuts:
        steps = jax.random.uniform(jax.random.fold_in(jax.random.fold_in(rng, 6), dim), (parts,), jnp.float32, least / len(cuts), largest / len(cuts))
        level = level * jnp.repeat(jnp.exp(steps), shape[dim] // parts).reshape((-1,) + (1,) * (len(shape) - 1 - dim))
    return level


def gaussian(own_key, shape, spread, limit, shards=(), kind=jnp.bfloat16):
    drawn = spread * jax.random.normal(own_key, shape, jnp.float32)
    if shards:
        drawn = drawn * block_scale(own_key, shape, shards, -0.22, 0.18)
    return jnp.clip(drawn, -limit, limit).astype(kind)


def setup_inputs(seed: int = 0) -> dict:
    seeds = jax.random.split(jax.random.key(seed), 10)
    tokens = gaussian(seeds[0], (MB, SEQS, SLOT, D), 1.0, 6.0, ((1, 4), (2, 4)))
    cotangent = gaussian(seeds[1], (MB, SEQS, SLOT, D), 1.0, 6.0, ((1, 4), (2, 4)))
    lengths = draw_lengths(jax.random.fold_in(seeds[9], 71), 0)
    gain_attn = jnp.clip(1.0 + 0.1 * jax.random.normal(seeds[3], (2, D), jnp.float32), 0.5, 1.5)
    w_qkv = gaussian(seeds[4], (2, 3, D, D), D ** -0.5, 0.1875, ((0, 2), (2, 4)))
    w_out = gaussian(seeds[5], (2, D, D), (max(4 * D // SLOT, 1)) ** -0.5, 3.0, ((0, 2), (1, 4)))
    gain_ffn = jnp.clip(1.0 + 0.1 * jax.random.normal(seeds[6], (2, D), jnp.float32), 0.5, 1.5)
    w_gate_up = gaussian(seeds[7], (2, 2, FF, D), D ** -0.5, 0.1875, ((0, 2), (2, 4)))
    w_down = gaussian(seeds[8], (2, FF, D), FF ** -0.5, 0.109375, ((0, 2), (1, 4)))
    return dict(tokens=tokens, cotangent=cotangent, lengths=lengths, gain_attn=gain_attn, w_qkv=w_qkv, w_out=w_out, gain_ffn=gain_ffn, w_gate_up=w_gate_up, w_down=w_down)


EPSILON = 1e-05
ROPE_BASE = 10000.0
NEG_LARGE = -1e+30
HIGHEST = lax.Precision.HIGHEST

@jax.custom_vjp
def low(v):
    return lax.optimization_barrier(v.astype(jnp.bfloat16)).astype(jnp.float32)

@jax.custom_vjp
def low_back(v):
    return v

def low_keep(v):
    return (low(v), None)

def low_pass(kept, grad):
    return (grad,)

def back_keep(v):
    return (v, None)

def back_low(kept, grad):
    return (low(grad),)
low.defvjp(low_keep, low_pass)
low_back.defvjp(back_keep, back_low)

def rope_tables(span):
    position = jnp.arange(span, dtype=jnp.float32)
    freqs = ROPE_BASE ** (-jnp.arange(0, HD, 2, dtype=jnp.float32) / HD)
    angle = position[:, None] * freqs[None, :]
    cosine = jnp.concatenate([jnp.cos(angle), jnp.cos(angle)], -1)
    sine = jnp.concatenate([jnp.sin(angle), jnp.sin(angle)], -1)
    return (cosine, sine)

def rotate(values):
    half = HD // 2
    return jnp.concatenate([-values[..., half:], values[..., :half]], -1)

def apply_rope(values, cosine, sine):
    return values * cosine[:, None, :] + rotate(values) * sine[:, None, :]

def attend(query, keys, mixed, length):
    block = min(512, SLOT)
    count_blocks = SLOT // block
    scale = HD ** (-0.5)
    key_pos = jnp.arange(SLOT, dtype=jnp.int32)

    def one_block(item):
        rows, start = item
        scores = low_back(jnp.einsum('qhd,khd->hqk', rows, keys, precision=HIGHEST) * scale)
        query_pos = start + jnp.arange(block, dtype=jnp.int32)
        allowed = (key_pos[None, :] <= query_pos[:, None]) & (key_pos[None, :] < length)
        scores = jnp.where(allowed[None], scores, NEG_LARGE)
        soft = low(jax.nn.softmax(scores, axis=-1))
        return jnp.einsum('hqk,khd->qhd', soft, mixed, precision=HIGHEST)
    starts = jnp.arange(count_blocks, dtype=jnp.int32) * block
    result = lax.map(jax.checkpoint(one_block), (query.reshape(count_blocks, block, H, HD), starts))
    return result.reshape(SLOT, H, HD)

def layer(activations, length, gain_one, projection_weight, output_weight, gain_two, pair_weight, lower_weight, first_values):
    cosine, sine = rope_tables(SLOT)
    first_scale = lax.rsqrt(lax.optimization_barrier(jnp.mean(activations * activations, -1, keepdims=True)) + EPSILON)
    normed = low(activations * first_scale * gain_one)
    projected = low_back(jnp.einsum('ld,tcd->ltc', normed, projection_weight, precision=HIGHEST))
    shape = (SLOT, H, HD)
    query = low(apply_rope(projected[:, 0].reshape(shape), cosine, sine))
    keys = low(apply_rope(projected[:, 1].reshape(shape), cosine, sine))
    values = low(projected[:, 2])
    partner = values if first_values is None else first_values
    mixed = low(0.5 * values + 0.5 * partner)
    attended = low_back(low(attend(query, keys, mixed.reshape(shape), length).reshape(SLOT, D)))
    middle = activations + low_back(jnp.dot(attended, output_weight, precision=HIGHEST))
    second_scale = lax.rsqrt(lax.optimization_barrier(jnp.mean(middle * middle, -1, keepdims=True)) + EPSILON)
    normed_two = low(middle * second_scale * gain_two)
    gate_up = low_back(jnp.einsum('ld,tfd->ltf', normed_two, pair_weight, precision=HIGHEST))
    hidden_state = low(jax.nn.silu(gate_up[:, 0]) * gate_up[:, 1])
    result = middle + low_back(jnp.dot(hidden_state, lower_weight, precision=HIGHEST))
    live = jnp.arange(SLOT, dtype=jnp.int32) < length
    square = jnp.sum(jnp.where(live[:, None], mixed * mixed, 0.0))
    return (result, values, square)

def pair(rows, probe, length, weights):
    gain_one, projection_weight, output_weight, gain_two, pair_weight, lower_weight = weights
    first_out, first_values, square_one = layer(rows, length, gain_one[0], projection_weight[0], output_weight[0], gain_two[0], pair_weight[0], lower_weight[0], None)
    second_in = low(low_back(first_out)) + probe
    second_out, unused, square_two = layer(second_in, length, gain_one[1], projection_weight[1], output_weight[1], gain_two[1], pair_weight[1], lower_weight[1], low_back(first_values))
    return (second_out, (first_out, square_one, square_two))

def reference(tokens, cotangent, lengths, gain_attn, w_qkv, w_out, gain_ffn, w_gate_up, w_down):
    params = tuple((a.astype(jnp.float32) for a in (gain_attn, w_qkv, w_out, gain_ffn, w_gate_up, w_down)))
    items = MB * SEQS
    flat_in = tokens.reshape(items, SLOT, D)
    flat_cot = cotangent.reshape(items, SLOT, D)
    flat_len = lengths.reshape(items).astype(jnp.int32)

    def step(sums, item):
        rows, upstream, length = item

        def whole(rows_float, probe, gain_one, projection_weight, output_weight, gain_two, pair_weight, lower_weight):
            return pair(rows_float, probe, length, (gain_one, projection_weight, output_weight, gain_two, pair_weight, lower_weight))
        rows_float = rows.astype(jnp.float32)
        output, pullback, extras = jax.vjp(whole, rows_float, jnp.zeros_like(rows_float), *params, has_aux=True)
        grads = pullback(upstream.astype(jnp.float32))
        sums = tuple((a + b for a, b in zip(sums, grads[2:])))
        first_out, square_one, square_two = extras
        return (sums, (first_out.astype(jnp.bfloat16), output.astype(jnp.bfloat16), grads[0], grads[1], square_one, square_two))
    zeros = tuple((jnp.zeros_like(a) for a in params))
    sums, outs = lax.scan(step, zeros, (flat_in, flat_cot, flat_len))
    shape = (MB, SEQS, SLOT, D)
    layer_out = jnp.stack([outs[0].reshape(shape), outs[1].reshape(shape)])
    input_grads = jnp.stack([outs[2].reshape(shape), outs[3].reshape(shape)])
    count = jnp.sum(lengths.astype(jnp.float32)) * D
    value_norms = jnp.sqrt(jnp.stack([jnp.sum(outs[4]), jnp.sum(outs[5])]) / count)
    return (layer_out, input_grads, sums[0], sums[1], sums[2], sums[3], sums[4], sums[5], value_norms)
```

```python
import functools

import jax
import jax.numpy as jnp
from jax import lax
from jax.experimental import pallas as pl
from jax.experimental.pallas import tpu as pltpu
from jax.sharding import PartitionSpec as P

HD = 64
EPSILON = 1e-05
ROPE_BASE = 10000.0
NEG_LARGE = -1e30
MESH = pl.DeviceIdType.MESH
F32 = jnp.float32
LOW = jnp.bfloat16
VMEM_BYTES = 56 << 20


def mm(a, b):
    return lax.dot_general(a, b, (((1,), (0,)), ((), ())), preferred_element_type=F32)


def mm_nt(a, b):
    return lax.dot_general(a, b, (((1,), (1,)), ((), ())), preferred_element_type=F32)


def mm_tn(a, b):
    return lax.dot_general(a, b, (((0,), (0,)), ((), ())), preferred_element_type=F32)


class Team:
    def __init__(self, chips):
        self.chips = chips
        self.core = lax.axis_index("section")
        self.group = lax.axis_index("dp")
        self.along = lax.axis_index("mp")
        self.half = self.along // chips
        self.seat = self.along % chips

    def chip(self, offset):
        return (self.seat + offset) % self.chips

    def sibling(self):
        return (1 - self.core, self.group, self.along)

    def peer(self, offset):
        return (self.core, self.group, self.half * self.chips + self.chip(offset))

    def mine(self, offset):
        return self.chip(offset) + self.core * self.chips

    def other(self, offset):
        return self.chip(offset) + (1 - self.core) * self.chips

    def enter(self):
        barrier = pltpu.get_barrier_semaphore()
        partners = [self.sibling()] + [self.peer(o) for o in range(1, self.chips)]
        for device in partners:
            pl.semaphore_signal(barrier, inc=1, device_id=device, device_id_type=MESH)
        pl.semaphore_wait(barrier, len(partners))


def remote(src, dst, send, recv, device):
    return pltpu.make_async_remote_copy(
        src_ref=src, dst_ref=dst, send_sem=send, recv_sem=recv, device_id=device, device_id_type=MESH
    )


def block(rank, rows):
    return pl.ds(pl.multiple_of(rank * rows, rows), rows)


class Gather:
    def __init__(self, team, buf, rows, send, recv):
        self.team, self.buf, self.rows, self.send, self.recv = team, buf, rows, send, recv
        self.started = []

    def _copy(self, rank, slot, device):
        part = self.buf.at[block(rank, self.rows)]
        return remote(part, part, self.send.at[slot], self.recv.at[slot], device)

    def start(self):
        team = self.team
        for o in range(1, team.chips):
            self.started.append(self._copy(team.mine(0), o, team.peer(o)))
        self.started.append(self._copy(team.mine(0), 0, team.sibling()))
        for copy in self.started:
            copy.start()

    def arrivals(self):
        team = self.team
        yield True, 0
        self._copy(team.other(0), 0, team.sibling()).wait_recv()
        yield False, 0
        for o in range(1, team.chips):
            back = team.chips - o
            self._copy(team.mine(back), o, team.peer(back)).wait_recv()
            forward = self._copy(team.mine(back), team.chips - 1 + o, team.sibling())
            forward.start()
            self.started.append(forward)
            yield True, back
            self._copy(team.other(back), team.chips - 1 + o, team.sibling()).wait_recv()
            yield False, back

    def finish(self):
        for copy in self.started:
            copy.wait_send()


class Reduce:
    def __init__(self, team, rows, scratch):
        self.team, self.rows = team, rows
        (self.out, self.held, self.into, self.leave, self.land, self.own, self.xs, self.xr, self.us, self.ur) = scratch
        self.started = []

    def put_other(self, o, value):
        self.out[o] = value.astype(LOW)
        copy = remote(self.out.at[o], self.into.at[o], self.xs.at[o], self.xr.at[o], self.team.sibling())
        copy.start()
        self.started.append(copy)

    def put_mine(self, o, value):
        if o == 0:
            self.own[...] = value
        else:
            self.held[...] = value

    def pass_on(self, o):
        remote(self.out.at[o], self.into.at[o], self.xs.at[o], self.xr.at[o], self.team.sibling()).wait_recv()
        self.leave[o - 1] = (self.held[...] + self.into[o].astype(F32)).astype(LOW)
        copy = remote(
            self.leave.at[o - 1], self.land.at[o - 1], self.us.at[o - 1], self.ur.at[o - 1], self.team.peer(o)
        )
        copy.start()
        self.started.append(copy)

    def finish(self):
        remote(self.out.at[0], self.into.at[0], self.xs.at[0], self.xr.at[0], self.team.sibling()).wait_recv()
        for o in range(1, self.team.chips):
            remote(
                self.leave.at[o - 1], self.land.at[o - 1], self.us.at[o - 1], self.ur.at[o - 1], self.team.peer(o)
            ).wait_recv()
        for copy in self.started:
            copy.wait_send()

    def total(self, rows):
        total = self.own[rows] + self.into[0, rows].astype(F32)
        for o in range(self.team.chips - 1):
            total = total + self.land[o, rows].astype(F32)
        return total


def gather_scratch(chips):
    return [pltpu.SemaphoreType.DMA((2 * chips - 1,)), pltpu.SemaphoreType.DMA((2 * chips - 1,))]


def reduce_scratch(chips, rows, width):
    return [
        pltpu.VMEM((chips, rows, width), LOW),
        pltpu.VMEM((rows, width), F32),
        pltpu.VMEM((chips, rows, width), LOW),
        pltpu.VMEM((chips - 1, rows, width), LOW),
        pltpu.VMEM((chips - 1, rows, width), LOW),
        pltpu.VMEM((rows, width), F32),
        pltpu.SemaphoreType.DMA((chips,)),
        pltpu.SemaphoreType.DMA((chips,)),
        pltpu.SemaphoreType.DMA((chips - 1,)),
        pltpu.SemaphoreType.DMA((chips - 1,)),
    ]


N_REDUCE = 10


def by_rows(rows, body):
    step = min(32, rows)

    @pl.loop(0, rows // step)
    def _(i):
        body(pl.ds(pl.multiple_of(i * step, step), step))


def swap_halves(u):
    columns, half = u.shape[1], HD // 2
    if columns % 128:
        parts = []
        for at in range(0, columns, HD):
            parts += [u[:, at + half : at + HD], u[:, at : at + half]]
        return jnp.concatenate(parts, 1)
    lane = lax.broadcasted_iota(jnp.int32, u.shape, 1)
    return jnp.where(lane % HD < half, pltpu.roll(u, columns - half, 1), pltpu.roll(u, half, 1))


def head_row(columns, head):
    lane = lax.broadcasted_iota(jnp.int32, (1, columns), 1)
    return (lane // HD == head).astype(F32).astype(LOW)


def norm_into(buf, at, rows, read, gain_ref):
    step = min(32, rows)

    @pl.loop(0, rows // step)
    def _(i):
        values = read(pl.ds(pl.multiple_of(i * step, step), step))
        scale = lax.rsqrt(jnp.mean(values * values, -1, keepdims=True) + EPSILON)
        buf[pl.ds(pl.multiple_of(at + i * step, step), step)] = (values * scale * gain_ref[...]).astype(LOW)


def norm_back(rows, read_values, read_grad, gain_ref, read_outer, write, gain_grad_ref):
    gain_grad_ref[...] = jnp.zeros_like(gain_grad_ref)

    def body(sl):
        values = read_values(sl)
        scale = lax.rsqrt(jnp.mean(values * values, -1, keepdims=True) + EPSILON)
        unit = values * scale
        grad = read_grad(sl)
        gain_grad_ref[...] += jnp.sum(grad * unit, 0, keepdims=True)
        inner = grad * gain_ref[...]
        write(sl, read_outer(sl) + scale * (inner - unit * jnp.mean(inner * unit, -1, keepdims=True)))

    by_rows(rows, body)


def attend_kernel(chips, first, *refs):
    refs = list(refs)
    x_ref, gain_ref, w_ref, cos_ref, sin_ref, bias_ref = refs[:6]
    refs = refs[6:]
    before_ref = None if first else refs.pop(0)
    x1_ref, h_out, q_ref, k_ref, m_ref, o_ref, log_ref = refs[:7]
    h_ref, keep_sem, gs, gr = refs[7:11]
    team = Team(chips)
    rows, span = x_ref.shape[0], h_ref.shape[0]
    columns = w_ref.shape[0] // 4
    heads = columns // HD
    team.enter()
    norm_into(h_ref, team.mine(0) * rows, rows, lambda sl: x_ref[sl].astype(F32), gain_ref)
    gather = Gather(team, h_ref, rows, gs, gr)
    gather.start()
    for own, o in gather.arrivals():
        sl = block(team.mine(o) if own else team.other(o), rows)
        normed = h_ref[sl]
        cosine, sine = cos_ref[sl], sin_ref[sl]
        u = mm_nt(normed, w_ref[0:columns])
        q_ref[sl] = (u * cosine + swap_halves(u) * sine).astype(LOW) * jnp.asarray(HD**-0.5, LOW)
        u = mm_nt(normed, w_ref[columns : 2 * columns])
        k_ref[sl] = (u * cosine + swap_halves(u) * sine).astype(LOW)
        v = mm_nt(normed, w_ref[2 * columns : 3 * columns]).astype(LOW)
        m_ref[sl] = v if first else (0.5 * v.astype(F32) + 0.5 * before_ref[sl].astype(F32)).astype(LOW)
    keep = pltpu.make_async_copy(h_ref, h_out, keep_sem)
    keep.start()

    size = min(256, span)
    lanes = 128
    for qb in range(span // size):
        upto = (qb + 1) * size
        at = slice(qb * size, upto)

        def one_head(head, carry):
            out, logs = carry
            mask = head_row(columns, head)
            scores = mm_nt(q_ref[at] * mask, k_ref[0:upto]) + bias_ref[:, 0:upto]
            row = lax.broadcasted_iota(jnp.int32, scores.shape, 0) + qb * size
            column = lax.broadcasted_iota(jnp.int32, scores.shape, 1)
            scores = jnp.where(column <= row, scores, NEG_LARGE)
            peak = jnp.max(scores, -1, keepdims=True)
            weights = jnp.exp(scores - peak)
            total = jnp.sum(weights, -1, keepdims=True)
            part = mm(weights.astype(LOW), m_ref[0:upto])
            out = out + part * (mask.astype(F32) * (1.0 / total))
            lane = lax.broadcasted_iota(jnp.int32, logs.shape, 1)
            logs = jnp.where(lane == head, peak + jnp.log(total), logs)
            return out, logs

        out, logs = lax.fori_loop(
            0, heads, one_head, (jnp.zeros((size, columns), F32), jnp.zeros((size, lanes), F32))
        )
        o_ref[at] = out.astype(LOW)
        log_ref[:, at] = jnp.transpose(logs)[0 : log_ref.shape[0]]

    reduce = Reduce(team, rows, refs[11:])

    def part(rank):
        return mm(o_ref[block(rank, rows)], w_ref[3 * columns : 4 * columns])

    for o in range(1, chips):
        reduce.put_other(o, part(team.other(o)))
    for o in range(1, chips):
        reduce.put_mine(o, part(team.mine(o)))
        reduce.pass_on(o)
    reduce.put_other(0, part(team.other(0)))
    reduce.put_mine(0, part(team.mine(0)))
    reduce.finish()

    def close(sl):
        x1_ref[sl] = x_ref[sl].astype(F32) + reduce.total(sl)

    by_rows(rows, close)
    gather.finish()
    keep.wait()


def feed_kernel(chips, x1_ref, gain_ref, w_ref, y_ref, h_out, gate_ref, up_ref, z_ref, h_ref, keep_sem, gs, gr, *scratch):
    team = Team(chips)
    rows = x1_ref.shape[0]
    hidden = w_ref.shape[0] // 3
    team.enter()
    norm_into(h_ref, team.mine(0) * rows, rows, lambda sl: x1_ref[sl], gain_ref)
    gather = Gather(team, h_ref, rows, gs, gr)
    reduce = Reduce(team, rows, scratch)
    gather.start()
    for own, o in gather.arrivals():
        sl = block(team.mine(o) if own else team.other(o), rows)
        normed = h_ref[sl]
        gate = mm_nt(normed, w_ref[0:hidden])
        up = mm_nt(normed, w_ref[hidden : 2 * hidden])
        gate_ref[sl] = gate.astype(LOW)
        up_ref[sl] = up.astype(LOW)
        z_ref[sl] = (gate / (1.0 + jnp.exp(-gate)) * up).astype(LOW)
        value = mm(z_ref[sl], w_ref[2 * hidden : 3 * hidden])
        if own:
            reduce.put_mine(o, value)
        else:
            reduce.put_other(o, value)
            if o:
                reduce.pass_on(o)
    keep = pltpu.make_async_copy(h_ref, h_out, keep_sem)
    keep.start()
    reduce.finish()

    def close(sl):
        y_ref[sl] = (x1_ref[sl] + reduce.total(sl)).astype(LOW)

    by_rows(rows, close)
    gather.finish()
    keep.wait()


def columns_of(width):
    step = min(256, width)
    return [slice(at, at + step) for at in range(0, width, step)]


def feed_back_kernel(
    chips, g_ref, x1_ref, gain_ref, w_ref, h_ref, gate_ref, up_ref, z_ref,
    dx1_ref, gain_grad_ref, w_grad_ref, grad_ref, dgate_ref, dup_ref, gs, gr, *scratch,
):
    team = Team(chips)
    rows, width = g_ref.shape
    hidden = w_ref.shape[0] // 3
    team.enter()
    grad_ref[block(team.mine(0), rows)] = g_ref[...]
    gather = Gather(team, grad_ref, rows, gs, gr)
    reduce = Reduce(team, rows, scratch)
    gather.start()
    for own, o in gather.arrivals():
        sl = block(team.mine(o) if own else team.other(o), rows)
        dz = mm_nt(grad_ref[sl], w_ref[2 * hidden : 3 * hidden])
        gate = gate_ref[sl].astype(F32)
        sigma = 1.0 / (1.0 + jnp.exp(-gate))
        dgate_ref[sl] = (dz * up_ref[sl].astype(F32) * sigma * (1.0 + gate * (1.0 - sigma))).astype(LOW)
        dup_ref[sl] = (dz * gate * sigma).astype(LOW)
        value = mm(dgate_ref[sl], w_ref[0:hidden]) + mm(dup_ref[sl], w_ref[hidden : 2 * hidden])
        if own:
            reduce.put_mine(o, value)
        else:
            reduce.put_other(o, value)
            if o:
                reduce.pass_on(o)
    for at in columns_of(width):
        w_grad_ref[0:hidden, at] = mm_tn(dgate_ref[...], h_ref[:, at]).astype(LOW)
        w_grad_ref[hidden : 2 * hidden, at] = mm_tn(dup_ref[...], h_ref[:, at]).astype(LOW)
        w_grad_ref[2 * hidden : 3 * hidden, at] = mm_tn(z_ref[...], grad_ref[:, at]).astype(LOW)
    reduce.finish()

    def write(sl, value):
        dx1_ref[sl] = value

    norm_back(
        rows, lambda sl: x1_ref[sl], reduce.total, gain_ref, lambda sl: g_ref[sl].astype(F32), write, gain_grad_ref
    )
    gather.finish()


def attend_back_kernel(chips, last, *refs):
    refs = list(refs)
    dx1_ref, x_ref, gain_ref, w_ref, h_ref, q_ref, k_ref, m_ref, o_ref, log_ref, cos_ref, sin_ref, bias_ref = refs[:13]
    refs = refs[13:]
    value_grad_ref = None if last else refs.pop(0)
    grad_in_ref, gain_grad_ref, w_grad_ref = refs[:3]
    refs = refs[3:]
    value_sent_ref = refs.pop(0) if last else None
    grad_ref, do_ref, inner_ref, kt_ref, dm_ref, dk_ref, dq_ref, dqkv_ref, mask_ref, gs, gr = refs[:11]
    team = Team(chips)
    rows, width = dx1_ref.shape
    span, columns = q_ref.shape
    heads = columns // HD
    team.enter()
    at = team.mine(0) * rows

    def low_rows(sl):
        grad_ref[pl.ds(pl.multiple_of(at + sl.start, sl.size), sl.size)] = dx1_ref[sl].astype(LOW)

    by_rows(rows, low_rows)
    gather = Gather(team, grad_ref, rows, gs, gr)
    gather.start()
    kt_ref[...] = jnp.transpose(k_ref[...])
    dm_ref[...] = jnp.zeros_like(dm_ref)
    dk_ref[...] = jnp.zeros_like(dk_ref)
    dq_ref[...] = jnp.zeros_like(dq_ref)
    for own, o in gather.arrivals():
        sl = block(team.mine(o) if own else team.other(o), rows)
        do_ref[sl] = mm_nt(grad_ref[sl], w_ref[3 * columns : 4 * columns]).astype(LOW)
    for part in columns_of(width):
        w_grad_ref[3 * columns : 4 * columns, part] = mm_tn(o_ref[...], grad_ref[:, part]).astype(LOW)

    pad = inner_ref.shape[0]
    pick = (
        lax.broadcasted_iota(jnp.int32, (pad, columns), 1) // HD == lax.broadcasted_iota(jnp.int32, (pad, columns), 0)
    )
    pick = pick.astype(F32).astype(LOW)
    size = min(256, span)
    for b in range(span // size):
        sl = slice(b * size, (b + 1) * size)
        product = do_ref[sl].astype(F32) * o_ref[sl].astype(F32)
        high = product.astype(LOW)
        rest = (product - high.astype(F32)).astype(LOW)
        inner_ref[:, sl] = mm_nt(pick, high) + mm_nt(pick, rest)

    @pl.loop(0, span // size)
    def _(kb):
        ks = pl.ds(pl.multiple_of(kb * size, size), size)

        @pl.loop(kb, span // size)
        def _(qb):
            qs = pl.ds(pl.multiple_of(qb * size, size), size)
            key = lax.broadcasted_iota(jnp.int32, (size, size), 0) + kb * size
            query = lax.broadcasted_iota(jnp.int32, (size, size), 1) + qb * size
            mask_ref[...] = jnp.where(key <= query, 0.0, NEG_LARGE) + bias_ref[ks]
            for head in range(heads):
                mask = head_row(columns, head)
                q = q_ref[qs] * mask
                do = do_ref[qs] * mask
                soft = jnp.exp(mm_nt(k_ref[ks], q) + mask_ref[...] - log_ref[head : head + 1, qs])
                dsoft = mm_nt(m_ref[ks], do)
                ds = (soft * (dsoft - inner_ref[head : head + 1, qs])).astype(LOW)
                dm_ref[ks] += mm(soft.astype(LOW), do)
                dk_ref[ks] += mm(ds, q)
                lines = slice(head * HD, (head + 1) * HD)
                dq_ref[lines, qs] += mm(kt_ref[lines, ks], ds)

    for b in range(span // size):
        sl = slice(b * size, (b + 1) * size)
        cosine, sine = cos_ref[sl], sin_ref[sl]
        dq = jnp.transpose(dq_ref[:, sl]) * HD**-0.5
        dqkv_ref[0, sl] = (dq * cosine - swap_halves(dq) * sine).astype(LOW)
        dk = dk_ref[sl]
        dqkv_ref[1, sl] = (dk * cosine - swap_halves(dk) * sine).astype(LOW)
        if last:
            half = (0.5 * dm_ref[sl]).astype(LOW)
            dqkv_ref[2, sl] = half
            value_sent_ref[sl] = half
        else:
            dqkv_ref[2, sl] = (dm_ref[sl] + value_grad_ref[sl].astype(F32)).astype(LOW)

    reduce = Reduce(team, rows, refs[11:])

    def part(rank):
        sl = block(rank, rows)
        total = mm(dqkv_ref[0, sl], w_ref[0:columns])
        for t in (1, 2):
            total = total + mm(dqkv_ref[t, sl], w_ref[t * columns : (t + 1) * columns])
        return total

    for o in range(1, chips):
        reduce.put_other(o, part(team.other(o)))
    for o in range(1, chips):
        reduce.put_mine(o, part(team.mine(o)))
        reduce.pass_on(o)
    reduce.put_other(0, part(team.other(0)))
    reduce.put_mine(0, part(team.mine(0)))
    for piece in columns_of(width):
        for t in range(3):
            w_grad_ref[t * columns : (t + 1) * columns, piece] = mm_tn(dqkv_ref[t], h_ref[:, piece]).astype(LOW)
    reduce.finish()

    def write(sl, value):
        grad_in_ref[sl] = value

    norm_back(
        rows, lambda sl: x_ref[sl].astype(F32), reduce.total, gain_ref, lambda sl: dx1_ref[sl], write, gain_grad_ref
    )
    gather.finish()


def call(kernel, ident, flops, outs, scratch, *args):
    vmem = pl.BlockSpec(memory_space=pltpu.VMEM)
    moved = sum(a.size * a.dtype.itemsize for a in args)
    return pl.pallas_call(
        kernel,
        out_shape=[jax.ShapeDtypeStruct(shape, dtype) for shape, dtype, _ in outs],
        in_specs=[vmem] * len(args),
        out_specs=[vmem if inside else pl.BlockSpec(memory_space=pl.ANY) for _, _, inside in outs],
        scratch_shapes=scratch,
        cost_estimate=pl.CostEstimate(flops=flops, bytes_accessed=moved, transcendentals=0),
        compiler_params=pltpu.CompilerParams(
            collective_id=ident, has_side_effects=True, vmem_limit_bytes=VMEM_BYTES
        ),
    )(*args)


def rope_tables(span, columns):
    position = jnp.arange(span, dtype=F32)
    freqs = ROPE_BASE ** (-jnp.arange(0, HD, 2, dtype=F32) / HD)
    angle = position[:, None] * freqs[None, :]
    heads = columns // HD
    cosine = jnp.tile(jnp.concatenate([jnp.cos(angle), jnp.cos(angle)], -1), (1, heads))
    sine = jnp.tile(jnp.concatenate([-jnp.sin(angle), jnp.sin(angle)], -1), (1, heads))
    return cosine, sine


def local(tokens, cotangent, lengths, gain_attn, w_qkv, w_out, gain_ffn, w_gate_up, w_down):
    cores, groups, members = lax.axis_size("section"), lax.axis_size("dp"), lax.axis_size("mp")
    micro, sequences, rows, width = tokens.shape
    assert cores == 2 and micro == 2 and sequences == 1 and members % 2 == 0 and members >= 4
    chips = members // 2
    span = rows * members
    columns, hidden = w_out.shape[1], w_down.shape[1]
    padded = -(-(columns // HD) // 8) * 8
    core, along = lax.axis_index("section"), lax.axis_index("mp")
    half = along // chips
    home = core == half
    both = ("section", "mp")

    def device(c, m):
        return c * members + m

    def far(m):
        return (m + chips) % members

    def own_rows(blocks):
        pairs = [(device(1 - m // chips, far(m)), device(1 - m // chips, m)) for m in range(members)]
        came = lax.ppermute(jnp.where(core == 0, blocks[1, 0], blocks[0, 0]), both, pairs)
        return jnp.where(home, jnp.where(core == 0, blocks[0, 0], blocks[1, 0]), came)

    def share_weights(own):
        quarter = width // groups
        piece = lax.dynamic_slice_in_dim(own, lax.axis_index("dp") * quarter, quarter, 1)
        came = lax.ppermute(piece, "mp", [(m, far(m)) for m in range(members)])
        there = lax.all_gather(came, "dp", axis=1, tiled=True)
        swapped = lax.ppermute(jnp.where(home, there, own), "section", [(0, 1), (1, 0)])
        kept = jnp.where(home, own, there)
        return jnp.where(core == 0, kept, swapped), jnp.where(core == 0, swapped, kept)

    def share_gradient(layer, part):
        summed = lax.psum_scatter(part, "dp", scatter_dimension=1, tiled=True)
        pairs = [(device(m // chips, far(m)), device(layer, m)) for m in range(members)]
        away = lax.ppermute(summed, both, pairs)
        pairs = [(device(m // chips, m), device(layer, m)) for m in range(members) if m // chips != layer]
        near = lax.ppermute(summed, both, pairs)
        return away.astype(F32) + jnp.where(half == layer, summed, near).astype(F32)

    def placed(first, second):
        same = jnp.where(core == 0, first, second)
        cross = jnp.where(core == 0, second, first)
        pairs = [(device(m // chips, far(m)), device(m // chips, m)) for m in range(members)]
        from_far = lax.ppermute(same, both, pairs)
        pairs = [(device(m // chips, far(m)), device(1 - m // chips, m)) for m in range(members)]
        from_far_cross = lax.ppermute(cross, both, pairs)
        pairs = [(device(m // chips, m), device(1 - m // chips, m)) for m in range(members)]
        from_near = lax.ppermute(cross, both, pairs)
        here = jnp.where(home, same, from_near)
        there = jnp.where(home, from_far, from_far_cross)
        swap = half == 0
        return jnp.stack([jnp.where(swap, here, there), jnp.where(swap, there, here)])[:, None]

    x = own_rows(tokens)
    attn_weights = share_weights(jnp.concatenate([w_qkv[0].reshape(3 * columns, width), w_out[0]], 0))
    feed_weights = share_weights(jnp.concatenate([w_gate_up[0].reshape(2 * hidden, width), w_down[0]], 0))
    gains = lax.all_gather(jnp.stack([gain_attn[0], gain_ffn[0]]), "section")
    top = own_rows(cotangent)
    length = lax.dynamic_index_in_dim(lengths[:, 0], half, 0, keepdims=False)
    live = jnp.arange(span) < length
    bias = jnp.where(live, 0.0, NEG_LARGE).astype(F32)
    cosine, sine = rope_tables(span, columns)

    def vec(shape, dtype):
        return pltpu.VMEM(shape, dtype)

    inside, outside = True, False
    whole = (span, width)
    keep = [vec(whole, LOW), pltpu.SemaphoreType.DMA] + gather_scratch(chips)
    reducing = reduce_scratch(chips, rows, width)
    kept = []
    squares = []
    values = None
    for layer in range(2):
        gain = gains[layer, 0][None]
        args = [x, gain, attn_weights[layer], cosine, sine, bias[None]]
        if layer:
            args.append(values)
        x1, h, q, k, m, o, logs = call(
            functools.partial(attend_kernel, chips, layer == 0),
            layer,
            8 * span * width * columns + 4 * span * span * columns,
            [((rows, width), F32, inside), (whole, LOW, outside)]
            + [((span, columns), LOW, inside)] * 4
            + [((padded, span), F32, inside)],
            keep + reducing,
            *args,
        )
        if layer == 0:
            values = m
        squares.append(jnp.sum(jnp.where(live[:, None], jnp.square(m.astype(F32)), 0.0)))
        y, h2, gate, up, z = call(
            functools.partial(feed_kernel, chips),
            2,
            6 * span * width * hidden,
            [((rows, width), LOW, inside), (whole, LOW, outside)] + [((span, hidden), LOW, inside)] * 3,
            keep + reducing,
            x1,
            gains[layer, 1][None],
            feed_weights[layer],
        )
        kept.append((x, x1, h, q, k, m, o, logs, h2, gate, up, z, y))
        x = y

    grad, value_grad = top, None
    feed_grads, attn_grads, gain_grads, input_grads = [None] * 2, [None] * 2, [None] * 2, [None] * 2
    for layer in (1, 0):
        x, x1, h, q, k, m, o, logs, h2, gate, up, z, y = kept[layer]
        dx1, feed_gain, feed_part = call(
            functools.partial(feed_back_kernel, chips),
            3,
            12 * span * width * hidden,
            [((rows, width), F32, inside), ((1, width), F32, inside), ((3 * hidden, width), LOW, inside)],
            [vec(whole, LOW), vec((span, hidden), LOW), vec((span, hidden), LOW)] + gather_scratch(chips) + reducing,
            grad, x1, gains[layer, 1][None], feed_weights[layer], h2, gate, up, z,
        )
        feed_grads[layer] = share_gradient(layer, feed_part)
        args = [dx1, x, gains[layer, 0][None], attn_weights[layer], h, q, k, m, o, logs, cosine, sine, bias[:, None]]
        outs = [((rows, width), F32, inside), ((1, width), F32, inside), ((4 * columns, width), LOW, inside)]
        if layer:
            outs.append(((span, columns), LOW, inside))
        else:
            args.append(value_grad)
        size = min(256, span)
        results = call(
            functools.partial(attend_back_kernel, chips, layer == 1),
            4 + layer,
            16 * span * width * columns + 10 * span * span * columns,
            outs,
            [
                vec(whole, LOW), vec((span, columns), LOW), vec((padded, span), F32), vec((columns, span), LOW),
                vec((span, columns), F32), vec((span, columns), F32), vec((columns, span), F32),
                vec((3, span, columns), LOW), vec((size, size), F32),
            ] + gather_scratch(chips) + reducing,
            *args,
        )
        input_grads[layer], attn_gain, attn_part = results[:3]
        value_grad = results[3] if layer else None
        grad = input_grads[layer].astype(LOW)
        attn_grads[layer] = share_gradient(layer, attn_part)
        gain_grads[layer] = jnp.concatenate([attn_gain, feed_gain], 0)

    def own_layer(pair):
        return jnp.where(core == 0, pair[0], pair[1])

    def gathered(pair):
        return lax.all_gather(own_layer(pair).astype(LOW), "dp", axis=1, tiled=True).astype(F32)

    feed_sums, attn_sums = gathered(feed_grads), gathered(attn_grads)
    totals, roots, count = lax.psum(
        (jnp.stack(gain_grads), jnp.stack(squares), jnp.sum(lengths).astype(F32) / (cores * members)),
        ("section", "dp", "mp"),
    )
    gain_sums = own_layer(totals)
    return (
        placed(kept[0][-1], kept[1][-1])[None],
        placed(input_grads[0].astype(LOW), input_grads[1].astype(LOW)).astype(F32)[None],
        gain_sums[0:1],
        attn_sums[: 3 * columns].reshape(w_qkv.shape),
        attn_sums[3 * columns :][None],
        gain_sums[1:2],
        feed_sums[: 2 * hidden].reshape(w_gate_up.shape),
        feed_sums[2 * hidden :][None],
        jnp.sqrt(own_layer(roots) / (count * width)).reshape(1),
    )


def solution(mesh):
    return jax.shard_map(
        local,
        mesh=mesh,
        in_specs=(
            P(None, "dp", "mp", None),
            P(None, "dp", "mp", None),
            P(None, "dp"),
            P("section", None),
            P("section", None, "mp", None),
            P("section", "mp", None),
            P("section", None),
            P("section", None, "mp", None),
            P("section", "mp", None),
        ),
        out_specs=(
            P("section", None, "dp", "mp", None),
            P("section", None, "dp", "mp", None),
            P("section", None),
            P("section", None, "mp", None),
            P("section", "mp", None),
            P("section", None),
            P("section", None, "mp", None),
            P("section", "mp", None),
            P("section"),
        ),
        check_vma=False,
    )
```

```python
import functools

import jax
import jax.numpy as jnp
from jax import lax
from jax.experimental import pallas as pl
from jax.experimental.pallas import tpu as pltpu
from jax.sharding import PartitionSpec as P

HD = 64
EPSILON = 1e-05
ROPE_BASE = 10000.0
NEG_LARGE = -1e30
MESH = pl.DeviceIdType.MESH
F32 = jnp.float32
LOW = jnp.bfloat16
VMEM_BYTES = 56 << 20
WAITING = 12


def mm(a, b):
    return lax.dot_general(a, b, (((1,), (0,)), ((), ())), preferred_element_type=F32)


def mm_nt(a, b):
    return lax.dot_general(a, b, (((1,), (1,)), ((), ())), preferred_element_type=F32)


def mm_tn(a, b):
    return lax.dot_general(a, b, (((0,), (0,)), ((), ())), preferred_element_type=F32)


class Team:
    def __init__(self, chips):
        self.chips = chips
        self.groups = lax.axis_size("dp")
        self.core = lax.axis_index("section")
        self.group = lax.axis_index("dp")
        self.along = lax.axis_index("mp")
        self.half = self.along // chips
        self.seat = self.along % chips
        self.home = self.core == self.half

    def chip(self, offset):
        return (self.seat + offset) % self.chips

    def sibling(self):
        return (1 - self.core, self.group, self.along)

    def peer(self, offset):
        return (self.core, self.group, self.half * self.chips + self.chip(offset))

    def mine(self, offset):
        return self.chip(offset) + self.core * self.chips

    def other(self, offset):
        return self.chip(offset) + (1 - self.core) * self.chips

    def dp(self, offset):
        return (self.core, (self.group + offset) % self.groups, self.along)

    def far(self, core):
        return (core, self.group, (self.along + self.chips) % (2 * self.chips))

    def partners(self):
        return (
            [self.sibling(), self.far(0), self.far(1)]
            + [self.peer(o) for o in range(1, self.chips)]
            + [self.dp(o) for o in range(1, self.groups)]
        )

    def member(self, offset):
        return (self.core, self.group, (self.along + offset) % (2 * self.chips))

    def all_partners(self):
        return (
            [self.sibling(), self.far(1 - self.core)]
            + [self.member(o) for o in range(1, 2 * self.chips)]
            + [self.dp(o) for o in range(1, self.groups)]
        )

    def enter(self, partners):
        barrier = pltpu.get_barrier_semaphore()
        for device in partners:
            pl.semaphore_signal(barrier, inc=1, device_id=device, device_id_type=MESH)
        pl.semaphore_wait(barrier, len(partners))


def remote(src, dst, send, recv, device):
    return pltpu.make_async_remote_copy(
        src_ref=src, dst_ref=dst, send_sem=send, recv_sem=recv, device_id=device, device_id_type=MESH
    )


def block(rank, rows):
    return pl.ds(pl.multiple_of(rank * rows, rows), rows)


class Gather:
    def __init__(self, team, buf, rows, send, recv):
        self.team, self.buf, self.rows, self.send, self.recv = team, buf, rows, send, recv
        self.started = []

    def _copy(self, rank, slot, device):
        part = self.buf.at[block(rank, self.rows)]
        return remote(part, part, self.send.at[slot], self.recv.at[slot], device)

    def start(self):
        team = self.team
        for o in range(1, team.chips):
            self.started.append(self._copy(team.mine(0), o, team.peer(o)))
        self.started.append(self._copy(team.mine(0), 0, team.sibling()))
        for copy in self.started:
            copy.start()

    def arrivals(self):
        team = self.team
        yield True, 0
        self._copy(team.other(0), 0, team.sibling()).wait_recv()
        yield False, 0
        for o in range(1, team.chips):
            back = team.chips - o
            self._copy(team.mine(back), o, team.peer(back)).wait_recv()
            forward = self._copy(team.mine(back), team.chips - 1 + o, team.sibling())
            forward.start()
            self.started.append(forward)
            yield True, back
            self._copy(team.other(back), team.chips - 1 + o, team.sibling()).wait_recv()
            yield False, back

    def finish(self):
        for copy in self.started:
            copy.wait_send()


class Reduce:
    def __init__(self, team, rows, scratch):
        self.team, self.rows = team, rows
        (self.out, self.held, self.into, self.leave, self.land, self.own, self.xs, self.xr, self.us, self.ur) = scratch
        self.started = []

    def put_other(self, o, value):
        self.out[o] = value.astype(LOW)
        copy = remote(self.out.at[o], self.into.at[o], self.xs.at[o], self.xr.at[o], self.team.sibling())
        copy.start()
        self.started.append(copy)

    def put_mine(self, o, value):
        if o == 0:
            self.own[...] = value
        else:
            self.held[...] = value

    def pass_on(self, o):
        remote(self.out.at[o], self.into.at[o], self.xs.at[o], self.xr.at[o], self.team.sibling()).wait_recv()
        self.leave[o - 1] = (self.held[...] + self.into[o].astype(F32)).astype(LOW)
        copy = remote(
            self.leave.at[o - 1], self.land.at[o - 1], self.us.at[o - 1], self.ur.at[o - 1], self.team.peer(o)
        )
        copy.start()
        self.started.append(copy)

    def finish(self):
        remote(self.out.at[0], self.into.at[0], self.xs.at[0], self.xr.at[0], self.team.sibling()).wait_recv()
        for o in range(1, self.team.chips):
            remote(
                self.leave.at[o - 1], self.land.at[o - 1], self.us.at[o - 1], self.ur.at[o - 1], self.team.peer(o)
            ).wait_recv()
        for copy in self.started:
            copy.wait_send()

    def total(self, rows):
        total = self.own[rows] + self.into[0, rows].astype(F32)
        for o in range(self.team.chips - 1):
            total = total + self.land[o, rows].astype(F32)
        return total


def gather_scratch(chips):
    return [pltpu.SemaphoreType.DMA((2 * chips - 1,)), pltpu.SemaphoreType.DMA((2 * chips - 1,))]


def reduce_scratch(chips, rows, width):
    return [
        pltpu.VMEM((chips, rows, width), LOW),
        pltpu.VMEM((rows, width), F32),
        pltpu.VMEM((chips, rows, width), LOW),
        pltpu.VMEM((chips - 1, rows, width), LOW),
        pltpu.VMEM((chips - 1, rows, width), LOW),
        pltpu.VMEM((rows, width), F32),
        pltpu.SemaphoreType.DMA((chips,)),
        pltpu.SemaphoreType.DMA((chips,)),
        pltpu.SemaphoreType.DMA((chips - 1,)),
        pltpu.SemaphoreType.DMA((chips - 1,)),
    ]


N_REDUCE = 10


def by_rows(rows, body):
    step = min(32, rows)

    @pl.loop(0, rows // step)
    def _(i):
        body(pl.ds(pl.multiple_of(i * step, step), step))


def swap_halves(u):
    columns, half = u.shape[1], HD // 2
    if columns % 128:
        parts = []
        for at in range(0, columns, HD):
            parts += [u[:, at + half : at + HD], u[:, at : at + half]]
        return jnp.concatenate(parts, 1)
    lane = lax.broadcasted_iota(jnp.int32, u.shape, 1)
    return jnp.where(lane % HD < half, pltpu.roll(u, columns - half, 1), pltpu.roll(u, half, 1))


def head_row(columns, head):
    lane = lax.broadcasted_iota(jnp.int32, (1, columns), 1)
    return (lane // HD == head).astype(F32).astype(LOW)


def norm_into(buf, at, rows, read, gain_ref):
    step = min(32, rows)

    @pl.loop(0, rows // step)
    def _(i):
        values = read(pl.ds(pl.multiple_of(i * step, step), step))
        scale = lax.rsqrt(jnp.mean(values * values, -1, keepdims=True) + EPSILON)
        buf[pl.ds(pl.multiple_of(at + i * step, step), step)] = (values * scale * gain_ref[...]).astype(LOW)


def norm_back(rows, read_values, read_grad, gain_ref, read_outer, write, gain_grad_ref):
    gain_grad_ref[...] = jnp.zeros_like(gain_grad_ref)

    def body(sl):
        values = read_values(sl)
        scale = lax.rsqrt(jnp.mean(values * values, -1, keepdims=True) + EPSILON)
        unit = values * scale
        grad = read_grad(sl)
        gain_grad_ref[...] += jnp.sum(grad * unit, 0, keepdims=True)
        inner = grad * gain_ref[...]
        write(sl, read_outer(sl) + scale * (inner - unit * jnp.mean(inner * unit, -1, keepdims=True)))

    by_rows(rows, body)


def attend_kernel(team, hooks, *refs, first):
    refs = list(refs)
    x_ref, gain_ref, bias_ref, cos_ref, sin_ref = refs[:5]
    refs = refs[5:]
    before_ref = None if first else refs.pop(0)
    w_ref, x1_ref, h_ref, q_ref, k_ref, m_ref, o_ref, log_ref, gs, gr = refs[:10]
    chips = team.chips
    rows, span = x_ref.shape[0], h_ref.shape[0]
    columns = w_ref.shape[0] // 4
    heads = columns // HD
    norm_into(h_ref, team.mine(0) * rows, rows, lambda sl: x_ref[sl].astype(F32), gain_ref)
    gather = Gather(team, h_ref, rows, gs, gr)
    gather.start()
    hooks.weights.wait()
    for i in range(2 if first else 3):
        hooks.need(i)
    for own, o in gather.arrivals():
        sl = block(team.mine(o) if own else team.other(o), rows)
        normed = h_ref[sl]
        cosine, sine = cos_ref[sl], sin_ref[sl]
        u = mm_nt(normed, w_ref[0:columns])
        q_ref[sl] = (u * cosine + swap_halves(u) * sine).astype(LOW) * jnp.asarray(HD**-0.5, LOW)
        u = mm_nt(normed, w_ref[columns : 2 * columns])
        k_ref[sl] = (u * cosine + swap_halves(u) * sine).astype(LOW)
        v = mm_nt(normed, w_ref[2 * columns : 3 * columns]).astype(LOW)
        m_ref[sl] = v if first else (0.5 * v.astype(F32) + 0.5 * before_ref[sl].astype(F32)).astype(LOW)
    for i in range(4):
        hooks.done(i)

    size = min(256, span)
    lanes = 128
    for qb in range(span // size):
        upto = (qb + 1) * size
        at = slice(qb * size, upto)

        def one_head(head, carry):
            out, logs = carry
            mask = head_row(columns, head)
            scores = mm_nt(q_ref[at] * mask, k_ref[0:upto]) + bias_ref[:, 0:upto]
            row = lax.broadcasted_iota(jnp.int32, scores.shape, 0) + qb * size
            column = lax.broadcasted_iota(jnp.int32, scores.shape, 1)
            scores = jnp.where(column <= row, scores, NEG_LARGE)
            peak = jnp.max(scores, -1, keepdims=True)
            weights = jnp.exp(scores - peak)
            total = jnp.sum(weights, -1, keepdims=True)
            part = mm(weights.astype(LOW), m_ref[0:upto])
            out = out + part * (mask.astype(F32) * (1.0 / total))
            lane = lax.broadcasted_iota(jnp.int32, logs.shape, 1)
            logs = jnp.where(lane == head, peak + jnp.log(total), logs)
            return out, logs

        out, logs = lax.fori_loop(
            0, heads, one_head, (jnp.zeros((size, columns), F32), jnp.zeros((size, lanes), F32))
        )
        o_ref[at] = out.astype(LOW)
        log_ref[:, at] = jnp.transpose(logs)[0 : log_ref.shape[0]]

    hooks.done(4)
    hooks.done(5)
    hooks.middle()
    reduce = Reduce(team, rows, refs[10:])

    def part(rank):
        return mm(o_ref[block(rank, rows)], w_ref[3 * columns : 4 * columns])

    for o in range(1, chips):
        reduce.put_other(o, part(team.other(o)))
    for o in range(1, chips):
        reduce.put_mine(o, part(team.mine(o)))
        reduce.pass_on(o)
    reduce.put_other(0, part(team.other(0)))
    reduce.put_mine(0, part(team.mine(0)))
    reduce.finish()

    def close(sl):
        x1_ref[sl] = x_ref[sl].astype(F32) + reduce.total(sl)

    by_rows(rows, close)
    gather.finish()


def feed_kernel(team, hooks, x1_ref, gain_ref, w_ref, y_ref, h_ref, gate_ref, up_ref, z_ref, gs, gr, *scratch):
    chips = team.chips
    rows = x1_ref.shape[0]
    hidden = w_ref.shape[0] // 3
    norm_into(h_ref, team.mine(0) * rows, rows, lambda sl: x1_ref[sl], gain_ref)
    gather = Gather(team, h_ref, rows, gs, gr)
    reduce = Reduce(team, rows, scratch)
    gather.start()
    hooks.weights.wait()
    for own, o in gather.arrivals():
        sl = block(team.mine(o) if own else team.other(o), rows)
        normed = h_ref[sl]
        gate = mm_nt(normed, w_ref[0:hidden])
        up = mm_nt(normed, w_ref[hidden : 2 * hidden])
        gate_ref[sl] = gate.astype(LOW)
        up_ref[sl] = up.astype(LOW)
        z_ref[sl] = (gate / (1.0 + jnp.exp(-gate)) * up).astype(LOW)
        value = mm(z_ref[sl], w_ref[2 * hidden : 3 * hidden])
        if own:
            reduce.put_mine(o, value)
        else:
            reduce.put_other(o, value)
            if o:
                reduce.pass_on(o)
    for i in range(4):
        hooks.done(i)
    reduce.finish()

    def close(sl):
        y_ref[sl] = (x1_ref[sl] + reduce.total(sl)).astype(LOW)

    by_rows(rows, close)
    gather.finish()


def columns_of(width):
    step = min(256, width)
    return [slice(at, at + step) for at in range(0, width, step)]


def feed_back_kernel(
    team, hooks, g_ref, x1_ref, gain_ref, gate_ref, up_ref, h_ref, z_ref, w_ref,
    dx1_ref, gain_grad_ref, w_grad_ref, grad_ref, dgate_ref, dup_ref, gs, gr, *scratch,
):
    chips = team.chips
    rows, width = g_ref.shape
    hidden = w_ref.shape[0] // 3
    grad_ref[block(team.mine(0), rows)] = g_ref[...]
    gather = Gather(team, grad_ref, rows, gs, gr)
    reduce = Reduce(team, rows, scratch)
    gather.start()
    hooks.weights.wait()
    hooks.need(0)
    hooks.need(1)
    for own, o in gather.arrivals():
        sl = block(team.mine(o) if own else team.other(o), rows)
        dz = mm_nt(grad_ref[sl], w_ref[2 * hidden : 3 * hidden])
        gate = gate_ref[sl].astype(F32)
        sigma = 1.0 / (1.0 + jnp.exp(-gate))
        dgate_ref[sl] = (dz * up_ref[sl].astype(F32) * sigma * (1.0 + gate * (1.0 - sigma))).astype(LOW)
        dup_ref[sl] = (dz * gate * sigma).astype(LOW)
        value = mm(dgate_ref[sl], w_ref[0:hidden]) + mm(dup_ref[sl], w_ref[hidden : 2 * hidden])
        if own:
            reduce.put_mine(o, value)
        else:
            reduce.put_other(o, value)
            if o:
                reduce.pass_on(o)
    hooks.need(2)
    hooks.need(3)
    for at in columns_of(width):
        w_grad_ref[0:hidden, at] = mm_tn(dgate_ref[...], h_ref[:, at]).astype(LOW)
        w_grad_ref[hidden : 2 * hidden, at] = mm_tn(dup_ref[...], h_ref[:, at]).astype(LOW)
        w_grad_ref[2 * hidden : 3 * hidden, at] = mm_tn(z_ref[...], grad_ref[:, at]).astype(LOW)
    hooks.done(0)
    reduce.finish()

    def write(sl, value):
        dx1_ref[sl] = value

    norm_back(
        rows, lambda sl: x1_ref[sl], reduce.total, gain_ref, lambda sl: g_ref[sl].astype(F32), write, gain_grad_ref
    )
    gather.finish()


def attend_back_kernel(team, hooks, *refs, last):
    refs = list(refs)
    dx1_ref, gain_ref, bias_ref, k_ref, o_ref, q_ref, m_ref, log_ref, cos_ref, sin_ref, h_ref, x_ref = refs[:12]
    refs = refs[12:]
    value_grad_ref = None if last else refs.pop(0)
    w_ref, grad_in_ref, gain_grad_ref = refs[:3]
    refs = refs[3:]
    value_sent_ref = refs.pop(0) if last else None
    w_grad_ref, grad_ref, do_ref, inner_ref, kt_ref, dm_ref, dk_ref, dq_ref, dqkv_ref, mask_ref, gs, gr = refs[:12]
    chips = team.chips
    rows, width = dx1_ref.shape
    span, columns = q_ref.shape
    heads = columns // HD
    at = team.mine(0) * rows

    def low_rows(sl):
        grad_ref[pl.ds(pl.multiple_of(at + sl.start, sl.size), sl.size)] = dx1_ref[sl].astype(LOW)

    by_rows(rows, low_rows)
    gather = Gather(team, grad_ref, rows, gs, gr)
    gather.start()
    hooks.need(0)
    kt_ref[...] = jnp.transpose(k_ref[...])
    dm_ref[...] = jnp.zeros_like(dm_ref)
    dk_ref[...] = jnp.zeros_like(dk_ref)
    dq_ref[...] = jnp.zeros_like(dq_ref)
    hooks.weights.wait()
    for i in range(1, 9 if last else 10):
        hooks.need(i)
    for own, o in gather.arrivals():
        sl = block(team.mine(o) if own else team.other(o), rows)
        do_ref[sl] = mm_nt(grad_ref[sl], w_ref[3 * columns : 4 * columns]).astype(LOW)
    for part in columns_of(width):
        w_grad_ref[3 * columns : 4 * columns, part] = mm_tn(o_ref[...], grad_ref[:, part]).astype(LOW)

    pad = inner_ref.shape[0]
    pick = (
        lax.broadcasted_iota(jnp.int32, (pad, columns), 1) // HD == lax.broadcasted_iota(jnp.int32, (pad, columns), 0)
    )
    pick = pick.astype(F32).astype(LOW)
    size = min(256, span)
    for b in range(span // size):
        sl = slice(b * size, (b + 1) * size)
        product = do_ref[sl].astype(F32) * o_ref[sl].astype(F32)
        high = product.astype(LOW)
        rest = (product - high.astype(F32)).astype(LOW)
        inner_ref[:, sl] = mm_nt(pick, high) + mm_nt(pick, rest)

    @pl.loop(0, span // size)
    def _(kb):
        ks = pl.ds(pl.multiple_of(kb * size, size), size)

        @pl.loop(kb, span // size)
        def _(qb):
            qs = pl.ds(pl.multiple_of(qb * size, size), size)
            key = lax.broadcasted_iota(jnp.int32, (size, size), 0) + kb * size
            query = lax.broadcasted_iota(jnp.int32, (size, size), 1) + qb * size
            mask_ref[...] = jnp.where(key <= query, 0.0, NEG_LARGE) + bias_ref[ks]
            for head in range(heads):
                mask = head_row(columns, head)
                q = q_ref[qs] * mask
                do = do_ref[qs] * mask
                soft = jnp.exp(mm_nt(k_ref[ks], q) + mask_ref[...] - log_ref[head : head + 1, qs])
                dsoft = mm_nt(m_ref[ks], do)
                ds = (soft * (dsoft - inner_ref[head : head + 1, qs])).astype(LOW)
                dm_ref[ks] += mm(soft.astype(LOW), do)
                dk_ref[ks] += mm(ds, q)
                lines = slice(head * HD, (head + 1) * HD)
                dq_ref[lines, qs] += mm(kt_ref[lines, ks], ds)

    for b in range(span // size):
        sl = slice(b * size, (b + 1) * size)
        cosine, sine = cos_ref[sl], sin_ref[sl]
        dq = jnp.transpose(dq_ref[:, sl]) * HD**-0.5
        dqkv_ref[0, sl] = (dq * cosine - swap_halves(dq) * sine).astype(LOW)
        dk = dk_ref[sl]
        dqkv_ref[1, sl] = (dk * cosine - swap_halves(dk) * sine).astype(LOW)
        if last:
            half = (0.5 * dm_ref[sl]).astype(LOW)
            dqkv_ref[2, sl] = half
            value_sent_ref[sl] = half
        else:
            dqkv_ref[2, sl] = (dm_ref[sl] + value_grad_ref[sl].astype(F32)).astype(LOW)

    reduce = Reduce(team, rows, refs[12:])

    def part(rank):
        sl = block(rank, rows)
        total = mm(dqkv_ref[0, sl], w_ref[0:columns])
        for t in (1, 2):
            total = total + mm(dqkv_ref[t, sl], w_ref[t * columns : (t + 1) * columns])
        return total

    for o in range(1, chips):
        reduce.put_other(o, part(team.other(o)))
    for o in range(1, chips):
        reduce.put_mine(o, part(team.mine(o)))
        reduce.pass_on(o)
    reduce.put_other(0, part(team.other(0)))
    reduce.put_mine(0, part(team.mine(0)))
    for piece in columns_of(width):
        for t in range(3):
            w_grad_ref[t * columns : (t + 1) * columns, piece] = mm_tn(dqkv_ref[t], h_ref[:, piece]).astype(LOW)
    hooks.done(0)
    reduce.finish()

    def write(sl, value):
        grad_in_ref[sl] = value

    norm_back(
        rows, lambda sl: x_ref[sl].astype(F32), reduce.total, gain_ref, lambda sl: dx1_ref[sl], write, gain_grad_ref
    )
    gather.finish()


def columns_at(ref, index, size):
    return ref.at[:, pl.ds(pl.multiple_of(index * size, size), size)]


class Local:
    def __init__(self, src, dst, sem):
        self.copy = pltpu.make_async_copy(src, dst, sem)
        self.start, self.wait = self.copy.start, self.copy.wait


class FarWeight:
    def __init__(self, layer, own):
        rows, width = own.shape
        self.layer, self.args = layer, [own]
        self.outs = [((rows, width // lax.axis_size("dp")), LOW)]
        self.sems = [1, 1]

    def bind(self, team, own, piece, send, recv):
        self.team, self.own, self.piece, self.send, self.recv = team, own, piece, send, recv

    def copy(self):
        team, size = self.team, self.piece.shape[1]
        return remote(
            columns_at(self.own, team.group, size), self.piece, self.send.at[0], self.recv.at[0], team.far(team.half)
        )

    def start(self):
        pl.when(self.team.core == self.layer)(lambda: self.copy().start())

    def middle(self):
        pass

    def finish(self):
        pl.when(self.team.core == self.layer)(lambda: self.copy().wait_send())
        pl.when(jnp.logical_not(self.team.home))(lambda: self.copy().wait_recv())


class NearWeight:
    def __init__(self, layer, own, piece=None):
        groups = lax.axis_size("dp")
        self.layer, self.args = layer, [own] + ([] if piece is None else [piece])
        self.outs = [(own.shape, LOW)]
        self.sems = [groups, groups]

    def bind(self, team, own, piece, full, send, recv):
        self.team, self.own, self.piece, self.full = team, own, piece, full
        self.send, self.recv = send, recv

    def cross(self):
        return remote(self.own, self.full, self.send.at[0], self.recv.at[0], self.team.sibling())

    def along(self, o):
        team, size = self.team, self.piece.shape[1]
        return remote(
            self.piece, columns_at(self.full, team.group, size), self.send.at[o], self.recv.at[o], team.dp(o)
        )

    def arriving(self, o):
        team, size = self.team, self.piece.shape[1]
        back = team.groups - o
        part = columns_at(self.full, (team.group + back) % team.groups, size)
        return remote(self.piece, part, self.send.at[o], self.recv.at[o], team.dp(back))

    def roles(self):
        team = self.team
        same = team.core == self.layer
        away = jnp.logical_not(team.home)
        return away & same, team.home & jnp.logical_not(same), away

    def start(self):
        gives, takes, away = self.roles()

        @pl.when(away)
        def _():
            for o in range(1, self.team.groups):
                self.along(o).start()

        pl.when(gives)(lambda: self.cross().start())

    def middle(self):
        pass

    def finish(self):
        gives, takes, away = self.roles()
        pl.when(gives)(lambda: self.cross().wait_send())
        pl.when(takes)(lambda: self.cross().wait_recv())

        @pl.when(away)
        def _():
            for o in range(1, self.team.groups):
                self.along(o).wait_send()
                self.arriving(o).wait_recv()


class WeightLoad:
    def __init__(self, layer, team, own, full, piece, buf, sems):
        self.layer, self.team, self.own, self.full = layer, team, own, full
        self.piece, self.buf, self.sems = piece, buf, sems

    def each(self, act):
        team, size = self.team, self.piece.shape[1]
        same = team.core == self.layer
        pl.when(team.home & same)(lambda: act(Local(self.own, self.buf, self.sems.at[0])))
        pl.when(team.home & jnp.logical_not(same))(lambda: act(Local(self.full, self.buf, self.sems.at[0])))

        @pl.when(jnp.logical_not(team.home))
        def _():
            act(Local(self.piece, columns_at(self.buf, team.group, size), self.sems.at[0]))
            for o in range(1, team.groups):
                at = (team.group + o) % team.groups
                act(Local(columns_at(self.full, at, size), columns_at(self.buf, at, size), self.sems.at[o]))

    def start(self):
        self.each(lambda c: c.start())

    def wait(self):
        self.each(lambda c: c.wait())


class WholeWeight:
    def __init__(self, layer, own):
        self.far, self.near = FarWeight(layer, own), NearWeight(layer, own)
        self.args = [own]
        self.outs = self.near.outs + self.far.outs
        self.sems = self.far.sems + self.near.sems

    def bind(self, team, own, full, piece, *sems):
        self.far.bind(team, own, piece, *sems[:2])
        self.near.bind(team, own, piece, full, *sems[2:])

    def start(self):
        self.far.start()

    def middle(self):
        self.far.finish()
        self.near.start()

    def finish(self):
        self.near.finish()


class OwnRows:
    def __init__(self, blocks):
        self.args, self.outs, self.sems = [blocks], [(blocks.shape[1:], LOW)], [1, 1]

    def bind(self, team, blocks, rows, send, recv):
        self.home = team.home
        self.copy = remote(blocks.at[1 - team.half], rows, send.at[0], recv.at[0], team.far(team.core))

    def start(self):
        pl.when(self.home)(lambda: self.copy.start())

    def middle(self):
        pass

    def finish(self):
        pl.when(self.home)(lambda: self.copy.wait_send())
        pl.when(jnp.logical_not(self.home))(lambda: self.copy.wait_recv())


class PlaceRows:
    def __init__(self, first, second):
        self.args, self.outs, self.sems = [first, second], [((2,) + first.shape, LOW)], [2, 2]

    def bind(self, team, first, second, placed, send, recv):
        self.team, self.layers, self.placed = team, (first, second), placed
        self.send, self.recv = send, recv

    def far(self, layer):
        slot = self.placed.at[self.team.half]
        return remote(self.layers[layer], slot, self.send.at[layer], self.recv.at[0], self.team.far(layer))

    def near(self, layer):
        slot = self.placed.at[self.team.half]
        return remote(self.layers[layer], slot, self.send.at[layer], self.recv.at[1], self.team.sibling())

    def each(self, act):
        team = self.team
        for layer in range(2):
            pl.when(team.home & (team.core != layer))(lambda: act(self.near(layer)))
            pl.when(jnp.logical_not(team.home))(lambda: act(self.far(layer)))

    def start(self):
        self.each(lambda c: c.start())

    def middle(self):
        pass

    def finish(self):
        self.each(lambda c: c.wait_send())
        team = self.team
        there = self.placed.at[1 - team.half]
        remote(self.layers[0], there, self.send.at[0], self.recv.at[0], team.far(0)).wait_recv()
        pl.when(jnp.logical_not(team.home))(lambda: self.near(0).wait_recv())


class Scatter:
    def __init__(self, part):
        rows, width = part.shape
        groups = lax.axis_size("dp")
        self.args, self.outs = [part], [((groups - 1, rows, width // groups), LOW)]
        self.sems = [groups - 1, groups - 1]

    def bind(self, team, part, land, send, recv):
        size = land.shape[2]
        self.copies = [
            remote(
                columns_at(part, (team.group + o) % team.groups, size),
                land.at[o - 1],
                send.at[o - 1],
                recv.at[o - 1],
                team.dp(o),
            )
            for o in range(1, team.groups)
        ]

    def start(self):
        for copy in self.copies:
            copy.start()

    def middle(self):
        pass

    def finish(self):
        for copy in self.copies:
            copy.wait()


class Swap:
    def __init__(self, layer, share):
        self.layer, self.args, self.sems = layer, [share], [1, 2]
        self.outs = [((2,) + share.shape, LOW)]

    def bind(self, team, share, land, send, recv):
        self.team = team
        self.far = remote(share, land.at[0], send.at[0], recv.at[0], team.far(self.layer))
        self.near = remote(share, land.at[1], send.at[0], recv.at[1], team.sibling())

    def each(self, act):
        team = self.team
        pl.when(jnp.logical_not(team.home))(lambda: act(self.far))
        pl.when(team.home & (team.core != self.layer))(lambda: act(self.near))

    def start(self):
        self.each(lambda c: c.start())

    def middle(self):
        pass

    def finish(self):
        self.each(lambda c: c.wait_send())
        team = self.team
        pl.when(team.core == self.layer)(lambda: self.far.wait_recv())
        pl.when((team.core == self.layer) & jnp.logical_not(team.home))(lambda: self.near.wait_recv())


class Spread:
    def __init__(self, share, width):
        groups = lax.axis_size("dp")
        self.args, self.outs, self.sems = [share], [((share.shape[0], width), LOW)], [groups - 1, groups - 1, 1]

    def bind(self, team, share, full, send, recv, here):
        self.team, self.share, self.full, self.send, self.recv = team, share, full, send, recv
        self.local = Local(share, columns_at(full, team.group, share.shape[1]), here.at[0])

    def copy(self, o, arriving=False):
        team, size = self.team, self.share.shape[1]
        group = (team.group + team.groups - o) % team.groups if arriving else team.group
        part = columns_at(self.full, group, size)
        return remote(self.share, part, self.send.at[o - 1], self.recv.at[o - 1], team.dp(o))

    def start(self):
        for o in range(1, self.team.groups):
            self.copy(o).start()
        self.local.start()

    def middle(self):
        pass

    def finish(self):
        self.local.wait()
        for o in range(1, self.team.groups):
            self.copy(o).wait_send()
            self.copy(o, arriving=True).wait_recv()


class Hooks:
    def __init__(self, late, drains, weights, jobs):
        self.late, self.drains, self.weights, self.jobs = late, drains, weights, jobs

    def need(self, index):
        self.late[index].wait()

    def done(self, index):
        self.drains[index].start()

    def middle(self):
        for job in self.jobs:
            job.middle()


def call(
    body, chips, ident, flops, args=(), late=(), weights=None, far_args=(), outs=(), far_outs=(), drained=(),
    scratch=(), jobs=(), partners=Team.partners,
):
    vmem, far = pl.BlockSpec(memory_space=pltpu.VMEM), pl.BlockSpec(memory_space=pl.ANY)
    job_args = [a for job in jobs for a in job.args]
    job_outs = [o for job in jobs for o in job.outs]
    job_sems = [pltpu.SemaphoreType.DMA((n,)) for job in jobs for n in job.sems]
    sources = list(weights[1:]) if weights else []
    groups = lax.axis_size("dp")

    def kernel(*refs):
        refs = list(refs)

        def take(n):
            taken = refs[:n]
            del refs[:n]
            return taken

        ins, late_ins, weight_ins = take(len(args)), take(len(late)), take(len(sources))
        far_ins, job_ins = take(len(far_args)), take(len(job_args))
        results, drained_results, job_results = take(len(outs) + len(far_outs)), take(len(drained)), take(len(job_outs))
        own, late_bufs, drain_bufs = take(len(scratch)), take(len(late)), take(len(drained))
        weight_bufs, late_sem, drain_sem, weight_sem = take(1 if weights else 0), *take(3)
        sems = refs
        team = Team(chips)
        loads = [Local(src, dst, late_sem.at[i]) for i, (src, dst) in enumerate(zip(late_ins, late_bufs))]
        load = WeightLoad(weights[0], team, *weight_ins, *weight_bufs, weight_sem) if weights else None
        if load:
            load.start()
        for copy in loads:
            copy.start()
        team.enter(partners(team))
        for job in jobs:
            parts = []
            for pool, n in ((job_ins, len(job.args)), (job_results, len(job.outs)), (sems, len(job.sems))):
                parts += pool[:n]
                del pool[:n]
            job.bind(team, *parts)
        for job in jobs:
            job.start()
        drains = [Local(src, dst, drain_sem.at[i]) for i, (src, dst) in enumerate(zip(drain_bufs, drained_results))]
        hooks = Hooks(loads, drains, load, jobs)
        body(team, hooks, *ins, *late_bufs, *weight_bufs, *far_ins, *results, *drain_bufs, *own)
        for job in jobs:
            job.finish()
        for copy in drains:
            copy.wait()

    def sem(n):
        return pltpu.SemaphoreType.DMA((max(n, 1),))

    moved = sum(a.size * a.dtype.itemsize for a in (*args, *late))
    results = pl.pallas_call(
        kernel,
        out_shape=[jax.ShapeDtypeStruct(shape, dtype) for shape, dtype in (*outs, *far_outs, *drained, *job_outs)],
        in_specs=[vmem] * len(args) + [far] * (len(late) + len(sources) + len(far_args) + len(job_args)),
        out_specs=[vmem] * len(outs) + [far] * (len(far_outs) + len(drained) + len(job_outs)),
        scratch_shapes=[
            *scratch,
            *(pltpu.VMEM(a.shape, a.dtype) for a in late),
            *(pltpu.VMEM(shape, dtype) for shape, dtype in drained),
            *(pltpu.VMEM(a.shape, a.dtype) for a in sources[:1]),
            sem(len(late)), sem(len(drained)), sem(groups), *job_sems,
        ],
        cost_estimate=pl.CostEstimate(flops=WAITING * flops, bytes_accessed=moved, transcendentals=0),
        compiler_params=pltpu.CompilerParams(
            collective_id=ident, has_side_effects=True, vmem_limit_bytes=VMEM_BYTES
        ),
    )(*args, *late, *sources, *far_args, *job_args)
    job_results = []
    at = len(outs) + len(far_outs) + len(drained)
    for job in jobs:
        job_results.append(results[at : at + len(job.outs)])
        at += len(job.outs)
    return results[: len(outs) + len(far_outs) + len(drained)], job_results


def only_jobs(team, hooks):
    hooks.middle()


def rope_tables(span, columns):
    position = jnp.arange(span, dtype=F32)
    freqs = ROPE_BASE ** (-jnp.arange(0, HD, 2, dtype=F32) / HD)
    angle = position[:, None] * freqs[None, :]
    heads = columns // HD
    cosine = jnp.tile(jnp.concatenate([jnp.cos(angle), jnp.cos(angle)], -1), (1, heads))
    sine = jnp.tile(jnp.concatenate([-jnp.sin(angle), jnp.sin(angle)], -1), (1, heads))
    return cosine, sine


def everywhere_sum(team, refs):
    small_ref, sum_ref, near, groups_ref, members_ref, send, recv, gs, gr, ms, mr = refs
    copy = remote(small_ref, near, send.at[0], recv.at[0], team.sibling())
    copy.start()
    copy.wait()
    groups_ref[team.group] = small_ref[...] + near[...]
    copies = []
    for o in range(1, team.groups):
        slot = groups_ref.at[team.group]
        copies.append(remote(slot, slot, gs.at[o - 1], gr.at[o - 1], team.dp(o)))
        copies[-1].start()
    for o, copy in enumerate(copies, 1):
        copy.wait_send()
        slot = groups_ref.at[(team.group + team.groups - o) % team.groups]
        remote(slot, slot, gs.at[o - 1], gr.at[o - 1], team.dp(o)).wait_recv()
    total = groups_ref[0]
    for g in range(1, team.groups):
        total = total + groups_ref[g]
    members = 2 * team.chips
    members_ref[team.along] = total
    copies = []
    for o in range(1, members):
        slot = members_ref.at[team.along]
        copies.append(remote(slot, slot, ms.at[o - 1], mr.at[o - 1], team.member(o)))
        copies[-1].start()
    for o, copy in enumerate(copies, 1):
        copy.wait_send()
        slot = members_ref.at[(team.along + members - o) % members]
        remote(slot, slot, ms.at[o - 1], mr.at[o - 1], team.member(o)).wait_recv()
    total = members_ref[0]
    for g in range(1, members):
        total = total + members_ref[g]
    sum_ref[...] = total


def by_tiles(rows, body):
    step = next(n for n in (64, 32, 16) if rows % n == 0)

    @pl.loop(0, rows // step)
    def _(i):
        body(pl.ds(pl.multiple_of(i * step, step), step))


def tail_kernel(team, hooks, *refs):
    refs = list(refs)
    feed_ref, feed_done, attn_done, small_ref, attn_part = refs[:5]
    sum_ref, feed_full, attn_full = refs[5:8]
    own, land, share, feed_land, attn_land, feed_out, attn_out = refs[8:15]
    own_sem, ss, sr, fs, fr, as_, ar, fos, for_, foh, aos, aor, aoh = refs[15:28]
    small = refs[28:]
    scatter = Scatter.__new__(Scatter)
    scatter.bind(team, attn_part, land, ss, sr)
    scatter.start()
    mine = Local(columns_at(attn_part, team.group, own.shape[1]), own, own_sem)
    mine.start()
    feed_swap, attn_swap = Swap.__new__(Swap), Swap.__new__(Swap)
    feed_swap.layer = attn_swap.layer = 0
    feed_swap.bind(team, feed_ref, feed_land, fs, fr)
    attn_swap.bind(team, share, attn_land, as_, ar)
    feed_swap.start()
    feed_spread, attn_spread = Spread.__new__(Spread), Spread.__new__(Spread)
    feed_spread.bind(team, feed_out, feed_full, fos, for_, foh)
    attn_spread.bind(team, attn_out, attn_full, aos, aor, aoh)
    last = team.core == 0

    @pl.when(jnp.logical_not(last))
    def _():
        feed_out[...] = feed_done[...]
        attn_out[...] = attn_done[...]
        feed_spread.start()
        attn_spread.start()

    def add(out, kept, landed, sl):
        near = jnp.where(team.home, kept[sl].astype(F32), landed[1, sl].astype(F32))
        out[sl] = (near + landed[0, sl].astype(F32)).astype(LOW)

    everywhere_sum(team, [small_ref, sum_ref, *small])
    feed_swap.finish()

    @pl.when(last)
    def _():
        by_tiles(feed_out.shape[0], lambda sl: add(feed_out, feed_ref, feed_land, sl))
        feed_spread.start()

    mine.wait()
    scatter.finish()

    def sum_up(sl):
        total = own[sl].astype(F32)
        for o in range(team.groups - 1):
            total = total + land[o, sl].astype(F32)
        share[sl] = total.astype(LOW)

    by_tiles(share.shape[0], sum_up)
    attn_swap.start()
    attn_swap.finish()

    @pl.when(last)
    def _():
        by_tiles(attn_out.shape[0], lambda sl: add(attn_out, share, attn_land, sl))
        attn_spread.start()

    feed_spread.finish()
    attn_spread.finish()


def local(tokens, cotangent, lengths, gain_attn, w_qkv, w_out, gain_ffn, w_gate_up, w_down):
    cores, groups, members = lax.axis_size("section"), lax.axis_size("dp"), lax.axis_size("mp")
    micro, sequences, rows, width = tokens.shape
    assert cores == 2 and micro == 2 and sequences == 1 and members % 2 == 0 and members >= 4
    chips = members // 2
    span = rows * members
    columns, hidden = w_out.shape[1], w_down.shape[1]
    quarter = width // groups
    padded = -(-(columns // HD) // 8) * 8
    core = lax.axis_index("section")
    half = lax.axis_index("mp") // chips
    home = core == half

    def vec(shape, dtype):
        return pltpu.VMEM(shape, dtype)

    def sem(n):
        return pltpu.SemaphoreType.DMA((n,))

    whole = (span, width)
    heads_shape = ((span, columns), LOW)
    hidden_shape = ((span, hidden), LOW)
    reducing = reduce_scratch(chips, rows, width)
    own_attn = jnp.concatenate([w_qkv[0].reshape(3 * columns, width), w_out[0]], 0)
    own_feed = jnp.concatenate([w_gate_up[0].reshape(2 * hidden, width), w_down[0]], 0)

    def own_rows(blocks, came):
        return jnp.where(home, lax.dynamic_index_in_dim(blocks[:, 0], half, 0, keepdims=False), came)

    def place(pair, placed):
        here = jnp.where(home, jnp.where(core == 0, pair[0], pair[1]), placed[half])
        return lax.dynamic_update_index_in_dim(placed, here, half, 0)

    _, ((came,), (full, piece)) = call(
        only_jobs, chips, 0, 0, jobs=[OwnRows(tokens[:, 0]), WholeWeight(0, own_attn)]
    )
    x = own_rows(tokens, came)
    attn_weights, feed_weights = [(0, own_attn, full, piece), None], [None] * 2
    gains = lax.all_gather(jnp.stack([gain_attn[0], gain_ffn[0]]), "section")
    length = lax.dynamic_index_in_dim(lengths[:, 0], half, 0, keepdims=False)
    live = jnp.arange(span) < length
    bias = jnp.where(live, 0.0, NEG_LARGE).astype(F32)
    cosine, sine = rope_tables(span, columns)

    def share_of(part, landed):
        mine = lax.dynamic_slice_in_dim(part, lax.axis_index("dp") * quarter, quarter, 1)
        return (mine.astype(F32) + jnp.sum(landed.astype(F32), 0)).astype(LOW)

    def done_of(share, landed):
        return (landed[0].astype(F32) + jnp.where(home, share, landed[1]).astype(F32)).astype(LOW)

    kept = []
    squares = []
    values = top = far_piece = None
    for layer in range(2):
        late = [cosine, sine]
        if layer:
            late.append(values)
            jobs = [NearWeight(1, own_feed, far_piece), OwnRows(cotangent[:, 0])]
        else:
            jobs = [WholeWeight(0, own_feed), FarWeight(1, own_attn)]
        (x1, h, q, k, m, o, logs), came = call(
            functools.partial(attend_kernel, first=layer == 0),
            chips,
            1 + layer,
            8 * span * width * columns + 4 * span * span * columns,
            args=[x, gains[layer, 0][None], bias[None]],
            late=late,
            weights=attn_weights[layer],
            outs=[((rows, width), F32)],
            drained=[(whole, LOW)] + [heads_shape] * 4 + [((padded, span), F32)],
            scratch=gather_scratch(chips) + reducing,
            jobs=jobs,
        )
        if layer:
            feed_weights[1] = (1, own_feed, came[0][0], far_piece)
            top = own_rows(cotangent, came[1][0])
            jobs = []
        else:
            feed_weights[0] = (0, own_feed, *came[0])
            attn_piece = came[1][0]
            values = m
            jobs = [NearWeight(1, own_attn, attn_piece), FarWeight(1, own_feed)]
        squares.append(jnp.sum(jnp.where(live[:, None], jnp.square(m.astype(F32)), 0.0)))
        (y, h2, gate, up, z), came = call(
            feed_kernel,
            chips,
            3 + layer,
            6 * span * width * hidden,
            args=[x1, gains[layer, 1][None]],
            weights=feed_weights[layer],
            outs=[((rows, width), LOW)],
            drained=[(whole, LOW)] + [hidden_shape] * 3,
            scratch=gather_scratch(chips) + reducing,
            jobs=jobs,
        )
        if layer == 0:
            attn_weights[1], far_piece = (1, own_attn, came[0][0], attn_piece), came[1][0]
        kept.append((x, x1, h, q, k, m, o, logs, h2, gate, up, z, y))
        x = y

    grad, value_grad = top, None
    gain_grads, input_grads = [None] * 2, [None] * 2
    feed_share = attn_share = feed_part = attn_part = feed_done = attn_done = layer_out = None
    for layer in (1, 0):
        x, x1, h, q, k, m, o, logs, h2, gate, up, z, y = kept[layer]
        if layer:
            jobs = [PlaceRows(kept[0][-1], kept[1][-1])]
        else:
            jobs = [Scatter(attn_part), Swap(1, feed_share)]
        (dx1, feed_gain, feed_part), came = call(
            feed_back_kernel,
            chips,
            5 + layer,
            12 * span * width * hidden,
            args=[grad, x1, gains[layer, 1][None]],
            late=[gate, up, h2, z],
            weights=feed_weights[layer],
            outs=[((rows, width), F32), ((1, width), F32)],
            drained=[((3 * hidden, width), LOW)],
            scratch=[vec(whole, LOW), vec((span, hidden), LOW), vec((span, hidden), LOW)]
            + gather_scratch(chips)
            + reducing,
            jobs=jobs,
        )
        if layer:
            layer_out = place((kept[0][-1], kept[1][-1]), came[0][0])
            jobs = [Scatter(feed_part)]
        else:
            attn_share = share_of(attn_part, came[0][0])
            feed_done = done_of(feed_share, came[1][0])
            jobs = [Scatter(feed_part), Swap(1, attn_share)]
        size = min(256, span)
        results, came = call(
            functools.partial(attend_back_kernel, last=layer == 1),
            chips,
            7 + layer,
            16 * span * width * columns + 10 * span * span * columns,
            args=[dx1, gains[layer, 0][None], bias[:, None]],
            late=[k, o, q, m, logs, cosine, sine, h, x] + ([] if layer else [value_grad]),
            weights=attn_weights[layer],
            outs=[((rows, width), F32), ((1, width), F32)] + ([heads_shape] if layer else []),
            drained=[((4 * columns, width), LOW)],
            scratch=[
                vec(whole, LOW), vec((span, columns), LOW), vec((padded, span), F32), vec((columns, span), LOW),
                vec((span, columns), F32), vec((span, columns), F32), vec((columns, span), F32),
                vec((3, span, columns), LOW), vec((size, size), F32),
            ] + gather_scratch(chips) + reducing,
            jobs=jobs,
        )
        input_grads[layer], attn_gain, attn_part = results[0], results[1], results[-1]
        value_grad = results[2] if layer else None
        grad = input_grads[layer].astype(LOW)
        feed_share = share_of(feed_part, came[0][0])
        if layer == 0:
            attn_done = done_of(attn_share, came[1][0])
        gain_grads[layer] = [attn_gain, feed_gain]

    lane = jnp.arange(width)[None]
    stats = jnp.where(lane == 0, squares[0], jnp.where(lane == 1, squares[1], 0.0))
    stats = jnp.where(lane == 2, jnp.sum(lengths).astype(F32), stats)
    small = jnp.concatenate(gain_grads[0] + gain_grads[1] + [stats, jnp.zeros((3, width), F32)], 0)
    low_grads = (input_grads[0].astype(LOW), input_grads[1].astype(LOW))
    (small, feed_sums, attn_sums), ((placed,),) = call(
        tail_kernel,
        chips,
        9,
        0,
        args=[feed_share, feed_done, attn_done, small],
        far_args=[attn_part],
        outs=[(small.shape, F32)],
        far_outs=[((3 * hidden, width), LOW), ((4 * columns, width), LOW)],
        scratch=[
            vec((4 * columns, quarter), LOW), vec((groups - 1, 4 * columns, quarter), LOW),
            vec((4 * columns, quarter), LOW), vec((2, 3 * hidden, quarter), LOW), vec((2, 4 * columns, quarter), LOW),
            vec((3 * hidden, quarter), LOW), vec((4 * columns, quarter), LOW), pltpu.SemaphoreType.DMA,
            sem(groups - 1), sem(groups - 1), sem(1), sem(2), sem(1), sem(2),
            sem(groups - 1), sem(groups - 1), sem(1), sem(groups - 1), sem(groups - 1), sem(1),
            vec(small.shape, F32), vec((groups,) + small.shape, F32), vec((members,) + small.shape, F32),
            sem(1), sem(1), sem(groups - 1), sem(groups - 1), sem(members - 1), sem(members - 1),
        ],
        jobs=[PlaceRows(*low_grads)],
        partners=Team.all_partners,
    )
    placed = place(low_grads, placed)
    gain_sums = jnp.where(core == 0, small[0:2], small[2:4])
    root = jnp.where(core == 0, small[4, 0], small[4, 1])
    count = small[4, 2] / (cores * members)
    feed_sums, attn_sums = feed_sums.astype(F32), attn_sums.astype(F32)
    return (
        layer_out[None, :, None],
        placed.astype(F32)[None, :, None],
        gain_sums[0:1],
        attn_sums[: 3 * columns].reshape(w_qkv.shape),
        attn_sums[3 * columns :][None],
        gain_sums[1:2],
        feed_sums[: 2 * hidden].reshape(w_gate_up.shape),
        feed_sums[2 * hidden :][None],
        jnp.sqrt(root / (count * width)).reshape(1),
    )


def solution(mesh):
    return jax.shard_map(
        local,
        mesh=mesh,
        in_specs=(
            P(None, "dp", "mp", None),
            P(None, "dp", "mp", None),
            P(None, "dp"),
            P("section", None),
            P("section", None, "mp", None),
            P("section", "mp", None),
            P("section", None),
            P("section", None, "mp", None),
            P("section", "mp", None),
        ),
        out_specs=(
            P("section", None, "dp", "mp", None),
            P("section", None, "dp", "mp", None),
            P("section", None),
            P("section", None, "mp", None),
            P("section", "mp", None),
            P("section", None),
            P("section", None, "mp", None),
            P("section", "mp", None),
            P("section"),
        ),
        check_vma=False,
    )
```

```python
import functools

import jax
import jax.numpy as jnp
from jax import lax
from jax.experimental import pallas as pl
from jax.experimental.pallas import tpu as pltpu
from jax.sharding import PartitionSpec as P

HD = 64
EPSILON = 1e-05
ROPE_BASE = 10000.0
NEG_LARGE = -1e30
MESH = pl.DeviceIdType.MESH
F32 = jnp.float32
LOW = jnp.bfloat16
VMEM_BYTES = 56 << 20
WAITING = 12


def mm(a, b):
    return lax.dot_general(a, b, (((1,), (0,)), ((), ())), preferred_element_type=F32)


def mm_nt(a, b):
    return lax.dot_general(a, b, (((1,), (1,)), ((), ())), preferred_element_type=F32)


def mm_tn(a, b):
    return lax.dot_general(a, b, (((0,), (0,)), ((), ())), preferred_element_type=F32)


def no(flag):
    return jnp.logical_not(flag)


class Team:
    def __init__(self, chips):
        self.chips = chips
        self.groups = lax.axis_size("dp")
        self.core = lax.axis_index("section")
        self.group = lax.axis_index("dp")
        self.along = lax.axis_index("mp")
        self.half = self.along // chips
        self.seat = self.along % chips
        self.home = self.core == self.half
        self.away = jnp.logical_not(self.home)

    def chip(self, offset):
        return (self.seat + offset) % self.chips

    def sibling(self):
        return (1 - self.core, self.group, self.along)

    def peer(self, offset):
        return (self.core, self.group, self.half * self.chips + self.chip(offset))

    def mine(self, offset):
        return self.chip(offset) + self.core * self.chips

    def other(self, offset):
        return self.chip(offset) + (1 - self.core) * self.chips

    def dp(self, offset):
        return (self.core, (self.group + offset) % self.groups, self.along)

    def far(self, core):
        return (core, self.group, (self.along + self.chips) % (2 * self.chips))

    def member(self, offset):
        return (self.core, self.group, (self.along + offset) % (2 * self.chips))

    def partners(self):
        return (
            [self.sibling(), self.far(0), self.far(1)]
            + [self.peer(o) for o in range(1, self.chips)]
            + [self.dp(o) for o in range(1, self.groups)]
        )

    def all_partners(self):
        return (
            [self.sibling(), self.far(1 - self.core)]
            + [self.member(o) for o in range(1, 2 * self.chips)]
            + [self.dp(o) for o in range(1, self.groups)]
        )

    def enter(self, partners):
        barrier = pltpu.get_barrier_semaphore()
        for device in partners:
            pl.semaphore_signal(barrier, inc=1, device_id=device, device_id_type=MESH)
        pl.semaphore_wait(barrier, len(partners))


def remote(src, dst, send, recv, device):
    return pltpu.make_async_remote_copy(
        src_ref=src, dst_ref=dst, send_sem=send, recv_sem=recv, device_id=device, device_id_type=MESH
    )


class Local:
    def __init__(self, src, dst, sem):
        self.copy = pltpu.make_async_copy(src, dst, sem)
        self.start, self.wait = self.copy.start, self.copy.wait


def block(rank, rows):
    return pl.ds(pl.multiple_of(rank * rows, rows), rows)


def columns_at(ref, index, size):
    return ref.at[:, pl.ds(pl.multiple_of(index * size, size), size)]


def lines(ref, start, rows):
    return ref.at[pl.ds(start, rows)]


def subs_of(rows):
    return max(1, rows // 64)


class Gather:
    def __init__(self, team, buf, rows, send, recv):
        self.team, self.buf, self.rows, self.send, self.recv = team, buf, rows, send, recv
        self.subs = subs_of(rows)
        self.size = rows // self.subs
        self.count = (team.chips - 1) * self.subs

    def run(self, rank, s):
        return pl.ds(pl.multiple_of(rank * self.rows + s * self.size, self.size), self.size)

    def _copy(self, part, slot, device):
        part = self.buf.at[part]
        return remote(part, part, self.send.at[slot], self.recv.at[slot], device)

    def near(self, rank):
        return self._copy(block(rank, self.rows), 2 * self.count, self.team.sibling())

    def direct(self, o, s):
        return self._copy(self.run(self.team.mine(0), s), (o - 1) * self.subs + s, self.team.peer(o))

    def incoming(self, o, s):
        back = self.team.chips - o
        return self._copy(self.run(self.team.mine(back), s), (o - 1) * self.subs + s, self.team.peer(back))

    def forward(self, o, s, rank):
        slot = self.count + (o - 1) * self.subs + s
        return self._copy(self.run(rank(self.team.chips - o), s), slot, self.team.sibling())

    def start(self):
        self.near(self.team.mine(0)).start()
        for s in range(self.subs):
            for o in range(1, self.team.chips):
                self.direct(o, s).start()

    def finish(self):
        self.near(self.team.mine(0)).wait_send()
        for o in range(1, self.team.chips):
            for s in range(self.subs):
                self.direct(o, s).wait_send()
                self.forward(o, s, self.team.mine).wait_send()

    def arrivals(self, work, between=lambda back, s: None, after=lambda back: None):
        team = self.team
        work([block(team.mine(0), self.rows)], 0, None)
        self.near(team.other(0)).wait_recv()
        work([block(team.other(0), self.rows)], 0, None)
        for o in range(1, team.chips):
            back = team.chips - o

            @pl.loop(0, self.subs)
            def _(s):
                self.incoming(o, s).wait_recv()
                self.forward(o, s, team.mine).start()
                between(back, s)
                self.forward(o, s, team.other).wait_recv()
                work([self.run(team.mine(back), s), self.run(team.other(back), s)], back, s)

            after(back)


def rows_at(ref, runs):
    return jnp.concatenate([ref[run] for run in runs], 0) if len(runs) > 1 else ref[runs[0]]


def put_rows(ref, runs, value):
    for i, run in enumerate(runs):
        ref[run] = value[i * run.size : (i + 1) * run.size]


class Reduce:
    def __init__(self, team, rows, scratch):
        self.team, self.rows = team, rows
        (self.out, self.held, self.into, self.leave, self.land, self.own, self.xs, self.xr, self.us, self.ur) = scratch
        self.subs = subs_of(rows)
        self.size = rows // self.subs

    def run(self, s):
        return pl.ds(0, self.rows) if s is None else pl.ds(pl.multiple_of(s * self.size, self.size), self.size)

    def slot(self, o, s):
        return o * self.subs + (0 if s is None else s)

    def cross(self, o, s):
        run, slot = self.run(s), self.slot(o, s)
        return remote(
            self.out.at[o, run], self.into.at[o, run], self.xs.at[slot], self.xr.at[slot], self.team.sibling()
        )

    def leaving(self, o, s):
        run, slot = self.run(s), self.slot(o - 1, s)
        return remote(
            self.leave.at[o - 1, run], self.land.at[o - 1, run], self.us.at[slot], self.ur.at[slot], self.team.peer(o)
        )

    def put_other(self, o, s, value):
        self.out[o, self.run(s)] = value.astype(LOW)
        self.cross(o, s).start()

    def hold(self, o, s, value):
        self.held[o - 1, self.run(s)] = value

    def keep(self, value):
        self.own[...] = value

    def pass_on(self, o, s):
        run = self.run(s)
        self.cross(o, s).wait_recv()
        self.leave[o - 1, run] = (self.held[o - 1, run] + self.into[o, run].astype(F32)).astype(LOW)
        self.leaving(o, s).start()

    def finish(self, fine):
        self.cross(0, None).wait()
        for o in range(1, self.team.chips):
            for s in range(self.subs) if fine else [None]:
                self.cross(o, s).wait_send()
                self.leaving(o, s).wait()

    def total(self, rows):
        total = self.own[rows] + self.into[0, rows].astype(F32)
        for o in range(self.team.chips - 1):
            total = total + self.land[o, rows].astype(F32)
        return total


def semaphores(n):
    return pltpu.SemaphoreType.DMA((max(n, 1),))


def gather_scratch(chips, rows):
    n = 2 * (chips - 1) * subs_of(rows) + 1
    return [semaphores(n), semaphores(n)]


def reduce_scratch(chips, rows, width):
    subs = subs_of(rows)
    return [
        pltpu.VMEM((chips, rows, width), LOW),
        pltpu.VMEM((chips - 1, rows, width), F32),
        pltpu.VMEM((chips, rows, width), LOW),
        pltpu.VMEM((chips - 1, rows, width), LOW),
        pltpu.VMEM((chips - 1, rows, width), LOW),
        pltpu.VMEM((rows, width), F32),
        semaphores(chips * subs),
        semaphores(chips * subs),
        semaphores((chips - 1) * subs),
        semaphores((chips - 1) * subs),
    ]


def by_rows(rows, body):
    step = min(32, rows)

    @pl.loop(0, rows // step)
    def _(i):
        body(pl.ds(pl.multiple_of(i * step, step), step))


def by_tiles(rows, body):
    step = next(n for n in (64, 32, 16) if rows % n == 0)

    @pl.loop(0, rows // step)
    def _(i):
        body(pl.ds(pl.multiple_of(i * step, step), step))


def swap_halves(u):
    columns, half = u.shape[1], HD // 2
    if columns % 128:
        parts = []
        for at in range(0, columns, HD):
            parts += [u[:, at + half : at + HD], u[:, at : at + half]]
        return jnp.concatenate(parts, 1)
    lane = lax.broadcasted_iota(jnp.int32, u.shape, 1)
    return jnp.where(lane % HD < half, pltpu.roll(u, columns - half, 1), pltpu.roll(u, half, 1))


def head_row(columns, head):
    lane = lax.broadcasted_iota(jnp.int32, (1, columns), 1)
    return (lane // HD == head).astype(F32).astype(LOW)


def norm_into(buf, at, rows, read, gain):
    step = min(32, rows)

    @pl.loop(0, rows // step)
    def _(i):
        values = read(pl.ds(pl.multiple_of(i * step, step), step))
        scale = lax.rsqrt(jnp.mean(values * values, -1, keepdims=True) + EPSILON)
        buf[pl.ds(pl.multiple_of(at + i * step, step), step)] = (values * scale * gain).astype(LOW)


def norm_back(rows, read_values, read_grad, gain, read_outer, write, gain_grad_ref):
    gain_grad_ref[...] = jnp.zeros_like(gain_grad_ref)

    def body(sl):
        values = read_values(sl)
        scale = lax.rsqrt(jnp.mean(values * values, -1, keepdims=True) + EPSILON)
        unit = values * scale
        grad = read_grad(sl)
        gain_grad_ref[...] += jnp.sum(grad * unit, 0, keepdims=True)
        inner = grad * gain
        write(sl, read_outer(sl) + scale * (inner - unit * jnp.mean(inner * unit, -1, keepdims=True)))

    by_rows(rows, body)


def columns_of(width):
    step = min(256, width)
    return [slice(at, at + step) for at in range(0, width, step)]


def attend_kernel(team, hooks, *refs, layer, weights=None):
    first = layer == 0
    refs = list(refs)

    def take(n):
        taken = refs[:n]
        del refs[:n]
        return taken

    gain_ref, bias_ref, *x_ref = take(2 if first else 3)
    cos_ref, sin_ref, *before_ref = take(2 if first else 3)
    if first:
        tokens_ref, *own_refs = take(1 + len(weights.arrays))
        x1_ref, square_ref, gains_ref = take(3)
        h_ref, q_ref, k_ref, m_ref, o_ref, log_ref, x_ref, w_ref = take(8)
    else:
        (x_ref,), gains_ref = x_ref, gain_ref
        w_ref, x1_ref, square_ref, h_ref, q_ref, k_ref, m_ref, o_ref, log_ref = take(9)
    gs, gr = take(2)
    reduce_refs = take(10)
    chips, members = team.chips, 2 * team.chips
    rows, span = x1_ref.shape[0], h_ref.shape[0]
    columns = w_ref.shape[0] // 4
    heads = columns // HD
    gather = Gather(team, h_ref, rows, gs, gr)

    def begin():
        norm_into(
            h_ref, team.mine(0) * rows, rows, lambda sl: x_ref[sl].astype(F32), gains_ref[2 * layer : 2 * layer + 1]
        )
        gather.start()

    if first:
        other_gain, fs, fr, ns, nr, one = refs
        over = remote(tokens_ref.at[1 - team.half], x_ref, one.at[0], one.at[1], team.far(team.core))
        here = Local(tokens_ref.at[team.half], x_ref, one.at[2])

        @pl.when(team.home)
        def _():
            over.start()
            here.start()

        gain_copy = remote(gain_ref, other_gain, one.at[3], one.at[4], team.sibling())
        gain_copy.start()
        share = columns_at(w_ref, team.group, w_ref.shape[1] // team.groups)
        far, near = FarWeight(0, weights), NearWeight(0, weights)
        far.bind(team, *own_refs, share, fs, fr)
        near.bind(team, *own_refs, share, w_ref, ns, nr)
        far.start()
        near.start_cross()
        holds = team.home & (team.core == 0)
        loads, start = [], 0
        for i, ref in enumerate(own_refs):
            loads.append(Local(ref, lines(w_ref, start, ref.shape[0]), one.at[5 + i]))
            start += ref.shape[0]

        @pl.when(holds)
        def _():
            for copy in loads:
                copy.start()

        gain_copy.wait()
        own = team.core == 0
        gains_ref[0:2] = jnp.where(own, gain_ref[...], other_gain[...])
        gains_ref[2:4] = jnp.where(own, other_gain[...], gain_ref[...])
        pl.when(team.home)(here.wait)
        pl.when(team.away)(over.wait_recv)
        begin()
        for i in range(len(weights.parts)):
            far.arrive(i)
            near.start_along(i)
        near.finish()
        far.sent()

        @pl.when(holds)
        def _():
            for copy in loads:
                copy.wait()

        pl.when(team.home)(over.wait_send)
        hooks.done(6)
        hooks.done(7)
    else:
        begin()
        hooks.weights.wait()
        hooks.need(2)
    hooks.need(0)
    hooks.need(1)

    def project(runs, back, s):
        normed = rows_at(h_ref, runs)
        cosine, sine = rows_at(cos_ref, runs), rows_at(sin_ref, runs)
        u = mm_nt(normed, w_ref[0:columns])
        put_rows(q_ref, runs, (u * cosine + swap_halves(u) * sine).astype(LOW) * jnp.asarray(HD**-0.5, LOW))
        u = mm_nt(normed, w_ref[columns : 2 * columns])
        put_rows(k_ref, runs, (u * cosine + swap_halves(u) * sine).astype(LOW))
        v = mm_nt(normed, w_ref[2 * columns : 3 * columns]).astype(LOW)
        if not first:
            v = (0.5 * v.astype(F32) + 0.5 * rows_at(before_ref[0], runs).astype(F32)).astype(LOW)
        put_rows(m_ref, runs, v)

    gather.arrivals(project)
    for i in range(4):
        hooks.done(i)
    hooks.middle(0)
    reduce = Reduce(team, rows, reduce_refs)

    def attention(qb):
        at, upto = slice(qb * rows, (qb + 1) * rows), (qb + 1) * rows

        def one_head(head, carry):
            out, logs = carry
            mask = head_row(columns, head)
            scores = mm_nt(q_ref[at] * mask, k_ref[0:upto]) + bias_ref[:, 0:upto]
            row = lax.broadcasted_iota(jnp.int32, scores.shape, 0) + qb * rows
            column = lax.broadcasted_iota(jnp.int32, scores.shape, 1)
            scores = jnp.where(column <= row, scores, NEG_LARGE)
            peak = jnp.max(scores, -1, keepdims=True)
            weights = jnp.exp(scores - peak)
            total = jnp.sum(weights, -1, keepdims=True)
            part = mm(weights.astype(LOW), m_ref[0:upto])
            out = out + part * (mask.astype(F32) * (1.0 / total))
            lane = lax.broadcasted_iota(jnp.int32, logs.shape, 1)
            logs = jnp.where(lane == head, peak + jnp.log(total), logs)
            return out, logs

        out, logs = lax.fori_loop(
            0, heads, one_head, (jnp.zeros((rows, columns), F32), jnp.zeros((rows, 128), F32))
        )
        o_ref[at] = out.astype(LOW)
        log_ref[qb] = jnp.transpose(logs)[0 : log_ref.shape[1]]

    @pl.loop(0, members)
    def _(p):
        o = chips - 1 - p // 2
        own = p % 2 == 1
        rank = team.chip(o) + jnp.where(own, team.core, 1 - team.core) * chips
        for qb in range(members):
            pl.when(rank == qb)(functools.partial(attention, qb))
        value = mm(o_ref[block(rank, rows)], w_ref[3 * columns : 4 * columns])
        pl.when(no(own))(lambda: reduce.put_other(o, None, value))

        @pl.when(own & (o > 0))
        def _():
            reduce.hold(o, None, value)
            reduce.pass_on(o, None)

        pl.when(own & (o == 0))(lambda: reduce.keep(value))
        pl.when(p == chips)(lambda: hooks.middle(1))

    hooks.done(4)
    hooks.done(5)
    hooks.middle(2)
    live = (bias_ref[...] == 0.0).astype(F32).astype(LOW)
    square = jnp.square(m_ref[...].astype(F32))
    high = square.astype(LOW)
    square_ref[...] = mm(live, high) + mm(live, (square - high.astype(F32)).astype(LOW))
    reduce.finish(False)

    def close(sl):
        x1_ref[sl] = x_ref[sl].astype(F32) + reduce.total(sl)

    by_rows(rows, close)
    gather.finish()


def stream(team, gather, reduce, work):
    def one(runs, back, s):
        value = work(runs)
        if s is not None:
            reduce.put_other(back, s, value[gather.size :])
            reduce.hold(back, s, value[: gather.size])
        elif one.kept:
            reduce.put_other(0, None, value)
        else:
            one.kept = True
            reduce.keep(value)

    one.kept = False

    def between(back, s):
        if gather.subs > 1:
            pl.when(s > 0)(lambda: reduce.pass_on(back, s - 1))

    gather.arrivals(one, between, lambda back: reduce.pass_on(back, gather.subs - 1))


def feed_kernel(
    team, hooks, x1_ref, gain_ref, w_ref, y_ref, h_ref, gate_ref, up_ref, z_ref, gs, gr, *scratch, layer
):
    rows = x1_ref.shape[0]
    hidden = w_ref.shape[0] // 3
    norm_into(h_ref, team.mine(0) * rows, rows, lambda sl: x1_ref[sl], gain_ref[2 * layer + 1 : 2 * layer + 2])
    gather = Gather(team, h_ref, rows, gs, gr)
    reduce = Reduce(team, rows, scratch)
    gather.start()
    hooks.weights.wait()

    def work(runs):
        normed = rows_at(h_ref, runs)
        gate = mm_nt(normed, w_ref[0:hidden])
        up = mm_nt(normed, w_ref[hidden : 2 * hidden])
        put_rows(gate_ref, runs, gate.astype(LOW))
        put_rows(up_ref, runs, up.astype(LOW))
        z = (gate / (1.0 + jnp.exp(-gate)) * up).astype(LOW)
        put_rows(z_ref, runs, z)
        return mm(z, w_ref[2 * hidden : 3 * hidden])

    stream(team, gather, reduce, work)
    for i in range(4):
        hooks.done(i)
    reduce.finish(True)

    def close(sl):
        y_ref[sl] = (x1_ref[sl] + reduce.total(sl)).astype(LOW)

    by_rows(rows, close)
    gather.finish()


def feed_back_kernel(
    team, hooks, g_ref, x1_ref, gain_ref, gate_ref, up_ref, h_ref, z_ref, w_ref,
    dx1_ref, gain_grad_ref, w_grad_ref, grad_ref, dgate_ref, dup_ref, gs, gr, *scratch, layer,
):
    rows, width = g_ref.shape
    hidden = w_ref.shape[0] // 3
    grad_ref[block(team.mine(0), rows)] = g_ref[...]
    gather = Gather(team, grad_ref, rows, gs, gr)
    reduce = Reduce(team, rows, scratch)
    gather.start()
    hooks.middle(0)
    hooks.weights.wait()
    hooks.need(0)
    hooks.need(1)

    def work(runs):
        dz = mm_nt(rows_at(grad_ref, runs), w_ref[2 * hidden : 3 * hidden])
        gate = rows_at(gate_ref, runs).astype(F32)
        sigma = 1.0 / (1.0 + jnp.exp(-gate))
        dgate = (dz * rows_at(up_ref, runs).astype(F32) * sigma * (1.0 + gate * (1.0 - sigma))).astype(LOW)
        dup = (dz * gate * sigma).astype(LOW)
        put_rows(dgate_ref, runs, dgate)
        put_rows(dup_ref, runs, dup)
        return mm(dgate, w_ref[0:hidden]) + mm(dup, w_ref[hidden : 2 * hidden])

    stream(team, gather, reduce, work)
    hooks.need(2)
    hooks.need(3)
    for at in columns_of(width):
        w_grad_ref[0:hidden, at] = mm_tn(dgate_ref[...], h_ref[:, at]).astype(LOW)
        w_grad_ref[hidden : 2 * hidden, at] = mm_tn(dup_ref[...], h_ref[:, at]).astype(LOW)
        w_grad_ref[2 * hidden : 3 * hidden, at] = mm_tn(z_ref[...], grad_ref[:, at]).astype(LOW)
    hooks.done(0)
    reduce.finish(True)

    def write(sl, value):
        dx1_ref[sl] = value

    norm_back(
        rows,
        lambda sl: x1_ref[sl],
        reduce.total,
        gain_ref[2 * layer + 1 : 2 * layer + 2],
        lambda sl: g_ref[sl].astype(F32),
        write,
        gain_grad_ref,
    )
    gather.finish()


def pair_slot(members, kb, qb):
    return kb * members - kb * (kb - 1) // 2 + qb - kb


def attend_back_kernel(team, hooks, *refs, layer, last):
    refs = list(refs)
    dx1_ref, gain_ref, bias_ref, k_ref, q_ref, log_ref, o_ref, m_ref, cos_ref, sin_ref, h_ref, x_ref = refs[:12]
    refs = refs[12:]
    value_grad_ref = None if last else refs.pop(0)
    w_ref, low_ref, gain_grad_ref = refs[:3]
    refs = refs[3:]
    value_sent_ref = refs.pop(0) if last else None
    w_grad_ref, grad_ref, do_ref, inner_ref, kt_ref, soft_ref, dm_ref, dk_ref, dq_ref, dqkv_ref, mask_ref = refs[:11]
    gs, gr = refs[11:13]
    chips, members = team.chips, 2 * team.chips
    rows, width = dx1_ref.shape
    span, columns = q_ref.shape
    heads = columns // HD
    at = team.mine(0) * rows

    def low_rows(sl):
        grad_ref[pl.ds(pl.multiple_of(at + sl.start, sl.size), sl.size)] = dx1_ref[sl].astype(LOW)

    by_rows(rows, low_rows)
    gather = Gather(team, grad_ref, rows, gs, gr)
    reduce = Reduce(team, rows, refs[13:])
    gather.start()
    for i in range(3):
        hooks.need(i)
    dq_ref[...] = jnp.zeros_like(dq_ref)

    @pl.loop(0, members)
    def _(kb):
        ks = block(kb, rows)
        kt_ref[kb] = jnp.transpose(k_ref[ks])

        @pl.loop(kb, members)
        def _(qb):
            key = lax.broadcasted_iota(jnp.int32, (rows, rows), 0) + kb * rows
            query = lax.broadcasted_iota(jnp.int32, (rows, rows), 1) + qb * rows
            mask_ref[...] = jnp.where(key <= query, 0.0, NEG_LARGE) + bias_ref[ks]
            for head in range(heads):
                q = q_ref[block(qb, rows)] * head_row(columns, head)
                scores = mm_nt(k_ref[ks], q) + mask_ref[...] - log_ref[qb, head : head + 1]
                soft_ref[pair_slot(members, kb, qb), head] = jnp.exp(scores).astype(LOW)

    hooks.middle(0)
    hooks.weights.wait()
    for i in range(3, 9 if last else 10):
        hooks.need(i)

    def upstream(runs, back, s):
        put_rows(do_ref, runs, mm_nt(rows_at(grad_ref, runs), w_ref[3 * columns : 4 * columns]).astype(LOW))

    gather.arrivals(upstream)
    pad = inner_ref.shape[1]
    pick = (
        lax.broadcasted_iota(jnp.int32, (pad, columns), 1) // HD == lax.broadcasted_iota(jnp.int32, (pad, columns), 0)
    )
    pick = pick.astype(F32).astype(LOW)

    @pl.loop(0, members)
    def _(b):
        sl = block(b, rows)
        product = do_ref[sl].astype(F32) * o_ref[sl].astype(F32)
        high = product.astype(LOW)
        rest = (product - high.astype(F32)).astype(LOW)
        inner_ref[b] = mm_nt(pick, high) + mm_nt(pick, rest)

    def owner(b):
        return (b % chips - team.seat + chips) % chips, b // chips == team.core

    def settle(b):
        o, own = owner(b)
        pl.when(own & (o > 0))(lambda: reduce.pass_on(o, None))

    @pl.loop(0, members)
    def _(kb):
        ks = block(kb, rows)
        dm_ref[...] = jnp.zeros_like(dm_ref)
        dk_ref[...] = jnp.zeros_like(dk_ref)

        @pl.loop(kb, members)
        def _(qb):
            qs = block(qb, rows)
            for head in range(heads):
                mask = head_row(columns, head)
                q, do = q_ref[qs] * mask, do_ref[qs] * mask
                soft = soft_ref[pair_slot(members, kb, qb), head]
                dsoft = mm_nt(m_ref[ks], do)
                ds = (soft.astype(F32) * (dsoft - inner_ref[qb, head : head + 1])).astype(LOW)
                dm_ref[...] += mm(soft, do)
                dk_ref[...] += mm(ds, q)
                part = slice(head * HD, (head + 1) * HD)
                dq_ref[qb, part] += mm(kt_ref[kb, part], ds)

        cosine, sine = cos_ref[ks], sin_ref[ks]
        dq = jnp.transpose(dq_ref[kb]) * HD**-0.5
        dqkv_ref[0, ks] = (dq * cosine - swap_halves(dq) * sine).astype(LOW)
        dk = dk_ref[...]
        dqkv_ref[1, ks] = (dk * cosine - swap_halves(dk) * sine).astype(LOW)
        if last:
            dv = (0.5 * dm_ref[...]).astype(LOW)
            value_sent_ref[ks] = dv
        else:
            dv = (dm_ref[...] + value_grad_ref[ks].astype(F32)).astype(LOW)
        dqkv_ref[2, ks] = dv
        value = mm(dqkv_ref[0, ks], w_ref[0:columns])
        for t in (1, 2):
            value = value + mm(dqkv_ref[t, ks], w_ref[t * columns : (t + 1) * columns])
        o, own = owner(kb)
        pl.when(no(own))(lambda: reduce.put_other(o, None, value))
        pl.when(own & (o > 0))(lambda: reduce.hold(o, None, value))
        pl.when(own & (o == 0))(lambda: reduce.keep(value))
        pl.when(kb > 0)(lambda: settle(kb - 1))

    settle(members - 1)
    for piece in columns_of(width):
        w_grad_ref[3 * columns : 4 * columns, piece] = mm_tn(o_ref[...], grad_ref[:, piece]).astype(LOW)
        for t in range(3):
            w_grad_ref[t * columns : (t + 1) * columns, piece] = mm_tn(dqkv_ref[t], h_ref[:, piece]).astype(LOW)
    hooks.done(0)
    reduce.finish(False)

    def write(sl, value):
        low_ref[sl] = value.astype(LOW)

    norm_back(
        rows,
        lambda sl: x_ref[sl].astype(F32),
        reduce.total,
        gain_ref[2 * layer : 2 * layer + 1],
        lambda sl: dx1_ref[sl],
        write,
        gain_grad_ref,
    )
    gather.finish()


class Parts:
    def __init__(self, arrays, parts):
        self.arrays, self.parts = arrays, parts
        self.lines = sum(a.shape[0] for a in arrays)
        self.width = arrays[0].shape[1]

    def own(self, refs, i):
        array, start, rows, _ = self.parts[i]
        return lines(refs[array], start, rows)

    def of_block(self, ref, i):
        _, _, rows, start = self.parts[i]
        return lines(ref, start, rows)


class Job:
    args, outs, sems, scratch = (), (), (), ()

    def middle(self, step):
        pass


class FarWeight(Job):
    def __init__(self, layer, block, at=None):
        self.layer, self.block, self.at, self.args = layer, block, at, list(block.arrays)
        self.outs = [((block.lines, block.width // lax.axis_size("dp")), LOW)]
        self.sems = [len(block.parts), len(block.parts)]

    def bind(self, team, *refs):
        *self.own, self.piece, self.send, self.recv = refs
        self.team = team

    def copy(self, i):
        team, size = self.team, self.piece.shape[1]
        return remote(
            columns_at(self.block.own(self.own, i), team.group, size),
            self.block.of_block(self.piece, i),
            self.send.at[i],
            self.recv.at[i],
            team.far(team.half),
        )

    def send_all(self):
        @pl.when(self.team.core == self.layer)
        def _():
            for i in range(len(self.block.parts)):
                self.copy(i).start()

    def start(self):
        if self.at is None:
            self.send_all()

    def middle(self, step):
        if self.at == step:
            self.send_all()

    def arrive(self, i):
        pl.when(self.team.away)(lambda: self.copy(i).wait_recv())

    def sent(self):
        @pl.when(self.team.core == self.layer)
        def _():
            for i in range(len(self.block.parts)):
                self.copy(i).wait_send()

    def finish(self):
        for i in range(len(self.block.parts)):
            self.arrive(i)
        self.sent()


class NearWeight(Job):
    def __init__(self, layer, block, piece=None):
        groups, n = lax.axis_size("dp"), len(block.parts)
        self.layer, self.block, self.n = layer, block, n
        self.args = list(block.arrays) + ([] if piece is None else [piece])
        self.outs = [((block.lines, block.width), LOW)]
        self.sems = [groups * n, groups * n]

    def bind(self, team, *refs):
        *self.own, self.piece, self.full, self.send, self.recv = refs
        self.team = team

    def cross(self, i):
        return remote(
            self.block.own(self.own, i),
            self.block.of_block(self.full, i),
            self.send.at[i],
            self.recv.at[i],
            self.team.sibling(),
        )

    def along(self, i, o, arriving=False):
        team, size = self.team, self.piece.shape[1]
        group = (team.group + team.groups - o) % team.groups if arriving else team.group
        return remote(
            self.block.of_block(self.piece, i),
            columns_at(self.block.of_block(self.full, i), group, size),
            self.send.at[o * self.n + i],
            self.recv.at[o * self.n + i],
            team.dp(o),
        )

    def start_cross(self):
        @pl.when(self.team.away & (self.team.core == self.layer))
        def _():
            for i in range(self.n):
                self.cross(i).start()

    def start_along(self, i):
        @pl.when(self.team.away)
        def _():
            for o in range(1, self.team.groups):
                self.along(i, o).start()

    def start(self):
        for i in range(self.n):
            self.start_along(i)
        self.start_cross()

    def finish(self):
        team = self.team
        same = team.core == self.layer

        @pl.when(team.away & same)
        def _():
            for i in range(self.n):
                self.cross(i).wait_send()

        @pl.when(team.home & no(same))
        def _():
            for i in range(self.n):
                self.cross(i).wait_recv()

        @pl.when(team.away)
        def _():
            for i in range(self.n):
                for o in range(1, team.groups):
                    self.along(i, o).wait_send()
                    self.along(i, o, arriving=True).wait_recv()


class WeightLoad:
    def __init__(self, layer, block, team, *refs):
        self.layer, self.block, self.team = layer, block, team
        *self.own, self.full, self.piece, self.buf, self.sems = refs

    def each(self, act):
        team, size = self.team, self.piece.shape[1]
        same = team.core == self.layer

        @pl.when(team.home & same)
        def _():
            start = 0
            for i, ref in enumerate(self.own):
                act(Local(ref, lines(self.buf, start, ref.shape[0]), self.sems.at[i]))
                start += ref.shape[0]

        pl.when(team.home & no(same))(lambda: act(Local(self.full, self.buf, self.sems.at[0])))

        @pl.when(team.away)
        def _():
            act(Local(self.piece, columns_at(self.buf, team.group, size), self.sems.at[0]))
            for o in range(1, team.groups):
                at = (team.group + o) % team.groups
                act(Local(columns_at(self.full, at, size), columns_at(self.buf, at, size), self.sems.at[o]))

    def start(self):
        self.each(lambda c: c.start())

    def wait(self):
        self.each(lambda c: c.wait())


class FullLoad:
    def __init__(self, team, full, buf, sems):
        self.copy = Local(full, buf, sems.at[0])
        self.start, self.wait = self.copy.start, self.copy.wait


class WholeWeight(Job):
    def __init__(self, layer, block, at, steps):
        self.far, self.near = FarWeight(layer, block, at), NearWeight(layer, block)
        self.steps, self.args = steps, list(block.arrays)
        self.outs = self.near.outs + self.far.outs
        self.sems = self.far.sems + self.near.sems

    def bind(self, team, *refs):
        *own, full, piece, far_send, far_recv, near_send, near_recv = refs
        self.far.bind(team, *own, piece, far_send, far_recv)
        self.near.bind(team, *own, piece, full, near_send, near_recv)

    def start(self):
        self.far.start()

    def middle(self, step):
        self.far.middle(step)
        if step == self.far.at:
            self.near.start_cross()
        for i, at in enumerate(self.steps):
            if at == step:
                self.far.arrive(i)
                self.near.start_along(i)

    def finish(self):
        self.near.finish()
        self.far.sent()


class OwnRows(Job):
    def __init__(self, blocks):
        self.args, self.outs, self.sems = [blocks], [(blocks.shape[1:], LOW)], [1, 1]

    def bind(self, team, blocks, rows, send, recv):
        self.team = team
        self.copy = remote(blocks.at[1 - team.half], rows, send.at[0], recv.at[0], team.far(team.core))

    def start(self):
        pl.when(self.team.home)(lambda: self.copy.start())

    def finish(self):
        pl.when(self.team.home)(lambda: self.copy.wait_send())
        pl.when(self.team.away)(lambda: self.copy.wait_recv())


class PlaceRows(Job):
    def __init__(self, first, second):
        self.args, self.outs, self.sems = [first, second], [((2,) + first.shape, LOW)], [2, 2]

    def bind(self, team, first, second, placed, send, recv):
        self.team, self.layers, self.placed = team, (first, second), placed
        self.send, self.recv = send, recv

    def far(self, layer):
        slot = self.placed.at[self.team.half]
        return remote(self.layers[layer], slot, self.send.at[layer], self.recv.at[0], self.team.far(layer))

    def near(self, layer):
        slot = self.placed.at[self.team.half]
        return remote(self.layers[layer], slot, self.send.at[layer], self.recv.at[1], self.team.sibling())

    def each(self, act):
        team = self.team
        for layer in range(2):
            pl.when(team.home & (team.core != layer))(lambda: act(self.near(layer)))
            pl.when(team.away)(lambda: act(self.far(layer)))

    def start(self):
        self.each(lambda c: c.start())

    def finish(self):
        self.each(lambda c: c.wait_send())
        team = self.team
        there = self.placed.at[1 - team.half]
        remote(self.layers[0], there, self.send.at[0], self.recv.at[0], team.far(0)).wait_recv()
        pl.when(team.away)(lambda: self.near(0).wait_recv())


class Scatter(Job):
    def __init__(self, part):
        rows, width = part.shape
        groups = lax.axis_size("dp")
        self.args, self.outs = [part], [((groups - 1, rows, width // groups), LOW)]
        self.sems = [groups - 1, groups - 1]

    def bind(self, team, part, land, send, recv):
        self.copies = scatter_copies(team, part, land, send, recv)

    def start(self):
        for copy in self.copies:
            copy.start()

    def finish(self):
        for copy in self.copies:
            copy.wait()


def scatter_copies(team, part, land, send, recv):
    return [
        remote(
            columns_at(part, (team.group + o) % team.groups, land.shape[2]),
            land.at[o - 1],
            send.at[o - 1],
            recv.at[o - 1],
            team.dp(o),
        )
        for o in range(1, team.groups)
    ]


class Swap:
    def __init__(self, team, layer, share, land, send, recv):
        self.team, self.layer = team, layer
        self.far = remote(share, land.at[0], send.at[0], recv.at[0], team.far(layer))
        self.near = remote(share, land.at[1], send.at[0], recv.at[1], team.sibling())

    def each(self, act):
        team = self.team
        pl.when(team.away)(lambda: act(self.far))
        pl.when(team.home & (team.core != self.layer))(lambda: act(self.near))

    def start(self):
        self.each(lambda c: c.start())

    def finish(self):
        self.each(lambda c: c.wait_send())
        team = self.team
        pl.when(team.core == self.layer)(lambda: self.far.wait_recv())
        pl.when((team.core == self.layer) & team.away)(lambda: self.near.wait_recv())


def add_landed(team, out, own, landed):
    def body(sl):
        total = own[sl].astype(F32)
        for o in range(team.groups - 1):
            total = total + landed[o, sl].astype(F32)
        out[sl] = total.astype(LOW)

    by_tiles(out.shape[0], body)


def add_swapped(team, out, share, landed):
    def body(sl):
        near = jnp.where(team.home, share[sl].astype(F32), landed[1, sl].astype(F32))
        out[sl] = (near + landed[0, sl].astype(F32)).astype(LOW)

    by_tiles(out.shape[0], body)


class SumSwap(Job):
    def __init__(self, layer, part, landed):
        share = landed.shape[1:]
        self.layer, self.args = layer, [part, landed]
        self.outs = [(share, LOW), ((2,) + share, LOW)]
        self.sems = [1, 2, 2, 1]
        self.scratch = [(share, LOW), (landed.shape, LOW), (share, LOW)]

    def bind(self, team, part, landed, share_out, land, send, recv, load, leave, own, came, share):
        self.team, self.own, self.came, self.share = team, own, came, share
        self.loads = [Local(columns_at(part, team.group, own.shape[1]), own, load.at[0]), Local(landed, came, load.at[1])]
        self.out = Local(share, share_out, leave.at[0])
        self.swap = Swap(team, self.layer, share, land, send, recv)

    def start(self):
        for copy in self.loads:
            copy.start()

    def middle(self, step):
        if step == 0:
            for copy in self.loads:
                copy.wait()
            add_landed(self.team, self.share, self.own, self.came)
            self.swap.start()
            self.out.start()

    def finish(self):
        self.swap.finish()
        self.out.wait()


class Spread:
    def __init__(self, team, share, fulls, send, recv, here):
        self.team, self.share, self.fulls, self.send, self.recv, self.here = team, share, fulls, send, recv, here
        self.low, self.high = sides(team.groups)

    @staticmethod
    def moves(groups):
        low, high = sides(groups)
        upper = [(True, (0, a), (0, 0)) for a in range(1, low)]
        upper += [(True, (b, 0), (0, a)) for b in range(1, high) for a in range(low)]
        lower = [(False, (b, 0), (0, 0)) for b in range(1, high)]
        lower += [(False, (0, a), (b, 0)) for a in range(1, low) for b in range(high)]
        return upper + lower

    def group(self, high, low):
        team = self.team
        return (
            (team.group // self.low + self.high - high) % self.high * self.low
            + (team.group % self.low + self.low - low) % self.low
        )

    def copies(self, first, arriving=False):
        team, size = self.team, self.share.shape[1]
        start = 0
        moves = self.moves(team.groups)
        for i, full in enumerate(self.fulls):
            rows = full.shape[0]
            cut = rows // 32 * 16
            for n, (upper, (high, low), (from_high, from_low)) in enumerate(moves):
                if ((from_high, from_low) == (0, 0)) != first:
                    continue
                at, count = (0, cut) if upper else (cut, rows - cut)
                slot = i * len(moves) + n
                back = arriving * high + from_high, arriving * low + from_low
                there = columns_at(lines(full, at, count), self.group(*back), size)
                src = lines(self.share, start + at, count) if first else there
                target = self.group(-high, -low)
                device = (team.core, target, team.along)
                yield remote(src, there, self.send.at[slot], self.recv.at[slot], device)
            start += rows

    def stays(self):
        start = 0
        for i, full in enumerate(self.fulls):
            there = columns_at(full, self.team.group, self.share.shape[1])
            yield Local(lines(self.share, start, full.shape[0]), there, self.here.at[i])
            start += full.shape[0]

    def start(self):
        for copy in (*self.copies(True), *self.stays()):
            copy.start()

    def middle(self):
        for copy in self.copies(True, arriving=True):
            copy.wait_recv()
        for copy in self.copies(False):
            copy.start()

    def finish(self):
        for copy in self.stays():
            copy.wait()
        for first in (True, False):
            for copy in self.copies(first):
                copy.wait_send()
        for copy in self.copies(False, arriving=True):
            copy.wait_recv()


def sides(groups):
    low = 2 if groups % 2 == 0 else 1
    return low, groups // low


class Hooks:
    def __init__(self, late, drains, weights, jobs):
        self.late, self.drains, self.weights, self.jobs = late, drains, weights, jobs

    def need(self, index):
        self.late[index].wait()

    def done(self, index):
        self.drains[index].start()

    def middle(self, step):
        for job in self.jobs:
            job.middle(step)


def call(
    body, chips, ident, flops, args=(), late=(), weights=None, far_args=(), outs=(), far_outs=(), drained=(),
    scratch=(), jobs=(), partners=Team.partners,
):
    vmem, far = pl.BlockSpec(memory_space=pltpu.VMEM), pl.BlockSpec(memory_space=pl.ANY)
    job_args = [a for job in jobs for a in job.args]
    job_outs = [o for job in jobs for o in job.outs]
    job_sems = [semaphores(n) for job in jobs for n in job.sems]
    job_scratch = [pltpu.VMEM(shape, dtype) for job in jobs for shape, dtype in job.scratch]
    sources = []
    if weights:
        sources = list(weights) if len(weights) == 1 else [*weights[1].arrays, *weights[2:]]
    weight_bufs = [pltpu.VMEM(a.shape, LOW) for a in (weights[0:1] if len(sources) == 1 else sources[-2:-1])]

    def kernel(*refs):
        refs = list(refs)

        def take(n):
            taken = refs[:n]
            del refs[:n]
            return taken

        ins, late_ins, weight_ins = take(len(args)), take(len(late)), take(len(sources))
        far_ins, job_ins = take(len(far_args)), take(len(job_args))
        results, drained_results, job_results = take(len(outs) + len(far_outs)), take(len(drained)), take(len(job_outs))
        own, late_bufs, drain_bufs = take(len(scratch)), take(len(late)), take(len(drained))
        weight_buf, (late_sem, drain_sem, weight_sem) = take(len(weight_bufs)), take(3)
        sems, buffers = take(len(job_sems)), refs
        team = Team(chips)
        loads = [Local(src, dst, late_sem.at[i]) for i, (src, dst) in enumerate(zip(late_ins, late_bufs))]
        load = None
        if len(sources) == 1:
            load = FullLoad(team, *weight_ins, *weight_buf, weight_sem)
        elif sources:
            load = WeightLoad(*weights[:2], team, *weight_ins, *weight_buf, weight_sem)
        if load:
            load.start()
        for copy in loads:
            copy.start()
        team.enter(partners(team))
        for job in jobs:
            parts = []
            for pool, n in (
                (job_ins, len(job.args)), (job_results, len(job.outs)),
                (sems, len(job.sems)), (buffers, len(job.scratch)),
            ):
                parts += pool[:n]
                del pool[:n]
            job.bind(team, *parts)
        for job in jobs:
            job.start()
        drains = [Local(src, dst, drain_sem.at[i]) for i, (src, dst) in enumerate(zip(drain_bufs, drained_results))]
        hooks = Hooks(loads, drains, load, jobs)
        body(team, hooks, *ins, *late_bufs, *weight_buf, *far_ins, *results, *drain_bufs, *own)
        for job in jobs:
            job.finish()
        for copy in drains:
            copy.wait()

    moved = sum(a.size * a.dtype.itemsize for a in (*args, *late))
    results = pl.pallas_call(
        kernel,
        out_shape=[jax.ShapeDtypeStruct(shape, dtype) for shape, dtype in (*outs, *far_outs, *drained, *job_outs)],
        in_specs=[vmem] * len(args) + [far] * (len(late) + len(sources) + len(far_args) + len(job_args)),
        out_specs=[vmem] * len(outs) + [far] * (len(far_outs) + len(drained) + len(job_outs)),
        scratch_shapes=[
            *scratch,
            *(pltpu.VMEM(a.shape, a.dtype) for a in late),
            *(pltpu.VMEM(shape, dtype) for shape, dtype in drained),
            *weight_bufs,
            semaphores(len(late)), semaphores(len(drained)), semaphores(lax.axis_size("dp")), *job_sems, *job_scratch,
        ],
        cost_estimate=pl.CostEstimate(flops=WAITING * flops, bytes_accessed=moved, transcendentals=0),
        compiler_params=pltpu.CompilerParams(
            collective_id=ident, has_side_effects=True, vmem_limit_bytes=VMEM_BYTES
        ),
    )(*args, *late, *sources, *far_args, *job_args)
    job_results = []
    at = len(outs) + len(far_outs) + len(drained)
    for job in jobs:
        job_results.append(results[at : at + len(job.outs)])
        at += len(job.outs)
    return results[: len(outs) + len(far_outs) + len(drained)], job_results


def rope_tables(span, columns):
    position = jnp.arange(span, dtype=F32)
    freqs = ROPE_BASE ** (-jnp.arange(0, HD, 2, dtype=F32) / HD)
    angle = position[:, None] * freqs[None, :]
    heads = columns // HD
    cosine = jnp.tile(jnp.concatenate([jnp.cos(angle), jnp.cos(angle)], -1), (1, heads))
    sine = jnp.tile(jnp.concatenate([-jnp.sin(angle), jnp.sin(angle)], -1), (1, heads))
    return cosine, sine


def everywhere_sum(team, refs):
    small_ref, sum_ref, near, groups_ref, members_ref, send, recv, gs, gr, ms, mr = refs
    copy = remote(small_ref, near, send.at[0], recv.at[0], team.sibling())
    copy.start()
    copy.wait()
    groups_ref[team.group] = small_ref[...] + near[...]

    def exchange(ref, mine, count, device, send, recv):
        for o in range(1, count):
            remote(ref.at[mine], ref.at[mine], send.at[o - 1], recv.at[o - 1], device(o)).start()
        for o in range(1, count):
            remote(ref.at[mine], ref.at[mine], send.at[o - 1], recv.at[o - 1], device(o)).wait_send()
            there = ref.at[(mine + count - o) % count]
            remote(there, there, send.at[o - 1], recv.at[o - 1], device(o)).wait_recv()
        total = ref[0]
        for i in range(1, count):
            total = total + ref[i]
        return total

    members = 2 * team.chips
    members_ref[team.along] = exchange(groups_ref, team.group, team.groups, team.dp, gs, gr)
    sum_ref[...] = exchange(members_ref, team.along, members, team.member, ms, mr)


def tail_kernel(team, hooks, *refs):
    refs = list(refs)

    def take(n):
        taken = refs[:n]
        del refs[:n]
        return taken

    small_parts = take(7)
    feed_came, feed_share1, feed_land1, attn_share1, attn_land1 = take(5)
    feed_part, attn_part = take(2)
    sum_ref, *fulls = take(5)
    feed_own, feed_share, feed_land, feed_out = take(4)
    attn_own, attn_came, attn_share, attn_land, attn_out = take(5)
    own_sem, ss, sr, fs, fr, as_, ar = take(7)
    feed_spread = Spread(team, feed_out, fulls[:2], *take(3))
    attn_spread = Spread(team, attn_out, fulls[2:], *take(3))
    small_ref, *small = refs
    last = team.core == 0
    size = feed_own.shape[1]
    scatter = scatter_copies(team, attn_part, attn_came, ss, sr)
    for copy in scatter:
        copy.start()
    loads = [
        Local(columns_at(feed_part, team.group, size), feed_own, own_sem.at[0]),
        Local(columns_at(attn_part, team.group, size), attn_own, own_sem.at[1]),
    ]
    for copy in loads:
        copy.start()
    feed_swap = Swap(team, 0, feed_share, feed_land, fs, fr)
    attn_swap = Swap(team, 0, attn_share, attn_land, as_, ar)
    hooks.need(0)
    loads[0].wait()
    add_landed(team, feed_share, feed_own, feed_came)
    feed_swap.start()
    for i in range(1, 5):
        hooks.need(i)

    @pl.when(no(last))
    def _():
        add_swapped(team, feed_out, feed_share1, feed_land1)
        feed_spread.start()
        add_swapped(team, attn_out, attn_share1, attn_land1)
        attn_spread.start()

    small_ref[...] = jnp.zeros_like(small_ref)
    for i, part in enumerate(small_parts):
        small_ref[i : i + 1, 0 : part.shape[1]] = part[...]
    everywhere_sum(team, [small_ref, sum_ref, *small])
    loads[1].wait()
    for copy in scatter:
        copy.wait()
    add_landed(team, attn_share, attn_own, attn_came)
    attn_swap.start()
    feed_swap.finish()

    @pl.when(last)
    def _():
        add_swapped(team, feed_out, feed_share, feed_land)
        feed_spread.start()

    attn_swap.finish()

    @pl.when(last)
    def _():
        add_swapped(team, attn_out, attn_share, attn_land)
        attn_spread.start()

    feed_spread.middle()
    attn_spread.middle()
    feed_spread.finish()
    attn_spread.finish()


def local(tokens, cotangent, lengths, gain_attn, w_qkv, w_out, gain_ffn, w_gate_up, w_down):
    cores, groups, members = lax.axis_size("section"), lax.axis_size("dp"), lax.axis_size("mp")
    micro, sequences, rows, width = tokens.shape
    assert cores == 2 and micro == 2 and sequences == 1 and members % 2 == 0 and members >= 4
    chips = members // 2
    span = rows * members
    columns, hidden = w_out.shape[1], w_down.shape[1]
    heads = columns // HD
    quarter = width // groups
    padded = -(-heads // 8) * 8
    core = lax.axis_index("section")
    half = lax.axis_index("mp") // chips
    home = core == half

    def vec(*shape, dtype=LOW):
        return pltpu.VMEM(shape, dtype)

    whole, of_heads, of_hidden, logs_shape = (span, width), (span, columns), (span, hidden), (members, padded, rows)
    team_scratch = gather_scratch(chips, rows) + reduce_scratch(chips, rows, width)
    own_attn = Parts(
        [w_qkv[0].reshape(3 * columns, width), w_out[0]],
        [(0, t * columns, columns, t * columns) for t in range(3)] + [(1, 0, columns, 3 * columns)],
    )
    own_feed = Parts(
        [w_gate_up[0].reshape(2 * hidden, width), w_down[0]],
        [(0, t * hidden, hidden, t * hidden) for t in range(2)] + [(1, 0, hidden, 2 * hidden)],
    )
    own_gains = jnp.concatenate([gain_attn, gain_ffn], 0)
    length = lax.dynamic_index_in_dim(lengths[:, 0], half, 0, keepdims=False)
    bias = jnp.where(jnp.arange(span) < length, 0.0, NEG_LARGE).astype(F32)
    cosine, sine = rope_tables(span, columns)

    def place(pair, placed):
        here = jnp.where(home, jnp.where(core == 0, pair[0], pair[1]), placed[half])
        return lax.dynamic_update_index_in_dim(placed, here, half, 0)

    x = gains = values = top = far_piece = attn_piece = None
    attn_weights, feed_weights = [None] * 2, [None] * 2
    kept, squares = [], []
    for layer in range(2):
        outs = [((rows, width), F32), ((1, columns), F32)]
        drained = [(whole, LOW)] + [(of_heads, LOW)] * 4 + [(logs_shape, F32)]
        if layer:
            jobs = [NearWeight(1, own_feed, far_piece), OwnRows(cotangent[:, 0])]
            more = dict(
                args=[gains, bias[None], x],
                late=[cosine, sine, values],
                weights=attn_weights[1],
                outs=outs,
                drained=drained,
                scratch=team_scratch,
            )
        else:
            jobs = [WholeWeight(0, own_feed, 0, (1, 1, 2)), FarWeight(1, own_attn, at=2)]
            n = len(own_attn.parts)
            more = dict(
                args=[own_gains, bias[None]],
                late=[cosine, sine],
                far_args=[tokens[:, 0], *own_attn.arrays],
                outs=outs + [((4, width), F32)],
                drained=drained + [((rows, width), LOW), ((4 * columns, width), LOW)],
                scratch=team_scratch
                + [vec(2, width, dtype=F32)]
                + [semaphores(n), semaphores(n), semaphores(groups * n), semaphores(groups * n), semaphores(7)],
            )
        results, came = call(
            functools.partial(attend_kernel, layer=layer, weights=own_attn),
            chips,
            layer,
            8 * span * width * columns + 4 * span * span * columns,
            jobs=jobs,
            **more,
        )
        x1, square = results[:2]
        squares.append(square)
        if layer:
            h, q, k, m, o, logs = results[2:]
            feed_weights[1] = (1, own_feed, came[0][0], far_piece)
            top = jnp.where(home, lax.dynamic_index_in_dim(cotangent[:, 0], half, 0, keepdims=False), came[1][0])
            jobs = []
        else:
            gains, h, q, k, m, o, logs, x, full = results[2:]
            attn_weights[0], values = (full,), m
            feed_weights[0] = (0, own_feed, *came[0])
            attn_piece = came[1][0]
            jobs = [NearWeight(1, own_attn, attn_piece), FarWeight(1, own_feed)]
        (y, h2, gate, up, z), came = call(
            functools.partial(feed_kernel, layer=layer),
            chips,
            2 + layer,
            6 * span * width * hidden,
            args=[x1, gains],
            weights=feed_weights[layer],
            outs=[((rows, width), LOW)],
            drained=[(whole, LOW)] + [(of_hidden, LOW)] * 3,
            scratch=team_scratch,
            jobs=jobs,
        )
        if layer == 0:
            attn_weights[1], far_piece = (1, own_attn, came[0][0], attn_piece), came[1][0]
        kept.append((x, x1, h, q, k, m, o, logs, h2, gate, up, z, y))
        x = y

    grad, value_grad = top, None
    gain_grads, low_grads = [None] * 2, [None] * 2
    feed_part = attn_part = feed_came = attn_came = feed_swapped = attn_swapped = layer_out = None
    for layer in (1, 0):
        x, x1, h, q, k, m, o, logs, h2, gate, up, z, y = kept[layer]
        if layer:
            jobs = [PlaceRows(kept[0][-1], kept[1][-1])]
        else:
            jobs = [SumSwap(1, feed_part, feed_came), Scatter(attn_part)]
        (dx1, feed_gain, feed_part), came = call(
            functools.partial(feed_back_kernel, layer=layer),
            chips,
            4 + layer,
            12 * span * width * hidden,
            args=[grad, x1, gains],
            late=[gate, up, h2, z],
            weights=feed_weights[layer],
            outs=[((rows, width), F32), ((1, width), F32)],
            drained=[((3 * hidden, width), LOW)],
            scratch=[vec(*whole), vec(*of_hidden), vec(*of_hidden)] + team_scratch,
            jobs=jobs,
        )
        if layer:
            layer_out = place((kept[0][-1], kept[1][-1]), came[0][0])
            jobs = []
        else:
            feed_swapped, attn_came = came[0], came[1][0]
            jobs = [SumSwap(1, attn_part, attn_came)]
        jobs.append(Scatter(feed_part))
        results, came = call(
            functools.partial(attend_back_kernel, layer=layer, last=layer == 1),
            chips,
            6 + layer,
            16 * span * width * columns + 10 * span * span * columns,
            args=[dx1, gains, bias[:, None]],
            late=[k, q, logs, o, m, cosine, sine, h, x] + ([] if layer else [value_grad]),
            weights=attn_weights[layer],
            outs=[((rows, width), LOW), ((1, width), F32)] + ([(of_heads, LOW)] if layer else []),
            drained=[((4 * columns, width), LOW)],
            scratch=[
                vec(*whole), vec(*of_heads), vec(*logs_shape, dtype=F32), vec(members, columns, rows),
                vec(members * (members + 1) // 2, heads, rows, rows), vec(rows, columns, dtype=F32),
                vec(rows, columns, dtype=F32), vec(members, columns, rows, dtype=F32), vec(3, *of_heads),
                vec(rows, rows, dtype=F32),
            ] + team_scratch,
            jobs=jobs,
        )
        low_grads[layer], attn_gain, attn_part = results[0], results[1], results[-1]
        value_grad = results[2] if layer else None
        grad = low_grads[layer]
        feed_came = came[-1][0]
        if layer == 0:
            attn_swapped = came[0]
        gain_grads[layer] = [attn_gain, feed_gain]

    count = jnp.broadcast_to(jnp.sum(lengths).astype(F32), (1, 128))
    share_feed, share_attn = (3 * hidden, quarter), (4 * columns, quarter)
    n_moves = 2 * len(Spread.moves(groups))
    small = (8, width)
    (sums, *grads), ((placed,),) = call(
        tail_kernel,
        chips,
        8,
        0,
        args=[*gain_grads[0], *gain_grads[1], *squares, count],
        late=[feed_came, *feed_swapped, *attn_swapped],
        far_args=[feed_part, attn_part],
        outs=[(small, F32)],
        far_outs=[((n, width), LOW) for n in (2 * hidden, hidden, 3 * columns, columns)],
        scratch=[
            vec(*share_feed), vec(*share_feed), vec(2, *share_feed), vec(*share_feed),
            vec(*share_attn), vec(groups - 1, *share_attn), vec(*share_attn), vec(2, *share_attn), vec(*share_attn),
            *(semaphores(n) for n in (2, groups - 1, groups - 1, 1, 2, 1, 2, n_moves, n_moves, 2, n_moves, n_moves, 2)),
            *(vec(*lead, *small, dtype=F32) for lead in ((), (), (groups,), (members,))),
            *(semaphores(n) for n in (1, 1, groups - 1, groups - 1, members - 1, members - 1)),
        ],
        jobs=[PlaceRows(*low_grads)],
        partners=Team.all_partners,
    )
    gain_sums = jnp.where(core == 0, sums[0:2], sums[2:4])
    square = jnp.sum(jnp.where(core == 0, sums[4], sums[5]))
    count = sums[6, 0] / (cores * members)
    pair_sum, lower_sum, projection_sum, output_sum = (a.astype(F32) for a in grads)
    return (
        layer_out[None, :, None],
        place(low_grads, placed).astype(F32)[None, :, None],
        gain_sums[0:1],
        projection_sum.reshape(w_qkv.shape),
        output_sum[None],
        gain_sums[1:2],
        pair_sum.reshape(w_gate_up.shape),
        lower_sum[None],
        jnp.sqrt(square / (count * width)).reshape(1),
    )


def solution(mesh):
    return jax.shard_map(
        local,
        mesh=mesh,
        in_specs=(
            P(None, "dp", "mp", None),
            P(None, "dp", "mp", None),
            P(None, "dp"),
            P("section", None),
            P("section", None, "mp", None),
            P("section", "mp", None),
            P("section", None),
            P("section", None, "mp", None),
            P("section", "mp", None),
        ),
        out_specs=(
            P("section", None, "dp", "mp", None),
            P("section", None, "dp", "mp", None),
            P("section", None),
            P("section", None, "mp", None),
            P("section", "mp", None),
            P("section", None),
            P("section", None, "mp", None),
            P("section", "mp", None),
            P("section"),
        ),
        check_vma=False,
    )
```

```python
import functools

import jax
import jax.numpy as jnp
from jax import lax
from jax.experimental import pallas as pl
from jax.experimental.pallas import tpu as pltpu
from jax.sharding import PartitionSpec as P

HD = 64
EPSILON = 1e-05
ROPE_BASE = 10000.0
NEG_LARGE = -1e30
MESH = pl.DeviceIdType.MESH
F32 = jnp.float32
LOW = jnp.bfloat16
VMEM_BYTES = 56 << 20
WAITING = 12


def mm(a, b):
    return lax.dot_general(a, b, (((1,), (0,)), ((), ())), preferred_element_type=F32)


def mm_nt(a, b):
    return lax.dot_general(a, b, (((1,), (1,)), ((), ())), preferred_element_type=F32)


def mm_tn(a, b):
    return lax.dot_general(a, b, (((0,), (0,)), ((), ())), preferred_element_type=F32)


def no(flag):
    return jnp.logical_not(flag)


class Team:
    def __init__(self, chips):
        self.chips = chips
        self.groups = lax.axis_size("dp")
        self.core = lax.axis_index("section")
        self.group = lax.axis_index("dp")
        self.along = lax.axis_index("mp")
        self.half = self.along // chips
        self.seat = self.along % chips
        self.home = self.core == self.half
        self.away = jnp.logical_not(self.home)

    def chip(self, offset):
        return (self.seat + offset) % self.chips

    def sibling(self):
        return (1 - self.core, self.group, self.along)

    def peer(self, offset):
        return (self.core, self.group, self.half * self.chips + self.chip(offset))

    def mine(self, offset):
        return self.chip(offset) + self.core * self.chips

    def other(self, offset):
        return self.chip(offset) + (1 - self.core) * self.chips

    def dp(self, offset):
        return (self.core, (self.group + offset) % self.groups, self.along)

    def far(self, core):
        return (core, self.group, (self.along + self.chips) % (2 * self.chips))

    def member(self, offset):
        return (self.core, self.group, (self.along + offset) % (2 * self.chips))

    def partners(self):
        return (
            [self.sibling(), self.far(0), self.far(1)]
            + [self.peer(o) for o in range(1, self.chips)]
            + [self.dp(o) for o in range(1, self.groups)]
        )

    def all_partners(self):
        return (
            [self.sibling(), self.far(1 - self.core)]
            + [self.member(o) for o in range(1, 2 * self.chips)]
            + [self.dp(o) for o in range(1, self.groups)]
        )

    def enter(self, partners):
        barrier = pltpu.get_barrier_semaphore()
        for device in partners:
            pl.semaphore_signal(barrier, inc=1, device_id=device, device_id_type=MESH)
        pl.semaphore_wait(barrier, len(partners))


def remote(src, dst, send, recv, device):
    return pltpu.make_async_remote_copy(
        src_ref=src, dst_ref=dst, send_sem=send, recv_sem=recv, device_id=device, device_id_type=MESH
    )


class Local:
    def __init__(self, src, dst, sem):
        self.copy = pltpu.make_async_copy(src, dst, sem)
        self.start, self.wait = self.copy.start, self.copy.wait


def block(rank, rows):
    return pl.ds(pl.multiple_of(rank * rows, rows), rows)


def columns_at(ref, index, size):
    return ref.at[:, pl.ds(pl.multiple_of(index * size, size), size)]


def lines(ref, start, rows):
    return ref.at[pl.ds(start, rows)]


def subs_of(rows):
    return max(1, rows // 64)


class Gather:
    def __init__(self, team, buf, rows, send, recv, source=None):
        self.team, self.buf, self.rows, self.send, self.recv = team, buf, rows, send, recv
        self.source = source
        self.subs = subs_of(rows)
        self.size = rows // self.subs
        self.count = (team.chips - 1) * self.subs
        self.met = False

    def meet(self):
        if not self.met:
            self.near(self.team.other(0)).wait_recv()
            self.met = True

    def run(self, rank, s):
        return pl.ds(pl.multiple_of(rank * self.rows + s * self.size, self.size), self.size)

    def _copy(self, part, slot, device, src=None):
        part = self.buf.at[part]
        return remote(part if src is None else src, part, self.send.at[slot], self.recv.at[slot], device)

    def near(self, rank, leaving=False):
        src = self.source if leaving else None
        return self._copy(block(rank, self.rows), 2 * self.count, self.team.sibling(), src)

    def direct(self, o, s):
        src = None if self.source is None else self.source.at[self.run(0, s)]
        return self._copy(self.run(self.team.mine(0), s), (o - 1) * self.subs + s, self.team.peer(o), src)

    def incoming(self, o, s):
        back = self.team.chips - o
        return self._copy(self.run(self.team.mine(back), s), (o - 1) * self.subs + s, self.team.peer(back))

    def forward(self, o, s, rank):
        slot = self.count + (o - 1) * self.subs + s
        return self._copy(self.run(rank(self.team.chips - o), s), slot, self.team.sibling())

    def start(self):
        self.near(self.team.mine(0), True).start()
        for s in range(self.subs):
            for o in range(1, self.team.chips):
                self.direct(o, s).start()

    def finish(self):
        self.near(self.team.mine(0), True).wait_send()
        for o in range(1, self.team.chips):
            for s in range(self.subs):
                self.direct(o, s).wait_send()
                self.forward(o, s, self.team.mine).wait_send()

    def pass_all(self):
        for o in range(1, self.team.chips):
            for s in range(self.subs):
                self.incoming(o, s).wait_recv()
                self.forward(o, s, self.team.mine).start()

    def receive_all(self):
        for o in range(1, self.team.chips):
            for s in range(self.subs):
                self.forward(o, s, self.team.other).wait_recv()

    def arrivals(self, work, between=lambda back, s: None, after=lambda back: None):
        team = self.team
        work([block(team.mine(0), self.rows)], 0, None)
        self.meet()
        work([block(team.other(0), self.rows)], 0, None)
        for o in range(1, team.chips):
            back = team.chips - o

            @pl.loop(0, self.subs)
            def _(s):
                self.incoming(o, s).wait_recv()
                self.forward(o, s, team.mine).start()
                between(back, s)
                self.forward(o, s, team.other).wait_recv()
                work([self.run(team.mine(back), s), self.run(team.other(back), s)], back, s)

            after(back)


def rows_at(ref, runs):
    return jnp.concatenate([ref[run] for run in runs], 0) if len(runs) > 1 else ref[runs[0]]


def put_rows(ref, runs, value):
    for i, run in enumerate(runs):
        ref[run] = value[i * run.size : (i + 1) * run.size]


class Reduce:
    def __init__(self, team, rows, scratch):
        self.team, self.rows = team, rows
        (self.out, self.held, self.into, self.leave, self.land, self.own, self.xs, self.xr, self.us, self.ur) = scratch
        self.subs = subs_of(rows)
        self.size = rows // self.subs

    def run(self, s):
        return pl.ds(0, self.rows) if s is None else pl.ds(pl.multiple_of(s * self.size, self.size), self.size)

    def slot(self, o, s):
        return o * self.subs + (0 if s is None else s)

    def cross(self, o, s):
        run, slot = self.run(s), self.slot(o, s)
        return remote(
            self.out.at[o, run], self.into.at[o, run], self.xs.at[slot], self.xr.at[slot], self.team.sibling()
        )

    def leaving(self, o, s):
        run, slot = self.run(s), self.slot(o - 1, s)
        return remote(
            self.leave.at[o - 1, run], self.land.at[o - 1, run], self.us.at[slot], self.ur.at[slot], self.team.peer(o)
        )

    def put_other(self, o, s, value):
        self.out[o, self.run(s)] = value.astype(LOW)
        self.cross(o, s).start()

    def hold(self, o, s, value):
        self.held[o - 1, self.run(s)] = value

    def keep(self, value):
        self.own[...] = value

    def pass_on(self, o, s):
        run = self.run(s)
        self.cross(o, s).wait_recv()
        self.leave[o - 1, run] = (self.held[o - 1, run] + self.into[o, run].astype(F32)).astype(LOW)
        self.leaving(o, s).start()

    def finish(self, fine):
        self.cross(0, None).wait()
        for o in range(1, self.team.chips):
            for s in range(self.subs) if fine else [None]:
                self.cross(o, s).wait_send()
                self.leaving(o, s).wait()

    def total(self, rows):
        total = self.own[rows] + self.into[0, rows].astype(F32)
        for o in range(self.team.chips - 1):
            total = total + self.land[o, rows].astype(F32)
        return total


def semaphores(n):
    return pltpu.SemaphoreType.DMA((max(n, 1),))


def gather_scratch(chips, rows):
    n = 2 * (chips - 1) * subs_of(rows) + 1
    return [semaphores(n), semaphores(n)]


def reduce_scratch(chips, rows, width):
    subs = subs_of(rows)
    return [
        pltpu.VMEM((chips, rows, width), LOW),
        pltpu.VMEM((chips - 1, rows, width), F32),
        pltpu.VMEM((chips, rows, width), LOW),
        pltpu.VMEM((chips - 1, rows, width), LOW),
        pltpu.VMEM((chips - 1, rows, width), LOW),
        pltpu.VMEM((rows, width), F32),
        semaphores(chips * subs),
        semaphores(chips * subs),
        semaphores((chips - 1) * subs),
        semaphores((chips - 1) * subs),
    ]


def by_rows(rows, body):
    step = min(32, rows)

    @pl.loop(0, rows // step)
    def _(i):
        body(pl.ds(pl.multiple_of(i * step, step), step))


def by_tiles(rows, body):
    step = next(n for n in (64, 32, 16) if rows % n == 0)

    @pl.loop(0, rows // step)
    def _(i):
        body(pl.ds(pl.multiple_of(i * step, step), step))


def swap_halves(u):
    columns, half = u.shape[1], HD // 2
    if columns % 128:
        parts = []
        for at in range(0, columns, HD):
            parts += [u[:, at + half : at + HD], u[:, at : at + half]]
        return jnp.concatenate(parts, 1)
    lane = lax.broadcasted_iota(jnp.int32, u.shape, 1)
    return jnp.where(lane % HD < half, pltpu.roll(u, columns - half, 1), pltpu.roll(u, half, 1))


def head_row(columns, head):
    lane = lax.broadcasted_iota(jnp.int32, (1, columns), 1)
    return (lane // HD == head).astype(F32).astype(LOW)


def norm_into(buf, at, rows, read, gain):
    step = min(32, rows)

    @pl.loop(0, rows // step)
    def _(i):
        values = read(pl.ds(pl.multiple_of(i * step, step), step))
        scale = lax.rsqrt(jnp.mean(values * values, -1, keepdims=True) + EPSILON)
        buf[pl.ds(pl.multiple_of(at + i * step, step), step)] = (values * scale * gain).astype(LOW)


def norm_back(rows, read_values, read_grad, gain, read_outer, write, gain_grad_ref):
    gain_grad_ref[...] = jnp.zeros_like(gain_grad_ref)

    def body(sl):
        values = read_values(sl)
        scale = lax.rsqrt(jnp.mean(values * values, -1, keepdims=True) + EPSILON)
        unit = values * scale
        grad = read_grad(sl)
        gain_grad_ref[...] += jnp.sum(grad * unit, 0, keepdims=True)
        inner = grad * gain
        write(sl, read_outer(sl) + scale * (inner - unit * jnp.mean(inner * unit, -1, keepdims=True)))

    by_rows(rows, body)


def columns_of(width):
    step = min(256, width)
    return [slice(at, at + step) for at in range(0, width, step)]


def attend_kernel(team, hooks, *refs, layer, weights=None):
    first = layer == 0
    refs = list(refs)

    def take(n):
        taken = refs[:n]
        del refs[:n]
        return taken

    gain_ref, bias_ref, *x_ref = take(2 if first else 3)
    cos_ref, sin_ref, *before_ref = take(2 if first else 3)
    if first:
        tokens_ref, *own_refs = take(1 + len(weights.arrays))
        x1_ref, square_ref, gains_ref = take(3)
        h_ref, q_ref, k_ref, m_ref, o_ref, log_ref, x_ref, w_ref = take(8)
    else:
        (x_ref,), gains_ref = x_ref, gain_ref
        w_ref, x1_ref, square_ref, h_ref, q_ref, k_ref, m_ref, o_ref, log_ref = take(9)
    gs, gr = take(2)
    reduce_refs = take(10)
    chips, members = team.chips, 2 * team.chips
    rows, span = x1_ref.shape[0], h_ref.shape[0]
    columns = w_ref.shape[0] // 4
    heads = columns // HD
    gather = Gather(team, h_ref, rows, gs, gr)

    def begin():
        norm_into(
            h_ref, team.mine(0) * rows, rows, lambda sl: x_ref[sl].astype(F32), gains_ref[2 * layer : 2 * layer + 1]
        )
        gather.start()

    if first:
        other_gain, fs, fr, ns, nr, one = refs
        over = remote(tokens_ref.at[1 - team.half], x_ref, one.at[0], one.at[1], team.far(team.core))
        here = Local(tokens_ref.at[team.half], x_ref, one.at[2])

        @pl.when(team.home)
        def _():
            over.start()
            here.start()

        gain_copy = remote(gain_ref, other_gain, one.at[3], one.at[4], team.sibling())
        gain_copy.start()
        share = columns_at(w_ref, team.group, w_ref.shape[1] // team.groups)
        far, near = FarWeight(0, weights), NearWeight(0, weights)
        far.bind(team, *own_refs, share, fs, fr)
        near.bind(team, *own_refs, share, w_ref, ns, nr)
        near.start_cross()
        holds = team.home & (team.core == 0)
        loads, start = [], 0
        for i, ref in enumerate(own_refs):
            loads.append(Local(ref, lines(w_ref, start, ref.shape[0]), one.at[5 + i]))
            start += ref.shape[0]

        @pl.when(holds)
        def _():
            for copy in loads:
                copy.start()

        pl.when(team.away)(far.start)
        gain_copy.wait()
        own = team.core == 0
        gains_ref[0:2] = jnp.where(own, gain_ref[...], other_gain[...])
        gains_ref[2:4] = jnp.where(own, other_gain[...], gain_ref[...])
        pl.when(team.home)(here.wait)
        pl.when(team.away)(over.wait_recv)
        begin()

        @pl.when(team.home)
        def _():
            over.wait_send()
            far.start()

        gather.meet()
        hooks.middle(0)
        for i in range(len(weights.parts)):
            far.arrive(i)
            near.start_along(i)
        near.finish()
        far.sent()

        @pl.when(holds)
        def _():
            for copy in loads:
                copy.wait()

        hooks.done(6)
        hooks.done(7)
    else:
        begin()
        hooks.middle(0)
        hooks.weights.wait()
        hooks.need(2)
    hooks.need(0)
    hooks.need(1)

    def project(runs, back, s):
        normed = rows_at(h_ref, runs)
        cosine, sine = rows_at(cos_ref, runs), rows_at(sin_ref, runs)
        u = mm_nt(normed, w_ref[0:columns])
        put_rows(q_ref, runs, (u * cosine + swap_halves(u) * sine).astype(LOW) * jnp.asarray(HD**-0.5, LOW))
        u = mm_nt(normed, w_ref[columns : 2 * columns])
        put_rows(k_ref, runs, (u * cosine + swap_halves(u) * sine).astype(LOW))
        v = mm_nt(normed, w_ref[2 * columns : 3 * columns]).astype(LOW)
        if not first:
            v = (0.5 * v.astype(F32) + 0.5 * rows_at(before_ref[0], runs).astype(F32)).astype(LOW)
        put_rows(m_ref, runs, v)

    gather.arrivals(project)
    for i in range(4):
        hooks.done(i)
    hooks.middle(1)
    reduce = Reduce(team, rows, reduce_refs)

    def attention(qb):
        at, upto = slice(qb * rows, (qb + 1) * rows), (qb + 1) * rows

        def one_head(head, carry):
            out, logs = carry
            mask = head_row(columns, head)
            scores = mm_nt(q_ref[at] * mask, k_ref[0:upto]) + bias_ref[:, 0:upto]
            row = lax.broadcasted_iota(jnp.int32, scores.shape, 0) + qb * rows
            column = lax.broadcasted_iota(jnp.int32, scores.shape, 1)
            scores = jnp.where(column <= row, scores, NEG_LARGE)
            peak = jnp.max(scores, -1, keepdims=True)
            weights = jnp.exp(scores - peak)
            total = jnp.sum(weights, -1, keepdims=True)
            part = mm(weights.astype(LOW), m_ref[0:upto])
            out = out + part * (mask.astype(F32) * (1.0 / total))
            lane = lax.broadcasted_iota(jnp.int32, logs.shape, 1)
            logs = jnp.where(lane == head, peak + jnp.log(total), logs)
            return out, logs

        out, logs = lax.fori_loop(
            0, heads, one_head, (jnp.zeros((rows, columns), F32), jnp.zeros((rows, 128), F32))
        )
        o_ref[at] = out.astype(LOW)
        log_ref[qb] = jnp.transpose(logs)[0 : log_ref.shape[1]]

    @pl.loop(0, members)
    def _(p):
        o = chips - 1 - p // 2
        own = p % 2 == 1
        rank = team.chip(o) + jnp.where(own, team.core, 1 - team.core) * chips
        for qb in range(members):
            pl.when(rank == qb)(functools.partial(attention, qb))
        value = mm(o_ref[block(rank, rows)], w_ref[3 * columns : 4 * columns])
        pl.when(no(own))(lambda: reduce.put_other(o, None, value))

        @pl.when(own & (o > 0))
        def _():
            reduce.hold(o, None, value)
            reduce.pass_on(o, None)

        pl.when(own & (o == 0))(lambda: reduce.keep(value))
        pl.when(p == chips)(lambda: hooks.middle(2))

    hooks.done(4)
    hooks.done(5)
    hooks.middle(3)
    live = (bias_ref[...] == 0.0).astype(F32).astype(LOW)
    square = jnp.square(m_ref[...].astype(F32))
    high = square.astype(LOW)
    square_ref[...] = mm(live, high) + mm(live, (square - high.astype(F32)).astype(LOW))
    reduce.finish(False)

    def close(sl):
        x1_ref[sl] = x_ref[sl].astype(F32) + reduce.total(sl)

    by_rows(rows, close)
    gather.finish()


def stream(team, gather, reduce, work, here=False):
    def one(runs, back, s):
        value = work(runs)
        if s is not None:
            reduce.put_other(back, s, value[gather.size :])
            reduce.hold(back, s, value[: gather.size])
        elif one.kept:
            reduce.put_other(0, None, value)
        else:
            one.kept = True
            reduce.keep(value)

    one.kept = False

    def between(back, s):
        if gather.subs > 1:
            pl.when(s > 0)(lambda: reduce.pass_on(back, s - 1))

    def after(back):
        reduce.pass_on(back, gather.subs - 1)

    if not here:
        gather.arrivals(one, between, after)
        return
    for back in range(1, team.chips):

        @pl.loop(0, gather.subs)
        def _(s):
            one([gather.run(team.mine(back), s), gather.run(team.other(back), s)], back, s)
            between(back, s)

        after(back)
    one([block(team.mine(0), gather.rows)], 0, None)
    one([block(team.other(0), gather.rows)], 0, None)


def feed_kernel(
    team, hooks, x1_ref, gain_ref, w_ref, y_ref, h_ref, gate_ref, up_ref, z_ref, gs, gr, *scratch, layer
):
    rows = x1_ref.shape[0]
    hidden = w_ref.shape[0] // 3
    norm_into(h_ref, team.mine(0) * rows, rows, lambda sl: x1_ref[sl], gain_ref[2 * layer + 1 : 2 * layer + 2])
    gather = Gather(team, h_ref, rows, gs, gr)
    reduce = Reduce(team, rows, scratch)
    gather.start()
    hooks.weights.wait()

    def work(runs):
        normed = rows_at(h_ref, runs)
        gate = mm_nt(normed, w_ref[0:hidden])
        up = mm_nt(normed, w_ref[hidden : 2 * hidden])
        put_rows(gate_ref, runs, gate.astype(LOW))
        put_rows(up_ref, runs, up.astype(LOW))
        z = (gate / (1.0 + jnp.exp(-gate)) * up).astype(LOW)
        put_rows(z_ref, runs, z)
        return mm(z, w_ref[2 * hidden : 3 * hidden])

    stream(team, gather, reduce, work)
    hooks.middle(0)
    for i in range(4):
        hooks.done(i)
    reduce.finish(True)

    def close(sl):
        y_ref[sl] = (x1_ref[sl] + reduce.total(sl)).astype(LOW)

    by_rows(rows, close)
    gather.finish()


def feed_back_kernel(
    team, hooks, g_ref, x1_ref, gain_ref, gate_ref, up_ref, h_ref, z_ref, w_ref, *refs, layer, gathered,
):
    refs = list(refs)
    there = refs.pop(0) if gathered else None
    dx1_ref, gain_grad_ref, w_grad_ref, grad_ref, dgate_ref, dup_ref, gs, gr, *scratch = refs
    rows, width = g_ref.shape
    hidden = w_ref.shape[0] // 3
    grad_ref[block(team.mine(0), rows)] = g_ref[...]
    gather = Gather(team, grad_ref, rows, gs, gr)
    reduce = Reduce(team, rows, scratch)
    if gathered:
        ranks = [team.other(0)] + [rank(o) for o in range(1, team.chips) for rank in (team.mine, team.other)]
        loads = []
        for i, rank in enumerate(ranks):
            at = block(rank, rows)
            loads.append(Local(there.at[at], grad_ref.at[at], gr.at[i]))
            loads[-1].start()
    else:
        gather.start()
    hooks.middle(0)
    hooks.weights.wait()
    hooks.need(0)
    hooks.need(1)
    if gathered:
        for copy in loads:
            copy.wait()

    def work(runs):
        dz = mm_nt(rows_at(grad_ref, runs), w_ref[2 * hidden : 3 * hidden])
        gate = rows_at(gate_ref, runs).astype(F32)
        sigma = 1.0 / (1.0 + jnp.exp(-gate))
        dgate = (dz * rows_at(up_ref, runs).astype(F32) * sigma * (1.0 + gate * (1.0 - sigma))).astype(LOW)
        dup = (dz * gate * sigma).astype(LOW)
        put_rows(dgate_ref, runs, dgate)
        put_rows(dup_ref, runs, dup)
        return mm(dgate, w_ref[0:hidden]) + mm(dup, w_ref[hidden : 2 * hidden])

    stream(team, gather, reduce, work, gathered)
    hooks.middle(1)
    hooks.need(2)
    hooks.need(3)
    for at in columns_of(width):
        w_grad_ref[0:hidden, at] = mm_tn(dgate_ref[...], h_ref[:, at]).astype(LOW)
        w_grad_ref[hidden : 2 * hidden, at] = mm_tn(dup_ref[...], h_ref[:, at]).astype(LOW)
        w_grad_ref[2 * hidden : 3 * hidden, at] = mm_tn(z_ref[...], grad_ref[:, at]).astype(LOW)
    hooks.done(0)
    reduce.finish(True)

    def write(sl, value):
        dx1_ref[sl] = value

    norm_back(
        rows,
        lambda sl: x1_ref[sl],
        reduce.total,
        gain_ref[2 * layer + 1 : 2 * layer + 2],
        lambda sl: g_ref[sl].astype(F32),
        write,
        gain_grad_ref,
    )
    if not gathered:
        gather.finish()


def pair_slot(members, kb, qb):
    return kb * members - kb * (kb - 1) // 2 + qb - kb


def attend_back_kernel(team, hooks, *refs, layer, last):
    refs = list(refs)
    dx1_ref, gain_ref, bias_ref, k_ref, q_ref, log_ref, o_ref, m_ref, cos_ref, sin_ref, h_ref, x_ref = refs[:12]
    refs = refs[12:]
    value_grad_ref = None if last else refs.pop(0)
    w_ref, low_ref, gain_grad_ref = refs[:3]
    refs = refs[3:]
    value_sent_ref = refs.pop(0) if last else None
    w_grad_ref, grad_ref, do_ref, inner_ref, kt_ref, soft_ref, dm_ref, dk_ref, dq_ref, dqkv_ref, mask_ref = refs[:11]
    gs, gr = refs[11:13]
    chips, members = team.chips, 2 * team.chips
    rows, width = dx1_ref.shape
    span, columns = q_ref.shape
    heads = columns // HD
    at = team.mine(0) * rows

    def low_rows(sl):
        grad_ref[pl.ds(pl.multiple_of(at + sl.start, sl.size), sl.size)] = dx1_ref[sl].astype(LOW)

    by_rows(rows, low_rows)
    gather = Gather(team, grad_ref, rows, gs, gr)
    reduce = Reduce(team, rows, refs[13:])
    gather.start()
    for i in range(3):
        hooks.need(i)
    dq_ref[...] = jnp.zeros_like(dq_ref)

    @pl.loop(0, members)
    def _(kb):
        ks = block(kb, rows)
        kt_ref[kb] = jnp.transpose(k_ref[ks])

        @pl.loop(kb, members)
        def _(qb):
            key = lax.broadcasted_iota(jnp.int32, (rows, rows), 0) + kb * rows
            query = lax.broadcasted_iota(jnp.int32, (rows, rows), 1) + qb * rows
            mask_ref[...] = jnp.where(key <= query, 0.0, NEG_LARGE) + bias_ref[ks]
            for head in range(heads):
                q = q_ref[block(qb, rows)] * head_row(columns, head)
                scores = mm_nt(k_ref[ks], q) + mask_ref[...] - log_ref[qb, head : head + 1]
                soft_ref[pair_slot(members, kb, qb), head] = jnp.exp(scores).astype(LOW)

    hooks.middle(0)
    hooks.weights.wait()
    for i in range(3, 9 if last else 10):
        hooks.need(i)

    def upstream(runs, back, s):
        put_rows(do_ref, runs, mm_nt(rows_at(grad_ref, runs), w_ref[3 * columns : 4 * columns]).astype(LOW))

    gather.arrivals(upstream)
    hooks.middle(1)
    pad = inner_ref.shape[1]
    pick = (
        lax.broadcasted_iota(jnp.int32, (pad, columns), 1) // HD == lax.broadcasted_iota(jnp.int32, (pad, columns), 0)
    )
    pick = pick.astype(F32).astype(LOW)

    @pl.loop(0, members)
    def _(b):
        sl = block(b, rows)
        product = do_ref[sl].astype(F32) * o_ref[sl].astype(F32)
        high = product.astype(LOW)
        rest = (product - high.astype(F32)).astype(LOW)
        inner_ref[b] = mm_nt(pick, high) + mm_nt(pick, rest)

    def owner(b):
        return (b % chips - team.seat + chips) % chips, b // chips == team.core

    def settle(b):
        o, own = owner(b)
        pl.when(own & (o > 0))(lambda: reduce.pass_on(o, None))

    @pl.loop(0, members)
    def _(kb):
        ks = block(kb, rows)
        dm_ref[...] = jnp.zeros_like(dm_ref)
        dk_ref[...] = jnp.zeros_like(dk_ref)

        @pl.loop(kb, members)
        def _(qb):
            qs = block(qb, rows)
            for head in range(heads):
                mask = head_row(columns, head)
                q, do = q_ref[qs] * mask, do_ref[qs] * mask
                soft = soft_ref[pair_slot(members, kb, qb), head]
                dsoft = mm_nt(m_ref[ks], do)
                ds = (soft.astype(F32) * (dsoft - inner_ref[qb, head : head + 1])).astype(LOW)
                dm_ref[...] += mm(soft, do)
                dk_ref[...] += mm(ds, q)
                part = slice(head * HD, (head + 1) * HD)
                dq_ref[qb, part] += mm(kt_ref[kb, part], ds)

        cosine, sine = cos_ref[ks], sin_ref[ks]
        dq = jnp.transpose(dq_ref[kb]) * HD**-0.5
        dqkv_ref[0, ks] = (dq * cosine - swap_halves(dq) * sine).astype(LOW)
        dk = dk_ref[...]
        dqkv_ref[1, ks] = (dk * cosine - swap_halves(dk) * sine).astype(LOW)
        if last:
            dv = (0.5 * dm_ref[...]).astype(LOW)
            value_sent_ref[ks] = dv
        else:
            dv = (dm_ref[...] + value_grad_ref[ks].astype(F32)).astype(LOW)
        dqkv_ref[2, ks] = dv
        value = mm(dqkv_ref[0, ks], w_ref[0:columns])
        for t in (1, 2):
            value = value + mm(dqkv_ref[t, ks], w_ref[t * columns : (t + 1) * columns])
        o, own = owner(kb)
        pl.when(no(own))(lambda: reduce.put_other(o, None, value))
        pl.when(own & (o > 0))(lambda: reduce.hold(o, None, value))
        pl.when(own & (o == 0))(lambda: reduce.keep(value))
        pl.when(kb > 0)(lambda: settle(kb - 1))

    settle(members - 1)
    hooks.middle(2)
    for piece in columns_of(width):
        w_grad_ref[3 * columns : 4 * columns, piece] = mm_tn(o_ref[...], grad_ref[:, piece]).astype(LOW)
        for t in range(3):
            w_grad_ref[t * columns : (t + 1) * columns, piece] = mm_tn(dqkv_ref[t], h_ref[:, piece]).astype(LOW)
    hooks.done(0)
    reduce.finish(False)

    def write(sl, value):
        low_ref[sl] = value.astype(LOW)

    norm_back(
        rows,
        lambda sl: x_ref[sl].astype(F32),
        reduce.total,
        gain_ref[2 * layer : 2 * layer + 1],
        lambda sl: dx1_ref[sl],
        write,
        gain_grad_ref,
    )
    gather.finish()


class Parts:
    def __init__(self, arrays, parts):
        self.arrays, self.parts = arrays, parts
        self.lines = sum(a.shape[0] for a in arrays)
        self.width = arrays[0].shape[1]

    def own(self, refs, i):
        array, start, rows, _ = self.parts[i]
        return lines(refs[array], start, rows)

    def of_block(self, ref, i):
        _, _, rows, start = self.parts[i]
        return lines(ref, start, rows)


class Job:
    args, outs, sems, scratch = (), (), (), ()
    at = None

    def middle(self, step):
        pass


class FarWeight(Job):
    def __init__(self, layer, block, at=None):
        self.layer, self.block, self.at, self.args = layer, block, at, list(block.arrays)
        self.outs = [((block.lines, block.width // lax.axis_size("dp")), LOW)]
        self.sems = [len(block.parts), len(block.parts)]

    def bind(self, team, *refs):
        *self.own, self.piece, self.send, self.recv = refs
        self.team = team

    def copy(self, i):
        team, size = self.team, self.piece.shape[1]
        return remote(
            columns_at(self.block.own(self.own, i), team.group, size),
            self.block.of_block(self.piece, i),
            self.send.at[i],
            self.recv.at[i],
            team.far(team.half),
        )

    def start(self):
        @pl.when(self.team.core == self.layer)
        def _():
            for i in range(len(self.block.parts)):
                self.copy(i).start()

    def arrive(self, i):
        pl.when(self.team.away)(lambda: self.copy(i).wait_recv())

    def sent(self):
        @pl.when(self.team.core == self.layer)
        def _():
            for i in range(len(self.block.parts)):
                self.copy(i).wait_send()

    def finish(self):
        for i in range(len(self.block.parts)):
            self.arrive(i)
        self.sent()


class NearWeight(Job):
    def __init__(self, layer, block, piece=None):
        groups, n = lax.axis_size("dp"), len(block.parts)
        self.layer, self.block, self.n = layer, block, n
        self.args = list(block.arrays) + ([] if piece is None else [piece])
        self.outs = [((block.lines, block.width), LOW)]
        self.sems = [groups * n, groups * n]

    def bind(self, team, *refs):
        *self.own, self.piece, self.full, self.send, self.recv = refs
        self.team = team

    def cross(self, i):
        return remote(
            self.block.own(self.own, i),
            self.block.of_block(self.full, i),
            self.send.at[i],
            self.recv.at[i],
            self.team.sibling(),
        )

    def along(self, i, o, arriving=False):
        team, size = self.team, self.piece.shape[1]
        group = (team.group + team.groups - o) % team.groups if arriving else team.group
        return remote(
            self.block.of_block(self.piece, i),
            columns_at(self.block.of_block(self.full, i), group, size),
            self.send.at[o * self.n + i],
            self.recv.at[o * self.n + i],
            team.dp(o),
        )

    def start_cross(self):
        @pl.when(self.team.away & (self.team.core == self.layer))
        def _():
            for i in range(self.n):
                self.cross(i).start()

    def start_along(self, i):
        @pl.when(self.team.away)
        def _():
            for o in range(1, self.team.groups):
                self.along(i, o).start()

    def start(self):
        for i in range(self.n):
            self.start_along(i)
        self.start_cross()

    def finish(self):
        team = self.team
        same = team.core == self.layer

        @pl.when(team.away & same)
        def _():
            for i in range(self.n):
                self.cross(i).wait_send()

        @pl.when(team.home & no(same))
        def _():
            for i in range(self.n):
                self.cross(i).wait_recv()

        @pl.when(team.away)
        def _():
            for i in range(self.n):
                for o in range(1, team.groups):
                    self.along(i, o).wait_send()
                    self.along(i, o, arriving=True).wait_recv()


class WeightLoad:
    def __init__(self, layer, block, team, *refs):
        self.layer, self.block, self.team = layer, block, team
        *self.own, self.full, self.piece, self.buf, self.sems = refs

    def each(self, act):
        team, size = self.team, self.piece.shape[1]
        same = team.core == self.layer

        @pl.when(team.home & same)
        def _():
            start = 0
            for i, ref in enumerate(self.own):
                act(Local(ref, lines(self.buf, start, ref.shape[0]), self.sems.at[i]))
                start += ref.shape[0]

        pl.when(team.home & no(same))(lambda: act(Local(self.full, self.buf, self.sems.at[0])))

        @pl.when(team.away)
        def _():
            act(Local(self.piece, columns_at(self.buf, team.group, size), self.sems.at[0]))
            for o in range(1, team.groups):
                at = (team.group + o) % team.groups
                act(Local(columns_at(self.full, at, size), columns_at(self.buf, at, size), self.sems.at[o]))

    def start(self):
        self.each(lambda c: c.start())

    def wait(self):
        self.each(lambda c: c.wait())


class FullLoad:
    def __init__(self, team, full, buf, sems):
        self.copy = Local(full, buf, sems.at[0])
        self.start, self.wait = self.copy.start, self.copy.wait


class WholeWeight(Job):
    def __init__(self, layer, block, at, steps):
        self.far, self.near = FarWeight(layer, block), NearWeight(layer, block)
        self.at, self.steps, self.args = at, steps, list(block.arrays)
        self.outs = self.near.outs + self.far.outs
        self.sems = self.far.sems + self.near.sems

    def bind(self, team, *refs):
        *own, full, piece, far_send, far_recv, near_send, near_recv = refs
        self.far.bind(team, *own, piece, far_send, far_recv)
        self.near.bind(team, *own, piece, full, near_send, near_recv)

    def start(self):
        self.far.start()
        self.near.start_cross()

    def middle(self, step):
        for i, at in enumerate(self.steps):
            if at == step:
                self.far.arrive(i)
                self.near.start_along(i)

    def finish(self):
        self.near.finish()
        self.far.sent()


class OwnRows(Job):
    def __init__(self, blocks):
        self.args, self.outs, self.sems = [blocks], [(blocks.shape[1:], LOW)], [1, 1]

    def bind(self, team, blocks, rows, send, recv):
        self.team = team
        self.copy = remote(blocks.at[1 - team.half], rows, send.at[0], recv.at[0], team.far(team.core))

    def start(self):
        pl.when(self.team.home)(lambda: self.copy.start())

    def finish(self):
        pl.when(self.team.home)(lambda: self.copy.wait_send())
        pl.when(self.team.away)(lambda: self.copy.wait_recv())


class TeamRows(Job):
    def __init__(self, rows, members):
        count, width = rows.shape
        n = 2 * (members // 2 - 1) * subs_of(count) + 1
        self.args, self.outs, self.sems = [rows], [((members * count, width), LOW)], [n, n]

    def bind(self, team, rows, whole, send, recv):
        self.gather = Gather(team, whole, rows.shape[0], send, recv, rows)

    def start(self):
        self.gather.start()

    def middle(self, step):
        if step == 0:
            self.gather.pass_all()

    def finish(self):
        self.gather.meet()
        self.gather.receive_all()
        self.gather.finish()


class Scatter(Job):
    def __init__(self, part, step):
        rows, width = part.shape
        groups = lax.axis_size("dp")
        low, high = sides(groups)
        size, cut = width // groups, rows // 32 * 16
        rest = rows - cut
        self.step, self.args, self.outs = step, [part], [((rows, size), LOW)]
        self.scratch = [
            ((max(low - 1, 1), high, cut, size), LOW), ((high, cut, size), LOW), ((max(high - 1, 1), cut, size), LOW),
            ((max(high - 1, 1), low, rest, size), LOW), ((low, rest, size), LOW), ((max(low - 1, 1), rest, size), LOW),
            ((rows, size), LOW),
        ]
        first, second = (low - 1) * high + (high - 1) * low, high + low - 2
        self.sems = [first, first, second, second, high + low, 1]

    def bind(self, team, part, out, fs, fr, ss, sr, load, leave, *buffers):
        self.team, self.part = team, part
        self.land, self.sums, self.last = buffers[0::3][:2], buffers[1:6:3], buffers[2:6:3]
        self.share = buffers[6]
        low, high = sides(team.groups)
        at_high, at_low = team.group // low, team.group % low
        size, cut = self.share.shape[1], self.sums[0].shape[1]
        upper, lower = lines(part, 0, cut), lines(part, cut, self.share.shape[0] - cut)

        def device(b, a):
            return (team.core, (at_high + b) % high * low + (at_low + a) % low, team.along)

        self.loads = [
            Local(columns_at(upper, b * low + at_low, size), self.sums[0].at[b], load.at[b]) for b in range(high)
        ] + [
            Local(columns_at(lower, at_high * low + a, size), self.sums[1].at[a], load.at[high + a]) for a in range(low)
        ]
        self.firsts = []
        for a in range(1, low):
            for b in range(high):
                src, dst = columns_at(upper, b * low + (at_low + a) % low, size), self.land[0].at[a - 1, b]
                self.firsts.append((src, dst, device(0, a)))
        for b in range(1, high):
            for a in range(low):
                src, dst = columns_at(lower, (at_high + b) % high * low + a, size), self.land[1].at[b - 1, a]
                self.firsts.append((src, dst, device(b, 0)))
        self.firsts = [remote(s, d, fs.at[i], fr.at[i], to) for i, (s, d, to) in enumerate(self.firsts)]
        self.seconds = [
            (self.sums[0].at[(at_high + b) % high], self.last[0].at[b - 1], device(b, 0)) for b in range(1, high)
        ] + [(self.sums[1].at[(at_low + a) % low], self.last[1].at[a - 1], device(0, a)) for a in range(1, low)]
        self.seconds = [remote(s, d, ss.at[i], sr.at[i], to) for i, (s, d, to) in enumerate(self.seconds)]
        self.kept = self.sums[0].at[at_high], self.sums[1].at[at_low]
        self.out = None if out is None else Local(self.share, out, leave.at[0])
        self.cut = cut

    def start(self):
        for copy in (*self.firsts, *self.loads):
            copy.start()

    def turn(self):
        for copy in (*self.firsts, *self.loads):
            copy.wait()
        for land, sums in zip(self.land, self.sums):
            for i in range(sums.shape[0]):
                add_rows(sums.at[i], 0, sums.at[i], [land.at[n, i] for n in range(land.shape[0])])
        for copy in self.seconds:
            copy.start()

    def middle(self, step):
        if step == self.step:
            self.turn()

    def close(self):
        for copy in self.seconds:
            copy.wait()
        for at, kept, last in zip((0, self.cut), self.kept, self.last):
            add_rows(self.share, at, kept, [last.at[n] for n in range(last.shape[0])])

    def finish(self):
        self.close()
        self.out.start()
        self.out.wait()


def add_rows(out, at, own, others):
    rows = own.shape[0]
    step = next(n for n in (64, 32, 16) if rows % n == 0)

    @pl.loop(0, rows // step)
    def _(i):
        sl = pl.ds(pl.multiple_of(i * step, step), step)
        total = own[sl].astype(F32)
        for other in others:
            total = total + other[sl].astype(F32)
        out[pl.ds(pl.multiple_of(at + i * step, 16), step)] = total.astype(LOW)


class Swap:
    def __init__(self, team, layer, share, land, send, recv):
        self.team, self.layer = team, layer
        self.far = remote(share, land.at[0], send.at[0], recv.at[0], team.far(layer))
        self.near = remote(share, land.at[1], send.at[0], recv.at[1], team.sibling())

    def each(self, act):
        team = self.team
        pl.when(team.away)(lambda: act(self.far))
        pl.when(team.home & (team.core != self.layer))(lambda: act(self.near))

    def start(self):
        self.each(lambda c: c.start())

    def finish(self):
        self.each(lambda c: c.wait_send())
        team = self.team
        pl.when(team.core == self.layer)(lambda: self.far.wait_recv())
        pl.when((team.core == self.layer) & team.away)(lambda: self.near.wait_recv())


def add_swapped(team, out, share, landed):
    def body(sl):
        near = jnp.where(team.home, share[sl].astype(F32), landed[1, sl].astype(F32))
        out[sl] = (near + landed[0, sl].astype(F32)).astype(LOW)

    by_tiles(out.shape[0], body)


class PlaceRows(Job):
    def __init__(self, first, second, at):
        self.args, self.outs, self.sems, self.at = [first, second], [((2,) + first.shape, LOW)], [1, 2] * 2, at

    def bind(self, team, first, second, placed, *sems):
        self.swaps = [Swap(team, 0, first, placed, *sems[:2]), Swap(team, 1, second, placed, *sems[2:])]

    def start(self):
        for swap in self.swaps:
            swap.start()

    def finish(self):
        for swap in self.swaps:
            swap.finish()


class Spread:
    def __init__(self, team, share, fulls, send, recv, here):
        self.team, self.share, self.fulls, self.send, self.recv, self.here = team, share, fulls, send, recv, here
        self.low, self.high = sides(team.groups)

    @staticmethod
    def moves(groups):
        low, high = sides(groups)
        upper = [(True, (0, a), (0, 0)) for a in range(1, low)]
        upper += [(True, (b, 0), (0, a)) for b in range(1, high) for a in range(low)]
        lower = [(False, (b, 0), (0, 0)) for b in range(1, high)]
        lower += [(False, (0, a), (b, 0)) for a in range(1, low) for b in range(high)]
        return upper + lower

    def group(self, high, low):
        team = self.team
        return (
            (team.group // self.low + self.high - high) % self.high * self.low
            + (team.group % self.low + self.low - low) % self.low
        )

    def copies(self, first, arriving=False):
        team, size = self.team, self.share.shape[1]
        start = 0
        moves = self.moves(team.groups)
        for i, full in enumerate(self.fulls):
            rows = full.shape[0]
            cut = rows // 32 * 16
            for n, (upper, (high, low), (from_high, from_low)) in enumerate(moves):
                if ((from_high, from_low) == (0, 0)) != first:
                    continue
                at, count = (0, cut) if upper else (cut, rows - cut)
                slot = i * len(moves) + n
                back = arriving * high + from_high, arriving * low + from_low
                there = columns_at(lines(full, at, count), self.group(*back), size)
                src = lines(self.share, start + at, count) if first else there
                target = self.group(-high, -low)
                device = (team.core, target, team.along)
                yield remote(src, there, self.send.at[slot], self.recv.at[slot], device)
            start += rows

    def stays(self):
        start = 0
        for i, full in enumerate(self.fulls):
            there = columns_at(full, self.team.group, self.share.shape[1])
            yield Local(lines(self.share, start, full.shape[0]), there, self.here.at[i])
            start += full.shape[0]

    def start(self):
        for copy in (*self.copies(True), *self.stays()):
            copy.start()

    def middle(self):
        for copy in self.copies(True, arriving=True):
            copy.wait_recv()
        for copy in self.copies(False):
            copy.start()

    def finish(self):
        for copy in self.stays():
            copy.wait()
        for first in (True, False):
            for copy in self.copies(first):
                copy.wait_send()
        for copy in self.copies(False, arriving=True):
            copy.wait_recv()


def sides(groups):
    low = 2 if groups % 2 == 0 else 1
    return low, groups // low


class Hooks:
    def __init__(self, late, drains, weights, jobs):
        self.late, self.drains, self.weights, self.jobs = late, drains, weights, jobs

    def need(self, index):
        self.late[index].wait()

    def done(self, index):
        self.drains[index].start()

    def middle(self, step):
        for job in self.jobs:
            if job.at == step:
                job.start()
            job.middle(step)


def call(
    body, chips, ident, flops, args=(), late=(), weights=None, far_args=(), outs=(), far_outs=(), drained=(),
    scratch=(), jobs=(), partners=Team.partners,
):
    vmem, far = pl.BlockSpec(memory_space=pltpu.VMEM), pl.BlockSpec(memory_space=pl.ANY)
    job_args = [a for job in jobs for a in job.args]
    job_outs = [o for job in jobs for o in job.outs]
    job_sems = [semaphores(n) for job in jobs for n in job.sems]
    job_scratch = [pltpu.VMEM(shape, dtype) for job in jobs for shape, dtype in job.scratch]
    sources = []
    if weights:
        sources = list(weights) if len(weights) == 1 else [*weights[1].arrays, *weights[2:]]
    weight_bufs = [pltpu.VMEM(a.shape, LOW) for a in (weights[0:1] if len(sources) == 1 else sources[-2:-1])]

    def kernel(*refs):
        refs = list(refs)

        def take(n):
            taken = refs[:n]
            del refs[:n]
            return taken

        ins, late_ins, weight_ins = take(len(args)), take(len(late)), take(len(sources))
        far_ins, job_ins = take(len(far_args)), take(len(job_args))
        results, drained_results, job_results = take(len(outs) + len(far_outs)), take(len(drained)), take(len(job_outs))
        own, late_bufs, drain_bufs = take(len(scratch)), take(len(late)), take(len(drained))
        weight_buf, (late_sem, drain_sem, weight_sem) = take(len(weight_bufs)), take(3)
        sems, buffers = take(len(job_sems)), refs
        team = Team(chips)
        loads = [Local(src, dst, late_sem.at[i]) for i, (src, dst) in enumerate(zip(late_ins, late_bufs))]
        load = None
        if len(sources) == 1:
            load = FullLoad(team, *weight_ins, *weight_buf, weight_sem)
        elif sources:
            load = WeightLoad(*weights[:2], team, *weight_ins, *weight_buf, weight_sem)
        if load:
            load.start()
        for copy in loads:
            copy.start()
        team.enter(partners(team))
        for job in jobs:
            parts = []
            for pool, n in (
                (job_ins, len(job.args)), (job_results, len(job.outs)),
                (sems, len(job.sems)), (buffers, len(job.scratch)),
            ):
                parts += pool[:n]
                del pool[:n]
            job.bind(team, *parts)
        for job in jobs:
            if job.at is None:
                job.start()
        drains = [Local(src, dst, drain_sem.at[i]) for i, (src, dst) in enumerate(zip(drain_bufs, drained_results))]
        hooks = Hooks(loads, drains, load, jobs)
        body(team, hooks, *ins, *late_bufs, *weight_buf, *far_ins, *results, *drain_bufs, *own)
        for job in jobs:
            job.finish()
        for copy in drains:
            copy.wait()

    moved = sum(a.size * a.dtype.itemsize for a in (*args, *late))
    results = pl.pallas_call(
        kernel,
        out_shape=[jax.ShapeDtypeStruct(shape, dtype) for shape, dtype in (*outs, *far_outs, *drained, *job_outs)],
        in_specs=[vmem] * len(args) + [far] * (len(late) + len(sources) + len(far_args) + len(job_args)),
        out_specs=[vmem] * len(outs) + [far] * (len(far_outs) + len(drained) + len(job_outs)),
        scratch_shapes=[
            *scratch,
            *(pltpu.VMEM(a.shape, a.dtype) for a in late),
            *(pltpu.VMEM(shape, dtype) for shape, dtype in drained),
            *weight_bufs,
            semaphores(len(late)), semaphores(len(drained)), semaphores(lax.axis_size("dp")), *job_sems, *job_scratch,
        ],
        cost_estimate=pl.CostEstimate(flops=WAITING * flops, bytes_accessed=moved, transcendentals=0),
        compiler_params=pltpu.CompilerParams(
            collective_id=ident, has_side_effects=True, vmem_limit_bytes=VMEM_BYTES
        ),
    )(*args, *late, *sources, *far_args, *job_args)
    job_results = []
    at = len(outs) + len(far_outs) + len(drained)
    for job in jobs:
        job_results.append(results[at : at + len(job.outs)])
        at += len(job.outs)
    return results[: len(outs) + len(far_outs) + len(drained)], job_results


def rope_tables(span, columns):
    position = jnp.arange(span, dtype=F32)
    freqs = ROPE_BASE ** (-jnp.arange(0, HD, 2, dtype=F32) / HD)
    angle = position[:, None] * freqs[None, :]
    heads = columns // HD
    cosine = jnp.tile(jnp.concatenate([jnp.cos(angle), jnp.cos(angle)], -1), (1, heads))
    sine = jnp.tile(jnp.concatenate([-jnp.sin(angle), jnp.sin(angle)], -1), (1, heads))
    return cosine, sine


def everywhere_sum(team, refs):
    small_ref, sum_ref, near, groups_ref, members_ref, send, recv, gs, gr, ms, mr = refs
    copy = remote(small_ref, near, send.at[0], recv.at[0], team.sibling())
    copy.start()
    copy.wait()
    groups_ref[team.group] = small_ref[...] + near[...]

    def exchange(ref, mine, count, device, send, recv):
        for o in range(1, count):
            remote(ref.at[mine], ref.at[mine], send.at[o - 1], recv.at[o - 1], device(o)).start()
        for o in range(1, count):
            remote(ref.at[mine], ref.at[mine], send.at[o - 1], recv.at[o - 1], device(o)).wait_send()
            there = ref.at[(mine + count - o) % count]
            remote(there, there, send.at[o - 1], recv.at[o - 1], device(o)).wait_recv()
        total = ref[0]
        for i in range(1, count):
            total = total + ref[i]
        return total

    members = 2 * team.chips
    members_ref[team.along] = exchange(groups_ref, team.group, team.groups, team.dp, gs, gr)
    sum_ref[...] = exchange(members_ref, team.along, members, team.member, ms, mr)


class Steps:
    def __init__(self, loads, weights, steps, done):
        self.loads, self.weights, self.steps, self.done = loads, weights, steps, done

    def need(self, index):
        self.loads[index].wait()

    def middle(self, step):
        self.steps.get(step, lambda: None)()


def last_kernel(team, hooks, *refs, block):
    refs = list(refs)

    def take(n):
        taken = refs[:n]
        del refs[:n]
        return taken

    g_ref, x1_ref, gain_ref, bias_ref, *small_parts = take(9)
    feed_in, feed_sources = take(4), take(len(block.arrays) + 2)
    attn_in, attn_full = take(10), take(1)[0]
    attn_part1, feed_share1, rows1 = take(3)
    sum_ref, low_ref, feed_part0, attn_part0, placed, *fulls = take(9)
    grad_feed, grad_attn, dx1_ref, feed_gain, attn_gain = take(5)
    feed_team, attn_team, reduce_refs = take(2), take(2), take(10)
    feed_own, feed_land, feed_out, attn_land, attn_out = take(5)
    load_sem, weight_sem, drain_sem = take(3)
    scatters = []
    for part, like in ((attn_part1, attn_out), (feed_part0, feed_out), (attn_part0, attn_out)):
        scatter = Scatter.__new__(Scatter)
        scatter.bind(team, part, None, *take(13))
        scatters.append(scatter)
    attn_scatter1, feed_scatter0, attn_scatter0 = scatters
    feed_swap1 = Swap(team, 1, feed_share1, feed_land, *take(2))
    attn_swap1 = Swap(team, 1, attn_scatter1.share, attn_land, *take(2))
    feed_swap0 = Swap(team, 0, feed_scatter0.share, feed_land, *take(2))
    attn_swap0 = Swap(team, 0, attn_scatter0.share, attn_land, *take(2))
    rows_swap1 = Swap(team, 1, rows1, placed, *take(2))
    rows_swap0 = Swap(team, 0, low_ref, placed, *take(2))
    feed_spread = Spread(team, feed_out, fulls[:2], *take(3))
    attn_spread = Spread(team, attn_out, fulls[2:], *take(3))
    small_ref, *small = refs
    width = g_ref.shape[1]
    last = team.core == 0
    attn_scatter1.start()
    own_load = Local(feed_share1, feed_own, drain_sem.at[2])
    own_load.start()

    def loads_of(sources, buffers):
        copies = [Local(src, dst, load_sem.at[i]) for i, (src, dst) in enumerate(zip(sources, buffers))]
        for copy in copies:
            copy.start()
        return copies

    def leaves(src, dst, sem, after):
        def done(index):
            copy = Local(src, dst, drain_sem.at[sem])
            copy.start()
            copy.wait()
            after()

        return done

    def after_feed():
        feed_scatter0.start()
        attn_scatter1.close()

    def feed_phase(gate, up, h, z, w, w_grad, dgate, dup):
        load = WeightLoad(0, block, team, *feed_sources, w, weight_sem)
        load.start()
        loads = loads_of(feed_in, (gate, up, h, z))
        steps = Steps(
            loads, load, {1: attn_scatter1.turn}, leaves(w_grad, feed_part0, 0, after_feed)
        )
        feed_back_kernel(
            team, steps, g_ref, x1_ref, gain_ref, gate, up, h, z, w,
            dx1_ref, feed_gain, w_grad, grad_feed, dgate, dup, *feed_team, *reduce_refs, layer=0, gathered=False,
        )

    def buffer(ref, dtype=LOW):
        return pltpu.VMEM(ref.shape, dtype)

    pl.run_scoped(
        feed_phase,
        *(buffer(ref) for ref in feed_in),
        pltpu.VMEM((block.lines, width), LOW),
        pltpu.VMEM((block.lines, width), LOW),
        *(buffer(ref) for ref in feed_in[:2]),
    )

    def after_gather():
        feed_swap1.start()
        attn_swap1.start()

    def after_attn():
        attn_scatter0.start()
        feed_scatter0.close()
        feed_swap0.start()
        rows_swap1.start()
        feed_swap1.finish()
        attn_swap1.finish()
        own_load.wait()

        @pl.when(no(last))
        def _():
            add_swapped(team, feed_out, feed_own, feed_land)
            feed_spread.start()
            add_swapped(team, attn_out, attn_scatter1.share, attn_land)
            attn_spread.start()

    def attn_phase(*scoped):
        loaded, w, w_grad, local_refs = scoped[:10], scoped[10], scoped[11], scoped[12:]
        load = FullLoad(team, attn_full, w, weight_sem)
        load.start()
        loads = loads_of(attn_in, loaded)
        steps = Steps(
            loads,
            load,
            {1: after_gather, 2: feed_scatter0.turn},
            leaves(w_grad, attn_part0, 1, after_attn),
        )
        attend_back_kernel(
            team, steps, dx1_ref, gain_ref, bias_ref, *loaded, w, low_ref, attn_gain, w_grad, grad_attn, *local_refs,
            *attn_team, *reduce_refs, layer=0, last=False,
        )

    rows, span, columns = g_ref.shape[0], attn_in[0].shape[0], attn_in[0].shape[1]
    pl.run_scoped(
        attn_phase,
        *(pltpu.VMEM(ref.shape, ref.dtype) for ref in attn_in),
        *[buffer(attn_full)] * 2,
        *attend_back_scratch(rows, span, columns, attn_in[2].shape),
    )
    attn_scatter0.turn()
    small_ref[...] = jnp.zeros_like(small_ref)
    for i, part in enumerate([attn_gain, feed_gain, *small_parts]):
        small_ref[i : i + 1, 0 : part.shape[1]] = part[...]
    everywhere_sum(team, [small_ref, sum_ref, *small])
    attn_scatter0.close()
    attn_swap0.start()
    rows_swap0.start()

    @pl.when(no(last))
    def _():
        feed_spread.middle()
        attn_spread.middle()

    feed_swap0.finish()

    @pl.when(last)
    def _():
        add_swapped(team, feed_out, feed_scatter0.share, feed_land)
        feed_spread.start()

    attn_swap0.finish()

    @pl.when(last)
    def _():
        add_swapped(team, attn_out, attn_scatter0.share, attn_land)
        attn_spread.start()
        feed_spread.middle()
        attn_spread.middle()

    rows_swap1.finish()
    rows_swap0.finish()
    feed_spread.finish()
    attn_spread.finish()


def attend_back_scratch(rows, span, columns, logs_shape):
    members = span // rows
    return [
        pltpu.VMEM(shape, dtype)
        for shape, dtype in (
            ((span, columns), LOW),
            (logs_shape, F32),
            ((members, columns, rows), LOW),
            ((members * (members + 1) // 2, columns // HD, rows, rows), LOW),
            ((rows, columns), F32),
            ((rows, columns), F32),
            ((members, columns, rows), F32),
            ((3, span, columns), LOW),
            ((rows, rows), F32),
        )
    ]


def local(tokens, cotangent, lengths, gain_attn, w_qkv, w_out, gain_ffn, w_gate_up, w_down):
    cores, groups, members = lax.axis_size("section"), lax.axis_size("dp"), lax.axis_size("mp")
    micro, sequences, rows, width = tokens.shape
    assert cores == 2 and micro == 2 and sequences == 1 and members % 2 == 0 and members >= 4
    chips = members // 2
    span = rows * members
    columns, hidden = w_out.shape[1], w_down.shape[1]
    heads = columns // HD
    quarter = width // groups
    padded = -(-heads // 8) * 8
    core = lax.axis_index("section")
    half = lax.axis_index("mp") // chips
    home = core == half

    def vec(*shape, dtype=LOW):
        return pltpu.VMEM(shape, dtype)

    whole, of_heads, of_hidden, logs_shape = (span, width), (span, columns), (span, hidden), (members, padded, rows)
    team_scratch = gather_scratch(chips, rows) + reduce_scratch(chips, rows, width)
    own_attn = Parts(
        [w_qkv[0].reshape(3 * columns, width), w_out[0]],
        [(0, t * columns, columns, t * columns) for t in range(3)] + [(1, 0, columns, 3 * columns)],
    )
    own_feed = Parts(
        [w_gate_up[0].reshape(2 * hidden, width), w_down[0]],
        [(0, t * hidden, hidden, t * hidden) for t in range(2)] + [(1, 0, hidden, 2 * hidden)],
    )
    own_gains = jnp.concatenate([gain_attn, gain_ffn], 0)
    length = lax.dynamic_index_in_dim(lengths[:, 0], half, 0, keepdims=False)
    bias = jnp.where(jnp.arange(span) < length, 0.0, NEG_LARGE).astype(F32)
    cosine, sine = rope_tables(span, columns)

    def place(pair, placed):
        here = jnp.where(home, jnp.where(core == 0, pair[0], pair[1]), placed[1])
        return jnp.where(half == 0, jnp.stack([here, placed[0]]), jnp.stack([placed[0], here]))

    x = gains = values = top = all_top = attn_piece = None
    attn_weights, feed_weights = [None] * 2, [None] * 2
    kept, squares = [], []
    for layer in range(2):
        outs = [((rows, width), F32), ((1, columns), F32)]
        drained = [(whole, LOW)] + [(of_heads, LOW)] * 4 + [(logs_shape, F32)]
        if layer:
            jobs = [WholeWeight(1, own_feed, 0, (1, 1, 2))]
            more = dict(
                args=[gains, bias[None], x],
                late=[cosine, sine, values],
                weights=attn_weights[1],
                outs=outs,
                drained=drained,
                scratch=team_scratch,
            )
        else:
            jobs = [WholeWeight(0, own_feed, 0, (2, 2, 3)), FarWeight(1, own_attn, at=2)]
            n = len(own_attn.parts)
            more = dict(
                args=[own_gains, bias[None]],
                late=[cosine, sine],
                far_args=[tokens[:, 0], *own_attn.arrays],
                outs=outs + [((4, width), F32)],
                drained=drained + [((rows, width), LOW), ((4 * columns, width), LOW)],
                scratch=team_scratch
                + [vec(2, width, dtype=F32)]
                + [semaphores(n), semaphores(n), semaphores(groups * n), semaphores(groups * n), semaphores(7)],
            )
        results, came = call(
            functools.partial(attend_kernel, layer=layer, weights=own_attn),
            chips,
            layer,
            8 * span * width * columns + 4 * span * span * columns,
            jobs=jobs,
            **more,
        )
        x1, square = results[:2]
        squares.append(square)
        if layer:
            h, q, k, m, o, logs = results[2:]
            feed_weights[1] = (1, own_feed, *came[0])
            jobs = [TeamRows(top, members)]
        else:
            gains, h, q, k, m, o, logs, x, full = results[2:]
            attn_weights[0], values = (full,), m
            feed_weights[0] = (0, own_feed, *came[0])
            attn_piece = came[1][0]
            jobs = [NearWeight(1, own_attn, attn_piece), OwnRows(cotangent[:, 0])]
        (y, h2, gate, up, z), came = call(
            functools.partial(feed_kernel, layer=layer),
            chips,
            2 + layer,
            6 * span * width * hidden,
            args=[x1, gains],
            weights=feed_weights[layer],
            outs=[((rows, width), LOW)],
            drained=[(whole, LOW)] + [(of_hidden, LOW)] * 3,
            scratch=team_scratch,
            jobs=jobs,
        )
        if layer == 0:
            attn_weights[1] = (1, own_attn, came[0][0], attn_piece)
            top = jnp.where(home, lax.dynamic_index_in_dim(cotangent[:, 0], half, 0, keepdims=False), came[1][0])
        else:
            all_top = came[0][0]
        kept.append((x, x1, h, q, k, m, o, logs, h2, gate, up, z, y))
        x = y

    y_first = kept[0][-1]
    x, x1, h, q, k, m, o, logs, h2, gate, up, z, y = kept[1]
    (dx1, feed_gain, feed_part), _ = call(
        functools.partial(feed_back_kernel, layer=1, gathered=True),
        chips,
        4,
        12 * span * width * hidden,
        args=[top, x1, gains],
        late=[gate, up, h2, z],
        weights=feed_weights[1],
        far_args=[all_top],
        outs=[((rows, width), F32), ((1, width), F32)],
        drained=[((3 * hidden, width), LOW)],
        scratch=[vec(*whole), vec(*of_hidden), vec(*of_hidden)] + team_scratch,
    )
    (low_grad1, attn_gain, value_grad, attn_part), ((feed_share,), (placed,)) = call(
        functools.partial(attend_back_kernel, layer=1, last=True),
        chips,
        5,
        16 * span * width * columns + 10 * span * span * columns,
        args=[dx1, gains, bias[:, None]],
        late=[k, q, logs, o, m, cosine, sine, h, x],
        weights=attn_weights[1],
        outs=[((rows, width), LOW), ((1, width), F32), (of_heads, LOW)],
        drained=[((4 * columns, width), LOW)],
        scratch=[vec(*whole)] + attend_back_scratch(rows, span, columns, logs_shape) + team_scratch,
        jobs=[Scatter(feed_part, 2), PlaceRows(y_first, y, 1)],
    )
    layer_out = place((y_first, y), placed)
    x, x1, h, q, k, m, o, logs, h2, gate, up, z, y = kept[0]
    count = jnp.broadcast_to(jnp.sum(lengths).astype(F32), (1, 128))
    share_feed, share_attn = (3 * hidden, quarter), (4 * columns, quarter)
    n_moves = 2 * len(Spread.moves(groups))
    small = (8, width)
    feed_like, attn_like = Scatter(feed_part, None), Scatter(attn_part, None)
    (sums, low_grad0, _, _, placed, *grads), _ = call(
        functools.partial(last_kernel, block=own_feed),
        chips,
        6,
        12 * span * width * hidden + 16 * span * width * columns + 10 * span * span * columns,
        args=[low_grad1, x1, gains, bias[:, None], attn_gain, feed_gain, *squares, count],
        far_args=[
            gate, up, h2, z, *own_feed.arrays, *feed_weights[0][2:],
            k, q, logs, o, m, cosine, sine, h, x, value_grad, *attn_weights[0],
            attn_part, feed_share, low_grad1,
        ],
        outs=[(small, F32), ((rows, width), LOW)],
        far_outs=[(feed_part.shape, LOW), (attn_part.shape, LOW), ((2, rows, width), LOW)]
        + [((n, width), LOW) for n in (2 * hidden, hidden, 3 * columns, columns)],
        drained=[],
        scratch=[
            vec(*whole), vec(*whole), vec(rows, width, dtype=F32),
            vec(1, width, dtype=F32), vec(1, width, dtype=F32),
            *gather_scratch(chips, rows), *gather_scratch(chips, rows), *reduce_scratch(chips, rows, width),
            vec(*share_feed), vec(2, *share_feed), vec(*share_feed), vec(2, *share_attn), vec(*share_attn),
            semaphores(10), semaphores(max(groups, 2)), semaphores(3),
            *(
                item
                for like in (attn_like, feed_like, attn_like)
                for item in (*(semaphores(n) for n in like.sems), *(vec(*shape) for shape, _ in like.scratch))
            ),
            *(semaphores(n) for n in (1, 2) * 6),
            *(semaphores(n) for n in (n_moves, n_moves, 2) * 2),
            *(vec(*lead, *small, dtype=F32) for lead in ((), (), (groups,), (members,))),
            *(semaphores(n) for n in (1, 1, groups - 1, groups - 1, members - 1, members - 1)),
        ],
        partners=Team.all_partners,
    )
    gain_sums = jnp.where(core == 0, sums[0:2], sums[2:4])
    square = jnp.sum(jnp.where(core == 0, sums[4], sums[5]))
    count = sums[6, 0] / (cores * members)
    pair_sum, lower_sum, projection_sum, output_sum = (a.astype(F32) for a in grads)
    return (
        layer_out[None, :, None],
        place((low_grad0, low_grad1), placed).astype(F32)[None, :, None],
        gain_sums[0:1],
        projection_sum.reshape(w_qkv.shape),
        output_sum[None],
        gain_sums[1:2],
        pair_sum.reshape(w_gate_up.shape),
        lower_sum[None],
        jnp.sqrt(square / (count * width)).reshape(1),
    )


def solution(mesh):
    return jax.shard_map(
        local,
        mesh=mesh,
        in_specs=(
            P(None, "dp", "mp", None),
            P(None, "dp", "mp", None),
            P(None, "dp"),
            P("section", None),
            P("section", None, "mp", None),
            P("section", "mp", None),
            P("section", None),
            P("section", None, "mp", None),
            P("section", "mp", None),
        ),
        out_specs=(
            P("section", None, "dp", "mp", None),
            P("section", None, "dp", "mp", None),
            P("section", None),
            P("section", None, "mp", None),
            P("section", "mp", None),
            P("section", None),
            P("section", None, "mp", None),
            P("section", "mp", None),
            P("section"),
        ),
        check_vma=False,
    )
```

```python
import functools

import jax
import jax.numpy as jnp
from jax import lax
from jax.experimental import pallas as pl
from jax.experimental.pallas import tpu as pltpu
from jax.sharding import PartitionSpec as P

HD = 64
EPSILON = 1e-05
ROPE_BASE = 10000.0
NEG_LARGE = -1e30
MESH = pl.DeviceIdType.MESH
F32 = jnp.float32
LOW = jnp.bfloat16
VMEM_BYTES = 56 << 20
WAITING = 12


def mm(a, b):
    return lax.dot_general(a, b, (((1,), (0,)), ((), ())), preferred_element_type=F32)


def mm_nt(a, b):
    return lax.dot_general(a, b, (((1,), (1,)), ((), ())), preferred_element_type=F32)


def mm_tn(a, b):
    return lax.dot_general(a, b, (((0,), (0,)), ((), ())), preferred_element_type=F32)


def no(flag):
    return jnp.logical_not(flag)


class Team:
    def __init__(self, chips):
        self.chips = chips
        self.groups = lax.axis_size("dp")
        self.core = lax.axis_index("section")
        self.group = lax.axis_index("dp")
        self.along = lax.axis_index("mp")
        self.half = self.along // chips
        self.seat = self.along % chips
        self.home = self.core == self.half
        self.away = jnp.logical_not(self.home)

    def chip(self, offset):
        return (self.seat + offset) % self.chips

    def sibling(self):
        return (1 - self.core, self.group, self.along)

    def peer(self, offset):
        return (self.core, self.group, self.half * self.chips + self.chip(offset))

    def mine(self, offset):
        return self.chip(offset) + self.core * self.chips

    def other(self, offset):
        return self.chip(offset) + (1 - self.core) * self.chips

    def dp(self, offset):
        return (self.core, (self.group + offset) % self.groups, self.along)

    def far(self, core):
        return (core, self.group, (self.along + self.chips) % (2 * self.chips))

    def member(self, offset):
        return (self.core, self.group, (self.along + offset) % (2 * self.chips))

    def partners(self):
        return (
            [self.sibling(), self.far(0), self.far(1)]
            + [self.peer(o) for o in range(1, self.chips)]
            + [self.dp(o) for o in range(1, self.groups)]
        )

    def all_partners(self):
        return (
            [self.sibling(), self.far(1 - self.core)]
            + [self.member(o) for o in range(1, 2 * self.chips)]
            + [self.dp(o) for o in range(1, self.groups)]
        )

    def enter(self, partners):
        barrier = pltpu.get_barrier_semaphore()
        for device in partners:
            pl.semaphore_signal(barrier, inc=1, device_id=device, device_id_type=MESH)
        pl.semaphore_wait(barrier, len(partners))


def remote(src, dst, send, recv, device):
    return pltpu.make_async_remote_copy(
        src_ref=src, dst_ref=dst, send_sem=send, recv_sem=recv, device_id=device, device_id_type=MESH
    )


class Local:
    def __init__(self, src, dst, sem):
        self.copy = pltpu.make_async_copy(src, dst, sem)
        self.start, self.wait = self.copy.start, self.copy.wait


def block(rank, rows):
    return pl.ds(pl.multiple_of(rank * rows, rows), rows)


def columns_at(ref, index, size):
    return ref.at[:, pl.ds(pl.multiple_of(index * size, size), size)]


def lines(ref, start, rows):
    return ref.at[pl.ds(start, rows)]


def subs_of(rows):
    return max(1, rows // 64)


class Gather:
    def __init__(self, team, buf, rows, send, recv, source=None):
        self.team, self.buf, self.rows, self.send, self.recv = team, buf, rows, send, recv
        self.source = source
        self.subs = subs_of(rows)
        self.size = rows // self.subs
        self.count = (team.chips - 1) * self.subs
        self.met = False

    def meet(self):
        if not self.met:
            self.near(self.team.other(0)).wait_recv()
            self.met = True

    def run(self, rank, s):
        return pl.ds(pl.multiple_of(rank * self.rows + s * self.size, self.size), self.size)

    def _copy(self, part, slot, device, src=None):
        part = self.buf.at[part]
        return remote(part if src is None else src, part, self.send.at[slot], self.recv.at[slot], device)

    def near(self, rank, leaving=False):
        src = self.source if leaving else None
        return self._copy(block(rank, self.rows), 2 * self.count, self.team.sibling(), src)

    def direct(self, o, s):
        src = None if self.source is None else self.source.at[self.run(0, s)]
        return self._copy(self.run(self.team.mine(0), s), (o - 1) * self.subs + s, self.team.peer(o), src)

    def incoming(self, o, s):
        back = self.team.chips - o
        return self._copy(self.run(self.team.mine(back), s), (o - 1) * self.subs + s, self.team.peer(back))

    def forward(self, o, s, rank):
        slot = self.count + (o - 1) * self.subs + s
        return self._copy(self.run(rank(self.team.chips - o), s), slot, self.team.sibling())

    def start(self):
        self.near(self.team.mine(0), True).start()
        for s in range(self.subs):
            for o in range(1, self.team.chips):
                self.direct(o, s).start()

    def finish(self):
        self.near(self.team.mine(0), True).wait_send()
        for o in range(1, self.team.chips):
            for s in range(self.subs):
                self.direct(o, s).wait_send()
                self.forward(o, s, self.team.mine).wait_send()

    def pass_all(self):
        for o in range(1, self.team.chips):
            for s in range(self.subs):
                self.incoming(o, s).wait_recv()
                self.forward(o, s, self.team.mine).start()

    def receive_all(self):
        for o in range(1, self.team.chips):
            for s in range(self.subs):
                self.forward(o, s, self.team.other).wait_recv()

    def arrivals(self, work, between=lambda back, s: None, after=lambda back: None):
        team = self.team
        work([block(team.mine(0), self.rows)], 0, None)
        self.meet()
        work([block(team.other(0), self.rows)], 0, None)
        for o in range(1, team.chips):
            back = team.chips - o

            @pl.loop(0, self.subs)
            def _(s):
                self.incoming(o, s).wait_recv()
                self.forward(o, s, team.mine).start()
                between(back, s)
                self.forward(o, s, team.other).wait_recv()
                work([self.run(team.mine(back), s), self.run(team.other(back), s)], back, s)

            after(back)


def rows_at(ref, runs):
    return jnp.concatenate([ref[run] for run in runs], 0) if len(runs) > 1 else ref[runs[0]]


def put_rows(ref, runs, value):
    for i, run in enumerate(runs):
        ref[run] = value[i * run.size : (i + 1) * run.size]


class Reduce:
    def __init__(self, team, rows, scratch):
        self.team, self.rows = team, rows
        (self.out, self.held, self.into, self.leave, self.land, self.own, self.xs, self.xr, self.us, self.ur) = scratch
        self.subs = subs_of(rows)
        self.size = rows // self.subs

    def run(self, s):
        return pl.ds(0, self.rows) if s is None else pl.ds(pl.multiple_of(s * self.size, self.size), self.size)

    def slot(self, o, s):
        return o * self.subs + (0 if s is None else s)

    def cross(self, o, s):
        run, slot = self.run(s), self.slot(o, s)
        return remote(
            self.out.at[o, run], self.into.at[o, run], self.xs.at[slot], self.xr.at[slot], self.team.sibling()
        )

    def leaving(self, o, s):
        run, slot = self.run(s), self.slot(o - 1, s)
        return remote(
            self.leave.at[o - 1, run], self.land.at[o - 1, run], self.us.at[slot], self.ur.at[slot], self.team.peer(o)
        )

    def put_other(self, o, s, value):
        self.out[o, self.run(s)] = value.astype(LOW)
        self.cross(o, s).start()

    def hold(self, o, s, value):
        self.held[o - 1, self.run(s)] = value

    def keep(self, value):
        self.own[...] = value

    def pass_on(self, o, s):
        run = self.run(s)
        self.cross(o, s).wait_recv()
        self.leave[o - 1, run] = (self.held[o - 1, run] + self.into[o, run].astype(F32)).astype(LOW)
        self.leaving(o, s).start()

    def finish(self, fine):
        self.cross(0, None).wait()
        for o in range(1, self.team.chips):
            for s in range(self.subs) if fine else [None]:
                self.cross(o, s).wait_send()
                self.leaving(o, s).wait()

    def total(self, rows):
        total = self.own[rows] + self.into[0, rows].astype(F32)
        for o in range(self.team.chips - 1):
            total = total + self.land[o, rows].astype(F32)
        return total


def semaphores(n):
    return pltpu.SemaphoreType.DMA((max(n, 1),))


def gather_scratch(chips, rows):
    n = 2 * (chips - 1) * subs_of(rows) + 1
    return [semaphores(n), semaphores(n)]


def reduce_scratch(chips, rows, width):
    subs = subs_of(rows)
    return [
        pltpu.VMEM((chips, rows, width), LOW),
        pltpu.VMEM((chips - 1, rows, width), F32),
        pltpu.VMEM((chips, rows, width), LOW),
        pltpu.VMEM((chips - 1, rows, width), LOW),
        pltpu.VMEM((chips - 1, rows, width), LOW),
        pltpu.VMEM((rows, width), F32),
        semaphores(chips * subs),
        semaphores(chips * subs),
        semaphores((chips - 1) * subs),
        semaphores((chips - 1) * subs),
    ]


def by_rows(rows, body):
    step = min(32, rows)

    @pl.loop(0, rows // step)
    def _(i):
        body(pl.ds(pl.multiple_of(i * step, step), step))


def by_tiles(rows, body):
    step = next(n for n in (64, 32, 16) if rows % n == 0)

    @pl.loop(0, rows // step)
    def _(i):
        body(pl.ds(pl.multiple_of(i * step, step), step))


def swap_halves(u):
    columns, half = u.shape[1], HD // 2
    if columns % 128:
        parts = []
        for at in range(0, columns, HD):
            parts += [u[:, at + half : at + HD], u[:, at : at + half]]
        return jnp.concatenate(parts, 1)
    lane = lax.broadcasted_iota(jnp.int32, u.shape, 1)
    return jnp.where(lane % HD < half, pltpu.roll(u, columns - half, 1), pltpu.roll(u, half, 1))


def wide(table, columns):
    return jnp.concatenate([table] * (columns // table.shape[1]), 1)


def head_row(columns, head):
    lane = lax.broadcasted_iota(jnp.int32, (1, columns), 1)
    return (lane // HD == head).astype(F32).astype(LOW)


def norm_into(buf, at, rows, read, gain):
    step = min(32, rows)

    @pl.loop(0, rows // step)
    def _(i):
        values = read(pl.ds(pl.multiple_of(i * step, step), step))
        scale = lax.rsqrt(jnp.mean(values * values, -1, keepdims=True) + EPSILON)
        buf[pl.ds(pl.multiple_of(at + i * step, step), step)] = (values * scale * gain).astype(LOW)


def norm_back(rows, read_values, read_grad, gain, read_outer, write, gain_grad_ref):
    gain_grad_ref[...] = jnp.zeros_like(gain_grad_ref)

    def body(sl):
        values = read_values(sl)
        scale = lax.rsqrt(jnp.mean(values * values, -1, keepdims=True) + EPSILON)
        unit = values * scale
        grad = read_grad(sl)
        gain_grad_ref[...] += jnp.sum(grad * unit, 0, keepdims=True)
        inner = grad * gain
        write(sl, read_outer(sl) + scale * (inner - unit * jnp.mean(inner * unit, -1, keepdims=True)))

    by_rows(rows, body)


def columns_of(width):
    step = min(256, width)
    return [slice(at, at + step) for at in range(0, width, step)]


def attend(
    team, steps, layer, x_ref, gains_ref, length, cos_ref, sin_ref, before_ref, w_ref, x1_ref, square_ref,
    h_ref, q_ref, k_ref, m_ref, o_ref, log_ref, gs, gr, reduce_refs,
):
    chips, members = team.chips, 2 * team.chips
    rows, span = x1_ref.shape[0], h_ref.shape[0]
    columns = w_ref.shape[0] // 4
    heads = columns // HD
    norm_into(
        h_ref, team.mine(0) * rows, rows, lambda sl: x_ref[sl].astype(F32), gains_ref[2 * layer : 2 * layer + 1]
    )
    gather = Gather(team, h_ref, rows, gs, gr)
    gather.start()
    gather.meet()
    steps.middle(0)
    if layer == 0:
        gather.pass_all()
    steps.weights.wait()

    def project(runs, back, s):
        normed = rows_at(h_ref, runs)
        cosine, sine = wide(rows_at(cos_ref, runs), columns), wide(rows_at(sin_ref, runs), columns)
        u = mm_nt(normed, w_ref[0:columns])
        put_rows(q_ref, runs, (u * cosine + swap_halves(u) * sine).astype(LOW) * jnp.asarray(HD**-0.5, LOW))
        u = mm_nt(normed, w_ref[columns : 2 * columns])
        put_rows(k_ref, runs, (u * cosine + swap_halves(u) * sine).astype(LOW))
        v = mm_nt(normed, w_ref[2 * columns : 3 * columns]).astype(LOW)
        if before_ref is not None:
            v = (0.5 * v.astype(F32) + 0.5 * rows_at(before_ref, runs).astype(F32)).astype(LOW)
        put_rows(m_ref, runs, v)

    if layer == 0:
        gather.receive_all()
        pl.loop(0, members)(lambda rank: project([block(rank, rows)], 0, None))
    else:
        gather.arrivals(project)
    for i in range(4):
        steps.done(i)
    steps.middle(1)
    reduce = Reduce(team, rows, reduce_refs)

    def attention(qb):
        at, upto = slice(qb * rows, (qb + 1) * rows), (qb + 1) * rows

        def one_head(head, carry):
            out, logs = carry
            mask = head_row(columns, head)
            scores = mm_nt(q_ref[at] * mask, k_ref[0:upto])
            row = lax.broadcasted_iota(jnp.int32, (rows, 1), 0) + qb * rows
            column = lax.broadcasted_iota(jnp.int32, scores.shape, 1)
            scores = jnp.where(column < jnp.minimum(row + 1, length), scores, NEG_LARGE)
            peak = jnp.max(scores, -1, keepdims=True)
            weights = jnp.exp(scores - peak)
            total = jnp.sum(weights, -1, keepdims=True)
            part = mm(weights.astype(LOW), m_ref[0:upto])
            out = out + part * (mask.astype(F32) * (1.0 / total))
            lane = lax.broadcasted_iota(jnp.int32, logs.shape, 1)
            logs = jnp.where(lane == head, peak + jnp.log(total), logs)
            return out, logs

        out, logs = lax.fori_loop(
            0, heads, one_head, (jnp.zeros((rows, columns), F32), jnp.zeros((rows, 128), F32))
        )
        o_ref[at] = out.astype(LOW)
        log_ref[qb] = jnp.transpose(logs)[0 : log_ref.shape[1]]

    @pl.loop(0, members)
    def _(p):
        o = chips - 1 - p // 2
        own = p % 2 == 1
        rank = team.chip(o) + jnp.where(own, team.core, 1 - team.core) * chips
        for qb in range(members):
            pl.when(rank == qb)(functools.partial(attention, qb))
        value = mm(o_ref[block(rank, rows)], w_ref[3 * columns : 4 * columns])
        pl.when(no(own))(lambda: reduce.put_other(o, None, value))

        @pl.when(own & (o > 0))
        def _():
            reduce.hold(o, None, value)
            reduce.pass_on(o, None)

        pl.when(own & (o == 0))(lambda: reduce.keep(value))
        pl.when(p == chips)(lambda: steps.middle(2))

    steps.done(4)
    steps.done(5)
    steps.middle(3)
    live = (lax.broadcasted_iota(jnp.int32, (1, span), 1) < length).astype(F32).astype(LOW)
    square = jnp.square(m_ref[...].astype(F32))
    high = square.astype(LOW)
    square_ref[...] = mm(live, high) + mm(live, (square - high.astype(F32)).astype(LOW))
    reduce.finish(False)

    def close(sl):
        x1_ref[sl] = x_ref[sl].astype(F32) + reduce.total(sl)

    by_rows(rows, close)
    gather.finish()


def stream(team, gather, reduce, work, here=False):
    def one(runs, back, s):
        value = work(runs)
        if s is not None:
            reduce.put_other(back, s, value[gather.size :])
            reduce.hold(back, s, value[: gather.size])
        elif one.kept:
            reduce.put_other(0, None, value)
        else:
            one.kept = True
            reduce.keep(value)

    one.kept = False

    def between(back, s):
        if gather.subs > 1:
            pl.when(s > 0)(lambda: reduce.pass_on(back, s - 1))

    def after(back):
        reduce.pass_on(back, gather.subs - 1)

    if not here:
        gather.arrivals(one, between, after)
        return
    for back in range(1, team.chips):

        @pl.loop(0, gather.subs)
        def _(s):
            one([gather.run(team.mine(back), s), gather.run(team.other(back), s)], back, s)
            between(back, s)

        after(back)
    one([block(team.mine(0), gather.rows)], 0, None)
    one([block(team.other(0), gather.rows)], 0, None)


def feed(
    team, steps, layer, x1_ref, gains_ref, w_ref, y_ref, h_ref, gate_ref, up_ref, z_ref, gs, gr, reduce_refs
):
    rows = x1_ref.shape[0]
    hidden = w_ref.shape[0] // 3
    norm_into(h_ref, team.mine(0) * rows, rows, lambda sl: x1_ref[sl], gains_ref[2 * layer + 1 : 2 * layer + 2])
    gather = Gather(team, h_ref, rows, gs, gr)
    reduce = Reduce(team, rows, reduce_refs)
    gather.start()
    steps.weights.wait()

    def work(runs):
        normed = rows_at(h_ref, runs)
        gate = mm_nt(normed, w_ref[0:hidden])
        up = mm_nt(normed, w_ref[hidden : 2 * hidden])
        put_rows(gate_ref, runs, gate.astype(LOW))
        put_rows(up_ref, runs, up.astype(LOW))
        z = (gate / (1.0 + jnp.exp(-gate)) * up).astype(LOW)
        put_rows(z_ref, runs, z)
        return mm(z, w_ref[2 * hidden : 3 * hidden])

    stream(team, gather, reduce, work)
    steps.middle(0)
    for i in range(4):
        steps.done(i)
    reduce.finish(True)

    def close(sl):
        y_ref[sl] = (x1_ref[sl] + reduce.total(sl)).astype(LOW)

    by_rows(rows, close)
    gather.finish()


def feed_back(
    team, steps, layer, gathered, g_ref, x1_ref, gain_ref, gate_ref, up_ref, h_ref, z_ref, w_ref, dx1_ref, gain_grad_ref,
    w_grad_ref, grad_ref, dgate_ref, dup_ref, gs, gr, reduce_refs,
):
    rows, width = x1_ref.shape
    hidden = w_ref.shape[0] // 3
    gather = Gather(team, grad_ref, rows, gs, gr)
    reduce = Reduce(team, rows, reduce_refs)
    own = block(team.mine(0), rows)
    if not gathered:
        grad_ref[own] = g_ref[...]
        gather.start()
    steps.middle(0)
    steps.weights.wait()
    steps.need(0)
    steps.need(1)

    def work(runs):
        dz = mm_nt(rows_at(grad_ref, runs), w_ref[2 * hidden : 3 * hidden])
        gate = rows_at(gate_ref, runs).astype(F32)
        sigma = 1.0 / (1.0 + jnp.exp(-gate))
        dgate = (dz * rows_at(up_ref, runs).astype(F32) * sigma * (1.0 + gate * (1.0 - sigma))).astype(LOW)
        dup = (dz * gate * sigma).astype(LOW)
        put_rows(dgate_ref, runs, dgate)
        put_rows(dup_ref, runs, dup)
        return mm(dgate, w_ref[0:hidden]) + mm(dup, w_ref[hidden : 2 * hidden])

    stream(team, gather, reduce, work, gathered)
    steps.middle(1)
    steps.need(2)
    steps.need(3)
    for at in columns_of(width):
        w_grad_ref[0:hidden, at] = mm_tn(dgate_ref[...], h_ref[:, at]).astype(LOW)
        w_grad_ref[hidden : 2 * hidden, at] = mm_tn(dup_ref[...], h_ref[:, at]).astype(LOW)
        w_grad_ref[2 * hidden : 3 * hidden, at] = mm_tn(z_ref[...], grad_ref[:, at]).astype(LOW)
    steps.done(0)
    reduce.finish(True)

    def outer(sl):
        return grad_ref[pl.ds(pl.multiple_of(own.start + sl.start, sl.size), sl.size)].astype(F32)

    def write(sl, value):
        dx1_ref[sl] = value

    gain = gain_ref[2 * layer + 1 : 2 * layer + 2]
    norm_back(rows, lambda sl: x1_ref[sl], reduce.total, gain, outer, write, gain_grad_ref)
    if not gathered:
        gather.finish()


def pair_slot(members, kb, qb):
    return kb * members - kb * (kb - 1) // 2 + qb - kb


def attend_back(
    team, steps, layer, dx1_ref, gain_ref, length, k_ref, q_ref, log_ref, o_ref, m_ref, cos_ref, sin_ref, h_ref, x_ref,
    value_grad_ref, w_ref, low_ref, gain_grad_ref, value_sent_ref, w_grad_ref, grad_ref, scratch, gs, gr, reduce_refs,
):
    do_ref, inner_ref, kt_ref, soft_ref, dm_ref, dk_ref, dq_ref, dqkv_ref, mask_ref = scratch
    last = value_grad_ref is None
    chips, members = team.chips, 2 * team.chips
    rows, width = dx1_ref.shape
    span, columns = q_ref.shape
    heads = columns // HD
    at = team.mine(0) * rows

    def low_rows(sl):
        grad_ref[pl.ds(pl.multiple_of(at + sl.start, sl.size), sl.size)] = dx1_ref[sl].astype(LOW)

    by_rows(rows, low_rows)
    gather = Gather(team, grad_ref, rows, gs, gr)
    reduce = Reduce(team, rows, reduce_refs)
    gather.start()
    for i in range(3):
        steps.need(i)
    dq_ref[...] = jnp.zeros_like(dq_ref)

    @pl.loop(0, members)
    def _(kb):
        ks = block(kb, rows)
        kt_ref[kb] = jnp.transpose(k_ref[ks])

        @pl.loop(kb, members)
        def _(qb):
            key = lax.broadcasted_iota(jnp.int32, (rows, rows), 0) + kb * rows
            query = lax.broadcasted_iota(jnp.int32, (rows, rows), 1) + qb * rows
            mask_ref[...] = jnp.where((key <= query) & (key < length), 0.0, NEG_LARGE)
            for head in range(heads):
                q = q_ref[block(qb, rows)] * head_row(columns, head)
                scores = mm_nt(k_ref[ks], q) + mask_ref[...] - log_ref[qb, head : head + 1]
                soft_ref[pair_slot(members, kb, qb), head] = jnp.exp(scores).astype(LOW)

    steps.middle(0)
    steps.weights.wait()
    for i in range(3, 9 if last else 10):
        steps.need(i)

    def upstream(runs, back, s):
        put_rows(do_ref, runs, mm_nt(rows_at(grad_ref, runs), w_ref[3 * columns : 4 * columns]).astype(LOW))

    gather.arrivals(upstream)
    steps.middle(1)
    pad = inner_ref.shape[1]
    pick = (
        lax.broadcasted_iota(jnp.int32, (pad, columns), 1) // HD == lax.broadcasted_iota(jnp.int32, (pad, columns), 0)
    )
    pick = pick.astype(F32).astype(LOW)

    @pl.loop(0, members)
    def _(b):
        sl = block(b, rows)
        product = do_ref[sl].astype(F32) * o_ref[sl].astype(F32)
        high = product.astype(LOW)
        rest = (product - high.astype(F32)).astype(LOW)
        inner_ref[b] = mm_nt(pick, high) + mm_nt(pick, rest)

    def owner(b):
        return (b % chips - team.seat + chips) % chips, b // chips == team.core

    def settle(b):
        o, own = owner(b)
        pl.when(own & (o > 0))(lambda: reduce.pass_on(o, None))

    @pl.loop(0, members)
    def _(kb):
        ks = block(kb, rows)
        dm_ref[...] = jnp.zeros_like(dm_ref)
        dk_ref[...] = jnp.zeros_like(dk_ref)

        @pl.loop(kb, members)
        def _(qb):
            qs = block(qb, rows)
            for head in range(heads):
                mask = head_row(columns, head)
                q, do = q_ref[qs] * mask, do_ref[qs] * mask
                soft = soft_ref[pair_slot(members, kb, qb), head]
                dsoft = mm_nt(m_ref[ks], do)
                ds = (soft.astype(F32) * (dsoft - inner_ref[qb, head : head + 1])).astype(LOW)
                dm_ref[...] += mm(soft, do)
                dk_ref[...] += mm(ds, q)
                part = slice(head * HD, (head + 1) * HD)
                dq_ref[qb, part] += mm(kt_ref[kb, part], ds)

        cosine, sine = wide(cos_ref[ks], columns), wide(sin_ref[ks], columns)
        dq = jnp.transpose(dq_ref[kb]) * HD**-0.5
        dqkv_ref[0, ks] = (dq * cosine - swap_halves(dq) * sine).astype(LOW)
        dk = dk_ref[...]
        dqkv_ref[1, ks] = (dk * cosine - swap_halves(dk) * sine).astype(LOW)
        if last:
            dv = (0.5 * dm_ref[...]).astype(LOW)
            value_sent_ref[ks] = dv
        else:
            dv = (dm_ref[...] + value_grad_ref[ks].astype(F32)).astype(LOW)
        dqkv_ref[2, ks] = dv
        value = mm(dqkv_ref[0, ks], w_ref[0:columns])
        for t in (1, 2):
            value = value + mm(dqkv_ref[t, ks], w_ref[t * columns : (t + 1) * columns])
        o, own = owner(kb)
        pl.when(no(own))(lambda: reduce.put_other(o, None, value))
        pl.when(own & (o > 0))(lambda: reduce.hold(o, None, value))
        pl.when(own & (o == 0))(lambda: reduce.keep(value))
        pl.when(kb > 0)(lambda: settle(kb - 1))

    settle(members - 1)
    steps.middle(2)
    for piece in columns_of(width):
        w_grad_ref[3 * columns : 4 * columns, piece] = mm_tn(o_ref[...], grad_ref[:, piece]).astype(LOW)
        for t in range(3):
            w_grad_ref[t * columns : (t + 1) * columns, piece] = mm_tn(dqkv_ref[t], h_ref[:, piece]).astype(LOW)
    steps.done(0)
    reduce.finish(False)

    def write(sl, value):
        low_ref[sl] = value.astype(LOW)

    norm_back(
        rows,
        lambda sl: x_ref[sl].astype(F32),
        reduce.total,
        gain_ref[2 * layer : 2 * layer + 1],
        lambda sl: dx1_ref[sl],
        write,
        gain_grad_ref,
    )
    gather.finish()


class Parts:
    def __init__(self, arrays, parts):
        self.arrays, self.parts = arrays, parts
        self.lines = sum(a.shape[0] for a in arrays)
        self.width = arrays[0].shape[1]

    def own(self, refs, i):
        array, start, rows, _ = self.parts[i]
        return lines(refs[array], start, rows)

    def of_block(self, ref, i):
        _, _, rows, start = self.parts[i]
        return lines(ref, start, rows)


class Fetch:
    def __init__(self, team, layer, block, own, buf, far_send, far_recv, near_send, near_recv, here):
        self.team, self.block, self.own, self.buf, self.n = team, block, own, buf, len(block.parts)
        self.fs, self.fr, self.ns, self.nr = far_send, far_recv, near_send, near_recv
        self.size = block.width // team.groups
        holds = team.core == layer
        self.sends, self.gives, self.takes = holds, team.away & holds, team.home & no(holds)
        self.stays = team.home & holds
        self.loads, start = [], 0
        for i, ref in enumerate(own):
            self.loads.append(Local(ref, lines(buf, start, ref.shape[0]), here.at[i]))
            start += ref.shape[0]

    def far(self, i):
        team = self.team
        return remote(
            columns_at(self.block.own(self.own, i), team.group, self.size),
            columns_at(self.block.of_block(self.buf, i), team.group, self.size),
            self.fs.at[i],
            self.fr.at[i],
            team.far(team.half),
        )

    def cross(self, i):
        own, there = self.block.own(self.own, i), self.block.of_block(self.buf, i)
        return remote(own, there, self.ns.at[i], self.nr.at[i], self.team.sibling())

    def along(self, i, o, arriving=False):
        team = self.team
        group = (team.group + team.groups - o) % team.groups if arriving else team.group
        share, slot = columns_at(self.block.of_block(self.buf, i), group, self.size), o * self.n + i
        return remote(share, share, self.ns.at[slot], self.nr.at[slot], team.dp(o))

    def start_near(self):
        @pl.when(self.gives)
        def _():
            for i in range(self.n):
                self.cross(i).start()

        @pl.when(self.stays)
        def _():
            for copy in self.loads:
                copy.start()

    def start_far(self, parts=None):
        @pl.when(self.sends)
        def _():
            for i in range(self.n) if parts is None else parts:
                self.far(i).start()

    def pass_on(self, parts=None):
        @pl.when(self.team.away)
        def _():
            for i in range(self.n) if parts is None else parts:
                self.far(i).wait_recv()
                for o in range(1, self.team.groups):
                    self.along(i, o).start()

    def wait(self):
        @pl.when(self.sends)
        def _():
            for i in range(self.n):
                self.far(i).wait_send()

        @pl.when(self.gives)
        def _():
            for i in range(self.n):
                self.cross(i).wait_send()

        @pl.when(self.takes)
        def _():
            for i in range(self.n):
                self.cross(i).wait_recv()

        @pl.when(self.stays)
        def _():
            for copy in self.loads:
                copy.wait()

        @pl.when(self.team.away)
        def _():
            for i in range(self.n):
                for o in range(1, self.team.groups):
                    self.along(i, o).wait_send()
                    self.along(i, o, arriving=True).wait_recv()


class Scatter:
    @staticmethod
    def scratch(shape):
        rows, width = shape
        groups = lax.axis_size("dp")
        low, high = sides(groups)
        size, cut = width // groups, rows // 32 * 16
        rest = rows - cut
        first, second = (low - 1) * high + (high - 1) * low, high + low - 2
        return [
            *(semaphores(n) for n in (first, first, second, second, high + low)),
            pltpu.VMEM((max(low - 1, 1), high, cut, size), LOW),
            pltpu.VMEM((high, cut, size), LOW),
            pltpu.VMEM((max(high - 1, 1), cut, size), LOW),
            pltpu.VMEM((max(high - 1, 1), low, rest, size), LOW),
            pltpu.VMEM((low, rest, size), LOW),
            pltpu.VMEM((max(low - 1, 1), rest, size), LOW),
            pltpu.VMEM((rows, size), LOW),
        ]

    def __init__(self, team, part, fs, fr, ss, sr, load, *buffers):
        self.team, self.part = team, part
        self.land, self.sums, self.last = buffers[0::3][:2], buffers[1:6:3], buffers[2:6:3]
        self.share = buffers[6]
        low, high = sides(team.groups)
        at_high, at_low = team.group // low, team.group % low
        size, cut = self.share.shape[1], self.sums[0].shape[1]
        upper, lower = lines(part, 0, cut), lines(part, cut, self.share.shape[0] - cut)

        def device(b, a):
            return (team.core, (at_high + b) % high * low + (at_low + a) % low, team.along)

        self.loads = [
            Local(columns_at(upper, b * low + at_low, size), self.sums[0].at[b], load.at[b]) for b in range(high)
        ] + [
            Local(columns_at(lower, at_high * low + a, size), self.sums[1].at[a], load.at[high + a]) for a in range(low)
        ]
        self.firsts = []
        for a in range(1, low):
            for b in range(high):
                src, dst = columns_at(upper, b * low + (at_low + a) % low, size), self.land[0].at[a - 1, b]
                self.firsts.append((src, dst, device(0, a)))
        for b in range(1, high):
            for a in range(low):
                src, dst = columns_at(lower, (at_high + b) % high * low + a, size), self.land[1].at[b - 1, a]
                self.firsts.append((src, dst, device(b, 0)))
        self.firsts = [remote(s, d, fs.at[i], fr.at[i], to) for i, (s, d, to) in enumerate(self.firsts)]
        self.seconds = [
            (self.sums[0].at[(at_high + b) % high], self.last[0].at[b - 1], device(b, 0)) for b in range(1, high)
        ] + [(self.sums[1].at[(at_low + a) % low], self.last[1].at[a - 1], device(0, a)) for a in range(1, low)]
        self.seconds = [remote(s, d, ss.at[i], sr.at[i], to) for i, (s, d, to) in enumerate(self.seconds)]
        self.kept = self.sums[0].at[at_high], self.sums[1].at[at_low]
        self.cut = cut

    def start(self):
        for copy in (*self.firsts, *self.loads):
            copy.start()

    def turn(self):
        for copy in (*self.firsts, *self.loads):
            copy.wait()
        for land, sums in zip(self.land, self.sums):
            for i in range(sums.shape[0]):
                add_rows(sums.at[i], 0, sums.at[i], [land.at[n, i] for n in range(land.shape[0])])
        for copy in self.seconds:
            copy.start()

    def close(self):
        for copy in self.seconds:
            copy.wait()
        for at, kept, last in zip((0, self.cut), self.kept, self.last):
            add_rows(self.share, at, kept, [last.at[n] for n in range(last.shape[0])])


def add_rows(out, at, own, others):
    rows = own.shape[0]
    step = next(n for n in (64, 32, 16) if rows % n == 0)

    @pl.loop(0, rows // step)
    def _(i):
        sl = pl.ds(pl.multiple_of(i * step, step), step)
        total = own[sl].astype(F32)
        for other in others:
            total = total + other[sl].astype(F32)
        out[pl.ds(pl.multiple_of(at + i * step, 16), step)] = total.astype(LOW)


class Swap:
    def __init__(self, team, layer, share, land, send, recv):
        self.team, self.layer = team, layer
        self.far = remote(share, land.at[0], send.at[0], recv.at[0], team.far(layer))
        self.near = remote(share, land.at[1], send.at[0], recv.at[1], team.sibling())

    def each(self, act):
        team = self.team
        pl.when(team.away)(lambda: act(self.far))
        pl.when(team.home & (team.core != self.layer))(lambda: act(self.near))

    def start(self):
        self.each(lambda c: c.start())

    def finish(self):
        self.each(lambda c: c.wait_send())
        team = self.team
        pl.when(team.core == self.layer)(lambda: self.far.wait_recv())
        pl.when((team.core == self.layer) & team.away)(lambda: self.near.wait_recv())


def add_swapped(team, out, share, landed):
    def body(sl):
        near = jnp.where(team.home, share[sl].astype(F32), landed[1, sl].astype(F32))
        out[sl] = (near + landed[0, sl].astype(F32)).astype(LOW)

    by_tiles(out.shape[0], body)


class Spread:
    def __init__(self, team, share, fulls, send, recv, here):
        self.team, self.share, self.fulls, self.send, self.recv, self.here = team, share, fulls, send, recv, here
        self.low, self.high = sides(team.groups)

    @staticmethod
    def moves(groups):
        low, high = sides(groups)
        upper = [(True, (0, a), (0, 0)) for a in range(1, low)]
        upper += [(True, (b, 0), (0, a)) for b in range(1, high) for a in range(low)]
        lower = [(False, (b, 0), (0, 0)) for b in range(1, high)]
        lower += [(False, (0, a), (b, 0)) for a in range(1, low) for b in range(high)]
        return upper + lower

    def group(self, high, low):
        team = self.team
        return (
            (team.group // self.low + self.high - high) % self.high * self.low
            + (team.group % self.low + self.low - low) % self.low
        )

    def copies(self, first, arriving=False):
        team, size = self.team, self.share.shape[1]
        start = 0
        moves = self.moves(team.groups)
        for i, full in enumerate(self.fulls):
            rows = full.shape[0]
            cut = rows // 32 * 16
            for n, (upper, (high, low), (from_high, from_low)) in enumerate(moves):
                if ((from_high, from_low) == (0, 0)) != first:
                    continue
                at, count = (0, cut) if upper else (cut, rows - cut)
                slot = i * len(moves) + n
                back = arriving * high + from_high, arriving * low + from_low
                there = columns_at(lines(full, at, count), self.group(*back), size)
                src = lines(self.share, start + at, count) if first else there
                target = self.group(-high, -low)
                device = (team.core, target, team.along)
                yield remote(src, there, self.send.at[slot], self.recv.at[slot], device)
            start += rows

    def stays(self):
        start = 0
        for i, full in enumerate(self.fulls):
            there = columns_at(full, self.team.group, self.share.shape[1])
            yield Local(lines(self.share, start, full.shape[0]), there, self.here.at[i])
            start += full.shape[0]

    def start(self):
        for copy in (*self.copies(True), *self.stays()):
            copy.start()

    def middle(self):
        for copy in self.copies(True, arriving=True):
            copy.wait_recv()
        for copy in self.copies(False):
            copy.start()

    def finish(self):
        for copy in self.stays():
            copy.wait()
        for first in (True, False):
            for copy in self.copies(first):
                copy.wait_send()
        for copy in self.copies(False, arriving=True):
            copy.wait_recv()


def sides(groups):
    low = 2 if groups % 2 == 0 else 1
    return low, groups // low


def call(body, chips, ident, flops, lengths, args, far_args, outs, far_outs, drained, scratch, partners):
    vmem, far = pl.BlockSpec(memory_space=pltpu.VMEM), pl.BlockSpec(memory_space=pl.ANY)
    cuts = [1 + len(args) + len(far_args), len(outs) + len(far_outs), len(drained), len(drained), 1]

    def kernel(*refs):
        groups, start = [], 0
        for n in cuts:
            groups.append(refs[start : start + n])
            start += n
        ins, results, left, buffers, (drain_sem,) = groups
        team = Team(chips)
        team.enter(partners(team))
        drains = [Local(src, dst, drain_sem.at[i]) for i, (src, dst) in enumerate(zip(buffers, left))]
        body(team, lambda i: drains[i].start(), *ins, *results, *buffers, *refs[start:])
        for copy in drains:
            copy.wait()

    moved = sum(a.size * a.dtype.itemsize for a in (*args, *far_args))
    return pl.pallas_call(
        kernel,
        out_shape=[jax.ShapeDtypeStruct(shape, dtype) for shape, dtype in (*outs, *far_outs, *drained)],
        in_specs=[pl.BlockSpec(memory_space=pltpu.SMEM)] + [vmem] * len(args) + [far] * len(far_args),
        out_specs=[vmem] * len(outs) + [far] * (len(far_outs) + len(drained)),
        scratch_shapes=[*(pltpu.VMEM(shape, dtype) for shape, dtype in drained), semaphores(len(drained)), *scratch],
        cost_estimate=pl.CostEstimate(flops=WAITING * flops, bytes_accessed=moved, transcendentals=0),
        compiler_params=pltpu.CompilerParams(
            collective_id=ident, has_side_effects=True, vmem_limit_bytes=VMEM_BYTES
        ),
    )(lengths, *args, *far_args)


def rope_tables(span, columns):
    position = jnp.arange(span, dtype=F32)
    freqs = ROPE_BASE ** (-jnp.arange(0, HD, 2, dtype=F32) / HD)
    angle = position[:, None] * freqs[None, :]
    heads = columns // HD
    cosine = jnp.tile(jnp.concatenate([jnp.cos(angle), jnp.cos(angle)], -1), (1, heads))
    sine = jnp.tile(jnp.concatenate([-jnp.sin(angle), jnp.sin(angle)], -1), (1, heads))
    return cosine, sine


def everywhere_sum(team, refs):
    small_ref, sum_ref, near, groups_ref, members_ref, send, recv, gs, gr, ms, mr = refs
    copy = remote(small_ref, near, send.at[0], recv.at[0], team.sibling())
    copy.start()
    copy.wait()
    groups_ref[team.group] = small_ref[...] + near[...]

    def exchange(ref, mine, count, device, send, recv):
        for o in range(1, count):
            remote(ref.at[mine], ref.at[mine], send.at[o - 1], recv.at[o - 1], device(o)).start()
        for o in range(1, count):
            remote(ref.at[mine], ref.at[mine], send.at[o - 1], recv.at[o - 1], device(o)).wait_send()
            there = ref.at[(mine + count - o) % count]
            remote(there, there, send.at[o - 1], recv.at[o - 1], device(o)).wait_recv()
        total = ref[0]
        for i in range(1, count):
            total = total + ref[i]
        return total

    members = 2 * team.chips
    members_ref[team.along] = exchange(groups_ref, team.group, team.groups, team.dp, gs, gr)
    sum_ref[...] = exchange(members_ref, team.along, members, team.member, ms, mr)


class Steps:
    def __init__(self, weights, steps, done, loads=()):
        self.weights, self.steps, self.done, self.loads = weights, steps, done, loads

    def need(self, index):
        self.loads[index].wait()

    def middle(self, step):
        self.steps.get(step, lambda: None)()


class Waits:
    def __init__(self, *copies):
        self.copies = copies

    def wait(self):
        for copy in self.copies:
            copy.wait()


class Take:
    def __init__(self, refs):
        self.refs = list(refs)

    def __call__(self, n):
        taken = self.refs[:n]
        del self.refs[:n]
        return taken


KEPT = ("x", "x1", "h", "q", "k", "m", "o", "log", "h2", "gate", "up", "z", "w_attn", "w_feed")


def forward_kernel(team, done, *refs, attn_block, feed_block):
    take = Take(refs)
    lengths_ref, gain_ref, cos_far, sin_far, tokens_ref, cotangent_ref = take(6)
    length = lengths_ref[team.half, 0]
    own_attn, own_feed = take(len(attn_block.arrays)), take(len(feed_block.arrays))
    gains_ref, *squares = take(3)
    placed = take(1)[0]
    layers = [dict(zip(KEPT, take(len(KEPT)))) for _ in range(2)]
    y_ref, top_ref = take(2)
    other_gain, cos_ref, sin_ref, one = take(4)
    fetches = []
    for layer in range(2):
        for block_, own, name in ((attn_block, own_attn, "w_attn"), (feed_block, own_feed, "w_feed")):
            fetches.append(Fetch(team, layer, block_, own, layers[layer][name], *take(5)))
    attn_fetch, feed_fetch, attn_fetch1, feed_fetch1 = fetches
    team_sems = [take(2) for _ in range(5)]
    swap_sems, reduce_refs = take(2), take(10)
    x_ref = layers[0]["x"]
    rows = x_ref.shape[0]
    mine = block(team.mine(0), rows)
    over = remote(tokens_ref.at[1 - team.half], x_ref, one.at[0], one.at[1], team.far(team.core))
    here = Local(tokens_ref.at[team.half], x_ref, one.at[2])
    top_over = remote(cotangent_ref.at[1 - team.half], top_ref.at[mine], one.at[3], one.at[4], team.far(team.core))
    top_here = Local(cotangent_ref.at[team.half], top_ref.at[mine], one.at[5])
    top_gather = Gather(team, top_ref, rows, *team_sems[4])
    gain_copy = remote(gain_ref, other_gain, one.at[6], one.at[7], team.sibling())
    tables = [Local(cos_far, cos_ref, one.at[8]), Local(sin_far, sin_ref, one.at[9])]
    first_swap = Swap(team, 0, layers[1]["x"], placed, *swap_sems)

    @pl.when(team.home)
    def _():
        over.start()
        here.start()
        top_here.start()

    gain_copy.start()
    attn_fetch.start_near()
    for copy in tables:
        copy.start()
    gain_copy.wait()
    own = team.core == 0
    gains_ref[0:2] = jnp.where(own, gain_ref[...], other_gain[...])
    gains_ref[2:4] = jnp.where(own, other_gain[...], gain_ref[...])
    pl.when(team.home)(here.wait)
    pl.when(team.away)(over.wait_recv)

    def first_gather():
        pl.when(team.home)(over.wait_send)
        attn_fetch.start_far()
        feed_fetch.start_near()
        feed_fetch.start_far([0])
        attn_fetch.pass_on()

    def first_projected():
        feed_fetch.start_far([1, 2])
        feed_fetch.pass_on([0])

    def first_attended():
        feed_fetch.pass_on([1, 2])
        attn_fetch1.start_near()
        attn_fetch1.start_far()
        pl.when(team.home)(top_over.start)

    def first_fed():
        attn_fetch1.pass_on()
        feed_fetch1.start_near()
        feed_fetch1.start_far()

    def second_projected():
        feed_fetch1.pass_on([0])
        pl.when(team.home)(top_here.wait)
        pl.when(team.away)(top_over.wait_recv)
        top_gather.start()
        first_swap.start()

    steps = [
        {0: first_gather, 1: first_projected, 3: first_attended, 4: first_fed},
        {
            1: second_projected,
            2: lambda: feed_fetch1.pass_on([1]),
            3: lambda: feed_fetch1.pass_on([2]),
            4: top_gather.pass_all,
        },
    ]
    names = ("h", "q", "k", "m", "o", "log"), ("h2", "gate", "up", "z")
    for layer, kept in enumerate(layers):
        base = layer * len(KEPT)

        def leave(name):
            done(base + KEPT.index(name))

        leave("x")
        waits = Waits(fetches[2 * layer], *([] if layer else tables))
        attend(
            team, Steps(waits, steps[layer], lambda i: leave(names[0][i])), layer, kept["x"], gains_ref, length, cos_ref,
            sin_ref, layers[0]["m"] if layer else None, kept["w_attn"], kept["x1"], squares[layer],
            *(kept[name] for name in names[0]), *team_sems[2 * layer], reduce_refs,
        )
        leave("w_attn")
        leave("x1")
        after = layers[1]["x"] if layer == 0 else y_ref
        feed(
            team, Steps(fetches[2 * layer + 1], {0: steps[layer][4]}, lambda i: leave(names[1][i])), layer, kept["x1"],
            gains_ref, kept["w_feed"], after, *(kept[name] for name in names[1]), *team_sems[2 * layer + 1], reduce_refs,
        )
        leave("w_feed")
    done(2 * len(KEPT))
    pl.when(team.home)(top_over.wait_send)
    top_gather.meet()
    top_gather.receive_all()
    top_gather.finish()
    done(2 * len(KEPT) + 1)
    first_swap.finish()


class Backward:
    def __init__(self, team, take, layer, gathered, extra=0):
        self.team, self.layer, self.gathered = team, layer, gathered
        self.lengths, self.x1, self.gain = take(3)
        self.length = self.lengths[team.half, 0]
        self.g, *self.extra = take(1 + extra)
        self.feed_in, self.feed_full = take(4), take(1)[0]
        self.attn_in, self.attn_full = take(9), take(1)[0]
        self.value_grad = None if gathered else take(1)[0]

    def results(self, take):
        self.low, self.feed_gain, self.attn_gain = take(3)
        self.value_sent = take(1)[0] if self.gathered else None
        self.feed_part, self.attn_part = take(2)

    @staticmethod
    def scratch(chips, rows, span, width):
        return [
            pltpu.VMEM((span, width), LOW), pltpu.VMEM((span, width), LOW), pltpu.VMEM((rows, width), F32),
            *gather_scratch(chips, rows), *gather_scratch(chips, rows), *reduce_scratch(chips, rows, width),
            semaphores(10), semaphores(3),
        ]

    def buffers(self, take):
        self.grad_feed, self.grad_attn, self.dx1 = take(3)
        self.feed_team, self.attn_team, self.reduce = take(2), take(2), take(10)
        self.load_sem, self.own_sem = take(2)

    def loads(self, sources, buffers):
        copies = [Local(src, dst, self.load_sem.at[i]) for i, (src, dst) in enumerate(zip(sources, buffers))]
        for copy in copies:
            copy.start()
        return copies

    def leaves(self, src, dst, after):
        def done(index):
            copy = Local(src, dst, self.own_sem.at[1])
            copy.start()
            copy.wait()
            after()

        return done

    def weights(self, full, buf):
        copy = Local(full, buf, self.own_sem.at[0])
        copy.start()
        return copy

    def feed(self, steps, after):
        def phase(gate, up, h, z, w, w_grad, dgate, dup):
            loads = self.loads(self.feed_in, (gate, up, h, z))
            weights = [self.weights(self.feed_full, w)]
            if self.gathered:
                weights.append(Local(self.g, self.grad_feed, self.own_sem.at[2]))
                weights[1].start()
            feed_back(
                self.team, Steps(Waits(*weights), steps, self.leaves(w_grad, self.feed_part, after), loads), self.layer,
                self.gathered, self.g, self.x1, self.gain, gate, up, h, z, w, self.dx1, self.feed_gain, w_grad,
                self.grad_feed, dgate, dup, *self.feed_team, self.reduce,
            )

        like = [pltpu.VMEM(ref.shape, ref.dtype) for ref in (*self.feed_in, *[self.feed_full] * 2, *self.feed_in[:2])]
        pl.run_scoped(phase, *like)

    def attend(self, steps, after):
        sources = [*self.attn_in] + ([] if self.gathered else [self.value_grad])

        def phase(*scoped):
            take = Take(scoped)
            loaded, (w, w_grad) = take(len(sources)), take(2)
            loads = self.loads(sources, loaded)
            if self.gathered:
                loaded = [*loaded, None]
            weights = self.weights(self.attn_full, w)
            attend_back(
                self.team, Steps(weights, steps, self.leaves(w_grad, self.attn_part, after), loads), self.layer, self.dx1,
                self.gain, self.length, *loaded, w, self.low, self.attn_gain, self.value_sent, w_grad, self.grad_attn,
                take.refs, *self.attn_team, self.reduce,
            )

        rows, span, columns = self.x1.shape[0], *self.attn_in[0].shape
        pl.run_scoped(
            phase,
            *(pltpu.VMEM(ref.shape, ref.dtype) for ref in sources),
            *[pltpu.VMEM(self.attn_full.shape, LOW)] * 2,
            *attend_back_scratch(rows, span, columns, self.attn_in[2].shape),
        )


def second_back_kernel(team, done, *refs):
    take = Take(refs)
    back = Backward(team, take, 1, True)
    rows_ref = take(1)[0]
    back.results(take)
    placed, share_out = take(2)
    back.buffers(take)
    scatter = Scatter(team, back.feed_part, *take(12))
    swap = Swap(team, 1, rows_ref, placed, *take(2))
    (leave_sem,) = take(1)
    leave = Local(scatter.share, share_out, leave_sem.at[0])
    back.feed({}, scatter.start)
    back.attend({1: swap.start, 2: scatter.turn}, lambda: None)
    scatter.close()
    leave.start()
    leave.wait()
    swap.finish()


def last_kernel(team, done, *refs):
    take = Take(refs)
    back = Backward(team, take, 0, False, 4)
    attn_part1, feed_share1, rows1 = take(3)
    sum_ref = take(1)[0]
    back.results(take)
    placed, *fulls = take(5)
    back.buffers(take)
    feed_own, feed_land, feed_out, attn_land, attn_out, own_sem = take(6)
    attn_scatter1, feed_scatter0, attn_scatter0 = (
        Scatter(team, part, *take(12)) for part in (attn_part1, back.feed_part, back.attn_part)
    )
    feed_swap1 = Swap(team, 1, feed_share1, feed_land, *take(2))
    attn_swap1 = Swap(team, 1, attn_scatter1.share, attn_land, *take(2))
    feed_swap0 = Swap(team, 0, feed_scatter0.share, feed_land, *take(2))
    attn_swap0 = Swap(team, 0, attn_scatter0.share, attn_land, *take(2))
    rows_swap1 = Swap(team, 1, rows1, placed, *take(2))
    rows_swap0 = Swap(team, 0, back.low, placed, *take(2))
    feed_spread = Spread(team, feed_out, fulls[:2], *take(3))
    attn_spread = Spread(team, attn_out, fulls[2:], *take(3))
    small_ref, *small = take.refs
    last = team.core == 0
    attn_scatter1.start()
    rows_swap1.start()
    own_load = Local(feed_share1, feed_own, own_sem.at[0])
    own_load.start()

    def after_feed():
        feed_scatter0.start()
        attn_scatter1.close()

    def after_gather():
        feed_swap1.start()
        attn_swap1.start()

    def after_attn():
        attn_scatter0.start()
        feed_scatter0.close()
        feed_swap0.start()

    back.feed({1: attn_scatter1.turn}, after_feed)
    back.attend({1: after_gather, 2: feed_scatter0.turn}, after_attn)
    attn_scatter0.turn()
    feed_swap1.finish()
    attn_swap1.finish()
    own_load.wait()

    @pl.when(no(last))
    def _():
        add_swapped(team, feed_out, feed_own, feed_land)
        feed_spread.start()
        add_swapped(team, attn_out, attn_scatter1.share, attn_land)
        attn_spread.start()

    attn_scatter0.close()
    attn_swap0.start()
    small_ref[...] = jnp.zeros_like(small_ref)
    for i, part in enumerate([back.attn_gain, back.feed_gain, *back.extra]):
        small_ref[i : i + 1, 0 : part.shape[1]] = part[...]
    positions = back.lengths[0, 0] + back.lengths[1, 0]
    small_ref[6:7] = jnp.broadcast_to(positions, (1, small_ref.shape[1])).astype(F32)
    everywhere_sum(team, [small_ref, sum_ref, *small])

    @pl.when(no(last))
    def _():
        feed_spread.middle()
        attn_spread.middle()

    feed_swap0.finish()

    @pl.when(last)
    def _():
        add_swapped(team, feed_out, feed_scatter0.share, feed_land)
        feed_spread.start()

    attn_swap0.finish()
    rows_swap0.start()

    @pl.when(last)
    def _():
        add_swapped(team, attn_out, attn_scatter0.share, attn_land)
        attn_spread.start()
        feed_spread.middle()
        attn_spread.middle()

    rows_swap1.finish()
    rows_swap0.finish()
    feed_spread.finish()
    attn_spread.finish()


def attend_back_scratch(rows, span, columns, logs_shape):
    members = span // rows
    return [
        pltpu.VMEM(shape, dtype)
        for shape, dtype in (
            ((span, columns), LOW),
            (logs_shape, F32),
            ((members, columns, rows), LOW),
            ((members * (members + 1) // 2, columns // HD, rows, rows), LOW),
            ((rows, columns), F32),
            ((rows, columns), F32),
            ((members, columns, rows), F32),
            ((3, span, columns), LOW),
            ((rows, rows), F32),
        )
    ]


def finish(sums, outs, low_grads, grads, members):
    rows, width = outs[0].shape
    sizes = [rows] + [a.shape[0] for a in grads]
    steps = next(n for n in (4, 2, 1) if all(size % (16 * n) == 0 for size in sizes) or n == 1)
    chips = members // 2

    def kernel(sums_ref, *refs):
        take = Take(refs)
        out_refs, grad_refs, low_refs = take(4), take(3), take(len(grads))
        layer_out, input_grads, gain_one, gain_two, norm, *full = take.refs
        first = lax.axis_index("section") == 0
        half = lax.axis_index("mp") // chips
        home = lax.axis_index("section") == half

        def place(target, zero, one, placed):
            here = jnp.where(home, jnp.where(first, zero[...], one[...]), placed[1])
            target[0] = jnp.where(half == 0, here, placed[0]).astype(target.dtype)
            target[1] = jnp.where(half == 0, placed[0], here).astype(target.dtype)

        zero, one, placed0, placed1 = out_refs
        placed = [jnp.where(first, placed0[i], placed1[i]) for i in range(2)]
        place(layer_out, zero, one, placed)
        place(input_grads, *grad_refs)
        gain_one[...] = jnp.where(first, sums_ref[0:1], sums_ref[2:3])
        gain_two[...] = jnp.where(first, sums_ref[1:2], sums_ref[3:4])
        square = jnp.sum(jnp.where(first, sums_ref[4:5], sums_ref[5:6]), -1, keepdims=True)
        count = sums_ref[6:7, 0:1] / (2 * members)
        norm[...] = jnp.sqrt(square / (count * width))
        for low, result in zip(low_refs, full):
            result[...] = low[...].astype(F32)

    def cut(shape):
        if len(shape) == 3:
            return pl.BlockSpec((shape[0], shape[1] // steps, width), lambda i: (0, i, 0))
        return pl.BlockSpec((shape[0] // steps, width), lambda i: (i, 0))

    def whole(shape):
        return pl.BlockSpec(shape, lambda i: (0, 0))

    args = [*outs, *low_grads, *grads]
    results = [((2, rows, width), LOW), ((2, rows, width), F32)]
    small = [((1, width), F32), ((1, width), F32), ((1, 1), F32)]
    full = [(a.shape, F32) for a in grads]
    return pl.pallas_call(
        kernel,
        grid=(steps,),
        out_shape=[jax.ShapeDtypeStruct(shape, dtype) for shape, dtype in (*results, *small, *full)],
        in_specs=[whole(sums.shape), *(cut(a.shape) for a in args)],
        out_specs=[
            *(cut(shape) for shape, _ in results),
            *(whole(shape) for shape, _ in small),
            *(cut(shape) for shape, _ in full),
        ],
        compiler_params=pltpu.CompilerParams(vmem_limit_bytes=VMEM_BYTES),
    )(sums, *args)


def local(tokens, cotangent, lengths, gain_attn, w_qkv, w_out, gain_ffn, w_gate_up, w_down):
    cores, groups, members = lax.axis_size("section"), lax.axis_size("dp"), lax.axis_size("mp")
    micro, sequences, rows, width = tokens.shape
    assert cores == 2 and micro == 2 and sequences == 1 and members % 2 == 0 and members >= 4
    chips = members // 2
    span = rows * members
    columns, hidden = w_out.shape[1], w_down.shape[1]
    heads = columns // HD
    quarter = width // groups
    padded = -(-heads // 8) * 8

    def vec(*shape, dtype=LOW):
        return pltpu.VMEM(shape, dtype)

    whole, of_heads, of_hidden, logs_shape = (span, width), (span, columns), (span, hidden), (members, padded, rows)
    own_attn = Parts(
        [w_qkv[0].reshape(3 * columns, width), w_out[0]],
        [(0, t * columns, columns, t * columns) for t in range(3)] + [(1, 0, columns, 3 * columns)],
    )
    own_feed = Parts(
        [w_gate_up[0].reshape(2 * hidden, width), w_down[0]],
        [(0, t * hidden, hidden, t * hidden) for t in range(2)] + [(1, 0, hidden, 2 * hidden)],
    )
    own_gains = jnp.concatenate([gain_attn, gain_ffn], 0)
    cosine, sine = rope_tables(span, columns if columns % 128 else 128)

    def fetch_sems(block_):
        n = len(block_.parts)
        return [semaphores(k) for k in (n, n, groups * n, groups * n, len(block_.arrays))]

    row_block, attn_shape, feed_shape = ((rows, width), LOW), ((4 * columns, width), LOW), ((3 * hidden, width), LOW)
    kept_shapes = [row_block, ((rows, width), F32), (whole, LOW)] + [(of_heads, LOW)] * 4 + [(logs_shape, F32)]
    kept_shapes += [(whole, LOW)] + [(of_hidden, LOW)] * 3 + [attn_shape, feed_shape]
    flops = 8 * span * width * columns + 4 * span * span * columns + 6 * span * width * hidden
    placed_shape = ((2, rows, width), LOW)
    gains, square0, square1, placed0, *kept = call(
        functools.partial(forward_kernel, attn_block=own_attn, feed_block=own_feed),
        chips,
        0,
        2 * flops,
        lengths=lengths,
        args=[own_gains],
        far_args=[cosine, sine, tokens[:, 0], cotangent[:, 0], *own_attn.arrays, *own_feed.arrays],
        outs=[((4, width), F32)] + [((1, columns), F32)] * 2,
        far_outs=[placed_shape],
        drained=kept_shapes * 2 + [row_block, (whole, LOW)],
        scratch=[
            vec(2, width, dtype=F32), vec(*cosine.shape, dtype=F32), vec(*cosine.shape, dtype=F32), semaphores(10),
            *(fetch_sems(own_attn) + fetch_sems(own_feed)) * 2,
            *gather_scratch(chips, rows) * 5, semaphores(1), semaphores(2), *reduce_scratch(chips, rows, width),
        ],
        partners=Team.partners,
    )
    first, second = (dict(zip(KEPT, kept[at : at + len(KEPT)])) for at in (0, len(KEPT)))
    y, top = kept[2 * len(KEPT) :]

    def back_args(layer):
        args = [layer["x1"], gains]
        far_args = [layer[name] for name in ("gate", "up", "h2", "z", "w_feed", "k", "q", "log", "o", "m")]
        return args, far_args + [cosine, sine, layer["h"], layer["x"], layer["w_attn"]]

    share_feed, share_attn = (3 * hidden, quarter), (4 * columns, quarter)
    back_scratch = Backward.scratch(chips, rows, span, width)
    row_gain = ((1, width), F32)
    args, far_args = back_args(second)
    low_grad1, feed_gain, attn_gain, value_grad, _, attn_part, placed1, feed_share = call(
        second_back_kernel,
        chips,
        1,
        2 * flops,
        lengths=lengths,
        args=args,
        far_args=[top, *far_args, y],
        outs=[row_block, row_gain, row_gain, (of_heads, LOW)],
        far_outs=[feed_shape, attn_shape, placed_shape, (share_feed, LOW)],
        drained=[],
        scratch=[*back_scratch, *Scatter.scratch(feed_shape[0]), semaphores(1), semaphores(2), semaphores(1)],
        partners=Team.partners,
    )
    n_moves = 2 * len(Spread.moves(groups))
    small = (8, width)
    args, far_args = back_args(first)
    sums, low_grad0, _, _, _, _, placed, *grads = call(
        last_kernel,
        chips,
        2,
        2 * flops,
        lengths=lengths,
        args=[*args, low_grad1, attn_gain, feed_gain, square0, square1],
        far_args=[*far_args, value_grad, attn_part, feed_share, low_grad1],
        outs=[(small, F32), row_block, row_gain, row_gain],
        far_outs=[feed_shape, attn_shape, placed_shape]
        + [((n, width), LOW) for n in (2 * hidden, hidden, 3 * columns, columns)],
        drained=[],
        scratch=[
            *back_scratch,
            vec(*share_feed), vec(2, *share_feed), vec(*share_feed), vec(2, *share_attn), vec(*share_attn), semaphores(1),
            *Scatter.scratch(attn_shape[0]), *Scatter.scratch(feed_shape[0]), *Scatter.scratch(attn_shape[0]),
            *(semaphores(n) for n in (1, 2) * 6),
            *(semaphores(n) for n in (n_moves, n_moves, 2) * 2),
            *(vec(*lead, *small, dtype=F32) for lead in ((), (), (groups,), (members,))),
            *(semaphores(n) for n in (1, 1, groups - 1, groups - 1, members - 1, members - 1)),
        ],
        partners=Team.all_partners,
    )
    layer_out, input_grads, gain_one, gain_two, norm, *grads = finish(
        sums, [second["x"], y, placed0, placed1], [low_grad0, low_grad1, placed], grads, members
    )
    pair_sum, lower_sum, projection_sum, output_sum = grads
    return (
        layer_out[None, :, None],
        input_grads[None, :, None],
        gain_one,
        projection_sum.reshape(w_qkv.shape),
        output_sum[None],
        gain_two,
        pair_sum.reshape(w_gate_up.shape),
        lower_sum[None],
        norm.reshape(1),
    )


def solution(mesh):
    return jax.shard_map(
        local,
        mesh=mesh,
        in_specs=(
            P(None, "dp", "mp", None),
            P(None, "dp", "mp", None),
            P(None, "dp"),
            P("section", None),
            P("section", None, "mp", None),
            P("section", "mp", None),
            P("section", None),
            P("section", None, "mp", None),
            P("section", "mp", None),
        ),
        out_specs=(
            P("section", None, "dp", "mp", None),
            P("section", None, "dp", "mp", None),
            P("section", None),
            P("section", None, "mp", None),
            P("section", "mp", None),
            P("section", None),
            P("section", None, "mp", None),
            P("section", "mp", None),
            P("section"),
        ),
        check_vma=False,
    )
```

```python
import functools

import jax
import jax.numpy as jnp
from jax import lax
from jax.experimental import pallas as pl
from jax.experimental.pallas import tpu as pltpu
from jax.sharding import PartitionSpec as P

HD = 64
EPSILON = 1e-05
ROPE_BASE = 10000.0
NEG_LARGE = -1e30
MESH = pl.DeviceIdType.MESH
F32 = jnp.float32
LOW = jnp.bfloat16
VMEM_BYTES = 56 << 20
WAITING = 12


def mm(a, b):
    return lax.dot_general(a, b, (((1,), (0,)), ((), ())), preferred_element_type=F32)


def mm_nt(a, b):
    return lax.dot_general(a, b, (((1,), (1,)), ((), ())), preferred_element_type=F32)


def mm_tn(a, b):
    return lax.dot_general(a, b, (((0,), (0,)), ((), ())), preferred_element_type=F32)


def no(flag):
    return jnp.logical_not(flag)


class Team:
    def __init__(self, chips):
        self.chips = chips
        self.groups = lax.axis_size("dp")
        self.core = lax.axis_index("section")
        self.group = lax.axis_index("dp")
        self.along = lax.axis_index("mp")
        self.half = self.along // chips
        self.seat = self.along % chips
        self.home = self.core == self.half
        self.away = jnp.logical_not(self.home)

    def chip(self, offset):
        return (self.seat + offset) % self.chips

    def sibling(self):
        return (1 - self.core, self.group, self.along)

    def peer(self, offset):
        return (self.core, self.group, self.half * self.chips + self.chip(offset))

    def mine(self, offset):
        return self.chip(offset) + self.core * self.chips

    def other(self, offset):
        return self.chip(offset) + (1 - self.core) * self.chips

    def dp(self, offset):
        return (self.core, (self.group + offset) % self.groups, self.along)

    def far(self, core):
        return (core, self.group, (self.along + self.chips) % (2 * self.chips))

    def member(self, offset):
        return (self.core, self.group, (self.along + offset) % (2 * self.chips))

    def partners(self):
        return (
            [self.sibling(), self.far(0), self.far(1)]
            + [self.peer(o) for o in range(1, self.chips)]
            + [self.dp(o) for o in range(1, self.groups)]
        )

    def all_partners(self):
        return (
            [self.sibling(), self.far(1 - self.core)]
            + [self.member(o) for o in range(1, 2 * self.chips)]
            + [self.dp(o) for o in range(1, self.groups)]
        )

    def enter(self, partners):
        barrier = pltpu.get_barrier_semaphore()
        for device in partners:
            pl.semaphore_signal(barrier, inc=1, device_id=device, device_id_type=MESH)
        pl.semaphore_wait(barrier, len(partners))


def remote(src, dst, send, recv, device):
    return pltpu.make_async_remote_copy(
        src_ref=src, dst_ref=dst, send_sem=send, recv_sem=recv, device_id=device, device_id_type=MESH
    )


class Local:
    def __init__(self, src, dst, sem):
        self.copy = pltpu.make_async_copy(src, dst, sem)
        self.start, self.wait = self.copy.start, self.copy.wait


def block(rank, rows):
    return pl.ds(pl.multiple_of(rank * rows, rows), rows)


def columns_at(ref, index, size):
    return ref.at[:, pl.ds(pl.multiple_of(index * size, size), size)]


def lines(ref, start, rows):
    return ref.at[pl.ds(start, rows)]


def subs_of(rows):
    return max(1, rows // 64)


class Gather:
    def __init__(self, team, buf, rows, send, recv, source=None):
        self.team, self.buf, self.rows, self.send, self.recv = team, buf, rows, send, recv
        self.source = source
        self.subs = subs_of(rows)
        self.size = rows // self.subs
        self.count = (team.chips - 1) * self.subs
        self.met = False

    def meet(self):
        if not self.met:
            self.near(self.team.other(0)).wait_recv()
            self.met = True

    def run(self, rank, s):
        return pl.ds(pl.multiple_of(rank * self.rows + s * self.size, self.size), self.size)

    def _copy(self, part, slot, device, src=None):
        part = self.buf.at[part]
        return remote(part if src is None else src, part, self.send.at[slot], self.recv.at[slot], device)

    def near(self, rank, leaving=False):
        src = self.source if leaving else None
        return self._copy(block(rank, self.rows), 2 * self.count, self.team.sibling(), src)

    def direct(self, o, s):
        src = None if self.source is None else self.source.at[self.run(0, s)]
        return self._copy(self.run(self.team.mine(0), s), (o - 1) * self.subs + s, self.team.peer(o), src)

    def incoming(self, o, s):
        back = self.team.chips - o
        return self._copy(self.run(self.team.mine(back), s), (o - 1) * self.subs + s, self.team.peer(back))

    def forward(self, o, s, rank):
        slot = self.count + (o - 1) * self.subs + s
        return self._copy(self.run(rank(self.team.chips - o), s), slot, self.team.sibling())

    def start(self):
        self.near(self.team.mine(0), True).start()
        for s in range(self.subs):
            for o in range(1, self.team.chips):
                self.direct(o, s).start()

    def finish(self):
        self.near(self.team.mine(0), True).wait_send()
        for o in range(1, self.team.chips):
            for s in range(self.subs):
                self.direct(o, s).wait_send()
                self.forward(o, s, self.team.mine).wait_send()

    def pass_all(self):
        for o in range(1, self.team.chips):
            for s in range(self.subs):
                self.incoming(o, s).wait_recv()
                self.forward(o, s, self.team.mine).start()

    def receive_all(self):
        for o in range(1, self.team.chips):
            for s in range(self.subs):
                self.forward(o, s, self.team.other).wait_recv()

    def arrivals(self, work, between=lambda back, s: None, after=lambda back: None):
        team = self.team
        work([block(team.mine(0), self.rows)], 0, None)
        self.meet()
        work([block(team.other(0), self.rows)], 0, None)
        for o in range(1, team.chips):
            back = team.chips - o

            @pl.loop(0, self.subs)
            def _(s):
                self.incoming(o, s).wait_recv()
                self.forward(o, s, team.mine).start()
                between(back, s)
                self.forward(o, s, team.other).wait_recv()
                work([self.run(team.mine(back), s), self.run(team.other(back), s)], back, s)

            after(back)


def rows_at(ref, runs):
    return jnp.concatenate([ref[run] for run in runs], 0) if len(runs) > 1 else ref[runs[0]]


def put_rows(ref, runs, value):
    for i, run in enumerate(runs):
        ref[run] = value[i * run.size : (i + 1) * run.size]


class Reduce:
    def __init__(self, team, rows, scratch):
        self.team, self.rows = team, rows
        (self.out, self.held, self.into, self.leave, self.land, self.own, self.xs, self.xr, self.us, self.ur) = scratch
        self.subs = subs_of(rows)
        self.size = rows // self.subs

    def run(self, s):
        return pl.ds(0, self.rows) if s is None else pl.ds(pl.multiple_of(s * self.size, self.size), self.size)

    def slot(self, o, s):
        return o * self.subs + (0 if s is None else s)

    def cross(self, o, s):
        run, slot = self.run(s), self.slot(o, s)
        return remote(
            self.out.at[o, run], self.into.at[o, run], self.xs.at[slot], self.xr.at[slot], self.team.sibling()
        )

    def leaving(self, o, s):
        run, slot = self.run(s), self.slot(o - 1, s)
        return remote(
            self.leave.at[o - 1, run], self.land.at[o - 1, run], self.us.at[slot], self.ur.at[slot], self.team.peer(o)
        )

    def put_other(self, o, s, value):
        self.out[o, self.run(s)] = value.astype(LOW)
        self.cross(o, s).start()

    def hold(self, o, s, value):
        self.held[o - 1, self.run(s)] = value

    def keep(self, value):
        self.own[...] = value

    def pass_on(self, o, s):
        run = self.run(s)
        self.cross(o, s).wait_recv()
        self.leave[o - 1, run] = (self.held[o - 1, run] + self.into[o, run].astype(F32)).astype(LOW)
        self.leaving(o, s).start()

    def finish(self, fine):
        self.cross(0, None).wait()
        for o in range(1, self.team.chips):
            for s in range(self.subs) if fine else [None]:
                self.cross(o, s).wait_send()
                self.leaving(o, s).wait()

    def total(self, rows):
        total = self.own[rows] + self.into[0, rows].astype(F32)
        for o in range(self.team.chips - 1):
            total = total + self.land[o, rows].astype(F32)
        return total


def semaphores(n):
    return pltpu.SemaphoreType.DMA((max(n, 1),))


def gather_scratch(chips, rows):
    n = 2 * (chips - 1) * subs_of(rows) + 1
    return [semaphores(n), semaphores(n)]


def reduce_scratch(chips, rows, width):
    subs = subs_of(rows)
    return [
        pltpu.VMEM((chips, rows, width), LOW),
        pltpu.VMEM((chips - 1, rows, width), F32),
        pltpu.VMEM((chips, rows, width), LOW),
        pltpu.VMEM((chips - 1, rows, width), LOW),
        pltpu.VMEM((chips - 1, rows, width), LOW),
        pltpu.VMEM((rows, width), F32),
        semaphores(chips * subs),
        semaphores(chips * subs),
        semaphores((chips - 1) * subs),
        semaphores((chips - 1) * subs),
    ]


def by_rows(rows, body):
    step = min(32, rows)

    @pl.loop(0, rows // step)
    def _(i):
        body(pl.ds(pl.multiple_of(i * step, step), step))


def by_tiles(rows, body):
    step = next(n for n in (64, 32, 16) if rows % n == 0)

    @pl.loop(0, rows // step)
    def _(i):
        body(pl.ds(pl.multiple_of(i * step, step), step))


def swap_halves(u):
    columns, half = u.shape[1], HD // 2
    if columns % 128:
        parts = []
        for at in range(0, columns, HD):
            parts += [u[:, at + half : at + HD], u[:, at : at + half]]
        return jnp.concatenate(parts, 1)
    lane = lax.broadcasted_iota(jnp.int32, u.shape, 1)
    return jnp.where(lane % HD < half, pltpu.roll(u, columns - half, 1), pltpu.roll(u, half, 1))


def wide(table, columns):
    return jnp.concatenate([table] * (columns // table.shape[1]), 1)


def head_row(columns, head):
    lane = lax.broadcasted_iota(jnp.int32, (1, columns), 1)
    return (lane // HD == head).astype(F32).astype(LOW)


def norm_into(buf, at, rows, read, gain):
    step = min(32, rows)

    @pl.loop(0, rows // step)
    def _(i):
        values = read(pl.ds(pl.multiple_of(i * step, step), step))
        scale = lax.rsqrt(jnp.mean(values * values, -1, keepdims=True) + EPSILON)
        buf[pl.ds(pl.multiple_of(at + i * step, step), step)] = (values * scale * gain).astype(LOW)


def norm_back(rows, read_values, read_grad, gain, read_outer, write, gain_grad_ref):
    gain_grad_ref[...] = jnp.zeros_like(gain_grad_ref)

    def body(sl):
        values = read_values(sl)
        scale = lax.rsqrt(jnp.mean(values * values, -1, keepdims=True) + EPSILON)
        unit = values * scale
        grad = read_grad(sl)
        gain_grad_ref[...] += jnp.sum(grad * unit, 0, keepdims=True)
        inner = grad * gain
        write(sl, read_outer(sl) + scale * (inner - unit * jnp.mean(inner * unit, -1, keepdims=True)))

    by_rows(rows, body)


def columns_of(width):
    step = min(256, width)
    return [slice(at, at + step) for at in range(0, width, step)]


def attend(
    team, steps, layer, x_ref, gains_ref, length, cos_ref, sin_ref, before_ref, w_ref, x1_ref, square_ref,
    h_ref, q_ref, k_ref, m_ref, o_ref, log_ref, gs, gr, reduce_refs,
):
    chips, members = team.chips, 2 * team.chips
    rows, span = x1_ref.shape[0], h_ref.shape[0]
    columns = w_ref.shape[0] // 4
    heads = columns // HD
    norm_into(
        h_ref, team.mine(0) * rows, rows, lambda sl: x_ref[sl].astype(F32), gains_ref[2 * layer : 2 * layer + 1]
    )
    gather = Gather(team, h_ref, rows, gs, gr)
    gather.start()
    gather.meet()
    steps.middle(0)
    if layer == 0:
        gather.pass_all()
    steps.weights.wait()

    def project(runs, back, s):
        normed = rows_at(h_ref, runs)
        cosine, sine = wide(rows_at(cos_ref, runs), columns), wide(rows_at(sin_ref, runs), columns)
        u = mm_nt(normed, w_ref[0:columns])
        put_rows(q_ref, runs, (u * cosine + swap_halves(u) * sine).astype(LOW) * jnp.asarray(HD**-0.5, LOW))
        u = mm_nt(normed, w_ref[columns : 2 * columns])
        put_rows(k_ref, runs, (u * cosine + swap_halves(u) * sine).astype(LOW))
        v = mm_nt(normed, w_ref[2 * columns : 3 * columns]).astype(LOW)
        if before_ref is not None:
            v = (0.5 * v.astype(F32) + 0.5 * rows_at(before_ref, runs).astype(F32)).astype(LOW)
        put_rows(m_ref, runs, v)

    if layer == 0:
        gather.receive_all()
        pl.loop(0, members)(lambda rank: project([block(rank, rows)], 0, None))
    else:
        gather.arrivals(project)
    for i in range(4):
        steps.done(i)
    steps.middle(1)
    reduce = Reduce(team, rows, reduce_refs)

    def attention(qb):
        at, upto = slice(qb * rows, (qb + 1) * rows), (qb + 1) * rows

        def one_head(head, carry):
            out, logs = carry
            mask = head_row(columns, head)
            scores = mm_nt(q_ref[at] * mask, k_ref[0:upto])
            row = lax.broadcasted_iota(jnp.int32, (rows, 1), 0) + qb * rows
            column = lax.broadcasted_iota(jnp.int32, scores.shape, 1)
            scores = jnp.where(column < jnp.minimum(row + 1, length), scores, NEG_LARGE)
            peak = jnp.max(scores, -1, keepdims=True)
            weights = jnp.exp(scores - peak)
            total = jnp.sum(weights, -1, keepdims=True)
            part = mm(weights.astype(LOW), m_ref[0:upto])
            out = out + part * (mask.astype(F32) * (1.0 / total))
            lane = lax.broadcasted_iota(jnp.int32, logs.shape, 1)
            logs = jnp.where(lane == head, peak + jnp.log(total), logs)
            return out, logs

        out, logs = lax.fori_loop(
            0, heads, one_head, (jnp.zeros((rows, columns), F32), jnp.zeros((rows, 128), F32))
        )
        o_ref[at] = out.astype(LOW)
        log_ref[qb] = jnp.transpose(logs)[0 : log_ref.shape[1]]

    @pl.loop(0, members)
    def _(p):
        o = chips - 1 - p // 2
        own = p % 2 == 1
        rank = team.chip(o) + jnp.where(own, team.core, 1 - team.core) * chips
        for qb in range(members):
            pl.when(rank == qb)(functools.partial(attention, qb))
        value = mm(o_ref[block(rank, rows)], w_ref[3 * columns : 4 * columns])
        pl.when(no(own))(lambda: reduce.put_other(o, None, value))

        @pl.when(own & (o > 0))
        def _():
            reduce.hold(o, None, value)
            reduce.pass_on(o, None)

        pl.when(own & (o == 0))(lambda: reduce.keep(value))
        pl.when(p == chips)(lambda: steps.middle(2))

    steps.done(4)
    steps.done(5)
    steps.middle(3)
    live = (lax.broadcasted_iota(jnp.int32, (1, span), 1) < length).astype(F32).astype(LOW)
    square = jnp.square(m_ref[...].astype(F32))
    high = square.astype(LOW)
    square_ref[...] = mm(live, high) + mm(live, (square - high.astype(F32)).astype(LOW))
    reduce.finish(False)

    def close(sl):
        x1_ref[sl] = x_ref[sl].astype(F32) + reduce.total(sl)

    by_rows(rows, close)
    gather.finish()


def stream(team, gather, reduce, work, here=False):
    def one(runs, back, s):
        value = work(runs)
        if s is not None:
            reduce.put_other(back, s, value[gather.size :])
            reduce.hold(back, s, value[: gather.size])
        elif one.kept:
            reduce.put_other(0, None, value)
        else:
            one.kept = True
            reduce.keep(value)

    one.kept = False

    def between(back, s):
        if gather.subs > 1:
            pl.when(s > 0)(lambda: reduce.pass_on(back, s - 1))

    def after(back):
        reduce.pass_on(back, gather.subs - 1)

    if not here:
        gather.arrivals(one, between, after)
        return
    for back in range(1, team.chips):

        @pl.loop(0, gather.subs)
        def _(s):
            one([gather.run(team.mine(back), s), gather.run(team.other(back), s)], back, s)
            between(back, s)

        after(back)
    one([block(team.mine(0), gather.rows)], 0, None)
    one([block(team.other(0), gather.rows)], 0, None)


def feed(
    team, steps, layer, x1_ref, gains_ref, w_ref, y_ref, h_ref, gate_ref, up_ref, z_ref, gs, gr, reduce_refs
):
    rows = x1_ref.shape[0]
    hidden = w_ref.shape[0] // 3
    norm_into(h_ref, team.mine(0) * rows, rows, lambda sl: x1_ref[sl], gains_ref[2 * layer + 1 : 2 * layer + 2])
    gather = Gather(team, h_ref, rows, gs, gr)
    reduce = Reduce(team, rows, reduce_refs)
    gather.start()
    steps.weights.wait()

    def work(runs):
        normed = rows_at(h_ref, runs)
        gate = mm_nt(normed, w_ref[0:hidden])
        up = mm_nt(normed, w_ref[hidden : 2 * hidden])
        put_rows(gate_ref, runs, gate.astype(LOW))
        put_rows(up_ref, runs, up.astype(LOW))
        z = (gate / (1.0 + jnp.exp(-gate)) * up).astype(LOW)
        put_rows(z_ref, runs, z)
        return mm(z, w_ref[2 * hidden : 3 * hidden])

    stream(team, gather, reduce, work)
    steps.middle(0)
    for i in range(4):
        steps.done(i)
    reduce.finish(True)

    def close(sl):
        y_ref[sl] = (x1_ref[sl] + reduce.total(sl)).astype(LOW)

    by_rows(rows, close)
    gather.finish()


def feed_back(
    team, steps, layer, gathered, g_ref, x1_ref, gain_ref, gate_ref, up_ref, h_ref, z_ref, w_ref, dx1_ref, gain_grad_ref,
    w_grad_ref, grad_ref, gs, gr, reduce_refs,
):
    rows, width = x1_ref.shape
    hidden = w_ref.shape[0] // 3
    gather = Gather(team, grad_ref, rows, gs, gr)
    reduce = Reduce(team, rows, reduce_refs)
    own = block(team.mine(0), rows)
    if not gathered:
        grad_ref[own] = g_ref[...]
        gather.start()
    steps.middle(0)
    steps.weights.wait()
    steps.need(0)
    steps.need(1)

    def work(runs):
        dz = mm_nt(rows_at(grad_ref, runs), w_ref[2 * hidden : 3 * hidden])
        gate = rows_at(gate_ref, runs).astype(F32)
        sigma = 1.0 / (1.0 + jnp.exp(-gate))
        dgate = (dz * rows_at(up_ref, runs).astype(F32) * sigma * (1.0 + gate * (1.0 - sigma))).astype(LOW)
        dup = (dz * gate * sigma).astype(LOW)
        put_rows(gate_ref, runs, dgate)
        put_rows(up_ref, runs, dup)
        return mm(dgate, w_ref[0:hidden]) + mm(dup, w_ref[hidden : 2 * hidden])

    stream(team, gather, reduce, work, gathered)
    steps.middle(1)
    steps.need(2)
    steps.need(3)
    for at in columns_of(width):
        w_grad_ref[0:hidden, at] = mm_tn(gate_ref[...], h_ref[:, at]).astype(LOW)
        w_grad_ref[hidden : 2 * hidden, at] = mm_tn(up_ref[...], h_ref[:, at]).astype(LOW)
        w_grad_ref[2 * hidden : 3 * hidden, at] = mm_tn(z_ref[...], grad_ref[:, at]).astype(LOW)
    steps.done(0)
    reduce.finish(True)

    steps.need(4)

    def outer(sl):
        return grad_ref[pl.ds(pl.multiple_of(own.start + sl.start, sl.size), sl.size)].astype(F32)

    def write(sl, value):
        dx1_ref[sl] = value

    gain = gain_ref[2 * layer + 1 : 2 * layer + 2]
    norm_back(rows, lambda sl: x1_ref[sl], reduce.total, gain, outer, write, gain_grad_ref)
    if not gathered:
        gather.finish()


def pair_slot(members, kb, qb):
    return kb * members - kb * (kb - 1) // 2 + qb - kb


def attend_back(
    team, steps, layer, dx1_ref, gain_ref, length, k_ref, q_ref, log_ref, o_ref, m_ref, cos_ref, sin_ref, h_ref, x_ref,
    value_grad_ref, w_ref, low_ref, gain_grad_ref, value_sent_ref, w_grad_ref, grad_ref, scratch, gs, gr, reduce_refs,
):
    do_ref, inner_ref, kt_ref, soft_ref, dm_ref, dk_ref, dq_ref, dqkv_ref, mask_ref = scratch
    last = value_grad_ref is None
    chips, members = team.chips, 2 * team.chips
    rows, width = dx1_ref.shape
    span, columns = q_ref.shape
    heads = columns // HD
    at = team.mine(0) * rows

    def low_rows(sl):
        grad_ref[pl.ds(pl.multiple_of(at + sl.start, sl.size), sl.size)] = dx1_ref[sl].astype(LOW)

    by_rows(rows, low_rows)
    gather = Gather(team, grad_ref, rows, gs, gr)
    reduce = Reduce(team, rows, reduce_refs)
    gather.start()
    for i in range(3):
        steps.need(i)
    dq_ref[...] = jnp.zeros_like(dq_ref)

    @pl.loop(0, members)
    def _(kb):
        ks = block(kb, rows)
        kt_ref[kb] = jnp.transpose(k_ref[ks])

        @pl.loop(kb, members)
        def _(qb):
            key = lax.broadcasted_iota(jnp.int32, (rows, rows), 0) + kb * rows
            query = lax.broadcasted_iota(jnp.int32, (rows, rows), 1) + qb * rows
            mask_ref[...] = jnp.where((key <= query) & (key < length), 0.0, NEG_LARGE)
            for head in range(heads):
                q = q_ref[block(qb, rows)] * head_row(columns, head)
                scores = mm_nt(k_ref[ks], q) + mask_ref[...] - log_ref[qb, head : head + 1]
                soft_ref[pair_slot(members, kb, qb), head] = jnp.exp(scores).astype(LOW)

    steps.middle(0)
    steps.weights.wait()
    for i in range(3, 9):
        steps.need(i)

    def upstream(runs, back, s):
        put_rows(do_ref, runs, mm_nt(rows_at(grad_ref, runs), w_ref[3 * columns : 4 * columns]).astype(LOW))

    gather.arrivals(upstream)
    steps.middle(1)
    pad = inner_ref.shape[1]
    pick = (
        lax.broadcasted_iota(jnp.int32, (pad, columns), 1) // HD == lax.broadcasted_iota(jnp.int32, (pad, columns), 0)
    )
    pick = pick.astype(F32).astype(LOW)

    @pl.loop(0, members)
    def _(b):
        sl = block(b, rows)
        product = do_ref[sl].astype(F32) * o_ref[sl].astype(F32)
        high = product.astype(LOW)
        rest = (product - high.astype(F32)).astype(LOW)
        inner_ref[b] = mm_nt(pick, high) + mm_nt(pick, rest)

    def owner(b):
        return (b % chips - team.seat + chips) % chips, b // chips == team.core

    def settle(b):
        o, own = owner(b)
        pl.when(own & (o > 0))(lambda: reduce.pass_on(o, None))

    @pl.loop(0, members)
    def _(kb):
        ks = block(kb, rows)
        dm_ref[...] = jnp.zeros_like(dm_ref)
        dk_ref[...] = jnp.zeros_like(dk_ref)

        @pl.loop(kb, members)
        def _(qb):
            qs = block(qb, rows)
            for head in range(heads):
                mask = head_row(columns, head)
                q, do = q_ref[qs] * mask, do_ref[qs] * mask
                soft = soft_ref[pair_slot(members, kb, qb), head]
                dsoft = mm_nt(m_ref[ks], do)
                ds = (soft.astype(F32) * (dsoft - inner_ref[qb, head : head + 1])).astype(LOW)
                dm_ref[...] += mm(soft, do)
                dk_ref[...] += mm(ds, q)
                part = slice(head * HD, (head + 1) * HD)
                dq_ref[qb, part] += mm(kt_ref[kb, part], ds)

        cosine, sine = wide(cos_ref[ks], columns), wide(sin_ref[ks], columns)
        dq = jnp.transpose(dq_ref[kb]) * HD**-0.5
        dqkv_ref[0, ks] = (dq * cosine - swap_halves(dq) * sine).astype(LOW)
        dk = dk_ref[...]
        dqkv_ref[1, ks] = (dk * cosine - swap_halves(dk) * sine).astype(LOW)
        if last:
            dv = (0.5 * dm_ref[...]).astype(LOW)
            value_sent_ref[ks] = dv
        else:
            dv = (dm_ref[...] + value_grad_ref[ks].astype(F32)).astype(LOW)
        dqkv_ref[2, ks] = dv
        value = mm(dqkv_ref[0, ks], w_ref[0:columns])
        for t in (1, 2):
            value = value + mm(dqkv_ref[t, ks], w_ref[t * columns : (t + 1) * columns])
        o, own = owner(kb)
        pl.when(no(own))(lambda: reduce.put_other(o, None, value))
        pl.when(own & (o > 0))(lambda: reduce.hold(o, None, value))
        pl.when(own & (o == 0))(lambda: reduce.keep(value))
        pl.when(kb > 0)(lambda: settle(kb - 1))

    settle(members - 1)
    steps.middle(2)
    for piece in columns_of(width):
        w_grad_ref[3 * columns : 4 * columns, piece] = mm_tn(o_ref[...], grad_ref[:, piece]).astype(LOW)
        for t in range(3):
            w_grad_ref[t * columns : (t + 1) * columns, piece] = mm_tn(dqkv_ref[t], h_ref[:, piece]).astype(LOW)
    steps.done(0)
    reduce.finish(False)

    def write(sl, value):
        low_ref[sl] = value.astype(LOW)

    norm_back(
        rows,
        lambda sl: x_ref[sl].astype(F32),
        reduce.total,
        gain_ref[2 * layer : 2 * layer + 1],
        lambda sl: dx1_ref[sl],
        write,
        gain_grad_ref,
    )
    gather.finish()


class Parts:
    def __init__(self, arrays, parts):
        self.arrays, self.parts = arrays, parts
        self.lines = sum(a.shape[0] for a in arrays)
        self.width = arrays[0].shape[1]

    def own(self, refs, i):
        array, start, rows, _ = self.parts[i]
        return lines(refs[array], start, rows)

    def of_block(self, ref, i):
        _, _, rows, start = self.parts[i]
        return lines(ref, start, rows)


class Fetch:
    def __init__(self, team, layer, block, own, buf, far_send, far_recv, near_send, near_recv, here):
        self.team, self.block, self.own, self.buf, self.n = team, block, own, buf, len(block.parts)
        self.fs, self.fr, self.ns, self.nr = far_send, far_recv, near_send, near_recv
        self.size = block.width // team.groups
        holds = team.core == layer
        self.sends, self.gives, self.takes = holds, team.away & holds, team.home & no(holds)
        self.stays = team.home & holds
        self.loads, start = [], 0
        for i, ref in enumerate(own):
            self.loads.append(Local(ref, lines(buf, start, ref.shape[0]), here.at[i]))
            start += ref.shape[0]

    def far(self, i):
        team = self.team
        return remote(
            columns_at(self.block.own(self.own, i), team.group, self.size),
            columns_at(self.block.of_block(self.buf, i), team.group, self.size),
            self.fs.at[i],
            self.fr.at[i],
            team.far(team.half),
        )

    def cross(self, i):
        own, there = self.block.own(self.own, i), self.block.of_block(self.buf, i)
        return remote(own, there, self.ns.at[i], self.nr.at[i], self.team.sibling())

    def along(self, i, o, arriving=False):
        team = self.team
        group = (team.group + team.groups - o) % team.groups if arriving else team.group
        share, slot = columns_at(self.block.of_block(self.buf, i), group, self.size), o * self.n + i
        return remote(share, share, self.ns.at[slot], self.nr.at[slot], team.dp(o))

    def start_near(self):
        @pl.when(self.gives)
        def _():
            for i in range(self.n):
                self.cross(i).start()

        @pl.when(self.stays)
        def _():
            for copy in self.loads:
                copy.start()

    def start_far(self, parts=None):
        @pl.when(self.sends)
        def _():
            for i in range(self.n) if parts is None else parts:
                self.far(i).start()

    def pass_on(self, parts=None):
        @pl.when(self.team.away)
        def _():
            for i in range(self.n) if parts is None else parts:
                self.far(i).wait_recv()
                for o in range(1, self.team.groups):
                    self.along(i, o).start()

    def wait(self):
        @pl.when(self.sends)
        def _():
            for i in range(self.n):
                self.far(i).wait_send()

        @pl.when(self.gives)
        def _():
            for i in range(self.n):
                self.cross(i).wait_send()

        @pl.when(self.takes)
        def _():
            for i in range(self.n):
                self.cross(i).wait_recv()

        @pl.when(self.stays)
        def _():
            for copy in self.loads:
                copy.wait()

        @pl.when(self.team.away)
        def _():
            for i in range(self.n):
                for o in range(1, self.team.groups):
                    self.along(i, o).wait_send()
                    self.along(i, o, arriving=True).wait_recv()


class Scatter:
    @staticmethod
    def scratch(shape):
        rows, width = shape
        groups = lax.axis_size("dp")
        low, high = sides(groups)
        size, cut = width // groups, rows // 32 * 16
        rest = rows - cut
        first, second = (low - 1) * high + (high - 1) * low, high + low - 2
        return [
            *(semaphores(n) for n in (first, first, second, second, high + low)),
            pltpu.VMEM((max(low - 1, 1), high, cut, size), LOW),
            pltpu.VMEM((high, cut, size), LOW),
            pltpu.VMEM((max(high - 1, 1), cut, size), LOW),
            pltpu.VMEM((max(high - 1, 1), low, rest, size), LOW),
            pltpu.VMEM((low, rest, size), LOW),
            pltpu.VMEM((max(low - 1, 1), rest, size), LOW),
            pltpu.VMEM((rows, size), LOW),
        ]

    def __init__(self, team, part, fs, fr, ss, sr, load, *buffers):
        self.team, self.part = team, part
        self.land, self.sums, self.last = buffers[0::3][:2], buffers[1:6:3], buffers[2:6:3]
        self.share = buffers[6]
        low, high = sides(team.groups)
        at_high, at_low = team.group // low, team.group % low
        size, cut = self.share.shape[1], self.sums[0].shape[1]
        upper, lower = lines(part, 0, cut), lines(part, cut, self.share.shape[0] - cut)

        def device(b, a):
            return (team.core, (at_high + b) % high * low + (at_low + a) % low, team.along)

        self.loads = [
            Local(columns_at(upper, b * low + at_low, size), self.sums[0].at[b], load.at[b]) for b in range(high)
        ] + [
            Local(columns_at(lower, at_high * low + a, size), self.sums[1].at[a], load.at[high + a]) for a in range(low)
        ]
        self.firsts = []
        for a in range(1, low):
            for b in range(high):
                src, dst = columns_at(upper, b * low + (at_low + a) % low, size), self.land[0].at[a - 1, b]
                self.firsts.append((src, dst, device(0, a)))
        for b in range(1, high):
            for a in range(low):
                src, dst = columns_at(lower, (at_high + b) % high * low + a, size), self.land[1].at[b - 1, a]
                self.firsts.append((src, dst, device(b, 0)))
        self.firsts = [remote(s, d, fs.at[i], fr.at[i], to) for i, (s, d, to) in enumerate(self.firsts)]
        self.seconds = [
            (self.sums[0].at[(at_high + b) % high], self.last[0].at[b - 1], device(b, 0)) for b in range(1, high)
        ] + [(self.sums[1].at[(at_low + a) % low], self.last[1].at[a - 1], device(0, a)) for a in range(1, low)]
        self.seconds = [remote(s, d, ss.at[i], sr.at[i], to) for i, (s, d, to) in enumerate(self.seconds)]
        self.kept = self.sums[0].at[at_high], self.sums[1].at[at_low]
        self.cut = cut

    def start(self):
        for copy in (*self.firsts, *self.loads):
            copy.start()

    def turn(self):
        for copy in (*self.firsts, *self.loads):
            copy.wait()
        for land, sums in zip(self.land, self.sums):
            for i in range(sums.shape[0]):
                add_rows(sums.at[i], 0, sums.at[i], [land.at[n, i] for n in range(land.shape[0])])
        for copy in self.seconds:
            copy.start()

    def close(self):
        for copy in self.seconds:
            copy.wait()
        for at, kept, last in zip((0, self.cut), self.kept, self.last):
            add_rows(self.share, at, kept, [last.at[n] for n in range(last.shape[0])])


def add_rows(out, at, own, others):
    rows = own.shape[0]
    step = next(n for n in (64, 32, 16) if rows % n == 0)

    @pl.loop(0, rows // step)
    def _(i):
        sl = pl.ds(pl.multiple_of(i * step, step), step)
        total = own[sl].astype(F32)
        for other in others:
            total = total + other[sl].astype(F32)
        out[pl.ds(pl.multiple_of(at + i * step, 16), step)] = total.astype(LOW)


class Swap:
    def __init__(self, team, layer, share, land, send, recv):
        self.team, self.layer = team, layer
        self.far = remote(share, land.at[0], send.at[0], recv.at[0], team.far(layer))
        self.near = remote(share, land.at[1], send.at[0], recv.at[1], team.sibling())

    def each(self, act):
        team = self.team
        pl.when(team.away)(lambda: act(self.far))
        pl.when(team.home & (team.core != self.layer))(lambda: act(self.near))

    def start(self):
        self.each(lambda c: c.start())

    def finish(self):
        self.each(lambda c: c.wait_send())
        team = self.team
        pl.when(team.core == self.layer)(lambda: self.far.wait_recv())
        pl.when((team.core == self.layer) & team.away)(lambda: self.near.wait_recv())


def add_swapped(team, out, share, landed):
    def body(sl):
        near = jnp.where(team.home, share[sl].astype(F32), landed[1, sl].astype(F32))
        out[sl] = (near + landed[0, sl].astype(F32)).astype(LOW)

    by_tiles(out.shape[0], body)


class Spread:
    def __init__(self, team, share, fulls, send, recv, here):
        self.team, self.share, self.fulls, self.send, self.recv, self.here = team, share, fulls, send, recv, here
        self.low, self.high = sides(team.groups)

    @staticmethod
    def moves(groups):
        low, high = sides(groups)
        upper = [(True, (0, a), (0, 0)) for a in range(1, low)]
        upper += [(True, (b, 0), (0, a)) for b in range(1, high) for a in range(low)]
        lower = [(False, (b, 0), (0, 0)) for b in range(1, high)]
        lower += [(False, (0, a), (b, 0)) for a in range(1, low) for b in range(high)]
        return upper + lower

    def group(self, high, low):
        team = self.team
        return (
            (team.group // self.low + self.high - high) % self.high * self.low
            + (team.group % self.low + self.low - low) % self.low
        )

    def copies(self, first, arriving=False):
        team, size = self.team, self.share.shape[1]
        start = 0
        moves = self.moves(team.groups)
        for i, full in enumerate(self.fulls):
            rows = full.shape[0]
            cut = rows // 32 * 16
            for n, (upper, (high, low), (from_high, from_low)) in enumerate(moves):
                if ((from_high, from_low) == (0, 0)) != first:
                    continue
                at, count = (0, cut) if upper else (cut, rows - cut)
                slot = i * len(moves) + n
                back = arriving * high + from_high, arriving * low + from_low
                there = columns_at(lines(full, at, count), self.group(*back), size)
                src = lines(self.share, start + at, count) if first else there
                target = self.group(-high, -low)
                device = (team.core, target, team.along)
                yield remote(src, there, self.send.at[slot], self.recv.at[slot], device)
            start += rows

    def stays(self):
        start = 0
        for i, full in enumerate(self.fulls):
            there = columns_at(full, self.team.group, self.share.shape[1])
            yield Local(lines(self.share, start, full.shape[0]), there, self.here.at[i])
            start += full.shape[0]

    def start(self):
        for copy in (*self.copies(True), *self.stays()):
            copy.start()

    def middle(self):
        for copy in self.copies(True, arriving=True):
            copy.wait_recv()
        for copy in self.copies(False):
            copy.start()

    def finish(self):
        for copy in self.stays():
            copy.wait()
        for first in (True, False):
            for copy in self.copies(first):
                copy.wait_send()
        for copy in self.copies(False, arriving=True):
            copy.wait_recv()


def sides(groups):
    low = 2 if groups % 2 == 0 else 1
    return low, groups // low


def call(body, chips, ident, flops, lengths, args, far_args, outs, far_outs, drained, scratch, partners):
    vmem, far = pl.BlockSpec(memory_space=pltpu.VMEM), pl.BlockSpec(memory_space=pl.ANY)
    cuts = [1 + len(args) + len(far_args), len(outs) + len(far_outs), len(drained), len(drained), 1]

    def kernel(*refs):
        groups, start = [], 0
        for n in cuts:
            groups.append(refs[start : start + n])
            start += n
        ins, results, left, buffers, (drain_sem,) = groups
        team = Team(chips)
        team.enter(partners(team))
        drains = [Local(src, dst, drain_sem.at[i]) for i, (src, dst) in enumerate(zip(buffers, left))]
        body(team, lambda i: drains[i].start(), *ins, *results, *buffers, *refs[start:])
        for copy in drains:
            copy.wait()

    moved = sum(a.size * a.dtype.itemsize for a in (*args, *far_args))
    return pl.pallas_call(
        kernel,
        out_shape=[jax.ShapeDtypeStruct(shape, dtype) for shape, dtype in (*outs, *far_outs, *drained)],
        in_specs=[pl.BlockSpec(memory_space=pltpu.SMEM)] + [vmem] * len(args) + [far] * len(far_args),
        out_specs=[vmem] * len(outs) + [far] * (len(far_outs) + len(drained)),
        scratch_shapes=[*(pltpu.VMEM(shape, dtype) for shape, dtype in drained), semaphores(len(drained)), *scratch],
        cost_estimate=pl.CostEstimate(flops=WAITING * flops, bytes_accessed=moved, transcendentals=0),
        compiler_params=pltpu.CompilerParams(
            collective_id=ident, has_side_effects=True, vmem_limit_bytes=VMEM_BYTES
        ),
    )(lengths, *args, *far_args)


def rope_tables(span, columns):
    position = jnp.arange(span, dtype=F32)
    freqs = ROPE_BASE ** (-jnp.arange(0, HD, 2, dtype=F32) / HD)
    angle = position[:, None] * freqs[None, :]
    heads = columns // HD
    cosine = jnp.tile(jnp.concatenate([jnp.cos(angle), jnp.cos(angle)], -1), (1, heads))
    sine = jnp.tile(jnp.concatenate([-jnp.sin(angle), jnp.sin(angle)], -1), (1, heads))
    return cosine, sine


def everywhere_sum(team, refs):
    small_ref, sum_ref, near, groups_ref, members_ref, send, recv, gs, gr, ms, mr = refs
    copy = remote(small_ref, near, send.at[0], recv.at[0], team.sibling())
    copy.start()
    copy.wait()
    groups_ref[team.group] = small_ref[...] + near[...]

    def exchange(ref, mine, count, device, send, recv):
        for o in range(1, count):
            remote(ref.at[mine], ref.at[mine], send.at[o - 1], recv.at[o - 1], device(o)).start()
        for o in range(1, count):
            remote(ref.at[mine], ref.at[mine], send.at[o - 1], recv.at[o - 1], device(o)).wait_send()
            there = ref.at[(mine + count - o) % count]
            remote(there, there, send.at[o - 1], recv.at[o - 1], device(o)).wait_recv()
        total = ref[0]
        for i in range(1, count):
            total = total + ref[i]
        return total

    members = 2 * team.chips
    members_ref[team.along] = exchange(groups_ref, team.group, team.groups, team.dp, gs, gr)
    sum_ref[...] = exchange(members_ref, team.along, members, team.member, ms, mr)


class Steps:
    def __init__(self, weights, steps, done, loads=()):
        self.weights, self.steps, self.done, self.loads = weights, steps, done, loads

    def need(self, index):
        self.loads[index].wait()

    def middle(self, step):
        self.steps.get(step, lambda: None)()


class Waits:
    def __init__(self, *copies):
        self.copies = copies

    def wait(self):
        for copy in self.copies:
            copy.wait()


class Take:
    def __init__(self, refs):
        self.refs = list(refs)

    def __call__(self, n):
        taken = self.refs[:n]
        del self.refs[:n]
        return taken


KEPT = ("x", "x1", "h", "q", "k", "m", "o", "log", "h2", "gate", "up", "z", "w_attn", "w_feed")


def forward_kernel(team, done, *refs, attn_block, feed_block):
    take = Take(refs)
    lengths_ref, *gain_refs = take(3)
    cos_far, sin_far, tokens_ref, cotangent_ref = take(4)
    length = lengths_ref[team.half, 0]
    own_attn, own_feed = take(len(attn_block.arrays)), take(len(feed_block.arrays))
    gains_ref, *squares = take(3)
    placed = take(1)[0]
    layers = [dict(zip(KEPT, take(len(KEPT)))) for _ in range(2)]
    y_ref, top_ref = take(2)
    gain_ref, other_gain, cos_ref, sin_ref, one = take(5)
    fetches = []
    for layer in range(2):
        for block_, own, name in ((attn_block, own_attn, "w_attn"), (feed_block, own_feed, "w_feed")):
            fetches.append(Fetch(team, layer, block_, own, layers[layer][name], *take(5)))
    attn_fetch, feed_fetch, attn_fetch1, feed_fetch1 = fetches
    team_sems = [take(2) for _ in range(5)]
    swap_sems, reduce_refs = take(2), take(10)
    x_ref = layers[0]["x"]
    rows = x_ref.shape[0]
    mine = block(team.mine(0), rows)
    over = remote(tokens_ref.at[1 - team.half], x_ref, one.at[0], one.at[1], team.far(team.core))
    here = Local(tokens_ref.at[team.half], x_ref, one.at[2])
    top_over = remote(cotangent_ref.at[1 - team.half], top_ref.at[mine], one.at[3], one.at[4], team.far(team.core))
    top_here = Local(cotangent_ref.at[team.half], top_ref.at[mine], one.at[5])
    top_gather = Gather(team, top_ref, rows, *team_sems[4])
    gain_copy = remote(gain_ref, other_gain, one.at[6], one.at[7], team.sibling())
    tables = [Local(cos_far, cos_ref, one.at[8]), Local(sin_far, sin_ref, one.at[9])]
    first_swap = Swap(team, 0, layers[1]["x"], placed, *swap_sems)

    @pl.when(team.home)
    def _():
        over.start()
        here.start()
        top_here.start()

    for i, ref in enumerate(gain_refs):
        gain_ref[i : i + 1] = ref[...]
    gain_copy.start()
    attn_fetch.start_near()
    attn_fetch.start_far()
    for copy in tables:
        copy.start()
    gain_copy.wait()
    own = team.core == 0
    gains_ref[0:2] = jnp.where(own, gain_ref[...], other_gain[...])
    gains_ref[2:4] = jnp.where(own, other_gain[...], gain_ref[...])
    pl.when(team.home)(here.wait)
    pl.when(team.away)(over.wait_recv)

    def first_gather():
        pl.when(team.home)(over.wait_send)
        feed_fetch.start_near()
        feed_fetch.start_far([0])
        attn_fetch.pass_on()

    def first_projected():
        feed_fetch.start_far([1, 2])
        feed_fetch.pass_on([0])

    def first_attended():
        feed_fetch.pass_on([1, 2])
        attn_fetch1.start_near()
        attn_fetch1.start_far()
        pl.when(team.home)(top_over.start)

    def first_fed():
        attn_fetch1.pass_on()
        feed_fetch1.start_near()
        feed_fetch1.start_far()

    def second_projected():
        feed_fetch1.pass_on([0])
        pl.when(team.home)(top_here.wait)
        pl.when(team.away)(top_over.wait_recv)
        top_gather.start()
        first_swap.start()

    steps = [
        {0: first_gather, 1: first_projected, 3: first_attended, 4: first_fed},
        {
            1: second_projected,
            2: lambda: feed_fetch1.pass_on([1]),
            3: lambda: feed_fetch1.pass_on([2]),
            4: top_gather.pass_all,
        },
    ]
    names = ("h", "q", "k", "m", "o", "log"), ("h2", "gate", "up", "z")
    for layer, kept in enumerate(layers):
        base = layer * len(KEPT)

        def leave(name):
            done(base + KEPT.index(name))

        leave("x")
        waits = Waits(fetches[2 * layer], *([] if layer else tables))
        attend(
            team, Steps(waits, steps[layer], lambda i: leave(names[0][i])), layer, kept["x"], gains_ref, length, cos_ref,
            sin_ref, layers[0]["m"] if layer else None, kept["w_attn"], kept["x1"], squares[layer],
            *(kept[name] for name in names[0]), *team_sems[2 * layer], reduce_refs,
        )
        leave("w_attn")
        leave("x1")
        after = layers[1]["x"] if layer == 0 else y_ref
        feed(
            team, Steps(fetches[2 * layer + 1], {0: steps[layer][4]}, lambda i: leave(names[1][i])), layer, kept["x1"],
            gains_ref, kept["w_feed"], after, *(kept[name] for name in names[1]), *team_sems[2 * layer + 1], reduce_refs,
        )
        leave("w_feed")
    done(2 * len(KEPT))
    pl.when(team.home)(top_over.wait_send)
    top_gather.meet()
    top_gather.receive_all()
    top_gather.finish()
    done(2 * len(KEPT) + 1)
    first_swap.finish()


class Backward:
    def __init__(self, team, layer, length, gain, x1, g, far, results, shared, feed_team, attn_team):
        self.team, self.layer, self.length, self.gain, self.x1, self.g = team, layer, length, gain, x1, g
        self.gathered = layer == 1
        take = Take(far)
        self.feed_in, self.feed_full = take(4), take(1)[0]
        self.attn_in, self.attn_full = take(9), take(1)[0]
        self.low, self.feed_gain, self.attn_gain, self.values, self.feed_part, self.attn_part = results
        take = Take(shared)
        self.grad_feed, self.grad_attn, self.dx1 = take(3)
        self.reduce = take(10)
        self.load_sem, self.own_sem = take(2)
        self.feed_team, self.attn_team = feed_team, attn_team

    @staticmethod
    def scratch(chips, rows, span, width):
        return [
            pltpu.VMEM((span, width), LOW), pltpu.VMEM((span, width), LOW), pltpu.VMEM((rows, width), F32),
            *reduce_scratch(chips, rows, width), semaphores(9), semaphores(3),
        ]

    def loads(self, sources, buffers):
        copies = [Local(src, dst, self.load_sem.at[i]) for i, (src, dst) in enumerate(zip(sources, buffers))]
        for copy in copies:
            copy.start()
        return copies

    def leaves(self, src, dst, after):
        def done(index):
            copy = Local(src, dst, self.own_sem.at[1])
            copy.start()
            copy.wait()
            after()

        return done

    def weights(self, full, buf):
        copy = Local(full, buf, self.own_sem.at[0])
        copy.start()
        return copy

    def feed(self, steps, after):
        def phase(gate, up, h, z, x1, w, w_grad):
            loads = self.loads((*self.feed_in, self.x1), (gate, up, h, z, x1))
            weights = [self.weights(self.feed_full, w)]
            if self.gathered:
                weights.append(Local(self.g, self.grad_feed, self.own_sem.at[2]))
                weights[1].start()
            feed_back(
                self.team, Steps(Waits(*weights), steps, self.leaves(w_grad, self.feed_part, after), loads), self.layer,
                self.gathered, self.g, x1, self.gain, gate, up, h, z, w, self.dx1, self.feed_gain, w_grad,
                self.grad_feed, *self.feed_team, self.reduce,
            )

        like = [pltpu.VMEM(ref.shape, ref.dtype) for ref in (*self.feed_in, self.x1, *[self.feed_full] * 2)]
        pl.run_scoped(phase, *like)

    def attend(self, steps, after):
        sources = self.attn_in
        came, sent = (None, self.values) if self.gathered else (self.values, None)

        def phase(*scoped):
            take = Take(scoped)
            loaded, (w, w_grad) = take(len(sources)), take(2)
            loads = self.loads(sources, loaded)
            weights = self.weights(self.attn_full, w)
            attend_back(
                self.team, Steps(weights, steps, self.leaves(w_grad, self.attn_part, after), loads), self.layer, self.dx1,
                self.gain, self.length, *loaded, came, w, self.low, self.attn_gain, sent, w_grad, self.grad_attn,
                take.refs, *self.attn_team, self.reduce,
            )

        rows, span, columns = self.x1.shape[0], *self.attn_in[0].shape
        pl.run_scoped(
            phase,
            *(pltpu.VMEM(ref.shape, ref.dtype) for ref in sources),
            *[pltpu.VMEM(self.attn_full.shape, LOW)] * 2,
            *attend_back_scratch(rows, span, columns, self.attn_in[2].shape),
        )


def back_kernel(team, done, *refs):
    take = Take(refs)
    lengths_ref, gain_ref, *squares = take(4)
    length = lengths_ref[team.half, 0]
    x1, x0, top_ref, rows_ref = take(4)
    far1, far0 = take(15), take(15)
    sum_ref, low1, low0 = take(3)
    parts1, parts0, (placed_out, placed_grad), fulls = take(2), take(2), take(2), take(4)
    shared = take(15)
    values, *gains = take(5)
    gathers = [take(2) for _ in range(3)]
    second = Backward(
        team, 1, length, gain_ref, x1, top_ref, far1, (low1, *gains[:2], values, *parts1), shared, [None] * 2, gathers[0]
    )
    first = Backward(
        team, 0, length, gain_ref, x0, low1, far0, (low0, *gains[2:], values, *parts0), shared, gathers[1], gathers[2]
    )
    feed_land, attn_land = take(2)
    feed_scatter1, attn_scatter1, feed_scatter0, attn_scatter0 = (
        Scatter(team, part, *take(12)) for part in (*parts1, *parts0)
    )
    feed_swap1 = Swap(team, 1, feed_scatter1.share, feed_land, *take(2))
    attn_swap1 = Swap(team, 1, attn_scatter1.share, attn_land, *take(2))
    feed_swap0 = Swap(team, 0, feed_scatter0.share, feed_land, *take(2))
    attn_swap0 = Swap(team, 0, attn_scatter0.share, attn_land, *take(2))
    out_swap = Swap(team, 1, rows_ref, placed_out, *take(2))
    rows_swap1 = Swap(team, 1, low1, placed_grad, *take(2))
    rows_swap0 = Swap(team, 0, low0, placed_grad, *take(2))
    feed_sems, attn_sems = take(3), take(3)
    feed_spread0, feed_spread1 = (
        Spread(team, scatter.share, fulls[:2], *feed_sems) for scatter in (feed_scatter0, feed_scatter1)
    )
    attn_spread0, attn_spread1 = (
        Spread(team, scatter.share, fulls[2:], *attn_sems) for scatter in (attn_scatter0, attn_scatter1)
    )
    small_ref, *small = take.refs
    last = team.core == 0

    def spread(core, swap, land, spread):
        swap.finish()

        @pl.when(team.core == core)
        def _():
            add_swapped(team, spread.share, spread.share, land)
            spread.start()

    def second_done():
        feed_scatter1.close()
        feed_swap1.start()
        attn_scatter1.start()

    def first_streamed():
        attn_scatter1.close()
        attn_swap1.start()
        spread(1, feed_swap1, feed_land, feed_spread1)

    def first_fed():
        feed_scatter0.start()

    def first_gathered():
        rows_swap1.start()
        pl.when(no(last))(feed_spread1.middle)
        spread(1, attn_swap1, attn_land, attn_spread1)

    def first_paired():
        feed_scatter0.turn()
        pl.when(no(last))(attn_spread1.middle)

    def first_done():
        attn_scatter0.start()
        feed_scatter0.close()
        feed_swap0.start()

    out_swap.start()
    second.feed({}, feed_scatter1.start)
    second.attend({2: feed_scatter1.turn}, second_done)
    first.feed({0: attn_scatter1.turn, 1: first_streamed}, first_fed)
    first.attend({1: first_gathered, 2: first_paired}, first_done)
    attn_scatter0.turn()
    attn_scatter0.close()
    attn_swap0.start()
    spread(0, feed_swap0, feed_land, feed_spread0)
    small_ref[...] = jnp.zeros_like(small_ref)
    for i, part in enumerate([first.attn_gain, first.feed_gain, second.attn_gain, second.feed_gain, *squares]):
        small_ref[i : i + 1, 0 : part.shape[1]] = part[...]
    positions = lengths_ref[0, 0] + lengths_ref[1, 0]
    small_ref[6:7] = jnp.broadcast_to(positions, (1, small_ref.shape[1])).astype(F32)
    everywhere_sum(team, [small_ref, sum_ref, *small])
    rows_swap0.start()
    spread(0, attn_swap0, attn_land, attn_spread0)

    @pl.when(last)
    def _():
        feed_spread0.middle()
        attn_spread0.middle()

    out_swap.finish()
    rows_swap1.finish()
    rows_swap0.finish()

    @pl.when(last)
    def _():
        feed_spread0.finish()
        attn_spread0.finish()

    @pl.when(no(last))
    def _():
        feed_spread1.finish()
        attn_spread1.finish()


def attend_back_scratch(rows, span, columns, logs_shape):
    members = span // rows
    return [
        pltpu.VMEM(shape, dtype)
        for shape, dtype in (
            ((span, columns), LOW),
            (logs_shape, F32),
            ((members, columns, rows), LOW),
            ((members * (members + 1) // 2, columns // HD, rows, rows), LOW),
            ((rows, columns), F32),
            ((rows, columns), F32),
            ((members, columns, rows), F32),
            ((3, span, columns), LOW),
            ((rows, rows), F32),
        )
    ]


def finish(sums, outs, low_grads, grads, members):
    rows, width = outs[0].shape
    sizes = [rows] + [a.shape[0] for a in grads]
    steps = next(n for n in (4, 2, 1) if all(size % (16 * n) == 0 for size in sizes) or n == 1)
    chips = members // 2

    def kernel(sums_ref, *refs):
        take = Take(refs)
        out_refs, grad_refs, low_refs = take(4), take(3), take(len(grads))
        layer_out, input_grads, gain_one, gain_two, norm, *full = take.refs
        first = lax.axis_index("section") == 0
        half = lax.axis_index("mp") // chips
        home = lax.axis_index("section") == half

        def place(target, zero, one, placed):
            here = jnp.where(home, jnp.where(first, zero[...], one[...]), placed[1])
            target[0] = jnp.where(half == 0, here, placed[0]).astype(target.dtype)
            target[1] = jnp.where(half == 0, placed[0], here).astype(target.dtype)

        zero, one, placed0, placed1 = out_refs
        placed = [jnp.where(first, placed0[i], placed1[i]) for i in range(2)]
        place(layer_out, zero, one, placed)
        place(input_grads, *grad_refs)
        gain_one[...] = jnp.where(first, sums_ref[0:1], sums_ref[2:3])
        gain_two[...] = jnp.where(first, sums_ref[1:2], sums_ref[3:4])
        square = jnp.sum(jnp.where(first, sums_ref[4:5], sums_ref[5:6]), -1, keepdims=True)
        count = sums_ref[6:7, 0:1] / (2 * members)
        norm[...] = jnp.sqrt(square / (count * width))
        for low, result in zip(low_refs, full):
            result[...] = low[...].astype(F32)

    def cut(shape):
        if len(shape) == 3:
            return pl.BlockSpec((shape[0], shape[1] // steps, width), lambda i: (0, i, 0))
        return pl.BlockSpec((shape[0] // steps, width), lambda i: (i, 0))

    def whole(shape):
        return pl.BlockSpec(shape, lambda i: (0, 0))

    args = [*outs, *low_grads, *grads]
    results = [((2, rows, width), LOW), ((2, rows, width), F32)]
    small = [((1, width), F32), ((1, width), F32), ((1, 1), F32)]
    full = [(a.shape, F32) for a in grads]
    return pl.pallas_call(
        kernel,
        grid=(steps,),
        out_shape=[jax.ShapeDtypeStruct(shape, dtype) for shape, dtype in (*results, *small, *full)],
        in_specs=[whole(sums.shape), *(cut(a.shape) for a in args)],
        out_specs=[
            *(cut(shape) for shape, _ in results),
            *(whole(shape) for shape, _ in small),
            *(cut(shape) for shape, _ in full),
        ],
        compiler_params=pltpu.CompilerParams(vmem_limit_bytes=VMEM_BYTES),
    )(sums, *args)


def local(tokens, cotangent, lengths, gain_attn, w_qkv, w_out, gain_ffn, w_gate_up, w_down):
    cores, groups, members = lax.axis_size("section"), lax.axis_size("dp"), lax.axis_size("mp")
    micro, sequences, rows, width = tokens.shape
    assert cores == 2 and micro == 2 and sequences == 1 and members % 2 == 0 and members >= 4
    chips = members // 2
    span = rows * members
    columns, hidden = w_out.shape[1], w_down.shape[1]
    heads = columns // HD
    quarter = width // groups
    padded = -(-heads // 8) * 8

    def vec(*shape, dtype=LOW):
        return pltpu.VMEM(shape, dtype)

    whole, of_heads, of_hidden, logs_shape = (span, width), (span, columns), (span, hidden), (members, padded, rows)
    own_attn = Parts(
        [w_qkv[0].reshape(3 * columns, width), w_out[0]],
        [(0, t * columns, columns, t * columns) for t in range(3)] + [(1, 0, columns, 3 * columns)],
    )
    own_feed = Parts(
        [w_gate_up[0].reshape(2 * hidden, width), w_down[0]],
        [(0, t * hidden, hidden, t * hidden) for t in range(2)] + [(1, 0, hidden, 2 * hidden)],
    )
    cosine, sine = rope_tables(span, columns if columns % 128 else 128)

    def fetch_sems(block_):
        n = len(block_.parts)
        return [semaphores(k) for k in (n, n, groups * n, groups * n, len(block_.arrays))]

    row_block, attn_shape, feed_shape = ((rows, width), LOW), ((4 * columns, width), LOW), ((3 * hidden, width), LOW)
    kept_shapes = [row_block, ((rows, width), F32), (whole, LOW)] + [(of_heads, LOW)] * 4 + [(logs_shape, F32)]
    kept_shapes += [(whole, LOW)] + [(of_hidden, LOW)] * 3 + [attn_shape, feed_shape]
    flops = 8 * span * width * columns + 4 * span * span * columns + 6 * span * width * hidden
    placed_shape = ((2, rows, width), LOW)
    gains, square0, square1, placed0, *kept = call(
        functools.partial(forward_kernel, attn_block=own_attn, feed_block=own_feed),
        chips,
        0,
        2 * flops,
        lengths=lengths,
        args=[gain_attn, gain_ffn],
        far_args=[cosine, sine, tokens[:, 0], cotangent[:, 0], *own_attn.arrays, *own_feed.arrays],
        outs=[((4, width), F32)] + [((1, columns), F32)] * 2,
        far_outs=[placed_shape],
        drained=kept_shapes * 2 + [row_block, (whole, LOW)],
        scratch=[
            vec(2, width, dtype=F32), vec(2, width, dtype=F32), vec(*cosine.shape, dtype=F32), vec(*cosine.shape, dtype=F32), semaphores(10),
            *(fetch_sems(own_attn) + fetch_sems(own_feed)) * 2,
            *gather_scratch(chips, rows) * 5, semaphores(1), semaphores(2), *reduce_scratch(chips, rows, width),
        ],
        partners=Team.partners,
    )
    first, second = (dict(zip(KEPT, kept[at : at + len(KEPT)])) for at in (0, len(KEPT)))
    y, top = kept[2 * len(KEPT) :]

    def back_args(layer):
        far_args = [layer[name] for name in ("gate", "up", "h2", "z", "w_feed", "k", "q", "log", "o", "m")]
        return far_args + [cosine, sine, layer["h"], layer["x"], layer["w_attn"]]

    share_feed, share_attn = (3 * hidden, quarter), (4 * columns, quarter)
    n_moves = 2 * len(Spread.moves(groups))
    small = (8, width)
    sums, low_grad1, low_grad0, _, _, _, _, placed1, placed, *grads = call(
        back_kernel,
        chips,
        1,
        4 * flops,
        lengths=lengths,
        args=[gains, square0, square1],
        far_args=[second["x1"], first["x1"], top, y, *back_args(second), *back_args(first)],
        outs=[(small, F32), row_block, row_block],
        far_outs=[feed_shape, attn_shape] * 2
        + [placed_shape] * 2
        + [((n, width), LOW) for n in (2 * hidden, hidden, 3 * columns, columns)],
        drained=[],
        scratch=[
            *Backward.scratch(chips, rows, span, width),
            vec(*of_heads), *(vec(1, width, dtype=F32) for _ in range(4)), *gather_scratch(chips, rows) * 3,
            vec(2, *share_feed), vec(2, *share_attn),
            *(Scatter.scratch(feed_shape[0]) + Scatter.scratch(attn_shape[0])) * 2,
            *(semaphores(n) for n in (1, 2) * 7),
            *(semaphores(n) for n in (n_moves, n_moves, 2) * 2),
            *(vec(*lead, *small, dtype=F32) for lead in ((), (), (groups,), (members,))),
            *(semaphores(n) for n in (1, 1, groups - 1, groups - 1, members - 1, members - 1)),
        ],
        partners=Team.all_partners,
    )
    layer_out, input_grads, gain_one, gain_two, norm, *grads = finish(
        sums, [second["x"], y, placed0, placed1], [low_grad0, low_grad1, placed], grads, members
    )
    pair_sum, lower_sum, projection_sum, output_sum = grads
    return (
        layer_out[None, :, None],
        input_grads[None, :, None],
        gain_one,
        projection_sum.reshape(w_qkv.shape),
        output_sum[None],
        gain_two,
        pair_sum.reshape(w_gate_up.shape),
        lower_sum[None],
        norm.reshape(1),
    )


def solution(mesh):
    return jax.shard_map(
        local,
        mesh=mesh,
        in_specs=(
            P(None, "dp", "mp", None),
            P(None, "dp", "mp", None),
            P(None, "dp"),
            P("section", None),
            P("section", None, "mp", None),
            P("section", "mp", None),
            P("section", None),
            P("section", None, "mp", None),
            P("section", "mp", None),
        ),
        out_specs=(
            P("section", None, "dp", "mp", None),
            P("section", None, "dp", "mp", None),
            P("section", None),
            P("section", None, "mp", None),
            P("section", "mp", None),
            P("section", None),
            P("section", None, "mp", None),
            P("section", "mp", None),
            P("section"),
        ),
        check_vma=False,
    )
```

```python
import functools

import jax
import jax.numpy as jnp
from jax import lax
from jax.experimental import pallas as pl
from jax.experimental.pallas import tpu as pltpu
from jax.sharding import PartitionSpec as P

HD = 64
EPSILON = 1e-05
ROPE_BASE = 10000.0
NEG_LARGE = -1e30
MESH = pl.DeviceIdType.MESH
F32 = jnp.float32
LOW = jnp.bfloat16
VMEM_BYTES = 56 << 20
WAITING = 12


def mm(a, b):
    return lax.dot_general(a, b, (((1,), (0,)), ((), ())), preferred_element_type=F32)


def mm_nt(a, b):
    return lax.dot_general(a, b, (((1,), (1,)), ((), ())), preferred_element_type=F32)


def mm_tn(a, b):
    return lax.dot_general(a, b, (((0,), (0,)), ((), ())), preferred_element_type=F32)


def no(flag):
    return jnp.logical_not(flag)


class Team:
    def __init__(self, chips):
        self.chips = chips
        self.groups = lax.axis_size("dp")
        self.core = lax.axis_index("section")
        self.group = lax.axis_index("dp")
        self.along = lax.axis_index("mp")
        self.half = self.along // chips
        self.seat = self.along % chips
        self.home = self.core == self.half
        self.away = jnp.logical_not(self.home)

    def chip(self, offset):
        return (self.seat + offset) % self.chips

    def sibling(self):
        return (1 - self.core, self.group, self.along)

    def peer(self, offset):
        return (self.core, self.group, self.half * self.chips + self.chip(offset))

    def mine(self, offset):
        return self.chip(offset) + self.core * self.chips

    def other(self, offset):
        return self.chip(offset) + (1 - self.core) * self.chips

    def dp(self, offset):
        return (self.core, (self.group + offset) % self.groups, self.along)

    def far(self, core):
        return (core, self.group, (self.along + self.chips) % (2 * self.chips))

    def member(self, offset):
        return (self.core, self.group, (self.along + offset) % (2 * self.chips))

    def partners(self):
        return (
            [self.sibling(), self.far(0), self.far(1)]
            + [self.peer(o) for o in range(1, self.chips)]
            + [self.dp(o) for o in range(1, self.groups)]
        )

    def all_partners(self):
        return (
            [self.sibling(), self.far(1 - self.core)]
            + [self.member(o) for o in range(1, 2 * self.chips)]
            + [self.dp(o) for o in range(1, self.groups)]
        )

    def enter(self, partners):
        barrier = pltpu.get_barrier_semaphore()
        for device in partners:
            pl.semaphore_signal(barrier, inc=1, device_id=device, device_id_type=MESH)
        pl.semaphore_wait(barrier, len(partners))


def remote(src, dst, send, recv, device):
    return pltpu.make_async_remote_copy(
        src_ref=src, dst_ref=dst, send_sem=send, recv_sem=recv, device_id=device, device_id_type=MESH
    )


class Local:
    def __init__(self, src, dst, sem):
        self.copy = pltpu.make_async_copy(src, dst, sem)
        self.start, self.wait = self.copy.start, self.copy.wait


def block(rank, rows):
    return pl.ds(pl.multiple_of(rank * rows, rows), rows)


def columns_at(ref, index, size):
    return ref.at[:, pl.ds(pl.multiple_of(index * size, size), size)]


def lines(ref, start, rows):
    return ref.at[pl.ds(start, rows)]


def subs_of(rows):
    return max(1, rows // 64)


class Gather:
    def __init__(self, team, buf, rows, send, recv, source=None):
        self.team, self.buf, self.rows, self.send, self.recv = team, buf, rows, send, recv
        self.source = source
        self.subs = subs_of(rows)
        self.size = rows // self.subs
        self.count = (team.chips - 1) * self.subs
        self.met = False

    def meet(self):
        if not self.met:
            self.near(self.team.other(0)).wait_recv()
            self.met = True

    def run(self, rank, s):
        return pl.ds(pl.multiple_of(rank * self.rows + s * self.size, self.size), self.size)

    def _copy(self, part, slot, device, src=None):
        part = self.buf.at[part]
        return remote(part if src is None else src, part, self.send.at[slot], self.recv.at[slot], device)

    def near(self, rank, leaving=False):
        src = self.source if leaving else None
        return self._copy(block(rank, self.rows), 2 * self.count, self.team.sibling(), src)

    def direct(self, o, s):
        src = None if self.source is None else self.source.at[self.run(0, s)]
        return self._copy(self.run(self.team.mine(0), s), (o - 1) * self.subs + s, self.team.peer(o), src)

    def incoming(self, o, s):
        back = self.team.chips - o
        return self._copy(self.run(self.team.mine(back), s), (o - 1) * self.subs + s, self.team.peer(back))

    def forward(self, o, s, rank):
        slot = self.count + (o - 1) * self.subs + s
        return self._copy(self.run(rank(self.team.chips - o), s), slot, self.team.sibling())

    def start(self):
        self.near(self.team.mine(0), True).start()
        for s in range(self.subs):
            for o in range(1, self.team.chips):
                self.direct(o, s).start()

    def finish(self):
        self.near(self.team.mine(0), True).wait_send()
        for o in range(1, self.team.chips):
            for s in range(self.subs):
                self.direct(o, s).wait_send()
                self.forward(o, s, self.team.mine).wait_send()

    def pass_all(self):
        for o in range(1, self.team.chips):
            for s in range(self.subs):
                self.incoming(o, s).wait_recv()
                self.forward(o, s, self.team.mine).start()

    def receive_all(self):
        for o in range(1, self.team.chips):
            for s in range(self.subs):
                self.forward(o, s, self.team.other).wait_recv()

    def arrivals(self, work, between=lambda back, s: None, after=lambda back: None):
        team = self.team
        work([block(team.mine(0), self.rows)], 0, None)
        self.meet()
        work([block(team.other(0), self.rows)], 0, None)
        for o in range(1, team.chips):
            back = team.chips - o

            @pl.loop(0, self.subs)
            def _(s):
                self.incoming(o, s).wait_recv()
                self.forward(o, s, team.mine).start()
                between(back, s)
                self.forward(o, s, team.other).wait_recv()
                work([self.run(team.mine(back), s), self.run(team.other(back), s)], back, s)

            after(back)


def rows_at(ref, runs):
    return jnp.concatenate([ref[run] for run in runs], 0) if len(runs) > 1 else ref[runs[0]]


def put_rows(ref, runs, value):
    for i, run in enumerate(runs):
        ref[run] = value[i * run.size : (i + 1) * run.size]


class Reduce:
    def __init__(self, team, rows, scratch):
        self.team, self.rows = team, rows
        (self.out, self.held, self.into, self.leave, self.land, self.own, self.xs, self.xr, self.us, self.ur) = scratch
        self.subs = subs_of(rows)
        self.size = rows // self.subs

    def run(self, s):
        return pl.ds(0, self.rows) if s is None else pl.ds(pl.multiple_of(s * self.size, self.size), self.size)

    def slot(self, o, s):
        return o * self.subs + (0 if s is None else s)

    def cross(self, o, s):
        run, slot = self.run(s), self.slot(o, s)
        return remote(
            self.out.at[o, run], self.into.at[o, run], self.xs.at[slot], self.xr.at[slot], self.team.sibling()
        )

    def leaving(self, o, s):
        run, slot = self.run(s), self.slot(o - 1, s)
        return remote(
            self.leave.at[o - 1, run], self.land.at[o - 1, run], self.us.at[slot], self.ur.at[slot], self.team.peer(o)
        )

    def put_other(self, o, s, value):
        self.out[o, self.run(s)] = value.astype(LOW)
        self.cross(o, s).start()

    def hold(self, o, s, value):
        self.held[o - 1, self.run(s)] = value

    def keep(self, value):
        self.own[...] = value

    def pass_on(self, o, s):
        run = self.run(s)
        self.cross(o, s).wait_recv()
        self.leave[o - 1, run] = (self.held[o - 1, run] + self.into[o, run].astype(F32)).astype(LOW)
        self.leaving(o, s).start()

    def finish(self, fine):
        self.cross(0, None).wait()
        for o in range(1, self.team.chips):
            for s in range(self.subs) if fine else [None]:
                self.cross(o, s).wait_send()
                self.leaving(o, s).wait()

    def total(self, rows):
        total = self.own[rows] + self.into[0, rows].astype(F32)
        for o in range(self.team.chips - 1):
            total = total + self.land[o, rows].astype(F32)
        return total


def semaphores(n):
    return pltpu.SemaphoreType.DMA((max(n, 1),))


def gather_scratch(chips, rows):
    n = 2 * (chips - 1) * subs_of(rows) + 1
    return [semaphores(n), semaphores(n)]


def reduce_scratch(chips, rows, width):
    subs = subs_of(rows)
    return [
        pltpu.VMEM((chips, rows, width), LOW),
        pltpu.VMEM((chips - 1, rows, width), F32),
        pltpu.VMEM((chips, rows, width), LOW),
        pltpu.VMEM((chips - 1, rows, width), LOW),
        pltpu.VMEM((chips - 1, rows, width), LOW),
        pltpu.VMEM((rows, width), F32),
        semaphores(chips * subs),
        semaphores(chips * subs),
        semaphores((chips - 1) * subs),
        semaphores((chips - 1) * subs),
    ]


def by_rows(rows, body):
    step = min(32, rows)

    @pl.loop(0, rows // step)
    def _(i):
        body(pl.ds(pl.multiple_of(i * step, step), step))


def by_tiles(rows, body):
    step = next(n for n in (64, 32, 16) if rows % n == 0)

    @pl.loop(0, rows // step)
    def _(i):
        body(pl.ds(pl.multiple_of(i * step, step), step))


def swap_halves(u):
    columns, half = u.shape[1], HD // 2
    if columns % 128:
        parts = []
        for at in range(0, columns, HD):
            parts += [u[:, at + half : at + HD], u[:, at : at + half]]
        return jnp.concatenate(parts, 1)
    lane = lax.broadcasted_iota(jnp.int32, u.shape, 1)
    return jnp.where(lane % HD < half, pltpu.roll(u, columns - half, 1), pltpu.roll(u, half, 1))


def wide(table, columns):
    return jnp.concatenate([table] * (columns // table.shape[1]), 1)


def head_row(columns, head):
    lane = lax.broadcasted_iota(jnp.int32, (1, columns), 1)
    return (lane // HD == head).astype(F32).astype(LOW)


def norm_into(buf, at, rows, read, gain):
    step = min(32, rows)

    @pl.loop(0, rows // step)
    def _(i):
        values = read(pl.ds(pl.multiple_of(i * step, step), step))
        scale = lax.rsqrt(jnp.mean(values * values, -1, keepdims=True) + EPSILON)
        buf[pl.ds(pl.multiple_of(at + i * step, step), step)] = (values * scale * gain).astype(LOW)


def norm_back(rows, read_values, read_grad, gain, read_outer, write, gain_grad_ref):
    gain_grad_ref[...] = jnp.zeros_like(gain_grad_ref)

    def body(sl):
        values = read_values(sl)
        scale = lax.rsqrt(jnp.mean(values * values, -1, keepdims=True) + EPSILON)
        unit = values * scale
        grad = read_grad(sl)
        gain_grad_ref[...] += jnp.sum(grad * unit, 0, keepdims=True)
        inner = grad * gain
        write(sl, read_outer(sl) + scale * (inner - unit * jnp.mean(inner * unit, -1, keepdims=True)))

    by_rows(rows, body)


def columns_of(width):
    step = min(256, width)
    return [slice(at, at + step) for at in range(0, width, step)]


def attend(
    team, steps, layer, x_ref, gains_ref, length, cos_ref, sin_ref, before_ref, w_ref, x1_ref, square_ref,
    h_ref, q_ref, k_ref, m_ref, o_ref, log_ref, gs, gr, reduce_refs,
):
    chips, members = team.chips, 2 * team.chips
    rows, span = x1_ref.shape[0], h_ref.shape[0]
    columns = w_ref.shape[0] // 4
    heads = columns // HD
    norm_into(
        h_ref, team.mine(0) * rows, rows, lambda sl: x_ref[sl].astype(F32), gains_ref[2 * layer : 2 * layer + 1]
    )
    gather = Gather(team, h_ref, rows, gs, gr)
    gather.start()
    gather.meet()
    steps.middle(0)
    if layer == 0:
        gather.pass_all()
    steps.weights.wait()

    def project(runs, back, s):
        normed = rows_at(h_ref, runs)
        cosine, sine = wide(rows_at(cos_ref, runs), columns), wide(rows_at(sin_ref, runs), columns)
        u = mm_nt(normed, w_ref[0:columns])
        put_rows(q_ref, runs, (u * cosine + swap_halves(u) * sine).astype(LOW) * jnp.asarray(HD**-0.5, LOW))
        u = mm_nt(normed, w_ref[columns : 2 * columns])
        put_rows(k_ref, runs, (u * cosine + swap_halves(u) * sine).astype(LOW))
        v = mm_nt(normed, w_ref[2 * columns : 3 * columns]).astype(LOW)
        if before_ref is not None:
            v = (0.5 * v.astype(F32) + 0.5 * rows_at(before_ref, runs).astype(F32)).astype(LOW)
        put_rows(m_ref, runs, v)

    if layer == 0:
        gather.receive_all()
        pl.loop(0, members)(lambda rank: project([block(rank, rows)], 0, None))
    else:
        gather.arrivals(project)
    for i in range(4):
        steps.done(i)
    steps.middle(1)
    reduce = Reduce(team, rows, reduce_refs)

    def attention(qb):
        at, upto = slice(qb * rows, (qb + 1) * rows), (qb + 1) * rows

        def one_head(head, carry):
            out, logs = carry
            mask = head_row(columns, head)
            scores = mm_nt(q_ref[at] * mask, k_ref[0:upto])
            row = lax.broadcasted_iota(jnp.int32, (rows, 1), 0) + qb * rows
            column = lax.broadcasted_iota(jnp.int32, scores.shape, 1)
            scores = jnp.where(column < jnp.minimum(row + 1, length), scores, NEG_LARGE)
            peak = jnp.max(scores, -1, keepdims=True)
            weights = jnp.exp(scores - peak)
            total = jnp.sum(weights, -1, keepdims=True)
            part = mm(weights.astype(LOW), m_ref[0:upto])
            out = out + part * (mask.astype(F32) * (1.0 / total))
            lane = lax.broadcasted_iota(jnp.int32, logs.shape, 1)
            logs = jnp.where(lane == head, peak + jnp.log(total), logs)
            return out, logs

        out, logs = lax.fori_loop(
            0, heads, one_head, (jnp.zeros((rows, columns), F32), jnp.zeros((rows, 128), F32))
        )
        o_ref[at] = out.astype(LOW)
        log_ref[qb] = jnp.transpose(logs)[0 : log_ref.shape[1]]

    @pl.loop(0, members)
    def _(p):
        o = chips - 1 - p // 2
        own = p % 2 == 1
        rank = team.chip(o) + jnp.where(own, team.core, 1 - team.core) * chips
        for qb in range(members):
            pl.when(rank == qb)(functools.partial(attention, qb))
        value = mm(o_ref[block(rank, rows)], w_ref[3 * columns : 4 * columns])
        pl.when(no(own))(lambda: reduce.put_other(o, None, value))

        @pl.when(own & (o > 0))
        def _():
            reduce.hold(o, None, value)
            reduce.pass_on(o, None)

        pl.when(own & (o == 0))(lambda: reduce.keep(value))
        pl.when(p == chips)(lambda: steps.middle(2))

    steps.done(4)
    steps.done(5)
    steps.middle(3)
    live = (lax.broadcasted_iota(jnp.int32, (1, span), 1) < length).astype(F32).astype(LOW)
    square = jnp.square(m_ref[...].astype(F32))
    high = square.astype(LOW)
    square_ref[...] = mm(live, high) + mm(live, (square - high.astype(F32)).astype(LOW))
    reduce.finish(False)

    def close(sl):
        x1_ref[sl] = x_ref[sl].astype(F32) + reduce.total(sl)

    by_rows(rows, close)
    gather.finish()


def stream(team, gather, reduce, work, here=False):
    def one(runs, back, s):
        value = work(runs)
        if s is not None:
            reduce.put_other(back, s, value[gather.size :])
            reduce.hold(back, s, value[: gather.size])
        elif one.kept:
            reduce.put_other(0, None, value)
        else:
            one.kept = True
            reduce.keep(value)

    one.kept = False

    def between(back, s):
        if gather.subs > 1:
            pl.when(s > 0)(lambda: reduce.pass_on(back, s - 1))

    def after(back):
        reduce.pass_on(back, gather.subs - 1)

    if not here:
        gather.arrivals(one, between, after)
        return
    for back in range(1, team.chips):

        @pl.loop(0, gather.subs)
        def _(s):
            one([gather.run(team.mine(back), s), gather.run(team.other(back), s)], back, s)
            between(back, s)

        after(back)
    one([block(team.mine(0), gather.rows)], 0, None)
    one([block(team.other(0), gather.rows)], 0, None)


def feed(
    team, steps, layer, x1_ref, gains_ref, w_ref, y_ref, h_ref, gate_ref, up_ref, z_ref, gs, gr, reduce_refs
):
    rows = x1_ref.shape[0]
    hidden = w_ref.shape[0] // 3
    norm_into(h_ref, team.mine(0) * rows, rows, lambda sl: x1_ref[sl], gains_ref[2 * layer + 1 : 2 * layer + 2])
    gather = Gather(team, h_ref, rows, gs, gr)
    reduce = Reduce(team, rows, reduce_refs)
    gather.start()
    steps.weights.wait()

    def work(runs):
        normed = rows_at(h_ref, runs)
        gate = mm_nt(normed, w_ref[0:hidden])
        up = mm_nt(normed, w_ref[hidden : 2 * hidden])
        put_rows(gate_ref, runs, gate.astype(LOW))
        put_rows(up_ref, runs, up.astype(LOW))
        z = (gate / (1.0 + jnp.exp(-gate)) * up).astype(LOW)
        put_rows(z_ref, runs, z)
        return mm(z, w_ref[2 * hidden : 3 * hidden])

    stream(team, gather, reduce, work)
    steps.middle(0)
    for i in range(4):
        steps.done(i)
    reduce.finish(True)

    def close(sl):
        y_ref[sl] = (x1_ref[sl] + reduce.total(sl)).astype(LOW)

    by_rows(rows, close)
    gather.finish()


def feed_back(
    team, steps, layer, gathered, g_ref, x1_ref, gain_ref, gate_ref, up_ref, h_ref, z_ref, w_ref, dx1_ref, gain_grad_ref,
    w_grad_ref, grad_ref, gs, gr, reduce_refs,
):
    rows, width = x1_ref.shape
    hidden = w_ref.shape[0] // 3
    gather = Gather(team, grad_ref, rows, gs, gr)
    reduce = Reduce(team, rows, reduce_refs)
    own = block(team.mine(0), rows)
    if not gathered:
        grad_ref[own] = g_ref[...]
        gather.start()
    steps.middle(0)
    steps.weights.wait()
    steps.need(0)
    steps.need(1)

    def work(runs):
        dz = mm_nt(rows_at(grad_ref, runs), w_ref[2 * hidden : 3 * hidden])
        gate = rows_at(gate_ref, runs).astype(F32)
        sigma = 1.0 / (1.0 + jnp.exp(-gate))
        dgate = (dz * rows_at(up_ref, runs).astype(F32) * sigma * (1.0 + gate * (1.0 - sigma))).astype(LOW)
        dup = (dz * gate * sigma).astype(LOW)
        put_rows(gate_ref, runs, dgate)
        put_rows(up_ref, runs, dup)
        return mm(dgate, w_ref[0:hidden]) + mm(dup, w_ref[hidden : 2 * hidden])

    stream(team, gather, reduce, work, gathered)
    steps.middle(1)
    steps.need(2)
    steps.need(3)
    for at in columns_of(width):
        w_grad_ref[0:hidden, at] = mm_tn(gate_ref[...], h_ref[:, at]).astype(LOW)
        w_grad_ref[hidden : 2 * hidden, at] = mm_tn(up_ref[...], h_ref[:, at]).astype(LOW)
        w_grad_ref[2 * hidden : 3 * hidden, at] = mm_tn(z_ref[...], grad_ref[:, at]).astype(LOW)
    steps.done(0)
    reduce.finish(True)

    steps.need(4)

    def outer(sl):
        return grad_ref[pl.ds(pl.multiple_of(own.start + sl.start, sl.size), sl.size)].astype(F32)

    def write(sl, value):
        dx1_ref[sl] = value

    gain = gain_ref[2 * layer + 1 : 2 * layer + 2]
    norm_back(rows, lambda sl: x1_ref[sl], reduce.total, gain, outer, write, gain_grad_ref)
    if not gathered:
        gather.finish()


def pair_slot(members, kb, qb):
    return kb * members - kb * (kb - 1) // 2 + qb - kb


def attend_back(
    team, steps, layer, dx1_ref, gain_ref, length, k_ref, q_ref, log_ref, o_ref, m_ref, cos_ref, sin_ref, h_ref, x_ref,
    value_grad_ref, w_ref, low_ref, gain_grad_ref, value_sent_ref, w_grad_ref, grad_ref, scratch, gs, gr, reduce_refs,
):
    do_ref, inner_ref, kt_ref, soft_ref, dm_ref, dk_ref, dq_ref, dqkv_ref, mask_ref = scratch
    last = value_grad_ref is None
    chips, members = team.chips, 2 * team.chips
    rows, width = dx1_ref.shape
    span, columns = q_ref.shape
    heads = columns // HD
    at = team.mine(0) * rows

    def low_rows(sl):
        grad_ref[pl.ds(pl.multiple_of(at + sl.start, sl.size), sl.size)] = dx1_ref[sl].astype(LOW)

    by_rows(rows, low_rows)
    gather = Gather(team, grad_ref, rows, gs, gr)
    reduce = Reduce(team, rows, reduce_refs)
    gather.start()
    for i in range(3):
        steps.need(i)
    dq_ref[...] = jnp.zeros_like(dq_ref)

    @pl.loop(0, members)
    def _(kb):
        ks = block(kb, rows)
        kt_ref[kb] = jnp.transpose(k_ref[ks])

        @pl.loop(kb, members)
        def _(qb):
            key = lax.broadcasted_iota(jnp.int32, (rows, rows), 0) + kb * rows
            query = lax.broadcasted_iota(jnp.int32, (rows, rows), 1) + qb * rows
            mask_ref[...] = jnp.where((key <= query) & (key < length), 0.0, NEG_LARGE)
            for head in range(heads):
                q = q_ref[block(qb, rows)] * head_row(columns, head)
                scores = mm_nt(k_ref[ks], q) + mask_ref[...] - log_ref[qb, head : head + 1]
                soft_ref[pair_slot(members, kb, qb), head] = jnp.exp(scores).astype(LOW)

    steps.middle(0)
    steps.weights.wait()
    for i in range(3, 9):
        steps.need(i)

    def upstream(runs, back, s):
        put_rows(do_ref, runs, mm_nt(rows_at(grad_ref, runs), w_ref[3 * columns : 4 * columns]).astype(LOW))

    gather.arrivals(upstream)
    steps.middle(1)
    pad = inner_ref.shape[1]
    pick = (
        lax.broadcasted_iota(jnp.int32, (pad, columns), 1) // HD == lax.broadcasted_iota(jnp.int32, (pad, columns), 0)
    )
    pick = pick.astype(F32).astype(LOW)

    @pl.loop(0, members)
    def _(b):
        sl = block(b, rows)
        product = do_ref[sl].astype(F32) * o_ref[sl].astype(F32)
        high = product.astype(LOW)
        rest = (product - high.astype(F32)).astype(LOW)
        inner_ref[b] = mm_nt(pick, high) + mm_nt(pick, rest)

    def owner(b):
        return (b % chips - team.seat + chips) % chips, b // chips == team.core

    def settle(b):
        o, own = owner(b)
        pl.when(own & (o > 0))(lambda: reduce.pass_on(o, None))

    @pl.loop(0, members)
    def _(kb):
        ks = block(kb, rows)
        dm_ref[...] = jnp.zeros_like(dm_ref)
        dk_ref[...] = jnp.zeros_like(dk_ref)

        @pl.loop(kb, members)
        def _(qb):
            qs = block(qb, rows)
            for head in range(heads):
                mask = head_row(columns, head)
                q, do = q_ref[qs] * mask, do_ref[qs] * mask
                soft = soft_ref[pair_slot(members, kb, qb), head]
                dsoft = mm_nt(m_ref[ks], do)
                ds = (soft.astype(F32) * (dsoft - inner_ref[qb, head : head + 1])).astype(LOW)
                dm_ref[...] += mm(soft, do)
                dk_ref[...] += mm(ds, q)
                part = slice(head * HD, (head + 1) * HD)
                dq_ref[qb, part] += mm(kt_ref[kb, part], ds)

        cosine, sine = wide(cos_ref[ks], columns), wide(sin_ref[ks], columns)
        dq = jnp.transpose(dq_ref[kb]) * HD**-0.5
        dqkv_ref[0, ks] = (dq * cosine - swap_halves(dq) * sine).astype(LOW)
        dk = dk_ref[...]
        dqkv_ref[1, ks] = (dk * cosine - swap_halves(dk) * sine).astype(LOW)
        if last:
            dv = (0.5 * dm_ref[...]).astype(LOW)
            value_sent_ref[ks] = dv
        else:
            dv = (dm_ref[...] + value_grad_ref[ks].astype(F32)).astype(LOW)
        dqkv_ref[2, ks] = dv
        value = mm(dqkv_ref[0, ks], w_ref[0:columns])
        for t in (1, 2):
            value = value + mm(dqkv_ref[t, ks], w_ref[t * columns : (t + 1) * columns])
        o, own = owner(kb)
        pl.when(no(own))(lambda: reduce.put_other(o, None, value))
        pl.when(own & (o > 0))(lambda: reduce.hold(o, None, value))
        pl.when(own & (o == 0))(lambda: reduce.keep(value))
        pl.when(kb > 0)(lambda: settle(kb - 1))

    settle(members - 1)
    steps.middle(2)
    for piece in columns_of(width):
        w_grad_ref[3 * columns : 4 * columns, piece] = mm_tn(o_ref[...], grad_ref[:, piece]).astype(LOW)
        for t in range(3):
            w_grad_ref[t * columns : (t + 1) * columns, piece] = mm_tn(dqkv_ref[t], h_ref[:, piece]).astype(LOW)
    steps.done(0)
    reduce.finish(False)

    def write(sl, value):
        low_ref[sl] = value.astype(LOW)

    norm_back(
        rows,
        lambda sl: x_ref[sl].astype(F32),
        reduce.total,
        gain_ref[2 * layer : 2 * layer + 1],
        lambda sl: dx1_ref[sl],
        write,
        gain_grad_ref,
    )
    gather.finish()


class Parts:
    def __init__(self, arrays, parts):
        self.arrays, self.parts = arrays, parts
        self.lines = sum(a.shape[0] for a in arrays)
        self.width = arrays[0].shape[1]

    def own(self, refs, i):
        array, start, rows, _ = self.parts[i]
        return lines(refs[array], start, rows)

    def of_block(self, ref, i):
        _, _, rows, start = self.parts[i]
        return lines(ref, start, rows)


class Fetch:
    def __init__(self, team, layer, block, own, buf, far_send, far_recv, near_send, near_recv, here):
        self.team, self.block, self.own, self.buf, self.n = team, block, own, buf, len(block.parts)
        self.fs, self.fr, self.ns, self.nr = far_send, far_recv, near_send, near_recv
        self.size = block.width // team.groups
        holds = team.core == layer
        self.sends, self.gives, self.takes = holds, team.away & holds, team.home & no(holds)
        self.stays = team.home & holds
        self.loads, start = [], 0
        for i, ref in enumerate(own):
            self.loads.append(Local(ref, lines(buf, start, ref.shape[0]), here.at[i]))
            start += ref.shape[0]

    def far(self, i):
        team = self.team
        return remote(
            columns_at(self.block.own(self.own, i), team.group, self.size),
            columns_at(self.block.of_block(self.buf, i), team.group, self.size),
            self.fs.at[i],
            self.fr.at[i],
            team.far(team.half),
        )

    def cross(self, i):
        own, there = self.block.own(self.own, i), self.block.of_block(self.buf, i)
        return remote(own, there, self.ns.at[i], self.nr.at[i], self.team.sibling())

    def along(self, i, o, arriving=False):
        team = self.team
        group = (team.group + team.groups - o) % team.groups if arriving else team.group
        share, slot = columns_at(self.block.of_block(self.buf, i), group, self.size), o * self.n + i
        return remote(share, share, self.ns.at[slot], self.nr.at[slot], team.dp(o))

    def start_near(self):
        @pl.when(self.gives)
        def _():
            for i in range(self.n):
                self.cross(i).start()

        @pl.when(self.stays)
        def _():
            for copy in self.loads:
                copy.start()

    def start_far(self, parts=None):
        @pl.when(self.sends)
        def _():
            for i in range(self.n) if parts is None else parts:
                self.far(i).start()

    def pass_on(self, parts=None):
        @pl.when(self.team.away)
        def _():
            for i in range(self.n) if parts is None else parts:
                self.far(i).wait_recv()
                for o in range(1, self.team.groups):
                    self.along(i, o).start()

    def wait(self):
        @pl.when(self.sends)
        def _():
            for i in range(self.n):
                self.far(i).wait_send()

        @pl.when(self.gives)
        def _():
            for i in range(self.n):
                self.cross(i).wait_send()

        @pl.when(self.takes)
        def _():
            for i in range(self.n):
                self.cross(i).wait_recv()

        @pl.when(self.stays)
        def _():
            for copy in self.loads:
                copy.wait()

        @pl.when(self.team.away)
        def _():
            for i in range(self.n):
                for o in range(1, self.team.groups):
                    self.along(i, o).wait_send()
                    self.along(i, o, arriving=True).wait_recv()


class Scatter:
    @staticmethod
    def scratch(shape):
        rows, width = shape
        groups = lax.axis_size("dp")
        low, high = sides(groups)
        size, cut = width // groups, rows // 32 * 16
        rest = rows - cut
        first, second = (low - 1) * high + (high - 1) * low, high + low - 2
        return [
            *(semaphores(n) for n in (first, first, second, second, high + low)),
            pltpu.VMEM((max(low - 1, 1), high, cut, size), LOW),
            pltpu.VMEM((high, cut, size), LOW),
            pltpu.VMEM((max(high - 1, 1), cut, size), LOW),
            pltpu.VMEM((max(high - 1, 1), low, rest, size), LOW),
            pltpu.VMEM((low, rest, size), LOW),
            pltpu.VMEM((max(low - 1, 1), rest, size), LOW),
            pltpu.VMEM((rows, size), LOW),
        ]

    def __init__(self, team, part, fs, fr, ss, sr, load, *buffers):
        self.team, self.part = team, part
        self.land, self.sums, self.last = buffers[0::3][:2], buffers[1:6:3], buffers[2:6:3]
        self.share = buffers[6]
        low, high = sides(team.groups)
        at_high, at_low = team.group // low, team.group % low
        size, cut = self.share.shape[1], self.sums[0].shape[1]
        upper, lower = lines(part, 0, cut), lines(part, cut, self.share.shape[0] - cut)

        def device(b, a):
            return (team.core, (at_high + b) % high * low + (at_low + a) % low, team.along)

        self.loads = [
            Local(columns_at(upper, b * low + at_low, size), self.sums[0].at[b], load.at[b]) for b in range(high)
        ] + [
            Local(columns_at(lower, at_high * low + a, size), self.sums[1].at[a], load.at[high + a]) for a in range(low)
        ]
        self.firsts = []
        for a in range(1, low):
            for b in range(high):
                src, dst = columns_at(upper, b * low + (at_low + a) % low, size), self.land[0].at[a - 1, b]
                self.firsts.append((src, dst, device(0, a)))
        for b in range(1, high):
            for a in range(low):
                src, dst = columns_at(lower, (at_high + b) % high * low + a, size), self.land[1].at[b - 1, a]
                self.firsts.append((src, dst, device(b, 0)))
        self.firsts = [remote(s, d, fs.at[i], fr.at[i], to) for i, (s, d, to) in enumerate(self.firsts)]
        self.seconds = [
            (self.sums[0].at[(at_high + b) % high], self.last[0].at[b - 1], device(b, 0)) for b in range(1, high)
        ] + [(self.sums[1].at[(at_low + a) % low], self.last[1].at[a - 1], device(0, a)) for a in range(1, low)]
        self.seconds = [remote(s, d, ss.at[i], sr.at[i], to) for i, (s, d, to) in enumerate(self.seconds)]
        self.kept = self.sums[0].at[at_high], self.sums[1].at[at_low]
        self.cut = cut

    def start(self):
        for copy in (*self.firsts, *self.loads):
            copy.start()

    def turn(self):
        for copy in (*self.firsts, *self.loads):
            copy.wait()
        for land, sums in zip(self.land, self.sums):
            for i in range(sums.shape[0]):
                add_rows(sums.at[i], 0, sums.at[i], [land.at[n, i] for n in range(land.shape[0])])
        for copy in self.seconds:
            copy.start()

    def close(self):
        for copy in self.seconds:
            copy.wait()
        for at, kept, last in zip((0, self.cut), self.kept, self.last):
            add_rows(self.share, at, kept, [last.at[n] for n in range(last.shape[0])])


def add_rows(out, at, own, others):
    rows = own.shape[0]
    step = next(n for n in (64, 32, 16) if rows % n == 0)

    @pl.loop(0, rows // step)
    def _(i):
        sl = pl.ds(pl.multiple_of(i * step, step), step)
        total = own[sl].astype(F32)
        for other in others:
            total = total + other[sl].astype(F32)
        out[pl.ds(pl.multiple_of(at + i * step, 16), step)] = total.astype(LOW)


class Swap:
    def __init__(self, team, layer, share, land, send, recv):
        self.team, self.layer = team, layer
        self.far = remote(share, land.at[0], send.at[0], recv.at[0], team.far(layer))
        self.near = remote(share, land.at[1], send.at[0], recv.at[1], team.sibling())

    def each(self, act):
        team = self.team
        pl.when(team.away)(lambda: act(self.far))
        pl.when(team.home & (team.core != self.layer))(lambda: act(self.near))

    def start(self):
        self.each(lambda c: c.start())

    def finish(self):
        self.each(lambda c: c.wait_send())
        team = self.team
        pl.when(team.core == self.layer)(lambda: self.far.wait_recv())
        pl.when((team.core == self.layer) & team.away)(lambda: self.near.wait_recv())


def add_swapped(team, out, share, landed):
    def body(sl):
        near = jnp.where(team.home, share[sl].astype(F32), landed[1, sl].astype(F32))
        out[sl] = (near + landed[0, sl].astype(F32)).astype(LOW)

    by_tiles(out.shape[0], body)


class Spread:
    def __init__(self, team, share, fulls, send, recv, here):
        self.team, self.share, self.fulls, self.send, self.recv, self.here = team, share, fulls, send, recv, here
        self.low, self.high = sides(team.groups)

    @staticmethod
    def moves(groups):
        low, high = sides(groups)
        upper = [(True, (0, a), (0, 0)) for a in range(1, low)]
        upper += [(True, (b, 0), (0, a)) for b in range(1, high) for a in range(low)]
        lower = [(False, (b, 0), (0, 0)) for b in range(1, high)]
        lower += [(False, (0, a), (b, 0)) for a in range(1, low) for b in range(high)]
        return upper + lower

    def group(self, high, low):
        team = self.team
        return (
            (team.group // self.low + self.high - high) % self.high * self.low
            + (team.group % self.low + self.low - low) % self.low
        )

    def copies(self, first, arriving=False):
        team, size = self.team, self.share.shape[1]
        start = 0
        moves = self.moves(team.groups)
        for i, full in enumerate(self.fulls):
            rows = full.shape[0]
            cut = rows // 32 * 16
            for n, (upper, (high, low), (from_high, from_low)) in enumerate(moves):
                if ((from_high, from_low) == (0, 0)) != first:
                    continue
                at, count = (0, cut) if upper else (cut, rows - cut)
                slot = i * len(moves) + n
                back = arriving * high + from_high, arriving * low + from_low
                there = columns_at(lines(full, at, count), self.group(*back), size)
                src = lines(self.share, start + at, count) if first else there
                target = self.group(-high, -low)
                device = (team.core, target, team.along)
                yield remote(src, there, self.send.at[slot], self.recv.at[slot], device)
            start += rows

    def stays(self):
        start = 0
        for i, full in enumerate(self.fulls):
            there = columns_at(full, self.team.group, self.share.shape[1])
            yield Local(lines(self.share, start, full.shape[0]), there, self.here.at[i])
            start += full.shape[0]

    def start(self):
        for copy in (*self.copies(True), *self.stays()):
            copy.start()

    def middle(self):
        for copy in self.copies(True, arriving=True):
            copy.wait_recv()
        for copy in self.copies(False):
            copy.start()

    def finish(self):
        for copy in self.stays():
            copy.wait()
        for first in (True, False):
            for copy in self.copies(first):
                copy.wait_send()
        for copy in self.copies(False, arriving=True):
            copy.wait_recv()


def sides(groups):
    low = 2 if groups % 2 == 0 else 1
    return low, groups // low


def call(body, chips, ident, flops, lengths, args, far_args, outs, far_outs, drained, scratch, partners):
    vmem, far = pl.BlockSpec(memory_space=pltpu.VMEM), pl.BlockSpec(memory_space=pl.ANY)
    cuts = [1 + len(args) + len(far_args), len(outs) + len(far_outs), len(drained), len(drained), 1]

    def kernel(*refs):
        groups, start = [], 0
        for n in cuts:
            groups.append(refs[start : start + n])
            start += n
        ins, results, left, buffers, (drain_sem,) = groups
        team = Team(chips)
        team.enter(partners(team))
        drains = [Local(src, dst, drain_sem.at[i]) for i, (src, dst) in enumerate(zip(buffers, left))]
        body(team, lambda i: drains[i].start(), *ins, *results, *buffers, *refs[start:])
        for copy in drains:
            copy.wait()

    moved = sum(a.size * a.dtype.itemsize for a in (*args, *far_args))
    return pl.pallas_call(
        kernel,
        out_shape=[jax.ShapeDtypeStruct(shape, dtype) for shape, dtype in (*outs, *far_outs, *drained)],
        in_specs=[pl.BlockSpec(memory_space=pltpu.SMEM)] + [vmem] * len(args) + [far] * len(far_args),
        out_specs=[vmem] * len(outs) + [far] * (len(far_outs) + len(drained)),
        scratch_shapes=[*(pltpu.VMEM(shape, dtype) for shape, dtype in drained), semaphores(len(drained)), *scratch],
        cost_estimate=pl.CostEstimate(flops=WAITING * flops, bytes_accessed=moved, transcendentals=0),
        compiler_params=pltpu.CompilerParams(
            collective_id=ident, has_side_effects=True, vmem_limit_bytes=VMEM_BYTES
        ),
    )(lengths, *args, *far_args)


def rope_tables(span, columns):
    position = jnp.arange(span, dtype=F32)
    freqs = ROPE_BASE ** (-jnp.arange(0, HD, 2, dtype=F32) / HD)
    angle = position[:, None] * freqs[None, :]
    heads = columns // HD
    cosine = jnp.tile(jnp.concatenate([jnp.cos(angle), jnp.cos(angle)], -1), (1, heads))
    sine = jnp.tile(jnp.concatenate([-jnp.sin(angle), jnp.sin(angle)], -1), (1, heads))
    return jnp.stack([cosine, sine])


def everywhere_sum(team, refs):
    small_ref, sum_ref, near, groups_ref, members_ref, send, recv, gs, gr, ms, mr = refs
    copy = remote(small_ref, near, send.at[0], recv.at[0], team.sibling())
    copy.start()
    copy.wait()
    groups_ref[team.group] = small_ref[...] + near[...]

    def exchange(ref, mine, count, device, send, recv):
        for o in range(1, count):
            remote(ref.at[mine], ref.at[mine], send.at[o - 1], recv.at[o - 1], device(o)).start()
        for o in range(1, count):
            remote(ref.at[mine], ref.at[mine], send.at[o - 1], recv.at[o - 1], device(o)).wait_send()
            there = ref.at[(mine + count - o) % count]
            remote(there, there, send.at[o - 1], recv.at[o - 1], device(o)).wait_recv()
        total = ref[0]
        for i in range(1, count):
            total = total + ref[i]
        return total

    members = 2 * team.chips
    members_ref[team.along] = exchange(groups_ref, team.group, team.groups, team.dp, gs, gr)
    sum_ref[...] = exchange(members_ref, team.along, members, team.member, ms, mr)


class Steps:
    def __init__(self, weights, steps, done, loads=()):
        self.weights, self.steps, self.done, self.loads = weights, steps, done, loads

    def need(self, index):
        self.loads[index].wait()

    def middle(self, step):
        self.steps.get(step, lambda: None)()


class Waits:
    def __init__(self, *copies):
        self.copies = copies

    def wait(self):
        for copy in self.copies:
            copy.wait()


class Take:
    def __init__(self, refs):
        self.refs = list(refs)

    def __call__(self, n):
        taken = self.refs[:n]
        del self.refs[:n]
        return taken


KEPT = ("x", "x1", "h", "q", "k", "m", "o", "log", "h2", "gate", "up", "z", "w_attn", "w_feed")


def forward_kernel(team, done, *refs, attn_block, feed_block):
    take = Take(refs)
    lengths_ref, *gain_refs = take(3)
    table_ref, tokens_ref, cotangent_ref = take(3)
    length = lengths_ref[team.half, 0]
    own_attn, own_feed = take(len(attn_block.arrays)), take(len(feed_block.arrays))
    gains_ref, *squares = take(3)
    placed = take(1)[0]
    layers = [dict(zip(KEPT, take(len(KEPT)))) for _ in range(2)]
    y_ref, top_ref = take(2)
    gain_ref, other_gain, cos_ref, sin_ref, one = take(5)
    fetches = []
    for layer in range(2):
        for block_, own, name in ((attn_block, own_attn, "w_attn"), (feed_block, own_feed, "w_feed")):
            fetches.append(Fetch(team, layer, block_, own, layers[layer][name], *take(5)))
    attn_fetch, feed_fetch, attn_fetch1, feed_fetch1 = fetches
    team_sems = [take(2) for _ in range(5)]
    swap_sems, reduce_refs = take(2), take(10)
    x_ref = layers[0]["x"]
    rows = x_ref.shape[0]
    mine = block(team.mine(0), rows)
    over = remote(tokens_ref.at[1 - team.half], x_ref, one.at[0], one.at[1], team.far(team.core))
    here = Local(tokens_ref.at[team.half], x_ref, one.at[2])
    top_over = remote(cotangent_ref.at[1 - team.half], top_ref.at[mine], one.at[3], one.at[4], team.far(team.core))
    top_here = Local(cotangent_ref.at[team.half], top_ref.at[mine], one.at[5])
    top_gather = Gather(team, top_ref, rows, *team_sems[4])
    gain_copy = remote(gain_ref, other_gain, one.at[6], one.at[7], team.sibling())
    tables = [Local(table_ref.at[0], cos_ref, one.at[8]), Local(table_ref.at[1], sin_ref, one.at[9])]
    first_swap = Swap(team, 0, layers[1]["x"], placed, *swap_sems)

    @pl.when(team.home)
    def _():
        over.start()
        here.start()
        top_here.start()

    for i, ref in enumerate(gain_refs):
        gain_ref[i : i + 1] = ref[...]
    gain_copy.start()
    attn_fetch.start_near()
    attn_fetch.start_far()
    for copy in tables:
        copy.start()
    gain_copy.wait()
    own = team.core == 0
    gains_ref[0:2] = jnp.where(own, gain_ref[...], other_gain[...])
    gains_ref[2:4] = jnp.where(own, other_gain[...], gain_ref[...])
    pl.when(team.home)(here.wait)
    pl.when(team.away)(over.wait_recv)

    def first_gather():
        pl.when(team.home)(over.wait_send)
        feed_fetch.start_near()
        feed_fetch.start_far([0])
        attn_fetch.pass_on()

    def first_projected():
        feed_fetch.start_far([1, 2])
        feed_fetch.pass_on([0])

    def first_attended():
        feed_fetch.pass_on([1, 2])
        attn_fetch1.start_near()
        attn_fetch1.start_far()
        pl.when(team.home)(top_over.start)

    def first_fed():
        attn_fetch1.pass_on()
        feed_fetch1.start_near()
        feed_fetch1.start_far()

    def second_projected():
        feed_fetch1.pass_on([0])
        pl.when(team.home)(top_here.wait)
        pl.when(team.away)(top_over.wait_recv)
        top_gather.start()
        first_swap.start()

    steps = [
        {0: first_gather, 1: first_projected, 3: first_attended, 4: first_fed},
        {
            1: second_projected,
            2: lambda: feed_fetch1.pass_on([1]),
            3: lambda: feed_fetch1.pass_on([2]),
            4: top_gather.pass_all,
        },
    ]
    names = ("h", "q", "k", "m", "o", "log"), ("h2", "gate", "up", "z")
    for layer, kept in enumerate(layers):
        base = layer * len(KEPT)

        def leave(name):
            done(base + KEPT.index(name))

        leave("x")
        waits = Waits(fetches[2 * layer], *([] if layer else tables))
        attend(
            team, Steps(waits, steps[layer], lambda i: leave(names[0][i])), layer, kept["x"], gains_ref, length, cos_ref,
            sin_ref, layers[0]["m"] if layer else None, kept["w_attn"], kept["x1"], squares[layer],
            *(kept[name] for name in names[0]), *team_sems[2 * layer], reduce_refs,
        )
        leave("w_attn")
        leave("x1")
        after = layers[1]["x"] if layer == 0 else y_ref
        feed(
            team, Steps(fetches[2 * layer + 1], {0: steps[layer][4]}, lambda i: leave(names[1][i])), layer, kept["x1"],
            gains_ref, kept["w_feed"], after, *(kept[name] for name in names[1]), *team_sems[2 * layer + 1], reduce_refs,
        )
        leave("w_feed")
    done(2 * len(KEPT))
    pl.when(team.home)(top_over.wait_send)
    top_gather.meet()
    top_gather.receive_all()
    top_gather.finish()
    done(2 * len(KEPT) + 1)
    first_swap.finish()


class Backward:
    def __init__(self, team, layer, length, gain, x1, g, far, results, shared, feed_team, attn_team):
        self.team, self.layer, self.length, self.gain, self.x1, self.g = team, layer, length, gain, x1, g
        self.gathered = layer == 1
        take = Take(far)
        self.feed_in, self.feed_full = take(4), take(1)[0]
        self.attn_in, self.attn_full = take(9), take(1)[0]
        self.low, self.feed_gain, self.attn_gain, self.values, self.feed_part, self.attn_part = results
        take = Take(shared)
        self.grad_feed, self.grad_attn, self.dx1 = take(3)
        self.reduce = take(10)
        self.load_sem, self.own_sem = take(2)
        self.feed_team, self.attn_team = feed_team, attn_team

    @staticmethod
    def scratch(chips, rows, span, width):
        return [
            pltpu.VMEM((span, width), LOW), pltpu.VMEM((span, width), LOW), pltpu.VMEM((rows, width), F32),
            *reduce_scratch(chips, rows, width), semaphores(9), semaphores(3),
        ]

    def loads(self, sources, buffers):
        copies = [Local(src, dst, self.load_sem.at[i]) for i, (src, dst) in enumerate(zip(sources, buffers))]
        for copy in copies:
            copy.start()
        return copies

    def leaves(self, src, dst, after):
        def done(index):
            copy = Local(src, dst, self.own_sem.at[1])
            copy.start()
            copy.wait()
            after()

        return done

    def weights(self, full, buf):
        copy = Local(full, buf, self.own_sem.at[0])
        copy.start()
        return copy

    def feed(self, steps, after):
        def phase(gate, up, h, z, x1, w, w_grad):
            loads = self.loads((*self.feed_in, self.x1), (gate, up, h, z, x1))
            weights = [self.weights(self.feed_full, w)]
            if self.gathered:
                weights.append(Local(self.g, self.grad_feed, self.own_sem.at[2]))
                weights[1].start()
            feed_back(
                self.team, Steps(Waits(*weights), steps, self.leaves(w_grad, self.feed_part, after), loads), self.layer,
                self.gathered, self.g, x1, self.gain, gate, up, h, z, w, self.dx1, self.feed_gain, w_grad,
                self.grad_feed, *self.feed_team, self.reduce,
            )

        like = [pltpu.VMEM(ref.shape, ref.dtype) for ref in (*self.feed_in, self.x1, *[self.feed_full] * 2)]
        pl.run_scoped(phase, *like)

    def attend(self, steps, after):
        sources = self.attn_in
        came, sent = (None, self.values) if self.gathered else (self.values, None)

        def phase(*scoped):
            take = Take(scoped)
            loaded, (w, w_grad) = take(len(sources)), take(2)
            loads = self.loads(sources, loaded)
            weights = self.weights(self.attn_full, w)
            attend_back(
                self.team, Steps(weights, steps, self.leaves(w_grad, self.attn_part, after), loads), self.layer, self.dx1,
                self.gain, self.length, *loaded, came, w, self.low, self.attn_gain, sent, w_grad, self.grad_attn,
                take.refs, *self.attn_team, self.reduce,
            )

        rows, span, columns = self.x1.shape[0], *self.attn_in[0].shape
        pl.run_scoped(
            phase,
            *(pltpu.VMEM(ref.shape, ref.dtype) for ref in sources),
            *[pltpu.VMEM(self.attn_full.shape, LOW)] * 2,
            *attend_back_scratch(rows, span, columns, self.attn_in[2].shape),
        )


def back_kernel(team, done, *refs):
    take = Take(refs)
    lengths_ref, gain_ref, *squares = take(4)
    length = lengths_ref[team.half, 0]
    x1, x0, top_ref, rows_ref = take(4)
    far1, far0 = ([*far[:10], far[10].at[0], far[10].at[1], *far[11:]] for far in (take(14), take(14)))
    sum_ref, low1, low0 = take(3)
    parts1, parts0, (placed_out, placed_grad), fulls = take(2), take(2), take(2), take(4)
    shared = take(15)
    values, *gains = take(5)
    gathers = [take(2) for _ in range(3)]
    second = Backward(
        team, 1, length, gain_ref, x1, top_ref, far1, (low1, *gains[:2], values, *parts1), shared, [None] * 2, gathers[0]
    )
    first = Backward(
        team, 0, length, gain_ref, x0, low1, far0, (low0, *gains[2:], values, *parts0), shared, gathers[1], gathers[2]
    )
    feed_land, attn_land = take(2)
    feed_scatter1, attn_scatter1, feed_scatter0, attn_scatter0 = (
        Scatter(team, part, *take(12)) for part in (*parts1, *parts0)
    )
    feed_swap1 = Swap(team, 1, feed_scatter1.share, feed_land, *take(2))
    attn_swap1 = Swap(team, 1, attn_scatter1.share, attn_land, *take(2))
    feed_swap0 = Swap(team, 0, feed_scatter0.share, feed_land, *take(2))
    attn_swap0 = Swap(team, 0, attn_scatter0.share, attn_land, *take(2))
    out_swap = Swap(team, 1, rows_ref, placed_out, *take(2))
    rows_swap1 = Swap(team, 1, low1, placed_grad, *take(2))
    rows_swap0 = Swap(team, 0, low0, placed_grad, *take(2))
    feed_sems, attn_sems = take(3), take(3)
    feed_spread0, feed_spread1 = (
        Spread(team, scatter.share, fulls[:2], *feed_sems) for scatter in (feed_scatter0, feed_scatter1)
    )
    attn_spread0, attn_spread1 = (
        Spread(team, scatter.share, fulls[2:], *attn_sems) for scatter in (attn_scatter0, attn_scatter1)
    )
    small_ref, *small = take.refs
    last = team.core == 0

    def spread(core, swap, land, spread):
        swap.finish()

        @pl.when(team.core == core)
        def _():
            add_swapped(team, spread.share, spread.share, land)
            spread.start()

    def second_done():
        feed_scatter1.close()
        feed_swap1.start()
        attn_scatter1.start()

    def first_streamed():
        attn_scatter1.close()
        attn_swap1.start()
        spread(1, feed_swap1, feed_land, feed_spread1)

    def first_fed():
        feed_scatter0.start()

    def first_gathered():
        rows_swap1.start()
        pl.when(no(last))(feed_spread1.middle)
        spread(1, attn_swap1, attn_land, attn_spread1)

    def first_paired():
        feed_scatter0.turn()
        pl.when(no(last))(attn_spread1.middle)

    def first_done():
        attn_scatter0.start()
        feed_scatter0.close()
        feed_swap0.start()

    out_swap.start()
    second.feed({}, feed_scatter1.start)
    second.attend({2: feed_scatter1.turn}, second_done)
    first.feed({0: attn_scatter1.turn, 1: first_streamed}, first_fed)
    first.attend({1: first_gathered, 2: first_paired}, first_done)
    attn_scatter0.turn()
    attn_scatter0.close()
    attn_swap0.start()
    spread(0, feed_swap0, feed_land, feed_spread0)
    small_ref[...] = jnp.zeros_like(small_ref)
    for i, part in enumerate([first.attn_gain, first.feed_gain, second.attn_gain, second.feed_gain, *squares]):
        small_ref[i : i + 1, 0 : part.shape[1]] = part[...]
    positions = lengths_ref[0, 0] + lengths_ref[1, 0]
    small_ref[6:7] = jnp.broadcast_to(positions, (1, small_ref.shape[1])).astype(F32)
    everywhere_sum(team, [small_ref, sum_ref, *small])
    rows_swap0.start()
    spread(0, attn_swap0, attn_land, attn_spread0)

    @pl.when(last)
    def _():
        feed_spread0.middle()
        attn_spread0.middle()

    out_swap.finish()
    rows_swap1.finish()
    rows_swap0.finish()

    @pl.when(last)
    def _():
        feed_spread0.finish()
        attn_spread0.finish()

    @pl.when(no(last))
    def _():
        feed_spread1.finish()
        attn_spread1.finish()


def attend_back_scratch(rows, span, columns, logs_shape):
    members = span // rows
    return [
        pltpu.VMEM(shape, dtype)
        for shape, dtype in (
            ((span, columns), LOW),
            (logs_shape, F32),
            ((members, columns, rows), LOW),
            ((members * (members + 1) // 2, columns // HD, rows, rows), LOW),
            ((rows, columns), F32),
            ((rows, columns), F32),
            ((members, columns, rows), F32),
            ((3, span, columns), LOW),
            ((rows, rows), F32),
        )
    ]


def finish(sums, outs, low_grads, grads, members):
    rows, width = outs[0].shape
    sizes = [rows] + [a.shape[0] for a in grads]
    steps = next(n for n in (4, 2, 1) if all(size % (16 * n) == 0 for size in sizes) or n == 1)
    chips = members // 2

    def kernel(sums_ref, *refs):
        take = Take(refs)
        out_refs, grad_refs, low_refs = take(4), take(3), take(len(grads))
        layer_out, input_grads, gain_one, gain_two, norm, *full = take.refs
        first = lax.axis_index("section") == 0
        half = lax.axis_index("mp") // chips
        home = lax.axis_index("section") == half

        def place(target, zero, one, placed):
            here = jnp.where(home, jnp.where(first, zero[...], one[...]), placed[1])
            target[0] = jnp.where(half == 0, here, placed[0]).astype(target.dtype)
            target[1] = jnp.where(half == 0, placed[0], here).astype(target.dtype)

        zero, one, placed0, placed1 = out_refs
        placed = [jnp.where(first, placed0[i], placed1[i]) for i in range(2)]
        place(layer_out, zero, one, placed)
        place(input_grads, *grad_refs)
        gain_one[...] = jnp.where(first, sums_ref[0:1], sums_ref[2:3])
        gain_two[...] = jnp.where(first, sums_ref[1:2], sums_ref[3:4])
        square = jnp.sum(jnp.where(first, sums_ref[4:5], sums_ref[5:6]), -1, keepdims=True)
        count = sums_ref[6:7, 0:1] / (2 * members)
        norm[...] = jnp.sqrt(square / (count * width))
        for low, result in zip(low_refs, full):
            result[...] = low[...].astype(F32)

    def cut(shape):
        if len(shape) == 3:
            return pl.BlockSpec((shape[0], shape[1] // steps, width), lambda i: (0, i, 0))
        return pl.BlockSpec((shape[0] // steps, width), lambda i: (i, 0))

    def whole(shape):
        return pl.BlockSpec(shape, lambda i: (0, 0))

    args = [*outs, *low_grads, *grads]
    results = [((2, rows, width), LOW), ((2, rows, width), F32)]
    small = [((1, width), F32), ((1, width), F32), ((1, 1), F32)]
    full = [(a.shape, F32) for a in grads]
    return pl.pallas_call(
        kernel,
        grid=(steps,),
        out_shape=[jax.ShapeDtypeStruct(shape, dtype) for shape, dtype in (*results, *small, *full)],
        in_specs=[whole(sums.shape), *(cut(a.shape) for a in args)],
        out_specs=[
            *(cut(shape) for shape, _ in results),
            *(whole(shape) for shape, _ in small),
            *(cut(shape) for shape, _ in full),
        ],
        compiler_params=pltpu.CompilerParams(vmem_limit_bytes=VMEM_BYTES),
    )(sums, *args)


def local(tokens, cotangent, lengths, gain_attn, w_qkv, w_out, gain_ffn, w_gate_up, w_down):
    cores, groups, members = lax.axis_size("section"), lax.axis_size("dp"), lax.axis_size("mp")
    micro, sequences, rows, width = tokens.shape
    assert cores == 2 and micro == 2 and sequences == 1 and members % 2 == 0 and members >= 4
    chips = members // 2
    span = rows * members
    columns, hidden = w_out.shape[1], w_down.shape[1]
    heads = columns // HD
    quarter = width // groups
    padded = -(-heads // 8) * 8

    def vec(*shape, dtype=LOW):
        return pltpu.VMEM(shape, dtype)

    whole, of_heads, of_hidden, logs_shape = (span, width), (span, columns), (span, hidden), (members, padded, rows)
    own_attn = Parts(
        [w_qkv[0].reshape(3 * columns, width), w_out[0]],
        [(0, t * columns, columns, t * columns) for t in range(3)] + [(1, 0, columns, 3 * columns)],
    )
    own_feed = Parts(
        [w_gate_up[0].reshape(2 * hidden, width), w_down[0]],
        [(0, t * hidden, hidden, t * hidden) for t in range(2)] + [(1, 0, hidden, 2 * hidden)],
    )
    table = rope_tables(span, columns if columns % 128 else 128)

    def fetch_sems(block_):
        n = len(block_.parts)
        return [semaphores(k) for k in (n, n, groups * n, groups * n, len(block_.arrays))]

    row_block, attn_shape, feed_shape = ((rows, width), LOW), ((4 * columns, width), LOW), ((3 * hidden, width), LOW)
    kept_shapes = [row_block, ((rows, width), F32), (whole, LOW)] + [(of_heads, LOW)] * 4 + [(logs_shape, F32)]
    kept_shapes += [(whole, LOW)] + [(of_hidden, LOW)] * 3 + [attn_shape, feed_shape]
    flops = 8 * span * width * columns + 4 * span * span * columns + 6 * span * width * hidden
    placed_shape = ((2, rows, width), LOW)
    gains, square0, square1, placed0, *kept = call(
        functools.partial(forward_kernel, attn_block=own_attn, feed_block=own_feed),
        chips,
        0,
        2 * flops,
        lengths=lengths,
        args=[gain_attn, gain_ffn],
        far_args=[table, tokens[:, 0], cotangent[:, 0], *own_attn.arrays, *own_feed.arrays],
        outs=[((4, width), F32)] + [((1, columns), F32)] * 2,
        far_outs=[placed_shape],
        drained=kept_shapes * 2 + [row_block, (whole, LOW)],
        scratch=[
            vec(2, width, dtype=F32), vec(2, width, dtype=F32), vec(*table.shape[1:], dtype=F32), vec(*table.shape[1:], dtype=F32), semaphores(10),
            *(fetch_sems(own_attn) + fetch_sems(own_feed)) * 2,
            *gather_scratch(chips, rows) * 5, semaphores(1), semaphores(2), *reduce_scratch(chips, rows, width),
        ],
        partners=Team.partners,
    )
    first, second = (dict(zip(KEPT, kept[at : at + len(KEPT)])) for at in (0, len(KEPT)))
    y, top = kept[2 * len(KEPT) :]

    def back_args(layer):
        far_args = [layer[name] for name in ("gate", "up", "h2", "z", "w_feed", "k", "q", "log", "o", "m")]
        return far_args + [table, layer["h"], layer["x"], layer["w_attn"]]

    share_feed, share_attn = (3 * hidden, quarter), (4 * columns, quarter)
    n_moves = 2 * len(Spread.moves(groups))
    small = (8, width)
    sums, low_grad1, low_grad0, _, _, _, _, placed1, placed, *grads = call(
        back_kernel,
        chips,
        1,
        4 * flops,
        lengths=lengths,
        args=[gains, square0, square1],
        far_args=[second["x1"], first["x1"], top, y, *back_args(second), *back_args(first)],
        outs=[(small, F32), row_block, row_block],
        far_outs=[feed_shape, attn_shape] * 2
        + [placed_shape] * 2
        + [((n, width), LOW) for n in (2 * hidden, hidden, 3 * columns, columns)],
        drained=[],
        scratch=[
            *Backward.scratch(chips, rows, span, width),
            vec(*of_heads), *(vec(1, width, dtype=F32) for _ in range(4)), *gather_scratch(chips, rows) * 3,
            vec(2, *share_feed), vec(2, *share_attn),
            *(Scatter.scratch(feed_shape[0]) + Scatter.scratch(attn_shape[0])) * 2,
            *(semaphores(n) for n in (1, 2) * 7),
            *(semaphores(n) for n in (n_moves, n_moves, 2) * 2),
            *(vec(*lead, *small, dtype=F32) for lead in ((), (), (groups,), (members,))),
            *(semaphores(n) for n in (1, 1, groups - 1, groups - 1, members - 1, members - 1)),
        ],
        partners=Team.all_partners,
    )
    layer_out, input_grads, gain_one, gain_two, norm, *grads = finish(
        sums, [second["x"], y, placed0, placed1], [low_grad0, low_grad1, placed], grads, members
    )
    pair_sum, lower_sum, projection_sum, output_sum = grads
    return (
        layer_out[None, :, None],
        input_grads[None, :, None],
        gain_one,
        projection_sum.reshape(w_qkv.shape),
        output_sum[None],
        gain_two,
        pair_sum.reshape(w_gate_up.shape),
        lower_sum[None],
        norm.reshape(1),
    )


def solution(mesh):
    return jax.shard_map(
        local,
        mesh=mesh,
        in_specs=(
            P(None, "dp", "mp", None),
            P(None, "dp", "mp", None),
            P(None, "dp"),
            P("section", None),
            P("section", None, "mp", None),
            P("section", "mp", None),
            P("section", None),
            P("section", None, "mp", None),
            P("section", "mp", None),
        ),
        out_specs=(
            P("section", None, "dp", "mp", None),
            P("section", None, "dp", "mp", None),
            P("section", None),
            P("section", None, "mp", None),
            P("section", "mp", None),
            P("section", None),
            P("section", None, "mp", None),
            P("section", "mp", None),
            P("section"),
        ),
        check_vma=False,
    )
```
